32 devices in a mesh: rep: 2 (over y), head: 4 (over x, core), row: 4 (over z).
Axes of the slice: x: 2, y: 2, z: 4, core: 2. Of those that a mesh axis runs over, the one named last changes fastest.
Arguments:
- hidden: bfloat16 [256, 2, 8192], P(('rep', 'row'), None, 'head'), parts along dimension 0, may hold values from -6 to 6
- input_norm_scale: float32 [8192], P('head'), may hold values from 0.5 to 1.5
- projection_signal: bfloat16 [8192, 4096], P('row', 'head'), may hold values from -0.0625 to 0.0625
- projection_gate: bfloat16 [8192, 4096], P('row', 'head'), may hold values from -0.0625 to 0.0625
- projection_step: bfloat16 [8192, 64], P('row', 'head'), may hold values from -0.0625 to 0.0625
- projection_input_output: bfloat16 [8192, 256], P('row'), may hold values from -0.0625 to 0.0625
- step_bias: float32 [64], P('head'), may hold values from -4 to 0
- head_decay_rate: float32 [64], P('head'), may hold values from 0.5 to 16
- head_skip_weight: float32 [64], P('head'), may hold values from 0.5 to 1.5
- gated_norm_scale: float32 [4096], P('head'), may hold values from 0.5 to 1.5
- adapter_down_weight: bfloat16 [512, 8192, 16], P('row', 'head'), may hold values from -0.0625 to 0.0625
- adapter_up_weight: bfloat16 [512, 16, 4096], P('row', None, 'head'), may hold values from -1.5 to 1.5
- output_weight: bfloat16 [4096, 8192], P('head'), may hold values from -0.125 to 0.125
- scan_state: bfloat16 [256, 64, 64, 128], P(('rep', 'row'), 'head'), parts along dimension 0, may hold values from -6 to 6
- stream_tenant_index: int32 [256], P(('rep', 'row')), parts along dimension 0, may hold values from 0 to 511, as said below
- live_block_rows: int32 [8], P(('rep', 'row')), parts along dimension 0, may hold values from 1 to 32
Outputs:
- mixed: bfloat16 [256, 2, 8192], P(('rep', 'row'), None, 'head'), parts along dimension 0
- new_state: bfloat16 [256, 64, 64, 128], P(('rep', 'row'), 'head'), parts along dimension 0
The draws below stay inside these ranges and needn't reach their ends.
There are 2 independent parts, one for each index of `rep`. The reference program is written for one: setup_inputs(seed, part) draws one part's arguments, and reference() takes and returns one part's arrays. A program takes and returns all parts, laid end to end along the dimension named above; an argument that names none is the same for every part. Nothing has to cross between parts.
Inputs may be any that keep to these rules, and one draw needn't show every extreme that they name: `stream_tenant_index`: a stream of block b has a tenant of b * 128 up to (b + 1) * 128 - 1.
All inputs are finite; a program needn't handle non-finite values.
Results may differ from the reference program's by a relative error of at most 0.02.
Values may be sent and summed in bfloat16 or wider, within the bound.
No kernel may reach another device: no remote copies, remote signals or barrier semaphores. Data moves between devices by JAX's collectives and lax.ppermute only.
A program may use at most 128 MiB of HBM per device.

```python
import math
import jax
import jax.numpy as jnp
from jax import lax

MODEL_WIDTH = 8192
HEADS = 64
HEAD_P = 64
STATE_N = 128
ADAPTER_RANK = 16
ADAPTER_COUNT = 512
POS = 2
S_DEV = 32
STREAMS = 128
INNER_WIDTH = 4096
N_HEAD = 4


def draw_stream_tenant_index(key, part):
    key_low, key_high = jax.random.split(jax.random.fold_in(key, 11))
    blocks = STREAMS // S_DEV
    per_block = ADAPTER_COUNT // blocks
    first = jax.random.randint(key_low, (STREAMS,), 0, per_block)
    second = jax.random.randint(key_high, (STREAMS,), 0, per_block)
    local = jnp.minimum(first, second)
    block = jnp.arange(STREAMS) // S_DEV
    tenants = block * per_block + local
    tenants = tenants.at[0].set(0).at[STREAMS - 1].set(ADAPTER_COUNT - 1)
    return tenants.astype(jnp.int32)


def draw_live_block_rows(key, part):
    key_low, key_high = jax.random.split(jax.random.fold_in(key, 23))
    blocks = STREAMS // S_DEV
    counts = jax.random.randint(key_low, (blocks,), 1, S_DEV + 1)
    fullest = jax.random.randint(key_high, (), 0, blocks)
    counts = counts.at[fullest].set(S_DEV)
    return counts.astype(jnp.int32)


def spiked(values, own_key, source, target, blocks, factor):
    def block_of(axis_at):
        return (jnp.arange(values.shape[axis_at]) // (values.shape[axis_at] // blocks)).reshape((-1,) + (1,) * (values.ndim - 1 - axis_at))

    near = jax.random.permutation(own_key, blocks)[block_of(target)]
    far = (block_of(target) + blocks // 2) % blocks
    return jnp.where((block_of(source) == near) | (block_of(source) == far), factor * values, values)


def steps_of(key, extent, pieces, least, top_value):
    gain = 1.0
    for dim, shards_of in pieces:
        draws = jax.random.uniform(jax.random.fold_in(jax.random.fold_in(key, 6), dim), (shards_of,), jnp.float32, least / len(pieces), top_value / len(pieces))
        gain = gain * jnp.repeat(jnp.exp(draws), extent[dim] // shards_of).reshape((-1,) + (1,) * (len(extent) - 1 - dim))
    return gain


def centred(key, dims, width, limit, shards=(), dtype=jnp.bfloat16):
    loudness = steps_of(key, dims, shards, -0.22, 0.18) if shards else 1.0
    drawn = jax.random.normal(key, dims, jnp.float32) * width * loudness
    return jnp.minimum(jnp.maximum(drawn, -limit), limit).astype(dtype)


def noise_with(own_key, extent, scale, bound, cuts, heavy, kind=jnp.bfloat16):
    values = scale * jax.random.normal(own_key, extent, jnp.float32)
    if cuts:
        values = values * steps_of(own_key, extent, cuts, -0.22, 0.18)
    return jnp.clip(spiked(values, jax.random.fold_in(own_key, 3), *heavy), -bound, bound).astype(kind)


def setup_inputs(seed: int = 0, part: int = 0) -> dict:
    keys = jax.random.split(jax.random.key(seed), 17)
    part_splits = jax.random.split(jax.random.fold_in(keys[16], part), 17)
    return {
        "hidden": centred(part_splits[0], (STREAMS, POS, MODEL_WIDTH), 1.0, 6.0, ((0, 4), (2, 4))),
        "input_norm_scale": jnp.clip(1.0 + 0.1 * jax.random.normal(keys[1], (MODEL_WIDTH,), jnp.float32), 0.5, 1.5),
        "projection_signal": centred(keys[2], (MODEL_WIDTH, INNER_WIDTH), MODEL_WIDTH ** -0.5, 0.0625, ((0, 4), (1, 4))),
        "projection_gate": centred(keys[3], (MODEL_WIDTH, INNER_WIDTH), MODEL_WIDTH ** -0.5, 0.0625, ((0, 4), (1, 4))),
        "projection_step": centred(keys[4], (MODEL_WIDTH, HEADS), MODEL_WIDTH ** -0.5, 0.0625, ((0, 4), (1, 4))),
        "projection_input_output": centred(keys[5], (MODEL_WIDTH, 2 * STATE_N), MODEL_WIDTH ** -0.5, 0.0625, ((0, 4),)),
        "step_bias": jnp.clip(-4.0 + 4.0 * jax.random.uniform(keys[6], (HEADS,), jnp.float32) ** steps_of(keys[6], (HEADS,), ((0, 4),), -0.2, 0.2), -4.0, 0.0),
        "head_decay_rate": jnp.clip(jnp.exp(math.log(16.0) - 3.465736 * jax.random.uniform(keys[7], (HEADS,), jnp.float32) ** steps_of(keys[7], (HEADS,), ((0, 4),), -0.2, 0.2)), 0.5, 16.0),
        "head_skip_weight": jnp.clip(0.5 + 1.0 * jax.random.uniform(keys[8], (HEADS,), jnp.float32) ** steps_of(keys[8], (HEADS,), ((0, 4),), -0.2, 0.2), 0.5, 1.5),
        "gated_norm_scale": jnp.clip(1.0 + 0.1 * jax.random.normal(keys[9], (INNER_WIDTH,), jnp.float32), 0.5, 1.5),
        "adapter_down_weight": centred(keys[10], (ADAPTER_COUNT, MODEL_WIDTH, ADAPTER_RANK), MODEL_WIDTH ** -0.5, 0.0625, ((0, 4), (1, 4))),
        "adapter_up_weight": centred(keys[11], (ADAPTER_COUNT, ADAPTER_RANK, INNER_WIDTH), ADAPTER_RANK ** -0.5, 1.5, ((0, 4), (2, 4))),
        "output_weight": noise_with(keys[12], (INNER_WIDTH, MODEL_WIDTH), INNER_WIDTH ** -0.5, 0.125, ((0, 4),), (0, 1, 4, 2.0)),
        "scan_state": centred(part_splits[13], (STREAMS, HEADS, HEAD_P, STATE_N), 1.0, 6.0, ((0, 4), (1, 4))),
        "stream_tenant_index": draw_stream_tenant_index(jax.random.fold_in(jax.random.fold_in(keys[16], part), 71), part),
        "live_block_rows": draw_live_block_rows(jax.random.fold_in(jax.random.fold_in(keys[16], part), 71), part),
    }


def reference(hidden, input_norm_scale, projection_signal, projection_gate, projection_step, projection_input_output, step_bias, head_decay_rate, head_skip_weight, gated_norm_scale, adapter_down_weight, adapter_up_weight, output_weight, scan_state, stream_tenant_index, live_block_rows):
    epsilon = 1e-05
    wide = hidden.astype(jnp.float32)
    inverse = lax.rsqrt(lax.optimization_barrier(jnp.sum(wide * wide, -1)) / MODEL_WIDTH + epsilon)
    scaled = (wide * input_norm_scale).astype(jnp.bfloat16)
    down_weight_rows = adapter_down_weight[stream_tenant_index].astype(jnp.float32)
    lowrank = (jnp.einsum('spd,sdr->spr', scaled.astype(jnp.float32), down_weight_rows) * inverse[..., None]).astype(jnp.bfloat16)
    normed = (wide * input_norm_scale * inverse[..., None]).astype(jnp.bfloat16)
    flat = normed.reshape(STREAMS * POS, MODEL_WIDTH)
    xin = jnp.dot(flat, projection_signal, preferred_element_type=jnp.float32).reshape(STREAMS, POS, INNER_WIDTH)
    zin = jnp.dot(flat, projection_gate, preferred_element_type=jnp.float32).reshape(STREAMS, POS, INNER_WIDTH)
    dtin = jnp.dot(flat, projection_step, preferred_element_type=jnp.float32).reshape(STREAMS, POS, HEADS)
    bcin = jnp.dot(flat, projection_input_output, preferred_element_type=jnp.float32).reshape(STREAMS, POS, 2 * STATE_N)
    up_weight_rows = adapter_up_weight[stream_tenant_index].astype(jnp.float32)
    signal = jax.nn.silu(xin + jnp.einsum('spr,srk->spk', lowrank.astype(jnp.float32), up_weight_rows))
    bgate = jax.nn.silu(bcin[..., :STATE_N])
    cgate = jax.nn.silu(bcin[..., STATE_N:])
    steps_dt = jax.nn.softplus(dtin + step_bias)
    decay = jnp.exp(-steps_dt * head_decay_rate)
    index = jnp.arange(STREAMS)
    live = index % S_DEV < live_block_rows[index // S_DEV]
    signal_heads = signal.reshape(STREAMS, POS, HEADS, HEAD_P)

    def one_head(inputs):
        state_head, decay_head, dt_head, signal_head, skip_head = inputs
        carried = state_head.astype(jnp.float32)
        outputs = []
        for position in range(POS):
            updated = carried * decay_head[:, position, None, None] + (dt_head[:, position, None] * signal_head[:, position])[:, :, None] * bgate[:, position, None, :]
            carried = jnp.where(live[:, None, None], updated, carried)
            outputs.append(lax.optimization_barrier(jnp.sum(carried * cgate[:, position, None, :], -1)) + skip_head * signal_head[:, position])
        return (carried.astype(jnp.bfloat16), jnp.stack(outputs, 1))
    states, outputs = lax.map(one_head, (jnp.moveaxis(scan_state, 1, 0), jnp.moveaxis(decay, 2, 0), jnp.moveaxis(steps_dt, 2, 0), jnp.moveaxis(signal_heads, 2, 0), head_skip_weight))
    new_state = jnp.moveaxis(states, 0, 1)
    result = jnp.moveaxis(outputs, 0, 2).reshape(STREAMS, POS, INNER_WIDTH)
    gated = result * jax.nn.silu(zin)
    outnorm = (gated * lax.rsqrt(lax.optimization_barrier(jnp.mean(gated * gated, -1)) + epsilon)[..., None] * gated_norm_scale).astype(jnp.bfloat16)
    out_flat = outnorm.reshape(STREAMS * POS, INNER_WIDTH)
    group_width = INNER_WIDTH // N_HEAD
    total = jnp.zeros((STREAMS * POS, MODEL_WIDTH), jnp.float32)
    for group in range(N_HEAD):
        part = jnp.dot(out_flat[:, group * group_width:(group + 1) * group_width], output_weight[group * group_width:(group + 1) * group_width], preferred_element_type=jnp.float32).astype(jnp.bfloat16)
        part = lax.optimization_barrier(part)
        total = total + part.astype(jnp.float32)
    mixer = total.reshape(STREAMS, POS, MODEL_WIDTH)
    mixed = (wide + jnp.where(live[:, None, None], mixer, 0.0)).astype(jnp.bfloat16)
    return (mixed, new_state)
```

```python
import functools

import jax
import jax.numpy as jnp
from jax import lax
from jax.experimental import pallas as pl
from jax.experimental.pallas import tpu as pltpu
from jax.sharding import PartitionSpec as P

BF16 = jnp.bfloat16
F32 = jnp.float32
VMEM_GRANT = 24 * 1024 * 1024


def swap(values, axis, distance):
    size = lax.axis_size(axis)
    return lax.ppermute(values, axis, [(i, i ^ distance) for i in range(size)])


def bits_of(size):
    return [1 << i for i in range(size.bit_length() - 1)]


def sum_over(values, axis):
    for distance in bits_of(lax.axis_size(axis)):
        values = values + swap(values, axis, distance)
    return values


def gather_relative(block, axis):
    blocks = block[None]
    order = [0]
    for distance in reversed(bits_of(lax.axis_size(axis))):
        other = swap(blocks, axis, distance)
        blocks = jnp.concatenate([blocks, other], 0)
        order = order + [i ^ distance for i in order]
    return blocks, order


def params(**more):
    return pltpu.CompilerParams(vmem_limit_bytes=VMEM_GRANT, **more)


def cost(flops, size):
    return pl.CostEstimate(flops=int(flops), bytes_accessed=int(size), transcendentals=0)


def ordered_rows(index_ref, blocks_ref):
    count = blocks_ref.shape[0]
    return jnp.concatenate([blocks_ref[index_ref[k]] for k in range(count)], 0)


def put_parts(acc, send_ref, keep_ref, columns):
    rows = send_ref.shape[1]
    count = acc.shape[0] // rows
    for k in range(count):
        target = send_ref if k % 2 else keep_ref
        target[k // 2, :, columns] = acc[k * rows : (k + 1) * rows].astype(target.dtype)


def project_body(index_ref, blocks_ref, weight_ref, send_ref, keep_ref):
    lhs = ordered_rows(index_ref, blocks_ref)
    acc = jnp.dot(lhs, weight_ref[...], preferred_element_type=F32)
    put_parts(acc, send_ref, keep_ref, slice(None))


def project(index, blocks, weight):
    count, rows, depth = blocks.shape
    columns = weight.shape[1]
    tile = min(columns, 256)
    half = jax.ShapeDtypeStruct((count // 2, rows, columns), BF16)
    part = pl.BlockSpec((count // 2, rows, tile), lambda i, s: (0, 0, i))
    return pl.pallas_call(
        project_body,
        out_shape=(half, half),
        grid_spec=pltpu.PrefetchScalarGridSpec(
            num_scalar_prefetch=1,
            grid=(columns // tile,),
            in_specs=[
                pl.BlockSpec((count, rows, depth), lambda i, s: (0, 0, 0)),
                pl.BlockSpec((depth, tile), lambda i, s: (0, i)),
            ],
            out_specs=(part, part),
        ),
        compiler_params=params(),
        cost_estimate=cost(
            2 * count * rows * depth * columns, 2 * (depth * columns + count * rows * (depth + columns))
        ),
        name="project",
    )(index, blocks, weight)


def project_small_body(index_ref, blocks_ref, weight_ref, step_ref, send_ref, keep_ref):
    lhs = ordered_rows(index_ref, blocks_ref)
    width = weight_ref.shape[1]
    acc = jnp.dot(lhs, weight_ref[...], preferred_element_type=F32)
    put_parts(acc, send_ref, keep_ref, slice(0, width))
    acc = lax.dot_general(lhs, step_ref[...], (((1,), (1,)), ((), ())), preferred_element_type=F32)
    put_parts(acc, send_ref, keep_ref, slice(width, width + step_ref.shape[0]))


def project_small(index, blocks, weight, step_rows):
    count, rows, depth = blocks.shape
    columns = weight.shape[1] + step_rows.shape[0]
    half = jax.ShapeDtypeStruct((count // 2, rows, columns), BF16)
    whole = pl.BlockSpec(memory_space=pltpu.VMEM)
    return pl.pallas_call(
        project_small_body,
        out_shape=(half, half),
        in_specs=[pl.BlockSpec(memory_space=pltpu.SMEM), whole, whole, whole],
        out_specs=(whole, whole),
        compiler_params=params(),
        cost_estimate=cost(
            2 * count * rows * depth * columns, 2 * (depth * columns + count * rows * (depth + columns))
        ),
        name="project_small",
    )(index, blocks, weight, step_rows)


def scatter_rows(send, keep, axis):
    terms = None
    for distance in bits_of(lax.axis_size(axis)):
        other = swap(send, axis, distance)
        if keep.shape[0] == 1:
            return [t[0] for t in ([keep] if terms is None else terms) + [other]]
        if terms is None:
            terms = [keep]
        now = terms + [other]
        send = sum(t[1::2].astype(F32) for t in now).astype(BF16)
        terms = [t[0::2] for t in now]
        keep = terms[0]
    return [t[0] for t in terms]


def state_read_body(pairs_ref, state_ref, out_ref):
    group, heads, head, width = state_ref.shape
    for g in range(group):
        state = state_ref[g].reshape(heads * head, width)
        both = lax.dot_general(
            pairs_ref[g], state, (((1,), (1,)), ((), ())), preferred_element_type=F32
        )
        out_ref[0, g : g + 1, :] = both[0:1] + both[2:3]
        out_ref[1, g : g + 1, :] = both[1:2] + both[3:4]


def state_read(pairs, state):
    streams, heads, head, width = state.shape
    group = 8
    inner = heads * head
    return pl.pallas_call(
        state_read_body,
        out_shape=jax.ShapeDtypeStruct((2, streams, inner), F32),
        grid=(streams // group,),
        in_specs=[
            pl.BlockSpec((group, pairs.shape[1], width), lambda i: (i, 0, 0)),
            pl.BlockSpec((group, heads, head, width), lambda i: (i, 0, 0, 0)),
        ],
        out_specs=pl.BlockSpec((2, group, inner), lambda i: (0, i, 0)),
        compiler_params=params(),
        cost_estimate=cost(32 * state.size, 2 * state.size),
        name="state_read",
    )(pairs, state)


def state_write_body(left_ref, right_ref, decay_ref, state_ref, out_ref):
    group, heads, head, width = state_ref.shape
    for g in range(group):
        outer = lax.dot_general(
            left_ref[g], right_ref[g], (((0,), (0,)), ((), ())), preferred_element_type=F32
        )
        scaled = state_ref[g].astype(F32) * decay_ref[g][:, None, :]
        out_ref[g] = (scaled + outer.reshape(heads, head, width)).astype(out_ref.dtype)


def state_write(left, right, decay, state):
    streams, heads, head, width = state.shape
    group = 4
    rank = left.shape[1]
    block = pl.BlockSpec((group, heads, head, width), lambda i: (i, 0, 0, 0))
    return pl.pallas_call(
        state_write_body,
        out_shape=jax.ShapeDtypeStruct(state.shape, state.dtype),
        grid=(streams // group,),
        in_specs=[
            pl.BlockSpec((group, rank, heads * head), lambda i: (i, 0, 0)),
            pl.BlockSpec((group, rank, width), lambda i: (i, 0, 0)),
            pl.BlockSpec((group, heads, width), lambda i: (i, 0, 0)),
            block,
        ],
        out_specs=block,
        compiler_params=params(),
        cost_estimate=cost(32 * state.size, 4 * state.size),
        name="state_write",
    )(left, right, decay, state)


def output_body(index_ref, lhs_ref, weight_ref, out_ref):
    out_ref[0] = jnp.dot(lhs_ref[...], weight_ref[...], preferred_element_type=F32).astype(out_ref.dtype)


def output_parts(index, lhs, weight, width):
    rows, depth = lhs.shape
    count = index.shape[0]
    tile = min(width, 512)
    tiles = width // tile
    return pl.pallas_call(
        output_body,
        out_shape=jax.ShapeDtypeStruct((count, rows, width), BF16),
        grid_spec=pltpu.PrefetchScalarGridSpec(
            num_scalar_prefetch=1,
            grid=(count, tiles),
            in_specs=[
                pl.BlockSpec((rows, depth), lambda j, t, s: (0, 0)),
                pl.BlockSpec((depth, tile), lambda j, t, s: (0, s[j] * tiles + t)),
            ],
            out_specs=pl.BlockSpec((1, rows, tile), lambda j, t, s: (j, 0, t)),
        ),
        compiler_params=params(),
        cost_estimate=cost(2 * rows * depth * width * count, 2 * depth * width * count),
        name="output_parts",
    )(index, lhs, weight)


def split(values):
    high = values.astype(BF16)
    return high, (values - high.astype(F32)).astype(BF16)


def on_device(
    hidden,
    input_norm_scale,
    projection_signal,
    projection_gate,
    projection_step,
    projection_input_output,
    step_bias,
    head_decay_rate,
    head_skip_weight,
    gated_norm_scale,
    adapter_down_weight,
    adapter_up_weight,
    output_weight,
    scan_state,
    stream_tenant_index,
    live_block_rows,
):
    epsilon = 1e-05
    streams, positions, feature_width = hidden.shape
    rows = streams * positions
    heads_n = lax.axis_size("head")
    rows_n = lax.axis_size("row")
    model_width = feature_width * heads_n
    depth, inner = projection_signal.shape
    inner_width = inner * heads_n
    heads_here = projection_step.shape[1]
    state_width = projection_input_output.shape[1] // 2
    head_at = lax.axis_index("head")
    row_at = lax.axis_index("row")

    wide = jnp.swapaxes(hidden, 0, 1).astype(F32)
    scaled = (wide * input_norm_scale).astype(BF16)
    scaled_flat = scaled.reshape(rows, feature_width)

    steps = jnp.arange(rows_n, dtype=jnp.int32)
    if heads_n == rows_n:
        turned = lax.ppermute(
            scaled_flat,
            ("head", "row"),
            [(h * rows_n + r, r * rows_n + h) for h in range(heads_n) for r in range(rows_n)],
        )
        blocks, order = gather_relative(turned, "head")
        place = jnp.asarray([order.index(i) for i in range(heads_n)], jnp.int32)
        index = place[head_at ^ row_at ^ steps]
    else:
        features = lax.all_gather(scaled_flat, "head", axis=1, tiled=True)
        blocks = lax.all_to_all(features, "row", split_axis=1, concat_axis=0, tiled=True)
        blocks = blocks.reshape(rows_n, rows, depth)
        index = row_at ^ steps

    small = project_small(index, blocks, projection_input_output, projection_step.T)
    small_terms = scatter_rows(*small, "row")
    signal_terms = scatter_rows(*project(index, blocks, projection_signal), "row")
    gate_terms = scatter_rows(*project(index, blocks, projection_gate), "row")

    tenant_local = stream_tenant_index - row_at * adapter_down_weight.shape[0]
    down_weight_rows = jnp.take(adapter_down_weight, tenant_local, axis=0)
    square_part = jnp.sum(wide * wide, -1)
    lowrank_part = jnp.einsum(
        "psd,sdr->psr", scaled, down_weight_rows, preferred_element_type=F32
    )
    sums = sum_over(jnp.concatenate([lowrank_part, square_part[..., None]], -1), "head")
    inverse = lax.rsqrt(sums[..., -1:] / model_width + epsilon)
    lowrank = (sums[..., :-1] * inverse).astype(BF16)
    up_weight_rows = jnp.take(adapter_up_weight, tenant_local, axis=0)
    adapted = jnp.einsum("psr,srk->psk", lowrank, up_weight_rows, preferred_element_type=F32)

    def total(terms):
        whole = sum(t.astype(F32) for t in terms)
        return whole.reshape(positions, streams, -1) * inverse

    small_in = total(small_terms)
    gates = jax.nn.silu(small_in[..., : 2 * state_width])
    bgate = gates[..., :state_width]
    cgate = gates[..., state_width:]
    live = jnp.arange(streams) < live_block_rows[0]
    steps_dt = jax.nn.softplus(small_in[..., 2 * state_width :] + step_bias)
    decay = jnp.where(live[:, None], jnp.exp(-steps_dt * head_decay_rate), 1.0)
    fed = jnp.where(live[:, None], steps_dt, 0.0)

    c_high, c_low = split(jnp.swapaxes(cgate, 0, 1))
    b_high, b_low = split(jnp.swapaxes(bgate, 0, 1))
    zero = jnp.zeros_like(c_high)
    read = state_read(jnp.concatenate([c_high, c_low, zero, zero], 1), scan_state)

    def expand(values):
        spread = jnp.broadcast_to(values[..., None], values.shape + (inner // heads_here,))
        return spread.reshape(values.shape[:-1] + (inner,))

    def inner_product(b, c):
        return jnp.sum(bgate[b] * cgate[c], -1, keepdims=True)

    both = decay[0] * decay[1]
    late = decay[1] * fed[0]
    base0 = expand(decay[0]) * read[0]
    base1 = expand(both) * read[1]
    own0 = expand(fed[0] * inner_product(0, 0) + head_skip_weight)
    own1 = expand(fed[1] * inner_product(1, 1) + head_skip_weight)
    cross = expand(late * inner_product(0, 1))
    feed0 = expand(late)
    feed1 = expand(fed[1])

    signal = jax.nn.silu(total(signal_terms) + adapted)
    result = jnp.stack([base0 + own0 * signal[0], base1 + cross * signal[0] + own1 * signal[1]])
    gated = result * jax.nn.silu(total(gate_terms))
    gate_squares = sum_over(jnp.sum(gated * gated, -1), "head")
    out_lhs = (gated * gated_norm_scale).astype(BF16).reshape(rows, inner)

    distances = jnp.arange(heads_n, dtype=jnp.int32) ^ head_at
    odd = output_parts(distances[1::2], out_lhs, output_weight, feature_width)
    even = output_parts(distances[0::2], out_lhs, output_weight, feature_width)
    mixer = sum(t.astype(F32) for t in scatter_rows(odd, even, "head"))
    mixer = mixer.reshape(positions, streams, feature_width)
    mixer = mixer * lax.rsqrt(gate_squares / inner_width + epsilon)[..., None]
    mixed = (wide + jnp.where(live[:, None], mixer, 0.0)).astype(BF16)

    feeds = jnp.stack([feed0 * signal[0], feed1 * signal[1]], 1)
    f_high, f_low = split(feeds)
    left = jnp.concatenate([f_high, f_low, f_high, jnp.zeros_like(f_high)], 1)
    right = jnp.concatenate([b_high, b_high, b_low, zero], 1)
    spread = jnp.broadcast_to(both[..., None], both.shape + (state_width,))
    new_state = state_write(left, right, spread, scan_state)
    return (jnp.swapaxes(mixed, 0, 1), new_state)


def solution(mesh):
    in_specs = (
        P(("rep", "row"), None, "head"),
        P("head"),
        P("row", "head"),
        P("row", "head"),
        P("row", "head"),
        P("row", None),
        P("head"),
        P("head"),
        P("head"),
        P("head"),
        P("row", "head", None),
        P("row", None, "head"),
        P("head", None),
        P(("rep", "row"), "head", None, None),
        P(("rep", "row")),
        P(("rep", "row")),
    )
    out_specs = (P(("rep", "row"), None, "head"), P(("rep", "row"), "head", None, None))
    return jax.shard_map(
        on_device, mesh=mesh, in_specs=in_specs, out_specs=out_specs, check_vma=False
    )
```

```python
import functools

import jax
import jax.numpy as jnp
from jax import lax
from jax.experimental import pallas as pl
from jax.experimental.pallas import tpu as pltpu
from jax.sharding import PartitionSpec as P

BF16 = jnp.bfloat16
F32 = jnp.float32
VMEM_GRANT = 24 * 1024 * 1024


def swap(values, axis, distance):
    size = lax.axis_size(axis)
    return lax.ppermute(values, axis, [(i, i ^ distance) for i in range(size)])


def bits_of(size):
    return [1 << i for i in range(size.bit_length() - 1)]


def sum_over(values, axis):
    for distance in bits_of(lax.axis_size(axis)):
        values = values + swap(values, axis, distance)
    return values


def reverse_bits(value, size):
    result = 0
    for distance in bits_of(size):
        result = result * 2 + (1 if value & distance else 0)
    return result


def gather_relative(block, axis):
    blocks, order = [block], [0]
    for distance in reversed(bits_of(lax.axis_size(axis))):
        blocks = blocks + [swap(b, axis, distance) for b in blocks]
        order = order + [i ^ distance for i in order]
    return blocks, order


def params(**more):
    return pltpu.CompilerParams(vmem_limit_bytes=VMEM_GRANT, **more)


def cost(flops, size):
    return pl.CostEstimate(flops=int(flops), bytes_accessed=int(size), transcendentals=0)


def in_hbm(values):
    return pltpu.with_memory_space_constraint(values, pltpu.HBM)


def project_body(count, tile, small, index_ref, *refs):
    blocks = refs[:count]
    weights = refs[count : count + 1 + 2 * small]
    send_ref, keep_ref, lhs, *scratch = refs[count + 1 + 2 * small :]
    held, semaphores = scratch[:-1], scratch[-1]
    rows = blocks[0].shape[0]
    columns = weights[0].shape[1]
    copies = []
    for i in range(count):
        at = pl.multiple_of(index_ref[i] * rows, rows)
        copies.append(
            pltpu.make_async_copy(blocks[i], lhs.at[pl.ds(at, rows), :], semaphores.at[i])
        )
    tiles = columns // tile
    for t in range(tiles):
        copies.append(
            pltpu.make_async_copy(
                weights[0].at[:, pl.ds(t * tile, tile)], held[0].at[t], semaphores.at[count + t]
            )
        )
    for i in range(2 * small):
        copies.append(
            pltpu.make_async_copy(weights[1 + i], held[1 + i], semaphores.at[count + tiles + i])
        )
    for copy in copies:
        copy.start()

    def put(acc, start):
        for k in range(count):
            target = send_ref if k % 2 else keep_ref
            target[k // 2, :, start : start + acc.shape[1]] = acc[
                k * rows : (k + 1) * rows
            ].astype(target.dtype)

    for copy in copies[:count]:
        copy.wait()
    for t in range(tiles):
        copies[count + t].wait()
        put(jnp.dot(lhs[...], held[0][t], preferred_element_type=F32), t * tile)
    if small:
        for copy in copies[count + tiles :]:
            copy.wait()
        put(jnp.dot(lhs[...], held[1][...], preferred_element_type=F32), columns)
        put(
            lax.dot_general(
                lhs[...], held[2][...], (((1,), (1,)), ((), ())), preferred_element_type=F32
            ),
            columns + held[1].shape[1],
        )


def project(index, blocks, weight, *small):
    count = len(blocks)
    rows, depth = blocks[0].shape
    columns = weight.shape[1]
    tile = min(columns, 256)
    wide = columns
    held = [pltpu.VMEM((columns // tile, depth, tile), BF16)]
    if small:
        wide += small[0].shape[1] + small[1].shape[0]
        held += [pltpu.VMEM(w.shape, BF16) for w in small]
    half = jax.ShapeDtypeStruct((count // 2, rows, wide), BF16)
    anywhere = pl.BlockSpec(memory_space=pl.ANY)
    whole = pl.BlockSpec(memory_space=pltpu.VMEM)
    return pl.pallas_call(
        functools.partial(project_body, count, tile, len(small) // 2),
        out_shape=(half, half),
        in_specs=[pl.BlockSpec(memory_space=pltpu.SMEM)] + [anywhere] * (count + 1 + len(small)),
        out_specs=(whole, whole),
        scratch_shapes=[pltpu.VMEM((count * rows, depth), BF16)]
        + held
        + [pltpu.SemaphoreType.DMA((count + columns // tile + len(small),))],
        compiler_params=params(),
        cost_estimate=cost(
            2 * count * rows * depth * wide, 2 * (depth * wide + count * rows * (depth + wide))
        ),
        name="project_signal" if small else "project_gate",
    )(index, *blocks, in_hbm(weight), *[in_hbm(w) for w in small])


def scatter_rows(send, keep, axis):
    terms = None
    for distance in bits_of(lax.axis_size(axis)):
        other = swap(send, axis, distance)
        if keep.shape[0] == 1:
            return [t[0] for t in ([keep] if terms is None else terms) + [other]]
        if terms is None:
            terms = [keep]
        now = terms + [other]
        send = sum(t[1::2].astype(F32) for t in now).astype(BF16)
        terms = [t[0::2] for t in now]
        keep = terms[0]
    return [t[0] for t in terms]


def softplus(values):
    return jnp.maximum(values, 0.0) + jnp.log1p(jnp.exp(-jnp.abs(values)))


def silu(values):
    return values / (1.0 + jnp.exp(-values))


def recur_body(
    terms,
    group,
    live_ref,
    *refs,
):
    term_refs = refs[:terms]
    inverse_ref, adapted_ref, bias_ref, rate_ref, skip_ref, state_ref = refs[terms : terms + 6]
    result_ref, feeds_ref, b_ref, both_ref, c_ref, read_ref, spread_ref, signal_ref = refs[terms + 6 :]
    _, heads, head, width = state_ref.shape
    streams, inner = feeds_ref.shape[1:]
    step = pl.program_id(0)

    @pl.when(step == 0)
    def _():
        total = sum(t[...].astype(F32) for t in term_refs) * inverse_ref[...]
        signal_ref[...] = silu(total[:, :inner] + adapted_ref[...])
        gates = silu(total[:, inner : inner + 2 * width])
        steps_dt = softplus(total[:, inner + 2 * width :] + bias_ref[...])
        b = [gates[p * streams : (p + 1) * streams, :width] for p in range(2)]
        c = [gates[p * streams : (p + 1) * streams, width:] for p in range(2)]
        for p in range(2):
            b_ref[p] = b[p]
            c_ref[p] = c[p]
        live = lax.broadcasted_iota(jnp.int32, (streams, heads), 0) < live_ref[0]
        dt = [steps_dt[p * streams : (p + 1) * streams] for p in range(2)]
        decay = [jnp.where(live, jnp.exp(-d * rate_ref[...]), 1.0) for d in dt]
        fed = [jnp.where(live, d, 0.0) for d in dt]

        def match(i, j):
            return jnp.sum(b[i] * c[j], -1, keepdims=True)

        both = decay[0] * decay[1]
        both_ref[...] = both
        late = decay[1] * fed[0]
        skip = skip_ref[...]
        factors = jnp.concatenate(
            [
                decay[0],
                both,
                fed[0] * match(0, 0) + skip,
                fed[1] * match(1, 1) + skip,
                late * match(0, 1),
                late,
                fed[1],
            ],
            0,
        )
        high, low = split(factors)
        place = lax.broadcasted_iota(jnp.int32, (heads, inner), 1) // head
        ones = (place == lax.broadcasted_iota(jnp.int32, (heads, inner), 0)).astype(BF16)
        spread_ref[...] = jnp.dot(high, ones, preferred_element_type=F32) + jnp.dot(
            low, ones, preferred_element_type=F32
        )

    at = pl.multiple_of(step * group, group)
    c = jnp.concatenate([c_ref[p, pl.ds(at, group), :] for p in range(2)], 0)
    lhs = jnp.concatenate(split(c), 0)
    for g in range(group):
        state = state_ref[g].reshape(inner, width)
        found = lax.dot_general(lhs, state, (((1,), (1,)), ((), ())), preferred_element_type=F32)
        for p in range(2):
            row = p * group + g
            low = 2 * group + row
            read_ref[p, pl.ds(at + g, 1), :] = found[row : row + 1] + found[low : low + 1]

    @pl.when(step == pl.num_programs(0) - 1)
    def _():
        factor = [spread_ref[i * streams : (i + 1) * streams, :] for i in range(7)]
        first = signal_ref[:streams, :]
        second = signal_ref[streams:, :]
        result_ref[:streams, :] = factor[0] * read_ref[0] + factor[2] * first
        result_ref[streams:, :] = factor[1] * read_ref[1] + factor[4] * first + factor[3] * second
        feeds_ref[0] = factor[5] * first
        feeds_ref[1] = factor[6] * second


def recur(live_rows, terms, inverse, adapted, bias, rate, skip, state):
    streams, heads, head, width = state.shape
    group = 8
    inner = heads * head
    rows = 2 * streams
    whole = pl.BlockSpec(memory_space=pltpu.VMEM)
    return pl.pallas_call(
        functools.partial(recur_body, len(terms), group),
        out_shape=(
            jax.ShapeDtypeStruct((rows, inner), F32),
            jax.ShapeDtypeStruct((2, streams, inner), F32),
            jax.ShapeDtypeStruct((2, streams, width), F32),
            jax.ShapeDtypeStruct((streams, heads), F32),
        ),
        grid=(streams // group,),
        in_specs=[pl.BlockSpec(memory_space=pltpu.SMEM)]
        + [whole] * (len(terms) + 5)
        + [pl.BlockSpec((group, heads, head, width), lambda i: (i, 0, 0, 0))],
        out_specs=(whole, whole, whole, whole),
        scratch_shapes=[
            pltpu.VMEM((2, streams, width), F32),
            pltpu.VMEM((2, streams, inner), F32),
            pltpu.VMEM((7 * streams, inner), F32),
            pltpu.VMEM((rows, inner), F32),
        ],
        compiler_params=params(),
        cost_estimate=cost(64 * state.size, 2 * state.size + 32 * rows * inner),
        name="recur",
    )(
        live_rows,
        *terms,
        inverse,
        adapted,
        bias[None],
        rate[None],
        skip[None],
        in_hbm(state),
    )


def state_write_body(left_ref, right_ref, decay_ref, state_ref, out_ref):
    group, heads, head, width = state_ref.shape
    for g in range(group):
        outer = lax.dot_general(
            left_ref[g], right_ref[g], (((0,), (0,)), ((), ())), preferred_element_type=F32
        )
        scaled = state_ref[g].astype(F32) * decay_ref[g][:, None, :]
        out_ref[g] = (scaled + outer.reshape(heads, head, width)).astype(out_ref.dtype)


def state_write(left, right, decay, state):
    streams, heads, head, width = state.shape
    group = 4
    rank = left.shape[1]
    block = pl.BlockSpec((group, heads, head, width), lambda i: (i, 0, 0, 0))
    return pl.pallas_call(
        state_write_body,
        out_shape=jax.ShapeDtypeStruct(state.shape, state.dtype),
        grid=(streams // group,),
        in_specs=[
            pl.BlockSpec((group, rank, heads * head), lambda i: (i, 0, 0)),
            pl.BlockSpec((group, rank, width), lambda i: (i, 0, 0)),
            pl.BlockSpec((group, heads, width), lambda i: (i, 0, 0)),
            block,
        ],
        out_specs=block,
        compiler_params=params(),
        cost_estimate=cost(32 * state.size, 4 * state.size),
        name="state_write",
    )(left, right, decay, in_hbm(state))


def output_first_body(terms, index_ref, *refs):
    term_refs = refs[:terms]
    inverse_ref, result_ref, scale_ref, weight_ref, out_ref, lhs_ref, squares_ref = refs[terms:]

    @pl.when((pl.program_id(0) == 0) & (pl.program_id(1) == 0))
    def _():
        total = sum(t[...].astype(F32) for t in term_refs) * inverse_ref[...]
        gated = result_ref[...] * silu(total)
        squares_ref[...] = jnp.sum(gated * gated, -1, keepdims=True)
        lhs_ref[...] = (gated * scale_ref[...]).astype(lhs_ref.dtype)

    out_ref[0] = jnp.dot(lhs_ref[...], weight_ref[...], preferred_element_type=F32).astype(out_ref.dtype)


def output_second_body(index_ref, lhs_ref, weight_ref, out_ref):
    out_ref[0] = jnp.dot(lhs_ref[...], weight_ref[...], preferred_element_type=F32).astype(out_ref.dtype)


def output_parts(index, weight, width, operands, first):
    rows, depth = operands[-1].shape if not first else operands[0].shape
    count = index.shape[0]
    tile = min(width, 1024)
    tiles = width // tile
    whole = pl.BlockSpec(memory_space=pltpu.VMEM)
    out_shape = [jax.ShapeDtypeStruct((count, rows, width), BF16)]
    out_specs = [pl.BlockSpec((1, rows, tile), lambda j, t, s: (j, 0, t))]
    if first:
        out_shape += [
            jax.ShapeDtypeStruct((rows, depth), BF16),
            jax.ShapeDtypeStruct((rows, 1), F32),
        ]
        out_specs += [whole, whole]
    return pl.pallas_call(
        functools.partial(output_first_body, len(operands) - 3) if first else output_second_body,
        out_shape=tuple(out_shape),
        grid_spec=pltpu.PrefetchScalarGridSpec(
            num_scalar_prefetch=1,
            grid=(count, tiles),
            in_specs=[whole] * len(operands)
            + [pl.BlockSpec((depth, tile), lambda j, t, s: (0, s[j] * tiles + t))],
            out_specs=tuple(out_specs),
        ),
        compiler_params=params(),
        cost_estimate=cost(2 * rows * depth * width * count, 2 * depth * width * count),
        name="output_first" if first else "output_second",
    )(index, *operands, in_hbm(weight))


def split(values):
    high = values.astype(BF16)
    return high, (values - high.astype(F32)).astype(BF16)


def on_device(
    hidden,
    input_norm_scale,
    projection_signal,
    projection_gate,
    projection_step,
    projection_input_output,
    step_bias,
    head_decay_rate,
    head_skip_weight,
    gated_norm_scale,
    adapter_down_weight,
    adapter_up_weight,
    output_weight,
    scan_state,
    stream_tenant_index,
    live_block_rows,
):
    epsilon = 1e-05
    streams, positions, feature_width = hidden.shape
    rows = streams * positions
    heads_n = lax.axis_size("head")
    rows_n = lax.axis_size("row")
    model_width = feature_width * heads_n
    depth, inner = projection_signal.shape
    inner_width = inner * heads_n
    heads_here = projection_step.shape[1]
    head_at = lax.axis_index("head")
    row_at = lax.axis_index("row")

    wide = jnp.swapaxes(hidden, 0, 1).astype(F32)
    scaled = (wide * input_norm_scale).astype(BF16)
    scaled_flat = scaled.reshape(rows, feature_width)

    if heads_n == rows_n:
        turned = lax.ppermute(
            scaled_flat,
            ("head", "row"),
            [
                (h * rows_n + r, reverse_bits(r, rows_n) * rows_n + h)
                for h in range(heads_n)
                for r in range(rows_n)
            ],
        )
        blocks, order = gather_relative(turned, "head")
        owner = jnp.asarray([reverse_bits(i, rows_n) for i in range(rows_n)], jnp.int32)
        index = owner[head_at ^ jnp.asarray(order, jnp.int32)] ^ row_at
    else:
        features = lax.all_gather(scaled_flat, "head", axis=1, tiled=True)
        blocks = lax.all_to_all(features, "row", split_axis=1, concat_axis=0, tiled=True)
        blocks = blocks.reshape(rows_n, rows, depth)
        blocks = [blocks[i] for i in range(rows_n)]
        index = jnp.arange(rows_n, dtype=jnp.int32) ^ row_at

    signal_parts = project(index, blocks, projection_signal, projection_input_output, projection_step.T)
    signal_terms = scatter_rows(*signal_parts, "row")
    gate_terms = scatter_rows(*project(index, blocks, projection_gate), "row")

    tenant_local = stream_tenant_index - row_at * adapter_down_weight.shape[0]
    down_weight_rows = jnp.take(adapter_down_weight, tenant_local, axis=0)
    square_part = jnp.sum(wide * wide, -1)
    lowrank_part = jnp.einsum(
        "psd,sdr->psr", scaled, down_weight_rows, preferred_element_type=F32
    )
    sums = sum_over(
        jnp.concatenate([lowrank_part, square_part[..., None]], -1).reshape(rows, -1), "head"
    )
    inverse = lax.rsqrt(sums[:, -1:] / model_width + epsilon)
    lowrank = (sums[:, :-1] * inverse).astype(BF16).reshape(positions, streams, -1)
    up_weight_rows = jnp.take(adapter_up_weight, tenant_local, axis=0)
    adapted = jnp.einsum("psr,srk->psk", lowrank, up_weight_rows, preferred_element_type=F32)

    result, feeds, bgate, both = recur(
        live_block_rows,
        signal_terms,
        inverse,
        adapted.reshape(rows, inner),
        step_bias,
        head_decay_rate,
        head_skip_weight,
        scan_state,
    )

    distances = jnp.arange(heads_n, dtype=jnp.int32) ^ head_at
    odd, out_lhs, gate_squares = output_parts(
        distances[1::2],
        output_weight,
        feature_width,
        [*gate_terms, inverse, result, gated_norm_scale[None]],
        True,
    )
    (even,) = output_parts(distances[0::2], output_weight, feature_width, [out_lhs], False)
    gate_squares = sum_over(gate_squares, "head")
    mixer = sum(t.astype(F32) for t in scatter_rows(odd, even, "head"))
    mixer = mixer * lax.rsqrt(gate_squares / inner_width + epsilon)
    mixer = mixer.reshape(positions, streams, feature_width)
    live = jnp.arange(streams) < live_block_rows[0]
    mixed = (wide + jnp.where(live[:, None], mixer, 0.0)).astype(BF16)

    b_high, b_low = split(jnp.swapaxes(bgate, 0, 1))
    f_high, f_low = split(jnp.swapaxes(feeds, 0, 1))
    left = jnp.concatenate([f_high, f_low, f_high, jnp.zeros_like(f_high)], 1)
    right = jnp.concatenate([b_high, b_high, b_low, jnp.zeros_like(b_high)], 1)
    spread = jnp.broadcast_to(both[..., None], both.shape + (bgate.shape[-1],))
    new_state = state_write(left, right, spread, scan_state)
    return (jnp.swapaxes(mixed, 0, 1), new_state)


def solution(mesh):
    in_specs = (
        P(("rep", "row"), None, "head"),
        P("head"),
        P("row", "head"),
        P("row", "head"),
        P("row", "head"),
        P("row", None),
        P("head"),
        P("head"),
        P("head"),
        P("head"),
        P("row", "head", None),
        P("row", None, "head"),
        P("head", None),
        P(("rep", "row"), "head", None, None),
        P(("rep", "row")),
        P(("rep", "row")),
    )
    out_specs = (P(("rep", "row"), None, "head"), P(("rep", "row"), "head", None, None))
    return jax.shard_map(
        on_device, mesh=mesh, in_specs=in_specs, out_specs=out_specs, check_vma=False
    )
```

```python
import functools

import jax
import jax.numpy as jnp
from jax import lax
from jax.experimental import pallas as pl
from jax.experimental.pallas import tpu as pltpu
from jax.sharding import PartitionSpec as P

BF16 = jnp.bfloat16
F32 = jnp.float32
VMEM_GRANT = 12 * 1024 * 1024


def swap(values, axis, distance):
    size = lax.axis_size(axis)
    return lax.ppermute(values, axis, [(i, i ^ distance) for i in range(size)])


def bits_of(size):
    return [1 << i for i in range(size.bit_length() - 1)]


def sum_over(values, axis):
    for distance in bits_of(lax.axis_size(axis)):
        values = values + swap(values, axis, distance)
    return values


def reverse_bits(value, size):
    result = 0
    for distance in bits_of(size):
        result = result * 2 + (1 if value & distance else 0)
    return result


def gather_relative(block, axis, beside):
    distances = list(reversed(bits_of(lax.axis_size(axis))))
    blocks, order = [block, swap(block, axis, distances[0])], [0, distances[0]]
    extra = beside(block)
    own = extra[0]
    for distance in distances[1:]:
        blocks = blocks + [swap(b, axis, distance) for b in [own] + blocks[1:]]
        order = order + [i ^ distance for i in order]
    return blocks, order, extra[1:]


def params(**more):
    return pltpu.CompilerParams(vmem_limit_bytes=VMEM_GRANT, **more)


def cost(flops, size):
    return pl.CostEstimate(flops=int(flops), bytes_accessed=int(size), transcendentals=0)


def in_hbm(values):
    return pltpu.with_memory_space_constraint(values, pltpu.HBM)


def load_body(pieces, after_ref, *refs):
    count = len(pieces)
    sources, targets, semaphores = refs[:count], refs[count : 2 * count], refs[2 * count]
    copies = []
    for source, target, parts in zip(sources, targets, pieces):
        step = source.shape[0] // parts
        for i in range(parts):
            at = pl.ds(i * step, step)
            copies.append(
                pltpu.make_async_copy(source.at[at], target.at[at], semaphores.at[len(copies)])
            )
    for copy in copies:
        copy.start()
    for copy in copies:
        copy.wait()


def load(after, passed, *weights):
    arrays = (passed, *weights)
    pieces = [1] + [8 if w.shape[0] % 128 == 0 else 1 for w in weights]
    size = sum(a.size * a.dtype.itemsize for a in arrays)
    return pl.pallas_call(
        functools.partial(load_body, pieces),
        out_shape=tuple(pltpu.VMEM(a.shape, a.dtype) for a in arrays),
        in_specs=[pl.BlockSpec(memory_space=pl.ANY)] * (1 + len(arrays)),
        out_specs=tuple(pl.BlockSpec(memory_space=pltpu.VMEM) for _ in arrays),
        scratch_shapes=[pltpu.SemaphoreType.DMA((sum(pieces),))],
        compiler_params=params(),
        cost_estimate=cost(0, 2 * size),
        name="load",
    )(after, passed, *[in_hbm(w) for w in weights])


def fill_rows(index_ref, blocks, lhs, semaphores):
    rows = blocks[0].shape[0]
    copies = []
    for i, block in enumerate(blocks):
        at = pl.multiple_of(index_ref[i] * rows, rows)
        copies.append(pltpu.make_async_copy(block, lhs.at[pl.ds(at, rows), :], semaphores.at[i]))
    for copy in copies:
        copy.start()
    for copy in copies:
        copy.wait()


def put_parts(acc, start, send_ref, keep_ref):
    rows = send_ref.shape[1]
    for k in range(acc.shape[0] // rows):
        target = send_ref if k % 2 else keep_ref
        target[k // 2, :, start : start + acc.shape[1]] = acc[k * rows : (k + 1) * rows].astype(
            target.dtype
        )


def project_signal_body(count, index_ref, *refs):
    blocks, refs = refs[:count], refs[count:]
    weight_ref, mix_ref, step_ref, send_ref, keep_ref, lhs_ref, semaphores = refs
    fill_rows(index_ref, blocks, lhs_ref, semaphores)
    lhs = lhs_ref[...]
    columns = weight_ref.shape[1]
    tile = min(columns, 512)
    for t in range(0, columns, tile):
        acc = jnp.dot(lhs, weight_ref[:, t : t + tile], preferred_element_type=F32)
        put_parts(acc, t, send_ref, keep_ref)
    acc = jnp.dot(lhs, mix_ref[...], preferred_element_type=F32)
    put_parts(acc, columns, send_ref, keep_ref)
    acc = lax.dot_general(lhs, step_ref[...], (((1,), (1,)), ((), ())), preferred_element_type=F32)
    put_parts(acc, columns + mix_ref.shape[1], send_ref, keep_ref)


def project_signal(index, blocks, weight, mix, step):
    count = len(blocks)
    rows, depth = blocks[0].shape
    columns = weight.shape[1] + mix.shape[1] + step.shape[0]
    half = jax.ShapeDtypeStruct((count // 2, rows, columns), BF16)
    whole = pl.BlockSpec(memory_space=pltpu.VMEM)
    return pl.pallas_call(
        functools.partial(project_signal_body, count),
        out_shape=(half, half, jax.ShapeDtypeStruct((count * rows, depth), BF16)),
        in_specs=[pl.BlockSpec(memory_space=pltpu.SMEM)]
        + [pl.BlockSpec(memory_space=pl.ANY)] * count
        + [whole] * 3,
        out_specs=(whole,) * 3,
        scratch_shapes=[pltpu.SemaphoreType.DMA((count,))],
        compiler_params=params(),
        cost_estimate=cost(2 * count * rows * depth * columns, 2 * depth * columns),
        name="project_signal",
    )(index, *blocks, weight, mix, step)


def project_gate_body(lhs_ref, weight_ref, sums_ref, after_ref, send_ref, keep_ref, out_ref):
    columns = weight_ref.shape[1]
    tile = min(columns, 512)
    for t in range(0, columns, tile):
        acc = jnp.dot(lhs_ref[...], weight_ref[:, t : t + tile], preferred_element_type=F32)
        put_parts(acc, t, send_ref, keep_ref)
    out_ref[...] = sums_ref[...]


def project_gate(rows, lhs, weight, sums, after):
    count = lhs.shape[0] // rows
    columns = weight.shape[1]
    half = jax.ShapeDtypeStruct((count // 2, rows, columns), BF16)
    whole = pl.BlockSpec(memory_space=pltpu.VMEM)
    return pl.pallas_call(
        project_gate_body,
        out_shape=(half, half, jax.ShapeDtypeStruct(sums.shape, sums.dtype)),
        in_specs=[whole, whole, whole, pl.BlockSpec(memory_space=pl.ANY)],
        out_specs=(whole,) * 3,
        compiler_params=params(),
        cost_estimate=cost(2 * lhs.size * columns, 2 * weight.size),
        name="project_gate",
    )(lhs, weight, sums, after)


def merge_body(terms, *refs):
    out_ref = refs[-1]
    for i in range(out_ref.shape[0]):
        total = sum(t[2 * i + 1].astype(F32) for t in refs[:terms])
        out_ref[i] = total.astype(out_ref.dtype)


def merge(terms, after):
    count, rows, columns = terms[0].shape
    whole = pl.BlockSpec(memory_space=pltpu.VMEM)
    return pl.pallas_call(
        functools.partial(merge_body, len(terms)),
        out_shape=jax.ShapeDtypeStruct((count // 2, rows, columns), BF16),
        in_specs=[whole] * len(terms) + [pl.BlockSpec(memory_space=pl.ANY)],
        out_specs=whole,
        compiler_params=params(),
        cost_estimate=cost(terms[0].size, 4 * terms[0].size),
        name="merge",
    )(*terms, after)


def scatter_rows(send, keep, axis, after=None):
    terms = [keep]
    for distance in bits_of(lax.axis_size(axis)):
        other = swap(send, axis, distance)
        now = [other] + terms
        if other.shape[0] == 1:
            return [t[0] for t in now], send
        if after is None:
            send = sum(t[1::2].astype(F32) for t in now).astype(BF16)
        else:
            send = merge(now, after)
        terms = [t[0::2] for t in now]
    return [t[0] for t in terms], send


def softplus(values):
    return jnp.maximum(values, 0.0) + jnp.log1p(jnp.exp(-jnp.abs(values)))


def silu(values):
    return values / (1.0 + jnp.exp(-values))


def recur_body(
    terms,
    group,
    live_ref,
    *refs,
):
    term_refs = refs[:terms]
    inverse_ref, adapted_ref, bias_ref, rate_ref, skip_ref, source_ref = refs[terms : terms + 6]
    result_ref, feeds_ref, b_ref, both_ref, state_ref, *scratch = refs[terms + 6 :]
    c_ref, read_ref, spread_ref, signal_ref, semaphores = scratch
    heads, head, width = state_ref.shape[1:]
    streams, inner = feeds_ref.shape[1:]
    step = pl.program_id(0)

    def fetch(i):
        at = pl.ds(i * group, group)
        return pltpu.make_async_copy(source_ref.at[at], state_ref.at[at], semaphores.at[i])

    @pl.when(step == 0)
    def _():
        for i in range(streams // group):
            fetch(i).start()
        total = sum(t[...].astype(F32) for t in term_refs) * inverse_ref[...]
        signal_ref[...] = silu(total[:, :inner] + adapted_ref[...])
        gates = silu(total[:, inner : inner + 2 * width])
        steps_dt = softplus(total[:, inner + 2 * width :] + bias_ref[...])
        b = [gates[p * streams : (p + 1) * streams, :width] for p in range(2)]
        c = [gates[p * streams : (p + 1) * streams, width:] for p in range(2)]
        for p in range(2):
            b_ref[p] = b[p]
            c_ref[p] = c[p]
        live = lax.broadcasted_iota(jnp.int32, (streams, heads), 0) < live_ref[0]
        dt = [steps_dt[p * streams : (p + 1) * streams] for p in range(2)]
        decay = [jnp.where(live, jnp.exp(-d * rate_ref[...]), 1.0) for d in dt]
        fed = [jnp.where(live, d, 0.0) for d in dt]

        def match(i, j):
            return jnp.sum(b[i] * c[j], -1, keepdims=True)

        both = decay[0] * decay[1]
        both_ref[...] = both
        late = decay[1] * fed[0]
        skip = skip_ref[...]
        factors = jnp.concatenate(
            [
                decay[0],
                both,
                fed[0] * match(0, 0) + skip,
                fed[1] * match(1, 1) + skip,
                late * match(0, 1),
                late,
                fed[1],
            ],
            0,
        )
        high, low = split(factors)
        place = lax.broadcasted_iota(jnp.int32, (heads, inner), 1) // head
        ones = (place == lax.broadcasted_iota(jnp.int32, (heads, inner), 0)).astype(BF16)
        spread_ref[...] = jnp.dot(high, ones, preferred_element_type=F32) + jnp.dot(
            low, ones, preferred_element_type=F32
        )

    fetch(step).wait()
    at = pl.multiple_of(step * group, group)
    c = jnp.concatenate([c_ref[p, pl.ds(at, group), :] for p in range(2)], 0)
    lhs = jnp.concatenate(split(c), 0)
    for g in range(group):
        state = state_ref[at + g].reshape(inner, width)
        found = lax.dot_general(lhs, state, (((1,), (1,)), ((), ())), preferred_element_type=F32)
        for p in range(2):
            row = p * group + g
            low = 2 * group + row
            read_ref[p, pl.ds(at + g, 1), :] = found[row : row + 1] + found[low : low + 1]

    @pl.when(step == pl.num_programs(0) - 1)
    def _():
        factor = [spread_ref[i * streams : (i + 1) * streams, :] for i in range(7)]
        first = signal_ref[:streams, :]
        second = signal_ref[streams:, :]
        result_ref[:streams, :] = factor[0] * read_ref[0] + factor[2] * first
        result_ref[streams:, :] = factor[1] * read_ref[1] + factor[4] * first + factor[3] * second
        feeds_ref[0] = factor[5] * first
        feeds_ref[1] = factor[6] * second


def recur(live_rows, terms, inverse, adapted, bias, rate, skip, state):
    streams, heads, head, width = state.shape
    group = 8
    inner = heads * head
    rows = 2 * streams
    whole = pl.BlockSpec(memory_space=pltpu.VMEM)
    return pl.pallas_call(
        functools.partial(recur_body, len(terms), group),
        out_shape=(
            jax.ShapeDtypeStruct((rows, inner), F32),
            jax.ShapeDtypeStruct((2, streams, inner), F32),
            jax.ShapeDtypeStruct((2, streams, width), F32),
            jax.ShapeDtypeStruct((streams, heads), F32),
            pltpu.VMEM(state.shape, state.dtype),
        ),
        grid=(streams // group,),
        in_specs=[pl.BlockSpec(memory_space=pltpu.SMEM)]
        + [whole] * (len(terms) + 5)
        + [pl.BlockSpec(memory_space=pl.ANY)],
        out_specs=(whole,) * 5,
        scratch_shapes=[
            pltpu.VMEM((2, streams, width), F32),
            pltpu.VMEM((2, streams, inner), F32),
            pltpu.VMEM((7 * streams, inner), F32),
            pltpu.VMEM((rows, inner), F32),
            pltpu.SemaphoreType.DMA((streams // group,)),
        ],
        compiler_params=params(),
        cost_estimate=cost(64 * state.size, 2 * state.size + 32 * rows * inner),
        name="recur",
    )(
        live_rows,
        *terms,
        inverse,
        adapted,
        bias[None],
        rate[None],
        skip[None],
        in_hbm(state),
    )


def state_write_body(left_ref, right_ref, decay_ref, state_ref, out_ref):
    group, heads, head, width = out_ref.shape
    at = pl.program_id(0) * group
    for g in range(group):
        outer = lax.dot_general(
            left_ref[g], right_ref[g], (((0,), (0,)), ((), ())), preferred_element_type=F32
        )
        scaled = state_ref[at + g].astype(F32) * decay_ref[g][:, None, :]
        out_ref[g] = (scaled + outer.reshape(heads, head, width)).astype(out_ref.dtype)


def state_write(left, right, decay, state):
    streams, heads, head, width = state.shape
    group = 4
    rank = left.shape[1]
    block = pl.BlockSpec((group, heads, head, width), lambda i: (i, 0, 0, 0))
    return pl.pallas_call(
        state_write_body,
        out_shape=jax.ShapeDtypeStruct(state.shape, state.dtype),
        grid=(streams // group,),
        in_specs=[
            pl.BlockSpec((group, rank, heads * head), lambda i: (i, 0, 0)),
            pl.BlockSpec((group, rank, width), lambda i: (i, 0, 0)),
            pl.BlockSpec((group, heads, width), lambda i: (i, 0, 0)),
            pl.BlockSpec(memory_space=pltpu.VMEM),
        ],
        out_specs=block,
        compiler_params=params(),
        cost_estimate=cost(32 * state.size, 4 * state.size),
        name="state_write",
    )(left, right, decay, state)


def output_tiles(index_ref, lhs_ref, weight_ref, out_ref):
    count, _, width = out_ref.shape
    tile = min(width, 512)
    for j in range(count):
        for t in range(0, width, tile):
            at = pl.multiple_of(index_ref[j] * width + t, tile)
            acc = jnp.dot(lhs_ref[...], weight_ref[:, pl.ds(at, tile)], preferred_element_type=F32)
            out_ref[j, :, t : t + tile] = acc.astype(out_ref.dtype)


def output_first_body(terms, index_ref, *refs):
    term_refs = refs[:terms]
    inverse_ref, result_ref, scale_ref, weight_ref, out_ref, lhs_ref, squares_ref = refs[terms:]
    total = sum(t[...].astype(F32) for t in term_refs) * inverse_ref[...]
    gated = result_ref[...] * silu(total)
    squares_ref[...] = jnp.sum(gated * gated, -1, keepdims=True)
    lhs_ref[...] = (gated * scale_ref[...]).astype(lhs_ref.dtype)
    output_tiles(index_ref, lhs_ref, weight_ref, out_ref)


def output_parts(index, weight, width, operands, first):
    rows, depth = operands[0].shape
    count = index.shape[0]
    whole = pl.BlockSpec(memory_space=pltpu.VMEM)
    out_shape = [jax.ShapeDtypeStruct((count, rows, width), BF16)]
    if first:
        out_shape += [
            jax.ShapeDtypeStruct((rows, depth), BF16),
            jax.ShapeDtypeStruct((rows, 1), F32),
        ]
    return pl.pallas_call(
        functools.partial(output_first_body, len(operands) - 3) if first else output_tiles,
        out_shape=tuple(out_shape),
        in_specs=[pl.BlockSpec(memory_space=pltpu.SMEM)] + [whole] * (len(operands) + 1),
        out_specs=(whole,) * len(out_shape),
        compiler_params=params(),
        cost_estimate=cost(2 * rows * depth * width * count, 2 * depth * width * count),
        name="output_first" if first else "output_second",
    )(index, *operands, weight)


def split(values):
    high = values.astype(BF16)
    return high, (values - high.astype(F32)).astype(BF16)


def on_device(
    hidden,
    input_norm_scale,
    projection_signal,
    projection_gate,
    projection_step,
    projection_input_output,
    step_bias,
    head_decay_rate,
    head_skip_weight,
    gated_norm_scale,
    adapter_down_weight,
    adapter_up_weight,
    output_weight,
    scan_state,
    stream_tenant_index,
    live_block_rows,
):
    epsilon = 1e-05
    streams, positions, feature_width = hidden.shape
    rows = streams * positions
    heads_n = lax.axis_size("head")
    rows_n = lax.axis_size("row")
    model_width = feature_width * heads_n
    depth, inner = projection_signal.shape
    inner_width = inner * heads_n
    heads_here = projection_step.shape[1]
    head_at = lax.axis_index("head")
    row_at = lax.axis_index("row")

    wide = jnp.swapaxes(hidden, 0, 1).astype(F32)
    scaled = (wide * input_norm_scale).astype(BF16)
    scaled_flat = scaled.reshape(rows, feature_width)

    in_weights = (projection_signal, projection_input_output, projection_gate)
    if heads_n == rows_n:
        turned = lax.ppermute(
            scaled_flat,
            ("head", "row"),
            [
                (h * rows_n + r, reverse_bits(r, rows_n) * rows_n + h)
                for h in range(heads_n)
                for r in range(rows_n)
            ],
        )
        blocks, order, weights = gather_relative(
            turned, "head", lambda block: load(block, block, *in_weights)
        )
        owner = jnp.asarray([reverse_bits(i, rows_n) for i in range(rows_n)], jnp.int32)
        index = owner[head_at ^ jnp.asarray(order, jnp.int32)] ^ row_at
    else:
        features = lax.all_gather(scaled_flat, "head", axis=1, tiled=True)
        blocks = lax.all_to_all(features, "row", split_axis=1, concat_axis=0, tiled=True)
        blocks = blocks.reshape(rows_n, rows, depth)
        blocks = [blocks[i] for i in range(rows_n)]
        weights = load(scaled_flat, scaled_flat, *in_weights)[1:]
        index = jnp.arange(rows_n, dtype=jnp.int32) ^ row_at

    tenant_local = stream_tenant_index - row_at * adapter_down_weight.shape[0]
    down_weight_rows = jnp.take(adapter_down_weight, tenant_local, axis=0)
    square_part = jnp.sum(wide * wide, -1)
    lowrank_part = jnp.einsum(
        "psd,sdr->psr", scaled, down_weight_rows, preferred_element_type=F32
    )
    sums = jnp.concatenate([lowrank_part, square_part[..., None]], -1).reshape(rows, -1)

    signal_weight, mix_weight, gate_weight = weights
    send, keep, lhs = project_signal(
        index, blocks, signal_weight, mix_weight, projection_step.T
    )
    gate_send, gate_keep, sums = project_gate(rows, lhs, gate_weight, sums, send)
    keep, out_weight = load(gate_send, keep, output_weight)
    signal_terms, last_send = scatter_rows(send, keep, "row")
    gate_terms, _ = scatter_rows(gate_send, gate_keep, "row", after=last_send)
    sums = sum_over(sums, "head")
    inverse = lax.rsqrt(sums[:, -1:] / model_width + epsilon)
    lowrank = (sums[:, :-1] * inverse).astype(BF16).reshape(positions, streams, -1)
    up_weight_rows = jnp.take(adapter_up_weight, tenant_local, axis=0)
    adapted = jnp.einsum("psr,srk->psk", lowrank, up_weight_rows, preferred_element_type=F32)

    result, feeds, bgate, both, state = recur(
        live_block_rows,
        signal_terms,
        inverse,
        adapted.reshape(rows, inner),
        step_bias,
        head_decay_rate,
        head_skip_weight,
        scan_state,
    )

    distances = jnp.arange(heads_n, dtype=jnp.int32) ^ head_at
    odd, out_lhs, gate_squares = output_parts(
        distances[1::2],
        out_weight,
        feature_width,
        [*gate_terms, inverse, result, gated_norm_scale[None]],
        True,
    )
    (even,) = output_parts(distances[0::2], out_weight, feature_width, [out_lhs], False)
    gate_squares = sum_over(gate_squares, "head")
    mixer = sum(t.astype(F32) for t in scatter_rows(odd, even, "head")[0])
    mixer = mixer * lax.rsqrt(gate_squares / inner_width + epsilon)
    mixer = mixer.reshape(positions, streams, feature_width)
    live = jnp.arange(streams) < live_block_rows[0]
    mixed = (wide + jnp.where(live[:, None], mixer, 0.0)).astype(BF16)

    b_high, b_low = split(jnp.swapaxes(bgate, 0, 1))
    f_high, f_low = split(jnp.swapaxes(feeds, 0, 1))
    left = jnp.concatenate([f_high, f_low, f_high, jnp.zeros_like(f_high)], 1)
    right = jnp.concatenate([b_high, b_high, b_low, jnp.zeros_like(b_high)], 1)
    spread = jnp.broadcast_to(both[..., None], both.shape + (bgate.shape[-1],))
    new_state = state_write(left, right, spread, state)
    return (jnp.swapaxes(mixed, 0, 1), new_state)


def solution(mesh):
    in_specs = (
        P(("rep", "row"), None, "head"),
        P("head"),
        P("row", "head"),
        P("row", "head"),
        P("row", "head"),
        P("row", None),
        P("head"),
        P("head"),
        P("head"),
        P("head"),
        P("row", "head", None),
        P("row", None, "head"),
        P("head", None),
        P(("rep", "row"), "head", None, None),
        P(("rep", "row")),
        P(("rep", "row")),
    )
    out_specs = (P(("rep", "row"), None, "head"), P(("rep", "row"), "head", None, None))
    return jax.shard_map(
        on_device, mesh=mesh, in_specs=in_specs, out_specs=out_specs, check_vma=False
    )
```

```python
import functools

import jax
import jax.numpy as jnp
from jax import lax
from jax.experimental import pallas as pl
from jax.experimental.pallas import tpu as pltpu
from jax.sharding import PartitionSpec as P

BF16 = jnp.bfloat16
EPSILON = 1e-05
F32 = jnp.float32
VMEM_GRANT = 12 * 1024 * 1024


def swap(values, axis, distance):
    size = lax.axis_size(axis)
    return lax.ppermute(values, axis, [(i, i ^ distance) for i in range(size)])


def bits_of(size):
    return [1 << i for i in range(size.bit_length() - 1)]


def sum_over(values, axis):
    for distance in bits_of(lax.axis_size(axis)):
        values = values + swap(values, axis, distance)
    return values


def reverse_bits(value, size):
    result = 0
    for distance in bits_of(size):
        result = result * 2 + (1 if value & distance else 0)
    return result


def gather_relative(parts, axis, beside):
    distances = list(reversed(bits_of(lax.axis_size(axis))))
    blocks = [(0, p, part) for p, part in enumerate(parts)]
    blocks += [(distances[0], p, swap(part, axis, distances[0])) for _, p, part in blocks]
    passed, *extra = beside(parts[0])
    for distance in distances[1:]:
        blocks += [
            (i ^ distance, p, swap(passed if (i, p) == (0, 0) else part, axis, distance))
            for i, p, part in blocks
        ]
    return [part for _, _, part in blocks], [(i, p) for i, p, _ in blocks], extra


def params(**more):
    return pltpu.CompilerParams(vmem_limit_bytes=VMEM_GRANT, **more)


def cost(flops, size):
    return pl.CostEstimate(flops=int(flops), bytes_accessed=int(size), transcendentals=0)


def in_hbm(values):
    return pltpu.with_memory_space_constraint(values, pltpu.HBM)


def load_body(pieces, after_ref, *refs):
    count = len(pieces)
    sources, targets, semaphores = refs[:count], refs[count : 2 * count], refs[2 * count]
    copies = []
    for source, target, parts in zip(sources, targets, pieces):
        step = source.shape[0] // parts
        for i in range(parts):
            at = pl.ds(i * step, step)
            copies.append(
                pltpu.make_async_copy(source.at[at], target.at[at], semaphores.at[len(copies)])
            )
    for copy in copies:
        copy.start()
    for copy in copies:
        copy.wait()


def load(after, passed, *weights):
    arrays = (*passed, *weights)
    pieces = [1] * len(passed) + [8 if w.shape[0] % 128 == 0 else 1 for w in weights]
    size = sum(a.size * a.dtype.itemsize for a in arrays)
    return pl.pallas_call(
        functools.partial(load_body, pieces),
        out_shape=tuple(pltpu.VMEM(a.shape, a.dtype) for a in arrays),
        in_specs=[pl.BlockSpec(memory_space=pl.ANY)] * (1 + len(arrays)),
        out_specs=tuple(pl.BlockSpec(memory_space=pltpu.VMEM) for _ in arrays),
        scratch_shapes=[pltpu.SemaphoreType.DMA((sum(pieces),))],
        compiler_params=params(),
        cost_estimate=cost(0, 2 * size),
        name="load",
    )(after, *passed, *[in_hbm(w) for w in weights])


def own_columns(rows, streams, rank):
    row = lax.broadcasted_iota(jnp.int32, (rows, streams * rank), 0) % streams
    return row == lax.broadcasted_iota(jnp.int32, (rows, streams * rank), 1) // rank


def adapt_body(tenant_ref, scaled_ref, squares_ref, down_ref, up_ref, sums_ref, up_rows_ref, *scratch):
    down_rows_ref, semaphores = scratch
    rank = down_ref.shape[1]
    streams = tenant_ref.shape[0]
    rows = scaled_ref.shape[0]
    downs, ups = [], []
    for s in range(streams):
        at = pl.ds(s * rank, rank)
        tenant = tenant_ref[s]
        downs.append(
            pltpu.make_async_copy(down_ref.at[tenant], down_rows_ref.at[at, :], semaphores.at[s])
        )
        ups.append(
            pltpu.make_async_copy(
                up_ref.at[tenant], up_rows_ref.at[at, :], semaphores.at[streams + s]
            )
        )
    for copy in downs + ups:
        copy.start()
    for copy in downs:
        copy.wait()
    every = lax.dot_general(
        scaled_ref[...],
        down_rows_ref[...],
        (((1,), (1,)), ((), ())),
        preferred_element_type=F32,
    )
    own = jnp.where(own_columns(rows, streams, rank), every, 0.0)
    fold = lax.broadcasted_iota(jnp.int32, (streams * rank, rank), 0) % rank
    fold = (fold == lax.broadcasted_iota(jnp.int32, (streams * rank, rank), 1)).astype(BF16)
    high, rest = split(own)
    middle, low = rest, (own - high.astype(F32) - rest.astype(F32)).astype(BF16)
    folded = sum(jnp.dot(x, fold, preferred_element_type=F32) for x in (high, middle, low))
    sums_ref[:, :rank] = folded
    sums_ref[:, rank:] = squares_ref[...]
    for copy in ups:
        copy.wait()


def adapt(tenants, scaled, squares, down, up):
    streams = tenants.shape[0]
    rows, depth = scaled.shape
    rank, inner = up.shape[1:]
    whole = pl.BlockSpec(memory_space=pltpu.VMEM)
    anywhere = pl.BlockSpec(memory_space=pl.ANY)
    return pl.pallas_call(
        adapt_body,
        out_shape=(
            jax.ShapeDtypeStruct((rows, rank + 1), F32),
            pltpu.VMEM((streams * rank, inner), BF16),
        ),
        in_specs=[pl.BlockSpec(memory_space=pltpu.SMEM), whole, whole, anywhere, anywhere],
        out_specs=(whole, whole),
        scratch_shapes=[
            pltpu.VMEM((streams * rank, depth), BF16),
            pltpu.SemaphoreType.DMA((2 * streams,)),
        ],
        compiler_params=params(),
        cost_estimate=cost(2 * rows * depth * streams * rank, 2 * streams * rank * (depth + inner)),
        name="adapt",
    )(tenants, scaled, squares, in_hbm(jnp.swapaxes(down, 1, 2)), in_hbm(up))


def fill_rows(index_ref, blocks, lhs, semaphores):
    rows = blocks[0].shape[0]
    copies = []
    for i, block in enumerate(blocks):
        at = pl.multiple_of(index_ref[i] * rows, rows)
        copies.append(pltpu.make_async_copy(block, lhs.at[pl.ds(at, rows), :], semaphores.at[i]))
    for copy in copies:
        copy.start()
    for copy in copies:
        copy.wait()


def put_parts(acc, start, send_ref, keep_ref):
    rows = send_ref.shape[1]
    for k in range(acc.shape[0] // rows):
        target = send_ref if k % 2 else keep_ref
        target[k // 2, :, start : start + acc.shape[1]] = acc[k * rows : (k + 1) * rows].astype(
            target.dtype
        )


def project_signal_body(count, index_ref, *refs):
    blocks, refs = refs[:count], refs[count:]
    weight_ref, mix_ref, step_ref, sums_ref, send_ref, keep_ref, lhs_ref, out_ref, semaphores = refs
    out_ref[...] = sums_ref[...]
    fill_rows(index_ref, blocks, lhs_ref, semaphores)
    lhs = lhs_ref[...]
    columns = weight_ref.shape[1]
    tile = min(columns, 512)
    for t in range(0, columns, tile):
        acc = jnp.dot(lhs, weight_ref[:, t : t + tile], preferred_element_type=F32)
        put_parts(acc, t, send_ref, keep_ref)
    acc = jnp.dot(lhs, mix_ref[...], preferred_element_type=F32)
    put_parts(acc, columns, send_ref, keep_ref)
    acc = lax.dot_general(lhs, step_ref[...], (((1,), (1,)), ((), ())), preferred_element_type=F32)
    put_parts(acc, columns + mix_ref.shape[1], send_ref, keep_ref)


def project_signal(index, blocks, owners, weight, mix, step, sums):
    pieces = len(blocks)
    depth = blocks[0].shape[1]
    count, rows = owners, pieces * blocks[0].shape[0] // owners
    columns = weight.shape[1] + mix.shape[1] + step.shape[0]
    half = jax.ShapeDtypeStruct((count // 2, rows, columns), BF16)
    whole = pl.BlockSpec(memory_space=pltpu.VMEM)
    return pl.pallas_call(
        functools.partial(project_signal_body, pieces),
        out_shape=(
            half,
            half,
            jax.ShapeDtypeStruct((count * rows, depth), BF16),
            jax.ShapeDtypeStruct(sums.shape, sums.dtype),
        ),
        in_specs=[pl.BlockSpec(memory_space=pltpu.SMEM)]
        + [pl.BlockSpec(memory_space=pl.ANY)] * pieces
        + [whole] * 4,
        out_specs=(whole,) * 4,
        scratch_shapes=[pltpu.SemaphoreType.DMA((pieces,))],
        compiler_params=params(),
        cost_estimate=cost(2 * count * rows * depth * columns, 2 * depth * columns),
        name="project_signal",
    )(index, *blocks, weight, mix, step, sums)


def project_gate_body(lhs_ref, weight_ref, after_ref, send_ref, keep_ref):
    columns = weight_ref.shape[1]
    tile = min(columns, 512)
    for t in range(0, columns, tile):
        acc = jnp.dot(lhs_ref[...], weight_ref[:, t : t + tile], preferred_element_type=F32)
        put_parts(acc, t, send_ref, keep_ref)


def project_gate(rows, lhs, weight, after):
    count = lhs.shape[0] // rows
    columns = weight.shape[1]
    half = jax.ShapeDtypeStruct((count // 2, rows, columns), BF16)
    whole = pl.BlockSpec(memory_space=pltpu.VMEM)
    return pl.pallas_call(
        project_gate_body,
        out_shape=(half, half),
        in_specs=[whole, whole, pl.BlockSpec(memory_space=pl.ANY)],
        out_specs=(whole,) * 2,
        compiler_params=params(),
        cost_estimate=cost(2 * lhs.size * columns, 2 * weight.size),
        name="project_gate",
    )(lhs, weight, after)


def scatter_rows(received, keep, axis, done=1):
    send = received
    terms = [received] + (keep if isinstance(keep, list) else [keep])
    for distance in bits_of(lax.axis_size(axis))[done:]:
        send = sum(t[1::2].astype(F32) for t in terms).astype(BF16)
        terms = [swap(send, axis, distance)] + [t[0::2] for t in terms]
    return [t[0] for t in terms], send


def softplus(values):
    return jnp.maximum(values, 0.0) + jnp.log1p(jnp.exp(-jnp.abs(values)))


def silu(values):
    return values / (1.0 + jnp.exp(-values))


def inverse_of(sums_ref, width):
    return lax.rsqrt(sums_ref[:, sums_ref.shape[1] - 1 :] / width + EPSILON)


def recur_body(
    terms,
    group,
    model_width,
    live_ref,
    *refs,
):
    term_refs = refs[:terms]
    sums_ref, up_ref, bias_ref, rate_ref, skip_ref, source_ref, _ = refs[terms : terms + 7]
    result_ref, feeds_ref, b_ref, both_ref, state_ref, *scratch = refs[terms + 7 :]
    c_ref, read_ref, spread_ref, signal_ref, semaphores = scratch
    heads, head, width = state_ref.shape[1:]
    streams, inner = feeds_ref.shape[1:]
    step = pl.program_id(0)

    def fetch(i):
        at = pl.ds(i * group, group)
        return pltpu.make_async_copy(source_ref.at[at], state_ref.at[at], semaphores.at[i])

    @pl.when(step == 0)
    def _():
        for i in range(streams // group):
            fetch(i).start()
        rows = sums_ref.shape[0]
        rank = sums_ref.shape[1] - 1
        inverse = inverse_of(sums_ref, model_width)
        lowrank = (sums_ref[:, :rank] * inverse).astype(BF16)
        repeat = lax.broadcasted_iota(jnp.int32, (rank, streams * rank), 1) % rank
        repeat = (repeat == lax.broadcasted_iota(jnp.int32, (rank, streams * rank), 0)).astype(BF16)
        every = jnp.dot(lowrank, repeat, preferred_element_type=F32)
        own = jnp.where(own_columns(rows, streams, rank), every, 0.0).astype(BF16)
        adapted = jnp.dot(own, up_ref[...], preferred_element_type=F32)
        total = sum(t[...].astype(F32) for t in term_refs) * inverse
        signal_ref[...] = silu(total[:, :inner] + adapted)
        gates = silu(total[:, inner : inner + 2 * width])
        steps_dt = softplus(total[:, inner + 2 * width :] + bias_ref[...])
        b = [gates[p * streams : (p + 1) * streams, :width] for p in range(2)]
        c = [gates[p * streams : (p + 1) * streams, width:] for p in range(2)]
        for p in range(2):
            b_ref[p] = b[p]
            c_ref[p] = c[p]
        live = lax.broadcasted_iota(jnp.int32, (streams, heads), 0) < live_ref[0]
        dt = [steps_dt[p * streams : (p + 1) * streams] for p in range(2)]
        decay = [jnp.where(live, jnp.exp(-d * rate_ref[...]), 1.0) for d in dt]
        fed = [jnp.where(live, d, 0.0) for d in dt]

        def match(i, j):
            return jnp.sum(b[i] * c[j], -1, keepdims=True)

        both = decay[0] * decay[1]
        both_ref[...] = both
        late = decay[1] * fed[0]
        skip = skip_ref[...]
        factors = jnp.concatenate(
            [
                decay[0],
                both,
                fed[0] * match(0, 0) + skip,
                fed[1] * match(1, 1) + skip,
                late * match(0, 1),
                late,
                fed[1],
            ],
            0,
        )
        high, low = split(factors)
        place = lax.broadcasted_iota(jnp.int32, (heads, inner), 1) // head
        ones = (place == lax.broadcasted_iota(jnp.int32, (heads, inner), 0)).astype(BF16)
        spread_ref[...] = jnp.dot(high, ones, preferred_element_type=F32) + jnp.dot(
            low, ones, preferred_element_type=F32
        )

    fetch(step).wait()
    at = pl.multiple_of(step * group, group)
    c = jnp.concatenate([c_ref[p, pl.ds(at, group), :] for p in range(2)], 0)
    lhs = jnp.concatenate(split(c), 0)
    for g in range(group):
        state = state_ref[at + g].reshape(inner, width)
        found = lax.dot_general(lhs, state, (((1,), (1,)), ((), ())), preferred_element_type=F32)
        for p in range(2):
            row = p * group + g
            low = 2 * group + row
            read_ref[p, pl.ds(at + g, 1), :] = found[row : row + 1] + found[low : low + 1]

    @pl.when(step == pl.num_programs(0) - 1)
    def _():
        factor = [spread_ref[i * streams : (i + 1) * streams, :] for i in range(7)]
        first = signal_ref[:streams, :]
        second = signal_ref[streams:, :]
        result_ref[:streams, :] = factor[0] * read_ref[0] + factor[2] * first
        result_ref[streams:, :] = factor[1] * read_ref[1] + factor[4] * first + factor[3] * second
        feeds_ref[0] = factor[5] * first
        feeds_ref[1] = factor[6] * second


def recur(model_width, after, live_rows, terms, sums, up_rows, bias, rate, skip, state):
    streams, heads, head, width = state.shape
    group = 8
    inner = heads * head
    rows = 2 * streams
    whole = pl.BlockSpec(memory_space=pltpu.VMEM)
    return pl.pallas_call(
        functools.partial(recur_body, len(terms), group, model_width),
        out_shape=(
            jax.ShapeDtypeStruct((rows, inner), F32),
            jax.ShapeDtypeStruct((2, streams, inner), F32),
            jax.ShapeDtypeStruct((2, streams, width), F32),
            jax.ShapeDtypeStruct((streams, heads), F32),
            pltpu.VMEM(state.shape, state.dtype),
        ),
        grid=(streams // group,),
        in_specs=[pl.BlockSpec(memory_space=pltpu.SMEM)]
        + [whole] * (len(terms) + 5)
        + [pl.BlockSpec(memory_space=pl.ANY)] * 2,
        out_specs=(whole,) * 5,
        scratch_shapes=[
            pltpu.VMEM((2, streams, width), F32),
            pltpu.VMEM((2, streams, inner), F32),
            pltpu.VMEM((7 * streams, inner), F32),
            pltpu.VMEM((rows, inner), F32),
            pltpu.SemaphoreType.DMA((streams // group,)),
        ],
        compiler_params=params(),
        cost_estimate=cost(64 * state.size, 2 * state.size + 32 * rows * inner),
        name="recur",
    )(
        live_rows,
        *terms,
        sums,
        up_rows,
        bias[None],
        rate[None],
        skip[None],
        in_hbm(state),
        after,
    )


def state_write_body(left_ref, right_ref, decay_ref, state_ref, out_ref):
    group, heads, head, width = out_ref.shape
    at = pl.program_id(0) * group
    for g in range(group):
        outer = lax.dot_general(
            left_ref[g], right_ref[g], (((0,), (0,)), ((), ())), preferred_element_type=F32
        )
        scaled = state_ref[at + g].astype(F32) * decay_ref[g][:, None, :]
        out_ref[g] = (scaled + outer.reshape(heads, head, width)).astype(out_ref.dtype)


def state_write(left, right, decay, state):
    streams, heads, head, width = state.shape
    group = 4
    rank = left.shape[1]
    block = pl.BlockSpec((group, heads, head, width), lambda i: (i, 0, 0, 0))
    return pl.pallas_call(
        state_write_body,
        out_shape=jax.ShapeDtypeStruct(state.shape, state.dtype),
        grid=(streams // group,),
        in_specs=[
            pl.BlockSpec((group, rank, heads * head), lambda i: (i, 0, 0)),
            pl.BlockSpec((group, rank, width), lambda i: (i, 0, 0)),
            pl.BlockSpec((group, heads, width), lambda i: (i, 0, 0)),
            pl.BlockSpec(memory_space=pltpu.VMEM),
        ],
        out_specs=block,
        compiler_params=params(),
        cost_estimate=cost(32 * state.size, 4 * state.size),
        name="state_write",
    )(left, right, decay, state)


def output_tiles(index_ref, lhs_ref, weight_ref, out_ref):
    count, _, width = out_ref.shape
    tile = min(width, 512)
    for j in range(count):
        for t in range(0, width, tile):
            at = pl.multiple_of(index_ref[j] * width + t, tile)
            acc = jnp.dot(lhs_ref[...], weight_ref[:, pl.ds(at, tile)], preferred_element_type=F32)
            out_ref[j, :, t : t + tile] = acc.astype(out_ref.dtype)


def output_first_body(terms, model_width, index_ref, *refs):
    term_refs = refs[:terms]
    sums_ref, result_ref, scale_ref, weight_ref, out_ref, lhs_ref, squares_ref = refs[terms:]
    total = sum(t[...].astype(F32) for t in term_refs) * inverse_of(sums_ref, model_width)
    gated = result_ref[...] * silu(total)
    squares_ref[...] = jnp.sum(gated * gated, -1, keepdims=True)
    lhs_ref[...] = (gated * scale_ref[...]).astype(lhs_ref.dtype)
    output_tiles(index_ref, lhs_ref, weight_ref, out_ref)


def output_rest_body(index_ref, lhs_ref, after_ref, weight_ref, out_ref):
    output_tiles(index_ref, lhs_ref, weight_ref, out_ref)


def output_parts(index, weight, width, operands, model_width=None):
    first = model_width is not None
    rows, depth = operands[0].shape
    count = index.shape[0]
    whole = pl.BlockSpec(memory_space=pltpu.VMEM)
    specs = [whole] * (len(operands) + 1)
    body = output_rest_body
    out_shape = [jax.ShapeDtypeStruct((count, rows, width), BF16)]
    if first:
        body = functools.partial(output_first_body, len(operands) - 3, model_width)
        out_shape += [
            jax.ShapeDtypeStruct((rows, depth), BF16),
            jax.ShapeDtypeStruct((rows, 1), F32),
        ]
    else:
        specs[1] = pl.BlockSpec(memory_space=pl.ANY)
    return pl.pallas_call(
        body,
        out_shape=tuple(out_shape),
        in_specs=[pl.BlockSpec(memory_space=pltpu.SMEM)] + specs,
        out_specs=(whole,) * len(out_shape),
        compiler_params=params(),
        cost_estimate=cost(2 * rows * depth * width * count, 2 * depth * width * count),
        name="output_first" if first else "output_rest",
    )(index, *operands, weight)


def split(values):
    high = values.astype(BF16)
    return high, (values - high.astype(F32)).astype(BF16)


def on_device(
    hidden,
    input_norm_scale,
    projection_signal,
    projection_gate,
    projection_step,
    projection_input_output,
    step_bias,
    head_decay_rate,
    head_skip_weight,
    gated_norm_scale,
    adapter_down_weight,
    adapter_up_weight,
    output_weight,
    scan_state,
    stream_tenant_index,
    live_block_rows,
):
    streams, positions, feature_width = hidden.shape
    rows = streams * positions
    heads_n = lax.axis_size("head")
    rows_n = lax.axis_size("row")
    model_width = feature_width * heads_n
    depth, inner = projection_signal.shape
    inner_width = inner * heads_n
    head_at = lax.axis_index("head")
    row_at = lax.axis_index("row")

    wide = jnp.swapaxes(hidden, 0, 1).astype(F32)
    scaled = (wide * input_norm_scale).astype(BF16)
    scaled_flat = scaled.reshape(rows, feature_width)

    tenant_local = stream_tenant_index - row_at * adapter_down_weight.shape[0]
    squares = jnp.sum(wide * wide, -1).reshape(rows, 1)
    sums, up_rows = adapt(tenant_local, scaled_flat, squares, adapter_down_weight, adapter_up_weight)

    in_weights = (projection_signal, projection_input_output, projection_gate)
    if heads_n == rows_n:
        turn = [
            (h * rows_n + r, reverse_bits(r, rows_n) * rows_n + h)
            for h in range(heads_n)
            for r in range(rows_n)
        ]
        blocks, order, weights = gather_relative(
            [lax.ppermute(scaled[p], ("head", "row"), turn) for p in range(positions)],
            "head",
            lambda block: load(sums, [block], *in_weights),
        )
        owner = jnp.asarray([reverse_bits(i, rows_n) for i in range(rows_n)], jnp.int32)
        owner = owner[head_at ^ jnp.asarray([i for i, _ in order], jnp.int32)] ^ row_at
        index = owner * positions + jnp.asarray([p for _, p in order], jnp.int32)
    else:
        features = lax.all_gather(scaled_flat, "head", axis=1, tiled=True)
        blocks = lax.all_to_all(features, "row", split_axis=1, concat_axis=0, tiled=True)
        blocks = blocks.reshape(rows_n, rows, depth)
        blocks = [blocks[i] for i in range(rows_n)]
        weights = load(sums, [scaled_flat], *in_weights)[1:]
        index = jnp.arange(rows_n, dtype=jnp.int32) ^ row_at

    signal_weight, mix_weight, gate_weight = weights
    send, keep, lhs, sums = project_signal(
        index, blocks, rows_n, signal_weight, mix_weight, projection_step.T, sums
    )
    received = swap(send, "row", 1)
    keep, out_weight = load(send, [keep], output_weight)
    gate_send, gate_keep = project_gate(rows, lhs, gate_weight, received)
    signal_terms, _ = scatter_rows(received, keep, "row")
    gate_terms, gate_last = scatter_rows(swap(gate_send, "row", 1), gate_keep, "row")
    sums = sum_over(sums, "head")

    result, feeds, bgate, both, state = recur(
        model_width,
        gate_last,
        live_block_rows,
        signal_terms,
        sums,
        up_rows,
        step_bias,
        head_decay_rate,
        head_skip_weight,
        scan_state,
    )

    distances = jnp.arange(heads_n, dtype=jnp.int32) ^ head_at
    first, out_lhs, gate_squares = output_parts(
        distances[3::4],
        out_weight,
        feature_width,
        [*gate_terms, sums, result, gated_norm_scale[None]],
        model_width,
    )
    (second,) = output_parts(distances[2::4], out_weight, feature_width, [out_lhs, first])
    send = (swap(first, "head", 1).astype(F32) + second.astype(F32)).astype(BF16)
    near = jnp.concatenate([distances[1::4], distances[0::4]])
    (rest,) = output_parts(near, out_weight, feature_width, [out_lhs, send])
    half = rest.shape[0] // 2
    kept = [swap(rest[:half], "head", 1), rest[half:]]
    mixer, _ = scatter_rows(swap(send, "head", 2), kept, "head", done=2)
    mixer = sum(t.astype(F32) for t in mixer)
    gate_squares = sum_over(gate_squares, "head")
    mixer = mixer * lax.rsqrt(gate_squares / inner_width + EPSILON)
    mixer = mixer.reshape(positions, streams, feature_width)
    live = jnp.arange(streams) < live_block_rows[0]
    mixed = (wide + jnp.where(live[:, None], mixer, 0.0)).astype(BF16)

    b_high, b_low = split(jnp.swapaxes(bgate, 0, 1))
    f_high, f_low = split(jnp.swapaxes(feeds, 0, 1))
    left = jnp.concatenate([f_high, f_low, f_high, jnp.zeros_like(f_high)], 1)
    right = jnp.concatenate([b_high, b_high, b_low, jnp.zeros_like(b_high)], 1)
    spread = jnp.broadcast_to(both[..., None], both.shape + (bgate.shape[-1],))
    new_state = state_write(left, right, spread, state)
    return (jnp.swapaxes(mixed, 0, 1), new_state)


def solution(mesh):
    in_specs = (
        P(("rep", "row"), None, "head"),
        P("head"),
        P("row", "head"),
        P("row", "head"),
        P("row", "head"),
        P("row", None),
        P("head"),
        P("head"),
        P("head"),
        P("head"),
        P("row", "head", None),
        P("row", None, "head"),
        P("head", None),
        P(("rep", "row"), "head", None, None),
        P(("rep", "row")),
        P(("rep", "row")),
    )
    out_specs = (P(("rep", "row"), None, "head"), P(("rep", "row"), "head", None, None))
    return jax.shard_map(
        on_device, mesh=mesh, in_specs=in_specs, out_specs=out_specs, check_vma=False
    )
```

```python
import functools

import jax
import jax.numpy as jnp
from jax import lax
from jax.experimental import pallas as pl
from jax.experimental.pallas import tpu as pltpu
from jax.sharding import PartitionSpec as P

BF16 = jnp.bfloat16
EPSILON = 1e-05
F32 = jnp.float32
VMEM_GRANT = 12 * 1024 * 1024


def swap(values, axis, distance):
    size = lax.axis_size(axis)
    return lax.ppermute(values, axis, [(i, i ^ distance) for i in range(size)])


def bits_of(size):
    return [1 << i for i in range(size.bit_length() - 1)]


def sum_over(values, axis):
    for distance in bits_of(lax.axis_size(axis)):
        values = values + swap(values, axis, distance)
    return values


def reverse_bits(value, size):
    bits = size.bit_length() - 1
    return sum(((value >> i) & 1) << (bits - 1 - i) for i in range(bits))


def gather_relative(parts, axis, order_after):
    distances = list(reversed(bits_of(lax.axis_size(axis))))
    parts = [lax.optimization_barrier((part, order_after))[0] for part in parts]
    blocks = [(0, p, part) for p, part in enumerate(parts)]
    for distance in distances:
        blocks += [(i ^ distance, p, swap(part, axis, distance)) for i, p, part in blocks]
    return [part for _, _, part in blocks], [(i, p) for i, p, _ in blocks]


def params(**more):
    return pltpu.CompilerParams(vmem_limit_bytes=VMEM_GRANT, **more)


def cost(flops, size):
    return pl.CostEstimate(flops=int(flops), bytes_accessed=int(size), transcendentals=0)


def in_hbm(values):
    return pltpu.with_memory_space_constraint(values, pltpu.HBM)


def load_body(pieces, after_ref, *refs):
    count = len(pieces)
    sources, targets, semaphores = refs[:count], refs[count : 2 * count], refs[2 * count]
    copies = []
    for source, target, parts in zip(sources, targets, pieces):
        step = source.shape[0] // parts
        for i in range(parts):
            at = pl.ds(i * step, step)
            copies.append(
                pltpu.make_async_copy(source.at[at], target.at[at], semaphores.at[len(copies)])
            )
    for copy in copies:
        copy.start()
    for copy in copies:
        copy.wait()


def load(after, passed, *weights):
    arrays = (*passed, *weights)
    pieces = [1] * len(passed) + [8 if w.shape[0] % 128 == 0 else 1 for w in weights]
    size = sum(a.size * a.dtype.itemsize for a in arrays)
    return pl.pallas_call(
        functools.partial(load_body, pieces),
        out_shape=tuple(pltpu.VMEM(a.shape, a.dtype) for a in arrays),
        in_specs=[pl.BlockSpec(memory_space=pl.ANY)] * (1 + len(arrays)),
        out_specs=tuple(pl.BlockSpec(memory_space=pltpu.VMEM) for _ in arrays),
        scratch_shapes=[pltpu.SemaphoreType.DMA((sum(pieces),))],
        compiler_params=params(),
        cost_estimate=cost(0, 2 * size),
        name="load",
    )(after, *passed, *[in_hbm(w) for w in weights])


def own_columns(rows, streams, rank):
    row = lax.broadcasted_iota(jnp.int32, (rows, streams * rank), 0) % streams
    return row == lax.broadcasted_iota(jnp.int32, (rows, streams * rank), 1) // rank


def adapt_body(tenant_ref, scaled_ref, squares_ref, down_ref, up_ref, sums_ref, up_rows_ref, *scratch):
    down_rows_ref, semaphores = scratch
    rank = down_ref.shape[1]
    streams = tenant_ref.shape[0]
    rows = scaled_ref.shape[0]
    first = lax.axis_index("row") * down_ref.shape[0]
    downs, ups = [], []
    for s in range(streams):
        at = pl.ds(s * rank, rank)
        tenant = tenant_ref[s] - first
        downs.append(
            pltpu.make_async_copy(down_ref.at[tenant], down_rows_ref.at[at, :], semaphores.at[s])
        )
        ups.append(
            pltpu.make_async_copy(
                up_ref.at[tenant], up_rows_ref.at[at, :], semaphores.at[streams + s]
            )
        )
    for copy in downs + ups:
        copy.start()
    for copy in downs:
        copy.wait()
    every = lax.dot_general(
        scaled_ref[...],
        down_rows_ref[...],
        (((1,), (1,)), ((), ())),
        preferred_element_type=F32,
    )
    own = jnp.where(own_columns(rows, streams, rank), every, 0.0)
    fold = lax.broadcasted_iota(jnp.int32, (streams * rank, rank), 0) % rank
    fold = (fold == lax.broadcasted_iota(jnp.int32, (streams * rank, rank), 1)).astype(BF16)
    high, rest = split(own)
    middle, low = rest, (own - high.astype(F32) - rest.astype(F32)).astype(BF16)
    folded = sum(jnp.dot(x, fold, preferred_element_type=F32) for x in (high, middle, low))
    sums_ref[:, :rank] = folded
    sums_ref[:, rank:] = squares_ref[...]
    for copy in ups:
        copy.wait()


def adapt(tenants, scaled, squares, down, up):
    streams = tenants.shape[0]
    rows, depth = scaled.shape
    rank, inner = up.shape[1:]
    whole = pl.BlockSpec(memory_space=pltpu.VMEM)
    anywhere = pl.BlockSpec(memory_space=pl.ANY)
    return pl.pallas_call(
        adapt_body,
        out_shape=(
            jax.ShapeDtypeStruct((rows, rank + 1), F32),
            pltpu.VMEM((streams * rank, inner), BF16),
        ),
        in_specs=[pl.BlockSpec(memory_space=pltpu.SMEM), whole, whole, anywhere, anywhere],
        out_specs=(whole, whole),
        scratch_shapes=[
            pltpu.VMEM((streams * rank, depth), BF16),
            pltpu.SemaphoreType.DMA((2 * streams,)),
        ],
        compiler_params=params(),
        cost_estimate=cost(2 * rows * depth * streams * rank, 2 * streams * rank * (depth + inner)),
        name="adapt",
    )(tenants, scaled, squares, in_hbm(jnp.swapaxes(down, 1, 2)), in_hbm(up))


def fill_rows(owners, order, blocks, lhs, semaphores):
    rows = blocks[0].shape[0]
    parts = len(blocks) // owners
    copies = []
    for i, block in enumerate(blocks):
        if order is None:
            owner, part = i, 0
        else:
            distance, part = order[i]
            owner = reverse_bits(lax.axis_index("head") ^ distance, owners)
        at = ((owner ^ lax.axis_index("row")) * parts + part) * rows
        at = pl.multiple_of(at, rows)
        copies.append(pltpu.make_async_copy(block, lhs.at[pl.ds(at, rows), :], semaphores.at[i]))
    for copy in copies:
        copy.start()
    for copy in copies:
        copy.wait()


def put_parts(acc, start, send_ref, keep_ref):
    rows = send_ref.shape[1]
    for k in range(acc.shape[0] // rows):
        target = send_ref if k % 2 else keep_ref
        target[k // 2, :, start : start + acc.shape[1]] = acc[k * rows : (k + 1) * rows].astype(
            target.dtype
        )


def project_signal_body(owners, order, count, *refs):
    blocks, refs = refs[:count], refs[count:]
    weight_ref, mix_ref, step_ref, send_ref, keep_ref, lhs_ref, semaphores = refs
    fill_rows(owners, order, blocks, lhs_ref, semaphores)
    lhs = lhs_ref[...]
    columns = weight_ref.shape[1]
    tile = min(columns, 512)
    for t in range(0, columns, tile):
        acc = jnp.dot(lhs, weight_ref[:, t : t + tile], preferred_element_type=F32)
        put_parts(acc, t, send_ref, keep_ref)
    acc = jnp.dot(lhs, mix_ref[...], preferred_element_type=F32)
    put_parts(acc, columns, send_ref, keep_ref)
    acc = lax.dot_general(lhs, step_ref[...], (((1,), (1,)), ((), ())), preferred_element_type=F32)
    put_parts(acc, columns + mix_ref.shape[1], send_ref, keep_ref)


def project_signal(blocks, order, owners, weight, mix, step):
    pieces = len(blocks)
    depth = blocks[0].shape[1]
    count, rows = owners, pieces * blocks[0].shape[0] // owners
    columns = weight.shape[1] + mix.shape[1] + step.shape[0]
    half = jax.ShapeDtypeStruct((count // 2, rows, columns), BF16)
    whole = pl.BlockSpec(memory_space=pltpu.VMEM)
    return pl.pallas_call(
        functools.partial(project_signal_body, owners, order, pieces),
        out_shape=(
            half,
            half,
            jax.ShapeDtypeStruct((count * rows, depth), BF16),
        ),
        in_specs=[pl.BlockSpec(memory_space=pl.ANY)] * pieces + [whole] * 3,
        out_specs=(whole,) * 3,
        scratch_shapes=[pltpu.SemaphoreType.DMA((pieces,))],
        compiler_params=params(),
        cost_estimate=cost(2 * count * rows * depth * columns, 2 * depth * columns),
        name="project_signal",
    )(*blocks, weight, mix, step)


def project_gate_body(lhs_ref, weight_ref, sums_ref, after_ref, send_ref, keep_ref, out_ref):
    out_ref[...] = sums_ref[...]
    columns = weight_ref.shape[1]
    tile = min(columns, 512)
    for t in range(0, columns, tile):
        acc = jnp.dot(lhs_ref[...], weight_ref[:, t : t + tile], preferred_element_type=F32)
        put_parts(acc, t, send_ref, keep_ref)


def project_gate(rows, lhs, weight, sums, after):
    count = lhs.shape[0] // rows
    columns = weight.shape[1]
    half = jax.ShapeDtypeStruct((count // 2, rows, columns), BF16)
    whole = pl.BlockSpec(memory_space=pltpu.VMEM)
    return pl.pallas_call(
        project_gate_body,
        out_shape=(half, half, jax.ShapeDtypeStruct(sums.shape, sums.dtype)),
        in_specs=[whole, whole, whole, pl.BlockSpec(memory_space=pl.ANY)],
        out_specs=(whole,) * 3,
        compiler_params=params(),
        cost_estimate=cost(2 * lhs.size * columns, 2 * weight.size),
        name="project_gate",
    )(lhs, weight, sums, after)


def scatter_rows(received, keep, axis, done=1):
    send = received
    terms = [received] + (keep if isinstance(keep, list) else [keep])
    for distance in bits_of(lax.axis_size(axis))[done:]:
        send = sum(t[1::2].astype(F32) for t in terms).astype(BF16)
        terms = [swap(send, axis, distance)] + [t[0::2] for t in terms]
    return [t[0] for t in terms], send


def softplus(values):
    return jnp.maximum(values, 0.0) + jnp.log1p(jnp.exp(-jnp.abs(values)))


def silu(values):
    return values / (1.0 + jnp.exp(-values))


def inverse_of(sums_ref, width):
    return lax.rsqrt(sums_ref[:, sums_ref.shape[1] - 1 :] / width + EPSILON)


def recur_body(
    terms,
    group,
    model_width,
    live_ref,
    *refs,
):
    term_refs = refs[:terms]
    sums_ref, up_ref, bias_ref, rate_ref, skip_ref, source_ref, _ = refs[terms : terms + 7]
    result_ref, feeds_ref, b_ref, both_ref, state_ref, *scratch = refs[terms + 7 :]
    c_ref, read_ref, spread_ref, signal_ref, semaphores = scratch
    heads, head, width = state_ref.shape[1:]
    streams, inner = feeds_ref.shape[1:]
    step = pl.program_id(0)

    def fetch(i):
        at = pl.ds(i * group, group)
        return pltpu.make_async_copy(source_ref.at[at], state_ref.at[at], semaphores.at[i])

    @pl.when(step == 0)
    def _():
        for i in range(streams // group):
            fetch(i).start()
        rows = sums_ref.shape[0]
        rank = sums_ref.shape[1] - 1
        inverse = inverse_of(sums_ref, model_width)
        lowrank = (sums_ref[:, :rank] * inverse).astype(BF16)
        repeat = lax.broadcasted_iota(jnp.int32, (rank, streams * rank), 1) % rank
        repeat = (repeat == lax.broadcasted_iota(jnp.int32, (rank, streams * rank), 0)).astype(BF16)
        every = jnp.dot(lowrank, repeat, preferred_element_type=F32)
        own = jnp.where(own_columns(rows, streams, rank), every, 0.0).astype(BF16)
        adapted = jnp.dot(own, up_ref[...], preferred_element_type=F32)
        total = sum(t[...].astype(F32) for t in term_refs) * inverse
        signal_ref[...] = silu(total[:, :inner] + adapted)
        gates = silu(total[:, inner : inner + 2 * width])
        steps_dt = softplus(total[:, inner + 2 * width :] + bias_ref[...])
        b = [gates[p * streams : (p + 1) * streams, :width] for p in range(2)]
        c = [gates[p * streams : (p + 1) * streams, width:] for p in range(2)]
        for p in range(2):
            b_ref[p] = b[p]
            c_ref[p] = c[p]
        live = lax.broadcasted_iota(jnp.int32, (streams, heads), 0) < live_ref[0]
        dt = [steps_dt[p * streams : (p + 1) * streams] for p in range(2)]
        decay = [jnp.where(live, jnp.exp(-d * rate_ref[...]), 1.0) for d in dt]
        fed = [jnp.where(live, d, 0.0) for d in dt]

        def match(i, j):
            return jnp.sum(b[i] * c[j], -1, keepdims=True)

        both = decay[0] * decay[1]
        both_ref[...] = both
        late = decay[1] * fed[0]
        skip = skip_ref[...]
        factors = jnp.concatenate(
            [
                decay[0],
                both,
                fed[0] * match(0, 0) + skip,
                fed[1] * match(1, 1) + skip,
                late * match(0, 1),
                late,
                fed[1],
            ],
            0,
        )
        high, low = split(factors)
        place = lax.broadcasted_iota(jnp.int32, (heads, inner), 1) // head
        ones = (place == lax.broadcasted_iota(jnp.int32, (heads, inner), 0)).astype(BF16)
        spread_ref[...] = jnp.dot(high, ones, preferred_element_type=F32) + jnp.dot(
            low, ones, preferred_element_type=F32
        )

    fetch(step).wait()
    at = pl.multiple_of(step * group, group)
    c = jnp.concatenate([c_ref[p, pl.ds(at, group), :] for p in range(2)], 0)
    lhs = jnp.concatenate(split(c), 0)
    for g in range(group):
        state = state_ref[at + g].reshape(inner, width)
        found = lax.dot_general(lhs, state, (((1,), (1,)), ((), ())), preferred_element_type=F32)
        for p in range(2):
            row = p * group + g
            low = 2 * group + row
            read_ref[p, pl.ds(at + g, 1), :] = found[row : row + 1] + found[low : low + 1]

    @pl.when(step == pl.num_programs(0) - 1)
    def _():
        factor = [spread_ref[i * streams : (i + 1) * streams, :] for i in range(7)]
        first = signal_ref[:streams, :]
        second = signal_ref[streams:, :]
        result_ref[:streams, :] = factor[0] * read_ref[0] + factor[2] * first
        result_ref[streams:, :] = factor[1] * read_ref[1] + factor[4] * first + factor[3] * second
        feeds_ref[0] = factor[5] * first
        feeds_ref[1] = factor[6] * second


def recur(model_width, after, live_rows, terms, sums, up_rows, bias, rate, skip, state):
    streams, heads, head, width = state.shape
    group = 8
    inner = heads * head
    rows = 2 * streams
    whole = pl.BlockSpec(memory_space=pltpu.VMEM)
    return pl.pallas_call(
        functools.partial(recur_body, len(terms), group, model_width),
        out_shape=(
            jax.ShapeDtypeStruct((rows, inner), F32),
            jax.ShapeDtypeStruct((2, streams, inner), F32),
            jax.ShapeDtypeStruct((2, streams, width), F32),
            jax.ShapeDtypeStruct((streams, heads), F32),
            pltpu.VMEM(state.shape, state.dtype),
        ),
        grid=(streams // group,),
        in_specs=[pl.BlockSpec(memory_space=pltpu.SMEM)]
        + [whole] * (len(terms) + 5)
        + [pl.BlockSpec(memory_space=pl.ANY)] * 2,
        out_specs=(whole,) * 5,
        scratch_shapes=[
            pltpu.VMEM((2, streams, width), F32),
            pltpu.VMEM((2, streams, inner), F32),
            pltpu.VMEM((7 * streams, inner), F32),
            pltpu.VMEM((rows, inner), F32),
            pltpu.SemaphoreType.DMA((streams // group,)),
        ],
        compiler_params=params(),
        cost_estimate=cost(64 * state.size, 2 * state.size + 32 * rows * inner),
        name="recur",
    )(
        live_rows,
        *terms,
        sums,
        up_rows,
        bias[None],
        rate[None],
        skip[None],
        in_hbm(state),
        after,
    )


def state_write_body(feeds_ref, b_ref, decay_ref, state_ref, out_ref):
    group, heads, head, width = out_ref.shape
    at = pl.multiple_of(pl.program_id(0) * group, group)
    feeds = [split(feeds_ref[p, pl.ds(at, group), :]) for p in range(2)]
    rights = [split(b_ref[p, pl.ds(at, group), :]) for p in range(2)]
    left = [f.astype(F32) for pair in feeds for f in (pair[0], pair[1], pair[0])]
    right = [f.astype(F32) for pair in rights for f in (pair[0], pair[0], pair[1])]
    left = jnp.concatenate(left, 0).astype(BF16)
    right = jnp.concatenate(right, 0)
    stream = lax.broadcasted_iota(jnp.int32, right.shape, 0) % group
    for g in range(0, group, 2):
        pair = jnp.concatenate([jnp.where(stream == g + i, right, 0.0) for i in range(2)], 1)
        outer = lax.dot_general(
            left, pair.astype(BF16), (((0,), (0,)), ((), ())), preferred_element_type=F32
        )
        for i in range(2):
            scaled = state_ref[at + g + i].astype(F32) * decay_ref[g + i][:, None, :]
            own = outer[:, i * width : (i + 1) * width].reshape(heads, head, width)
            out_ref[g + i] = (scaled + own).astype(out_ref.dtype)


def state_write(feeds, b, decay, state):
    streams, heads, head, width = state.shape
    group = 8
    whole = pl.BlockSpec(memory_space=pltpu.VMEM)
    return pl.pallas_call(
        state_write_body,
        out_shape=jax.ShapeDtypeStruct(state.shape, state.dtype),
        grid=(streams // group,),
        in_specs=[
            whole,
            whole,
            pl.BlockSpec((group, heads, width), lambda i: (i, 0, 0)),
            whole,
        ],
        out_specs=pl.BlockSpec((group, heads, head, width), lambda i: (i, 0, 0, 0)),
        compiler_params=params(),
        cost_estimate=cost(32 * state.size, 4 * state.size),
        name="state_write",
    )(feeds, b, decay, state)


def output_tiles(distances, lhs_ref, weight_ref, out_ref):
    width = out_ref.shape[2]
    tile = min(width, 512)
    for j, distance in enumerate(distances):
        for t in range(0, width, tile):
            at = pl.multiple_of((lax.axis_index("head") ^ distance) * width + t, tile)
            acc = jnp.dot(lhs_ref[...], weight_ref[:, pl.ds(at, tile)], preferred_element_type=F32)
            out_ref[j, :, t : t + tile] = acc.astype(out_ref.dtype)


def output_first_body(distances, terms, model_width, *refs):
    term_refs = refs[:terms]
    sums_ref, result_ref, scale_ref, weight_ref, out_ref, lhs_ref, squares_ref = refs[terms:]
    total = sum(t[...].astype(F32) for t in term_refs) * inverse_of(sums_ref, model_width)
    gated = result_ref[...] * silu(total)
    squares_ref[...] = jnp.sum(gated * gated, -1, keepdims=True)
    lhs_ref[...] = (gated * scale_ref[...]).astype(lhs_ref.dtype)
    output_tiles(distances, lhs_ref, weight_ref, out_ref)


def output_rest_body(distances, lhs_ref, after_ref, weight_ref, out_ref):
    output_tiles(distances, lhs_ref, weight_ref, out_ref)


def output_parts(distances, weight, width, operands, model_width=None):
    first = model_width is not None
    rows, depth = operands[0].shape
    count = len(distances)
    whole = pl.BlockSpec(memory_space=pltpu.VMEM)
    specs = [whole] * (len(operands) + 1)
    body = functools.partial(output_rest_body, distances)
    out_shape = [jax.ShapeDtypeStruct((count, rows, width), BF16)]
    if first:
        body = functools.partial(output_first_body, distances, len(operands) - 3, model_width)
        out_shape += [
            jax.ShapeDtypeStruct((rows, depth), BF16),
            jax.ShapeDtypeStruct((rows, 1), F32),
        ]
    else:
        specs[1] = pl.BlockSpec(memory_space=pl.ANY)
    return pl.pallas_call(
        body,
        out_shape=tuple(out_shape),
        in_specs=specs,
        out_specs=(whole,) * len(out_shape),
        compiler_params=params(),
        cost_estimate=cost(2 * rows * depth * width * count, 2 * depth * width * count),
        name="output_first" if first else "output_rest",
    )(*operands, weight)


def split(values):
    high = values.astype(BF16)
    return high, (values - high.astype(F32)).astype(BF16)


def on_device(
    hidden,
    input_norm_scale,
    projection_signal,
    projection_gate,
    projection_step,
    projection_input_output,
    step_bias,
    head_decay_rate,
    head_skip_weight,
    gated_norm_scale,
    adapter_down_weight,
    adapter_up_weight,
    output_weight,
    scan_state,
    stream_tenant_index,
    live_block_rows,
):
    streams, positions, feature_width = hidden.shape
    rows = streams * positions
    heads_n = lax.axis_size("head")
    rows_n = lax.axis_size("row")
    model_width = feature_width * heads_n
    depth, inner = projection_signal.shape
    inner_width = inner * heads_n

    wide = jnp.swapaxes(hidden, 0, 1).astype(F32)
    scaled = (wide * input_norm_scale).astype(BF16)
    scaled_flat = scaled.reshape(rows, feature_width)

    squares = jnp.sum(wide * wide, -1).reshape(rows, 1)
    sums, up_rows = adapt(stream_tenant_index, scaled_flat, squares, adapter_down_weight, adapter_up_weight)

    weights = load(sums, [], projection_signal, projection_input_output, projection_gate)
    if heads_n == rows_n:
        turn = [
            (h * rows_n + r, reverse_bits(r, rows_n) * rows_n + h)
            for h in range(heads_n)
            for r in range(rows_n)
        ]
        blocks, order = gather_relative(
            [lax.ppermute(scaled[p], ("head", "row"), turn) for p in range(positions)],
            "head",
            weights[0],
        )
    else:
        features = lax.all_gather(scaled_flat, "head", axis=1, tiled=True)
        blocks = lax.all_to_all(features, "row", split_axis=1, concat_axis=0, tiled=True)
        blocks = blocks.reshape(rows_n, rows, depth)
        blocks = [blocks[i] for i in range(rows_n)]
        order = None

    signal_weight, mix_weight, gate_weight = weights
    send, keep, lhs = project_signal(
        blocks, order, rows_n, signal_weight, mix_weight, projection_step.T
    )
    received = swap(send, "row", 1)
    keep, out_weight = load(send, [keep], output_weight)
    gate_send, gate_keep, sums = project_gate(rows, lhs, gate_weight, sums, received)
    signal_terms, _ = scatter_rows(received, keep, "row")
    gate_terms, gate_last = scatter_rows(swap(gate_send, "row", 1), gate_keep, "row")
    sums = sum_over(sums, "head")

    result, feeds, bgate, both, state = recur(
        model_width,
        gate_last,
        live_block_rows,
        signal_terms,
        sums,
        up_rows,
        step_bias,
        head_decay_rate,
        head_skip_weight,
        scan_state,
    )

    distances = list(range(heads_n))
    first, out_lhs, gate_squares = output_parts(
        distances[3::4],
        out_weight,
        feature_width,
        [*gate_terms, sums, result, gated_norm_scale[None]],
        model_width,
    )
    (second,) = output_parts(
        distances[2::4] + distances[1::4], out_weight, feature_width, [out_lhs, first]
    )
    half = second.shape[0] // 2
    send = (swap(first, "head", 1).astype(F32) + second[:half].astype(F32)).astype(BF16)
    received = swap(send, "head", 2)
    (rest,) = output_parts(distances[0::4], out_weight, feature_width, [out_lhs, send])
    kept = [swap(second[half:], "head", 1), rest]
    mixer, _ = scatter_rows(received, kept, "head", done=2)
    mixer = sum(t.astype(F32) for t in mixer)
    gate_squares = sum_over(gate_squares, "head")
    mixer = mixer * lax.rsqrt(gate_squares / inner_width + EPSILON)
    mixer = mixer.reshape(positions, streams, feature_width)
    live = jnp.arange(streams) < live_block_rows[0]
    mixed = (wide + jnp.where(live[:, None], mixer, 0.0)).astype(BF16)

    spread = jnp.broadcast_to(both[..., None], both.shape + (bgate.shape[-1],))
    new_state = state_write(feeds, bgate, spread, state)
    return (jnp.swapaxes(mixed, 0, 1), new_state)


def solution(mesh):
    in_specs = (
        P(("rep", "row"), None, "head"),
        P("head"),
        P("row", "head"),
        P("row", "head"),
        P("row", "head"),
        P("row", None),
        P("head"),
        P("head"),
        P("head"),
        P("head"),
        P("row", "head", None),
        P("row", None, "head"),
        P("head", None),
        P(("rep", "row"), "head", None, None),
        P(("rep", "row")),
        P(("rep", "row")),
    )
    out_specs = (P(("rep", "row"), None, "head"), P(("rep", "row"), "head", None, None))
    return jax.shard_map(
        on_device, mesh=mesh, in_specs=in_specs, out_specs=out_specs, check_vma=False
    )
```

```python
import functools

import jax
import jax.numpy as jnp
from jax import lax
from jax.experimental import pallas as pl
from jax.experimental.pallas import tpu as pltpu
from jax.sharding import PartitionSpec as P

BF16 = jnp.bfloat16
EPSILON = 1e-05
F32 = jnp.float32
VMEM_GRANT = 12 * 1024 * 1024


def swap(values, axis, distance):
    size = lax.axis_size(axis)
    return lax.ppermute(values, axis, [(i, i ^ distance) for i in range(size)])


def bits_of(size):
    return [1 << i for i in range(size.bit_length() - 1)]


def sum_over(values, axis):
    for distance in bits_of(lax.axis_size(axis)):
        values = values + swap(values, axis, distance)
    return values


def reverse_bits(value, size):
    bits = size.bit_length() - 1
    return sum(((value >> i) & 1) << (bits - 1 - i) for i in range(bits))


def params(**more):
    return pltpu.CompilerParams(vmem_limit_bytes=VMEM_GRANT, **more)


def cost(flops, size):
    return pl.CostEstimate(flops=int(flops), bytes_accessed=int(size), transcendentals=0)


def in_hbm(values):
    return pltpu.with_memory_space_constraint(values, pltpu.HBM)


def load_body(spans, after_ref, *refs):
    count = len(spans)
    sources, targets, semaphores = refs[:count], refs[count : 2 * count], refs[2 * count]
    copies = []
    for source, target, (start, rows, parts) in zip(sources, targets, spans):
        step = rows // parts
        for i in range(parts):
            copies.append(
                pltpu.make_async_copy(
                    source.at[pl.ds(start + i * step, step)],
                    target.at[pl.ds(i * step, step)],
                    semaphores.at[len(copies)],
                )
            )
    for copy in copies:
        copy.start()
    for copy in copies:
        copy.wait()


def load(after, passed, *weights):
    weights = [w if isinstance(w, tuple) else (w, 0, w.shape[0]) for w in weights]
    shapes = [p.shape for p in passed] + [(rows, *w.shape[1:]) for w, _, rows in weights]
    spans = [(0, p.shape[0], 1) for p in passed]
    spans += [(start, rows, 8 if rows % 128 == 0 else 1) for _, start, rows in weights]
    size = sum(rows * w.shape[1] * w.dtype.itemsize for w, _, rows in weights)
    return pl.pallas_call(
        functools.partial(load_body, spans),
        out_shape=tuple(pltpu.VMEM(shape, BF16) for shape in shapes),
        in_specs=[pl.BlockSpec(memory_space=pl.ANY)] * (1 + len(shapes)),
        out_specs=tuple(pl.BlockSpec(memory_space=pltpu.VMEM) for _ in shapes),
        scratch_shapes=[pltpu.SemaphoreType.DMA((sum(parts for _, _, parts in spans),))],
        compiler_params=params(),
        cost_estimate=cost(0, 2 * size),
        name="load",
    )(after, *passed, *[in_hbm(w) for w, _, _ in weights])


def own_columns(rows, streams, rank):
    row = lax.broadcasted_iota(jnp.int32, (rows, streams * rank), 0) % streams
    return row == lax.broadcasted_iota(jnp.int32, (rows, streams * rank), 1) // rank


def adapt_body(tenant_ref, scaled_ref, squares_ref, down_ref, up_ref, sums_ref, up_rows_ref, *scratch):
    down_rows_ref, semaphores = scratch
    rank = down_ref.shape[1]
    streams = tenant_ref.shape[0]
    rows = scaled_ref.shape[0]
    first = lax.axis_index("row") * down_ref.shape[0]
    downs, ups = [], []
    for s in range(streams):
        at = pl.ds(s * rank, rank)
        tenant = tenant_ref[s] - first
        downs.append(
            pltpu.make_async_copy(down_ref.at[tenant], down_rows_ref.at[at, :], semaphores.at[s])
        )
        ups.append(
            pltpu.make_async_copy(
                up_ref.at[tenant], up_rows_ref.at[at, :], semaphores.at[streams + s]
            )
        )
    for copy in downs + ups:
        copy.start()
    for copy in downs:
        copy.wait()
    every = lax.dot_general(
        scaled_ref[...],
        down_rows_ref[...],
        (((1,), (1,)), ((), ())),
        preferred_element_type=F32,
    )
    own = jnp.where(own_columns(rows, streams, rank), every, 0.0)
    fold = lax.broadcasted_iota(jnp.int32, (streams * rank, rank), 0) % rank
    fold = (fold == lax.broadcasted_iota(jnp.int32, (streams * rank, rank), 1)).astype(BF16)
    high, rest = split(own)
    middle, low = rest, (own - high.astype(F32) - rest.astype(F32)).astype(BF16)
    folded = sum(jnp.dot(x, fold, preferred_element_type=F32) for x in (high, middle, low))
    sums_ref[:, :rank] = folded
    sums_ref[:, rank:] = squares_ref[...]
    for copy in ups:
        copy.wait()


def adapt(tenants, scaled, squares, down, up):
    streams = tenants.shape[0]
    rows, depth = scaled.shape
    rank, inner = up.shape[1:]
    whole = pl.BlockSpec(memory_space=pltpu.VMEM)
    anywhere = pl.BlockSpec(memory_space=pl.ANY)
    return pl.pallas_call(
        adapt_body,
        out_shape=(
            jax.ShapeDtypeStruct((rows, rank + 1), F32),
            pltpu.VMEM((streams * rank, inner), BF16),
        ),
        in_specs=[pl.BlockSpec(memory_space=pltpu.SMEM), whole, whole, anywhere, anywhere],
        out_specs=(whole, whole),
        scratch_shapes=[
            pltpu.VMEM((streams * rank, depth), BF16),
            pltpu.SemaphoreType.DMA((2 * streams,)),
        ],
        compiler_params=params(),
        cost_estimate=cost(2 * rows * depth * streams * rank, 2 * streams * rank * (depth + inner)),
        name="adapt",
    )(tenants, scaled, squares, in_hbm(jnp.swapaxes(down, 1, 2)), in_hbm(up))


def project_signal_body(owners, order, *refs):
    blocks, refs = refs[: len(order)], refs[len(order) :]
    weight_ref, mix_ref, step_ref, send_ref, keep_ref, lhs_ref, semaphores = refs
    rows = blocks[0].shape[0]
    parts = len(blocks) // owners
    copies = []
    for i, block in enumerate(blocks):
        owner, part = order[i]
        away = (owner() ^ lax.axis_index("row")) % owners
        at = pl.multiple_of((away * parts + part) * rows, rows)
        copies.append(
            pltpu.make_async_copy(block, lhs_ref.at[pl.ds(at, rows), :], semaphores.at[i])
        )
    for copy in copies:
        copy.start()
    for copy in copies:
        copy.wait()
    lhs = lhs_ref[...]

    def put(acc, start):
        step = send_ref.shape[1]
        for k in range(owners):
            target = send_ref if k % 2 else keep_ref
            target[k // 2, :, start : start + acc.shape[1]] = acc[k * step : (k + 1) * step].astype(
                target.dtype
            )

    columns = weight_ref.shape[1]
    tile = min(columns, 512)
    for t in range(0, columns, tile):
        put(jnp.dot(lhs, weight_ref[:, t : t + tile], preferred_element_type=F32), t)
    put(jnp.dot(lhs, mix_ref[...], preferred_element_type=F32), columns)
    acc = lax.dot_general(lhs, step_ref[...], (((1,), (1,)), ((), ())), preferred_element_type=F32)
    put(acc, columns + mix_ref.shape[1])


def project_signal(blocks, order, owners, weight, mix, step, after):
    pieces = len(blocks)
    depth = blocks[0].shape[1]
    rows = pieces * blocks[0].shape[0]
    columns = weight.shape[1] + mix.shape[1] + step.shape[0]
    half = jax.ShapeDtypeStruct((owners // 2, rows // owners, columns), BF16)
    whole = pl.BlockSpec(memory_space=pltpu.VMEM)
    anywhere = pl.BlockSpec(memory_space=pl.ANY)

    def body(*refs):
        project_signal_body(owners, order, *refs[:pieces], *refs[pieces + 1 :])

    return pl.pallas_call(
        body,
        out_shape=(half, half, jax.ShapeDtypeStruct((rows, depth), BF16)),
        in_specs=[anywhere] * (pieces + 1) + [whole] * 3,
        out_specs=(whole,) * 3,
        scratch_shapes=[pltpu.SemaphoreType.DMA((pieces,))],
        compiler_params=params(),
        cost_estimate=cost(2 * rows * depth * columns, 2 * depth * columns),
        name="project_signal",
    )(*blocks, after, weight, mix, step)


def project_gate_body(groups, *refs):
    lhs_refs, refs = refs[:groups], refs[groups:]
    weight_ref, sums_ref, after_ref, send_ref, keep_ref, out_ref = refs
    out_ref[...] = sums_ref[...]
    rows = send_ref.shape[1]
    columns = weight_ref.shape[1]
    tile = min(columns, 512)
    first = group_of_own(groups)
    for t in range(0, columns, tile):
        for g, lhs_ref in enumerate(lhs_refs):
            acc = jnp.dot(lhs_ref[...], weight_ref[:, t : t + tile], preferred_element_type=F32)
            pairs = lhs_ref.shape[0] // (2 * rows)
            for k in range(2 * pairs):
                target = send_ref if k % 2 else keep_ref
                at = (first ^ g) * pairs + k // 2
                target[at, :, t : t + tile] = acc[k * rows : (k + 1) * rows].astype(target.dtype)


def group_of_own(groups):
    if groups == 1:
        return 0
    return (lax.axis_index("head") ^ lax.axis_index("row")) // 2


def project_gate(rows, lhs, weight, sums, after):
    count = sum(part.shape[0] for part in lhs) // rows
    columns = weight.shape[1]
    half = jax.ShapeDtypeStruct((count // 2, rows, columns), BF16)
    whole = pl.BlockSpec(memory_space=pltpu.VMEM)
    return pl.pallas_call(
        functools.partial(project_gate_body, len(lhs)),
        out_shape=(half, half, jax.ShapeDtypeStruct(sums.shape, sums.dtype)),
        in_specs=[whole] * (len(lhs) + 2) + [pl.BlockSpec(memory_space=pl.ANY)],
        out_specs=(whole,) * 3,
        compiler_params=params(),
        cost_estimate=cost(2 * count * rows * lhs[0].shape[1] * columns, 2 * weight.size),
        name="project_gate",
    )(*lhs, weight, sums, after)


def scatter_rows(received, keep, axis, done=1):
    send = received
    terms = [received] + (keep if isinstance(keep, list) else [keep])
    for distance in bits_of(lax.axis_size(axis))[done:]:
        send = sum(t[1::2].astype(F32) for t in terms).astype(BF16)
        terms = [swap(send, axis, distance)] + [t[0::2] for t in terms]
    return [t[0] for t in terms], send


def softplus(values):
    return jnp.maximum(values, 0.0) + jnp.log1p(jnp.exp(-jnp.abs(values)))


def silu(values):
    return values / (1.0 + jnp.exp(-values))


def inverse_of(sums_ref, width):
    return lax.rsqrt(sums_ref[:, sums_ref.shape[1] - 1 :] / width + EPSILON)


def recur_body(
    terms,
    group,
    model_width,
    live_ref,
    *refs,
):
    term_refs = refs[:terms]
    sums_ref, up_ref, bias_ref, rate_ref, skip_ref, source_ref, _ = refs[terms : terms + 7]
    result_ref, feeds_ref, b_ref, both_ref, state_ref, *scratch = refs[terms + 7 :]
    c_ref, read_ref, spread_ref, signal_ref, semaphores = scratch
    heads, head, width = state_ref.shape[1:]
    streams, inner = feeds_ref.shape[1:]
    step = pl.program_id(0)

    def fetch(i):
        at = pl.ds(i * group, group)
        return pltpu.make_async_copy(source_ref.at[at], state_ref.at[at], semaphores.at[i])

    @pl.when(step == 0)
    def _():
        for i in range(streams // group):
            fetch(i).start()
        rows = sums_ref.shape[0]
        rank = sums_ref.shape[1] - 1
        inverse = inverse_of(sums_ref, model_width)
        lowrank = (sums_ref[:, :rank] * inverse).astype(BF16)
        repeat = lax.broadcasted_iota(jnp.int32, (rank, streams * rank), 1) % rank
        repeat = (repeat == lax.broadcasted_iota(jnp.int32, (rank, streams * rank), 0)).astype(BF16)
        every = jnp.dot(lowrank, repeat, preferred_element_type=F32)
        own = jnp.where(own_columns(rows, streams, rank), every, 0.0).astype(BF16)
        adapted = jnp.dot(own, up_ref[...], preferred_element_type=F32)
        total = sum(t[...].astype(F32) for t in term_refs) * inverse
        signal_ref[...] = silu(total[:, :inner] + adapted)
        gates = silu(total[:, inner : inner + 2 * width])
        steps_dt = softplus(total[:, inner + 2 * width :] + bias_ref[...])
        b = [gates[p * streams : (p + 1) * streams, :width] for p in range(2)]
        c = [gates[p * streams : (p + 1) * streams, width:] for p in range(2)]
        for p in range(2):
            b_ref[p] = b[p]
            c_ref[p] = c[p]
        live = lax.broadcasted_iota(jnp.int32, (streams, heads), 0) < live_ref[0]
        dt = [steps_dt[p * streams : (p + 1) * streams] for p in range(2)]
        decay = [jnp.where(live, jnp.exp(-d * rate_ref[...]), 1.0) for d in dt]
        fed = [jnp.where(live, d, 0.0) for d in dt]

        def match(i, j):
            return jnp.sum(b[i] * c[j], -1, keepdims=True)

        both = decay[0] * decay[1]
        both_ref[...] = both
        late = decay[1] * fed[0]
        skip = skip_ref[...]
        factors = jnp.concatenate(
            [
                decay[0],
                both,
                fed[0] * match(0, 0) + skip,
                fed[1] * match(1, 1) + skip,
                late * match(0, 1),
                late,
                fed[1],
            ],
            0,
        )
        high, low = split(factors)
        place = lax.broadcasted_iota(jnp.int32, (heads, inner), 1) // head
        ones = (place == lax.broadcasted_iota(jnp.int32, (heads, inner), 0)).astype(BF16)
        spread_ref[...] = jnp.dot(high, ones, preferred_element_type=F32) + jnp.dot(
            low, ones, preferred_element_type=F32
        )

    fetch(step).wait()
    at = pl.multiple_of(step * group, group)
    c = jnp.concatenate([c_ref[p, pl.ds(at, group), :] for p in range(2)], 0)
    lhs = jnp.concatenate(split(c), 0)
    for g in range(group):
        state = state_ref[at + g].reshape(inner, width)
        found = lax.dot_general(lhs, state, (((1,), (1,)), ((), ())), preferred_element_type=F32)
        for p in range(2):
            row = p * group + g
            low = 2 * group + row
            read_ref[p, pl.ds(at + g, 1), :] = found[row : row + 1] + found[low : low + 1]

    @pl.when(step == pl.num_programs(0) - 1)
    def _():
        factor = [spread_ref[i * streams : (i + 1) * streams, :] for i in range(7)]
        first = signal_ref[:streams, :]
        second = signal_ref[streams:, :]
        result_ref[:streams, :] = factor[0] * read_ref[0] + factor[2] * first
        result_ref[streams:, :] = factor[1] * read_ref[1] + factor[4] * first + factor[3] * second
        feeds_ref[0] = factor[5] * first
        feeds_ref[1] = factor[6] * second


def recur(model_width, after, live_rows, terms, sums, up_rows, bias, rate, skip, state):
    streams, heads, head, width = state.shape
    group = 8
    inner = heads * head
    rows = 2 * streams
    whole = pl.BlockSpec(memory_space=pltpu.VMEM)
    return pl.pallas_call(
        functools.partial(recur_body, len(terms), group, model_width),
        out_shape=(
            jax.ShapeDtypeStruct((rows, inner), F32),
            jax.ShapeDtypeStruct((2, streams, inner), F32),
            jax.ShapeDtypeStruct((2, streams, width), F32),
            jax.ShapeDtypeStruct((streams, heads), F32),
            pltpu.VMEM(state.shape, state.dtype),
        ),
        grid=(streams // group,),
        in_specs=[pl.BlockSpec(memory_space=pltpu.SMEM)]
        + [whole] * (len(terms) + 5)
        + [pl.BlockSpec(memory_space=pl.ANY)] * 2,
        out_specs=(whole,) * 5,
        scratch_shapes=[
            pltpu.VMEM((2, streams, width), F32),
            pltpu.VMEM((2, streams, inner), F32),
            pltpu.VMEM((7 * streams, inner), F32),
            pltpu.VMEM((rows, inner), F32),
            pltpu.SemaphoreType.DMA((streams // group,)),
        ],
        compiler_params=params(),
        cost_estimate=cost(64 * state.size, 2 * state.size + 32 * rows * inner),
        name="recur",
    )(
        live_rows,
        *terms,
        sums,
        up_rows,
        bias[None],
        rate[None],
        skip[None],
        in_hbm(state),
        after,
    )


def state_write_body(feeds_ref, b_ref, decay_ref, state_ref, out_ref):
    group, heads, head, width = out_ref.shape
    at = pl.multiple_of(pl.program_id(0) * group, group)
    feeds = [split(feeds_ref[p, pl.ds(at, group), :]) for p in range(2)]
    rights = [split(b_ref[p, pl.ds(at, group), :]) for p in range(2)]
    left = [f.astype(F32) for pair in feeds for f in (pair[0], pair[1], pair[0])]
    right = [f.astype(F32) for pair in rights for f in (pair[0], pair[0], pair[1])]
    left = jnp.concatenate(left, 0).astype(BF16)
    right = jnp.concatenate(right, 0)
    stream = lax.broadcasted_iota(jnp.int32, right.shape, 0) % group
    for g in range(0, group, 2):
        pair = jnp.concatenate([jnp.where(stream == g + i, right, 0.0) for i in range(2)], 1)
        outer = lax.dot_general(
            left, pair.astype(BF16), (((0,), (0,)), ((), ())), preferred_element_type=F32
        )
        for i in range(2):
            scaled = state_ref[at + g + i].astype(F32) * decay_ref[g + i][:, None, :]
            own = outer[:, i * width : (i + 1) * width].reshape(heads, head, width)
            out_ref[g + i] = (scaled + own).astype(out_ref.dtype)


def state_write(feeds, b, decay, state):
    streams, heads, head, width = state.shape
    group = 8
    whole = pl.BlockSpec(memory_space=pltpu.VMEM)
    return pl.pallas_call(
        state_write_body,
        out_shape=jax.ShapeDtypeStruct(state.shape, state.dtype),
        grid=(streams // group,),
        in_specs=[
            whole,
            whole,
            pl.BlockSpec((group, heads, width), lambda i: (i, 0, 0)),
            whole,
        ],
        out_specs=pl.BlockSpec((group, heads, head, width), lambda i: (i, 0, 0, 0)),
        compiler_params=params(),
        cost_estimate=cost(32 * state.size, 4 * state.size),
        name="state_write",
    )(feeds, b, decay, state)


def output_tiles(distances, lhs_ref, weight_refs, out_ref):
    width = out_ref.shape[2]
    tile = min(width, 512)
    for j, distance in enumerate(distances):
        for t in range(0, width, tile):
            at = pl.multiple_of((lax.axis_index("head") ^ distance) * width + t, tile)
            acc, start = 0.0, 0
            for weight_ref in weight_refs:
                stop = start + weight_ref.shape[0]
                acc += jnp.dot(
                    lhs_ref[:, start:stop],
                    weight_ref[:, pl.ds(at, tile)],
                    preferred_element_type=F32,
                )
                start = stop
            out_ref[j, :, t : t + tile] = acc.astype(out_ref.dtype)


def output_first_body(distances, terms, model_width, *refs):
    term_refs = refs[:terms]
    sums_ref, result_ref, scale_ref, *weight_refs, out_ref, lhs_ref, squares_ref = refs[terms:]
    total = sum(t[...].astype(F32) for t in term_refs) * inverse_of(sums_ref, model_width)
    gated = result_ref[...] * silu(total)
    squares_ref[...] = jnp.sum(gated * gated, -1, keepdims=True)
    lhs_ref[...] = (gated * scale_ref[...]).astype(lhs_ref.dtype)
    output_tiles(distances, lhs_ref, weight_refs, out_ref)


def output_rest_body(distances, lhs_ref, after_ref, *refs):
    output_tiles(distances, lhs_ref, refs[:-1], refs[-1])


def output_parts(distances, weights, width, operands, model_width=None):
    first = model_width is not None
    rows, depth = operands[0].shape
    count = len(distances)
    whole = pl.BlockSpec(memory_space=pltpu.VMEM)
    specs = [whole] * (len(operands) + len(weights))
    body = functools.partial(output_rest_body, distances)
    out_shape = [jax.ShapeDtypeStruct((count, rows, width), BF16)]
    if first:
        body = functools.partial(output_first_body, distances, len(operands) - 3, model_width)
        out_shape += [
            jax.ShapeDtypeStruct((rows, depth), BF16),
            jax.ShapeDtypeStruct((rows, 1), F32),
        ]
    else:
        specs[1] = pl.BlockSpec(memory_space=pl.ANY)
    return pl.pallas_call(
        body,
        out_shape=tuple(out_shape),
        in_specs=specs,
        out_specs=(whole,) * len(out_shape),
        compiler_params=params(),
        cost_estimate=cost(2 * rows * depth * width * count, 2 * depth * width * count),
        name="output_first" if first else "output_rest",
    )(*operands, *weights)


def split(values):
    high = values.astype(BF16)
    return high, (values - high.astype(F32)).astype(BF16)


def on_device(
    hidden,
    input_norm_scale,
    projection_signal,
    projection_gate,
    projection_step,
    projection_input_output,
    step_bias,
    head_decay_rate,
    head_skip_weight,
    gated_norm_scale,
    adapter_down_weight,
    adapter_up_weight,
    output_weight,
    scan_state,
    stream_tenant_index,
    live_block_rows,
):
    streams, positions, feature_width = hidden.shape
    rows = streams * positions
    heads_n = lax.axis_size("head")
    rows_n = lax.axis_size("row")
    model_width = feature_width * heads_n
    depth, inner = projection_signal.shape
    inner_width = inner * heads_n

    wide = jnp.swapaxes(hidden, 0, 1).astype(F32)
    scaled = (wide * input_norm_scale).astype(BF16)
    scaled_flat = scaled.reshape(rows, feature_width)

    squares = jnp.sum(wide * wide, -1).reshape(rows, 1)
    sums, up_rows = adapt(stream_tenant_index, scaled_flat, squares, adapter_down_weight, adapter_up_weight)

    weights = load(sums, [], projection_signal, projection_input_output, projection_gate)
    signal_weights = (*weights[:2], projection_step.T)
    middle = output_weight.shape[0] // 2
    if heads_n == rows_n and len(bits_of(rows_n)) == 2:
        turn = [(h * rows_n + r, r * rows_n + h) for h in range(heads_n) for r in range(rows_n)]
        turned = [lax.ppermute(scaled[p], ("head", "row"), turn) for p in range(positions)]
        turned, _ = lax.optimization_barrier((turned, weights[0]))
        crossed = [swap(part, "head", 2) for part in turned]

        def order(distance):
            return [
                (lambda d=d: lax.axis_index("head") ^ d, p)
                for d in (distance, distance ^ 1)
                for p in range(positions)
            ]

        near = turned + [swap(part, "head", 1) for part in turned]
        near_send, near_keep, near_lhs = project_signal(near, order(0), 2, *signal_weights, sums)
        (out_early,) = load(near_send, [], (output_weight, 0, middle))
        near_other = swap(near_send, "row", 1)
        crossed, _ = lax.optimization_barrier((crossed, near_send))
        far = crossed + [swap(part, "head", 1) for part in crossed]
        far_send, far_keep, far_lhs = project_signal(far, order(2), 2, *signal_weights, out_early)
        far_other = swap(far_send, "row", 1)
        gate_send, gate_keep, sums = project_gate(
            rows, [near_lhs, far_lhs], weights[2], sums, far_send
        )
        far_keep, out_late = load(gate_send, [far_keep], (output_weight, middle, middle))
        own = group_of_own(2) == 0
        pick = [(near_keep, far_keep), (near_other, far_other)]
        last_send = sum(jnp.where(own, f, n).astype(F32) for n, f in pick).astype(BF16)
        signal_terms = [jnp.where(own, n, f)[0] for n, f in pick]
        signal_terms = [swap(last_send, "row", 2)[0]] + signal_terms
    else:
        features = lax.all_gather(scaled_flat, "head", axis=1, tiled=True)
        blocks = lax.all_to_all(features, "row", split_axis=1, concat_axis=0, tiled=True)
        blocks = blocks.reshape(rows_n, rows, depth)
        blocks = [blocks[i] for i in range(rows_n)]
        order = [(lambda i=i: i, 0) for i in range(rows_n)]
        send, keep, lhs = project_signal(blocks, order, rows_n, *signal_weights, sums)
        received = swap(send, "row", 1)
        gate_send, gate_keep, sums = project_gate(rows, [lhs], weights[2], sums, send)
        keep, out_early, out_late = load(
            gate_send, [keep], (output_weight, 0, middle), (output_weight, middle, middle)
        )
        signal_terms, _ = scatter_rows(received, keep, "row")
    out_weights = [out_early, out_late]
    gate_terms, gate_last = scatter_rows(swap(gate_send, "row", 1), gate_keep, "row")
    sums = sum_over(sums, "head")

    result, feeds, bgate, both, state = recur(
        model_width,
        gate_last,
        live_block_rows,
        signal_terms,
        sums,
        up_rows,
        step_bias,
        head_decay_rate,
        head_skip_weight,
        scan_state,
    )

    distances = list(range(heads_n))
    first, out_lhs, gate_squares = output_parts(
        distances[3::4],
        out_weights,
        feature_width,
        [*gate_terms, sums, result, gated_norm_scale[None]],
        model_width,
    )
    (rest,) = output_parts(
        distances[2::4] + distances[1::4] + distances[0::4],
        out_weights,
        feature_width,
        [out_lhs, first],
    )
    quarter = rest.shape[0] // 3
    second, third, fourth = (rest[i * quarter : (i + 1) * quarter] for i in range(3))
    send = (swap(first, "head", 1).astype(F32) + second.astype(F32)).astype(BF16)
    kept = [swap(third, "head", 1), fourth]
    mixer, _ = scatter_rows(swap(send, "head", 2), kept, "head", done=2)
    mixer = sum(t.astype(F32) for t in mixer)
    gate_squares = sum_over(gate_squares, "head")
    mixer = mixer * lax.rsqrt(gate_squares / inner_width + EPSILON)
    mixer = mixer.reshape(positions, streams, feature_width)
    live = jnp.arange(streams) < live_block_rows[0]
    mixed = (wide + jnp.where(live[:, None], mixer, 0.0)).astype(BF16)

    spread = jnp.broadcast_to(both[..., None], both.shape + (bgate.shape[-1],))
    new_state = state_write(feeds, bgate, spread, state)
    return (jnp.swapaxes(mixed, 0, 1), new_state)


def solution(mesh):
    in_specs = (
        P(("rep", "row"), None, "head"),
        P("head"),
        P("row", "head"),
        P("row", "head"),
        P("row", "head"),
        P("row", None),
        P("head"),
        P("head"),
        P("head"),
        P("head"),
        P("row", "head", None),
        P("row", None, "head"),
        P("head", None),
        P(("rep", "row"), "head", None, None),
        P(("rep", "row")),
        P(("rep", "row")),
    )
    out_specs = (P(("rep", "row"), None, "head"), P(("rep", "row"), "head", None, None))
    return jax.shard_map(
        on_device, mesh=mesh, in_specs=in_specs, out_specs=out_specs, check_vma=False
    )
```

```python
import functools

import jax
import jax.numpy as jnp
from jax import lax
from jax.experimental import pallas as pl
from jax.experimental.pallas import tpu as pltpu
from jax.sharding import PartitionSpec as P

BF16 = jnp.bfloat16
EPSILON = 1e-05
F32 = jnp.float32
VMEM_GRANT = 12 * 1024 * 1024


def swap(values, axis, distance):
    size = lax.axis_size(axis)
    return lax.ppermute(values, axis, [(i, i ^ distance) for i in range(size)])


def bits_of(size):
    return [1 << i for i in range(size.bit_length() - 1)]


def sum_over(values, axis):
    for distance in bits_of(lax.axis_size(axis)):
        values = values + swap(values, axis, distance)
    return values


def reverse_bits(value, size):
    bits = size.bit_length() - 1
    return sum(((value >> i) & 1) << (bits - 1 - i) for i in range(bits))


def params(**more):
    return pltpu.CompilerParams(vmem_limit_bytes=VMEM_GRANT, **more)


def cost(flops, size):
    return pl.CostEstimate(flops=int(flops), bytes_accessed=int(size), transcendentals=0)


def in_hbm(values):
    return pltpu.with_memory_space_constraint(values, pltpu.HBM)


def in_vmem(values):
    return pltpu.with_memory_space_constraint(values, pltpu.VMEM)


def load_body(spans, after_ref, *refs):
    count = len(spans)
    sources, targets, semaphores = refs[:count], refs[count : 2 * count], refs[2 * count]
    copies = []
    for source, target, (start, rows, parts) in zip(sources, targets, spans):
        step = rows // parts
        for i in range(parts):
            copies.append(
                pltpu.make_async_copy(
                    source.at[pl.ds(start + i * step, step)],
                    target.at[pl.ds(i * step, step)],
                    semaphores.at[len(copies)],
                )
            )
    for copy in copies:
        copy.start()
    for copy in copies:
        copy.wait()


def load(after, passed, *weights):
    weights = [w if isinstance(w, tuple) else (w, 0, w.shape[0]) for w in weights]
    shapes = [p.shape for p in passed] + [(rows, *w.shape[1:]) for w, _, rows in weights]
    spans = [(0, p.shape[0], 1) for p in passed]
    spans += [(start, rows, 8 if rows % 128 == 0 else 1) for _, start, rows in weights]
    size = sum(rows * w.shape[1] * w.dtype.itemsize for w, _, rows in weights)
    return pl.pallas_call(
        functools.partial(load_body, spans),
        out_shape=tuple(pltpu.VMEM(shape, BF16) for shape in shapes),
        in_specs=[pl.BlockSpec(memory_space=pl.ANY)] * (1 + len(shapes)),
        out_specs=tuple(pl.BlockSpec(memory_space=pltpu.VMEM) for _ in shapes),
        scratch_shapes=[pltpu.SemaphoreType.DMA((sum(parts for _, _, parts in spans),))],
        compiler_params=params(),
        cost_estimate=cost(0, 2 * size),
        name="load",
    )(after, *passed, *[in_hbm(w) for w, _, _ in weights])


def own_columns(rows, streams, rank):
    row = lax.broadcasted_iota(jnp.int32, (rows, streams * rank), 0) % streams
    return row == lax.broadcasted_iota(jnp.int32, (rows, streams * rank), 1) // rank


def adapt_body(tenant_ref, scaled_ref, squares_ref, down_ref, up_ref, sums_ref, up_rows_ref, *scratch):
    down_rows_ref, semaphores = scratch
    rank = down_ref.shape[1]
    streams = tenant_ref.shape[0]
    rows = scaled_ref.shape[0]
    first = lax.axis_index("row") * down_ref.shape[0]
    downs, ups = [], []
    for s in range(streams):
        at = pl.ds(s * rank, rank)
        tenant = tenant_ref[s] - first
        downs.append(
            pltpu.make_async_copy(down_ref.at[tenant], down_rows_ref.at[at, :], semaphores.at[s])
        )
        ups.append(
            pltpu.make_async_copy(
                up_ref.at[tenant], up_rows_ref.at[at, :], semaphores.at[streams + s]
            )
        )
    for copy in downs + ups:
        copy.start()
    for copy in downs:
        copy.wait()
    every = lax.dot_general(
        scaled_ref[...],
        down_rows_ref[...],
        (((1,), (1,)), ((), ())),
        preferred_element_type=F32,
    )
    own = jnp.where(own_columns(rows, streams, rank), every, 0.0)
    fold = lax.broadcasted_iota(jnp.int32, (streams * rank, rank), 0) % rank
    fold = (fold == lax.broadcasted_iota(jnp.int32, (streams * rank, rank), 1)).astype(BF16)
    high, rest = split(own)
    middle, low = rest, (own - high.astype(F32) - rest.astype(F32)).astype(BF16)
    folded = sum(jnp.dot(x, fold, preferred_element_type=F32) for x in (high, middle, low))
    sums_ref[:, :rank] = folded
    sums_ref[:, rank:] = squares_ref[...]
    for copy in ups:
        copy.wait()


def adapt(tenants, scaled, squares, down, up):
    streams = tenants.shape[0]
    rows, depth = scaled.shape
    rank, inner = up.shape[1:]
    whole = pl.BlockSpec(memory_space=pltpu.VMEM)
    anywhere = pl.BlockSpec(memory_space=pl.ANY)
    return pl.pallas_call(
        adapt_body,
        out_shape=(
            jax.ShapeDtypeStruct((rows, rank + 1), F32),
            pltpu.VMEM((streams * rank, inner), BF16),
        ),
        in_specs=[pl.BlockSpec(memory_space=pltpu.SMEM), whole, whole, anywhere, anywhere],
        out_specs=(whole, whole),
        scratch_shapes=[
            pltpu.VMEM((streams * rank, depth), BF16),
            pltpu.SemaphoreType.DMA((2 * streams,)),
        ],
        compiler_params=params(),
        cost_estimate=cost(2 * rows * depth * streams * rank, 2 * streams * rank * (depth + inner)),
        name="adapt",
    )(tenants, scaled, squares, in_hbm(jnp.swapaxes(down, 1, 2)), in_hbm(up))


def project_signal_body(owners, order, *refs):
    blocks, refs = refs[: len(order)], refs[len(order) :]
    weight_ref, mix_ref, step_ref, send_ref, keep_ref, lhs_ref, semaphores = refs
    rows = blocks[0].shape[0]
    parts = len(blocks) // owners
    copies = []
    for i, block in enumerate(blocks):
        owner, part = order[i]
        away = (owner() ^ lax.axis_index("row")) % owners
        at = pl.multiple_of((away * parts + part) * rows, rows)
        copies.append(
            pltpu.make_async_copy(block, lhs_ref.at[pl.ds(at, rows), :], semaphores.at[i])
        )
    for copy in copies:
        copy.start()
    for copy in copies:
        copy.wait()
    lhs = lhs_ref[...]

    def put(acc, start):
        step = send_ref.shape[1]
        for k in range(owners):
            target = send_ref if k % 2 else keep_ref
            target[k // 2, :, start : start + acc.shape[1]] = acc[k * step : (k + 1) * step].astype(
                target.dtype
            )

    columns = weight_ref.shape[1]
    tile = min(columns, 512)
    for t in range(0, columns, tile):
        put(jnp.dot(lhs, weight_ref[:, t : t + tile], preferred_element_type=F32), t)
    put(jnp.dot(lhs, mix_ref[...], preferred_element_type=F32), columns)
    acc = lax.dot_general(lhs, step_ref[...], (((1,), (1,)), ((), ())), preferred_element_type=F32)
    put(acc, columns + mix_ref.shape[1])


def project_signal(blocks, order, owners, weight, mix, step, after):
    pieces = len(blocks)
    depth = blocks[0].shape[1]
    rows = pieces * blocks[0].shape[0]
    columns = weight.shape[1] + mix.shape[1] + step.shape[0]
    half = jax.ShapeDtypeStruct((owners // 2, rows // owners, columns), BF16)
    whole = pl.BlockSpec(memory_space=pltpu.VMEM)
    anywhere = pl.BlockSpec(memory_space=pl.ANY)

    def body(*refs):
        project_signal_body(owners, order, *refs[:pieces], *refs[pieces + 1 :])

    return pl.pallas_call(
        body,
        out_shape=(half, half, jax.ShapeDtypeStruct((rows, depth), BF16)),
        in_specs=[anywhere] * (pieces + 1) + [whole] * 3,
        out_specs=(whole,) * 3,
        scratch_shapes=[pltpu.SemaphoreType.DMA((pieces,))],
        compiler_params=params(),
        cost_estimate=cost(2 * rows * depth * columns, 2 * depth * columns),
        name="project_signal",
    )(*blocks, after, in_vmem(weight), in_vmem(mix), step)


def project_gate_body(groups, *refs):
    lhs_refs, refs = refs[:groups], refs[groups:]
    weight_ref, after_ref, send_ref, keep_ref = refs
    rows = send_ref.shape[1]
    columns = weight_ref.shape[1]
    tile = min(columns, 512)
    first = group_of_own(groups)
    for t in range(0, columns, tile):
        for g, lhs_ref in enumerate(lhs_refs):
            acc = jnp.dot(lhs_ref[...], weight_ref[:, t : t + tile], preferred_element_type=F32)
            pairs = lhs_ref.shape[0] // (2 * rows)
            for k in range(2 * pairs):
                target = send_ref if k % 2 else keep_ref
                at = (first ^ g) * pairs + k // 2
                target[at, :, t : t + tile] = acc[k * rows : (k + 1) * rows].astype(target.dtype)


def group_of_own(groups):
    if groups == 1:
        return 0
    return (lax.axis_index("head") ^ lax.axis_index("row")) // 2


def project_gate(rows, lhs, weight, after):
    count = sum(part.shape[0] for part in lhs) // rows
    columns = weight.shape[1]
    half = jax.ShapeDtypeStruct((count // 2, rows, columns), BF16)
    whole = pl.BlockSpec(memory_space=pltpu.VMEM)
    return pl.pallas_call(
        functools.partial(project_gate_body, len(lhs)),
        out_shape=(half, half),
        in_specs=[whole] * (len(lhs) + 1) + [pl.BlockSpec(memory_space=pl.ANY)],
        out_specs=(whole,) * 2,
        compiler_params=params(),
        cost_estimate=cost(2 * count * rows * lhs[0].shape[1] * columns, 2 * weight.size),
        name="project_gate",
    )(*lhs, in_vmem(weight), after)


def scatter_rows(received, keep, axis, done=1):
    send = received
    terms = [received] + (keep if isinstance(keep, list) else [keep])
    for distance in bits_of(lax.axis_size(axis))[done:]:
        send = sum(t[1::2].astype(F32) for t in terms).astype(BF16)
        terms = [swap(send, axis, distance)] + [t[0::2] for t in terms]
    return [t[0] for t in terms], send


def softplus(values):
    return jnp.maximum(values, 0.0) + jnp.log1p(jnp.exp(-jnp.abs(values)))


def silu(values):
    return values / (1.0 + jnp.exp(-values))


def inverse_of(sums_ref, width):
    return lax.rsqrt(sums_ref[:, sums_ref.shape[1] - 1 :] / width + EPSILON)


def recur_body(
    terms,
    group,
    model_width,
    live_ref,
    *refs,
):
    term_refs = refs[:terms]
    sums_ref, up_ref, bias_ref, rate_ref, skip_ref, source_ref, _ = refs[terms : terms + 7]
    result_ref, feeds_ref, b_ref, both_ref, state_ref, *scratch = refs[terms + 7 :]
    c_ref, read_ref, spread_ref, signal_ref, semaphores = scratch
    heads, head, width = state_ref.shape[1:]
    streams, inner = feeds_ref.shape[1:]
    step = pl.program_id(0)

    def fetch(i):
        at = pl.ds(i * group, group)
        return pltpu.make_async_copy(source_ref.at[at], state_ref.at[at], semaphores.at[i])

    @pl.when(step == 0)
    def _():
        for i in range(streams // group):
            fetch(i).start()
        rows = sums_ref.shape[0]
        rank = sums_ref.shape[1] - 1
        inverse = inverse_of(sums_ref, model_width)
        lowrank = (sums_ref[:, :rank] * inverse).astype(BF16)
        repeat = lax.broadcasted_iota(jnp.int32, (rank, streams * rank), 1) % rank
        repeat = (repeat == lax.broadcasted_iota(jnp.int32, (rank, streams * rank), 0)).astype(BF16)
        every = jnp.dot(lowrank, repeat, preferred_element_type=F32)
        own = jnp.where(own_columns(rows, streams, rank), every, 0.0).astype(BF16)
        adapted = jnp.dot(own, up_ref[...], preferred_element_type=F32)
        total = sum(t[...].astype(F32) for t in term_refs) * inverse
        signal_ref[...] = silu(total[:, :inner] + adapted)
        gates = silu(total[:, inner : inner + 2 * width])
        steps_dt = softplus(total[:, inner + 2 * width :] + bias_ref[...])
        b = [gates[p * streams : (p + 1) * streams, :width] for p in range(2)]
        c = [gates[p * streams : (p + 1) * streams, width:] for p in range(2)]
        for p in range(2):
            b_ref[p] = b[p]
            c_ref[p] = c[p]
        live = lax.broadcasted_iota(jnp.int32, (streams, heads), 0) < live_ref[0]
        dt = [steps_dt[p * streams : (p + 1) * streams] for p in range(2)]
        decay = [jnp.where(live, jnp.exp(-d * rate_ref[...]), 1.0) for d in dt]
        fed = [jnp.where(live, d, 0.0) for d in dt]

        def match(i, j):
            return jnp.sum(b[i] * c[j], -1, keepdims=True)

        both = decay[0] * decay[1]
        both_ref[...] = both
        late = decay[1] * fed[0]
        skip = skip_ref[...]
        factors = jnp.concatenate(
            [
                decay[0],
                both,
                fed[0] * match(0, 0) + skip,
                fed[1] * match(1, 1) + skip,
                late * match(0, 1),
                late,
                fed[1],
            ],
            0,
        )
        high, low = split(factors)
        place = lax.broadcasted_iota(jnp.int32, (heads, inner), 1) // head
        ones = (place == lax.broadcasted_iota(jnp.int32, (heads, inner), 0)).astype(BF16)
        spread_ref[...] = jnp.dot(high, ones, preferred_element_type=F32) + jnp.dot(
            low, ones, preferred_element_type=F32
        )

    fetch(step).wait()
    at = pl.multiple_of(step * group, group)
    c = jnp.concatenate([c_ref[p, pl.ds(at, group), :] for p in range(2)], 0)
    lhs = jnp.concatenate(split(c), 0)
    for g in range(group):
        state = state_ref[at + g].reshape(inner, width)
        found = lax.dot_general(lhs, state, (((1,), (1,)), ((), ())), preferred_element_type=F32)
        for p in range(2):
            row = p * group + g
            low = 2 * group + row
            read_ref[p, pl.ds(at + g, 1), :] = found[row : row + 1] + found[low : low + 1]

    @pl.when(step == pl.num_programs(0) - 1)
    def _():
        factor = [spread_ref[i * streams : (i + 1) * streams, :] for i in range(7)]
        first = signal_ref[:streams, :]
        second = signal_ref[streams:, :]
        result_ref[:streams, :] = factor[0] * read_ref[0] + factor[2] * first
        result_ref[streams:, :] = factor[1] * read_ref[1] + factor[4] * first + factor[3] * second
        feeds_ref[0] = factor[5] * first
        feeds_ref[1] = factor[6] * second


def recur(model_width, after, live_rows, terms, sums, up_rows, bias, rate, skip, state):
    streams, heads, head, width = state.shape
    group = 8
    inner = heads * head
    rows = 2 * streams
    whole = pl.BlockSpec(memory_space=pltpu.VMEM)
    return pl.pallas_call(
        functools.partial(recur_body, len(terms), group, model_width),
        out_shape=(
            jax.ShapeDtypeStruct((rows, inner), F32),
            jax.ShapeDtypeStruct((2, streams, inner), F32),
            jax.ShapeDtypeStruct((2, streams, width), F32),
            jax.ShapeDtypeStruct((streams, heads), F32),
            pltpu.VMEM(state.shape, state.dtype),
        ),
        grid=(streams // group,),
        in_specs=[pl.BlockSpec(memory_space=pltpu.SMEM)]
        + [whole] * (len(terms) + 5)
        + [pl.BlockSpec(memory_space=pl.ANY)] * 2,
        out_specs=(whole,) * 5,
        scratch_shapes=[
            pltpu.VMEM((2, streams, width), F32),
            pltpu.VMEM((2, streams, inner), F32),
            pltpu.VMEM((7 * streams, inner), F32),
            pltpu.VMEM((rows, inner), F32),
            pltpu.SemaphoreType.DMA((streams // group,)),
        ],
        compiler_params=params(),
        cost_estimate=cost(64 * state.size, 2 * state.size + 32 * rows * inner),
        name="recur",
    )(
        live_rows,
        *terms,
        sums,
        up_rows,
        bias[None],
        rate[None],
        skip[None],
        in_hbm(state),
        after,
    )


def state_write_body(feeds_ref, b_ref, decay_ref, state_ref, out_ref):
    group, heads, head, width = out_ref.shape
    at = pl.multiple_of(pl.program_id(0) * group, group)
    feeds = [split(feeds_ref[p, pl.ds(at, group), :]) for p in range(2)]
    rights = [split(b_ref[p, pl.ds(at, group), :]) for p in range(2)]
    left = [f.astype(F32) for pair in feeds for f in (pair[0], pair[1], pair[0])]
    right = [f.astype(F32) for pair in rights for f in (pair[0], pair[0], pair[1])]
    left = jnp.concatenate(left, 0).astype(BF16)
    right = jnp.concatenate(right, 0)
    stream = lax.broadcasted_iota(jnp.int32, right.shape, 0) % group
    for g in range(0, group, 2):
        pair = jnp.concatenate([jnp.where(stream == g + i, right, 0.0) for i in range(2)], 1)
        outer = lax.dot_general(
            left, pair.astype(BF16), (((0,), (0,)), ((), ())), preferred_element_type=F32
        )
        for i in range(2):
            scaled = state_ref[at + g + i].astype(F32) * decay_ref[g + i][:, None, :]
            own = outer[:, i * width : (i + 1) * width].reshape(heads, head, width)
            out_ref[g + i] = (scaled + own).astype(out_ref.dtype)


def state_write(feeds, b, decay, state):
    streams, heads, head, width = state.shape
    group = 8
    whole = pl.BlockSpec(memory_space=pltpu.VMEM)
    return pl.pallas_call(
        state_write_body,
        out_shape=jax.ShapeDtypeStruct(state.shape, state.dtype),
        grid=(streams // group,),
        in_specs=[
            whole,
            whole,
            pl.BlockSpec((group, heads, width), lambda i: (i, 0, 0)),
            whole,
        ],
        out_specs=pl.BlockSpec((group, heads, head, width), lambda i: (i, 0, 0, 0)),
        compiler_params=params(),
        cost_estimate=cost(32 * state.size, 4 * state.size),
        name="state_write",
    )(feeds, b, decay, state)


def output_tiles(distances, lhs_ref, weight_refs, out_ref):
    width = out_ref.shape[2]
    tile = min(width, 512)
    for j, distance in enumerate(distances):
        for t in range(0, width, tile):
            at = pl.multiple_of((lax.axis_index("head") ^ distance) * width + t, tile)
            acc, start = 0.0, 0
            for weight_ref in weight_refs:
                stop = start + weight_ref.shape[0]
                acc += jnp.dot(
                    lhs_ref[:, start:stop],
                    weight_ref[:, pl.ds(at, tile)],
                    preferred_element_type=F32,
                )
                start = stop
            out_ref[j, :, t : t + tile] = acc.astype(out_ref.dtype)


def output_first_body(distances, terms, model_width, *refs):
    term_refs = refs[:terms]
    sums_ref, result_ref, scale_ref, *weight_refs, out_ref, lhs_ref, squares_ref = refs[terms:]
    total = sum(t[...].astype(F32) for t in term_refs) * inverse_of(sums_ref, model_width)
    gated = result_ref[...] * silu(total)
    squares_ref[...] = jnp.sum(gated * gated, -1, keepdims=True)
    lhs_ref[...] = (gated * scale_ref[...]).astype(lhs_ref.dtype)
    output_tiles(distances, lhs_ref, weight_refs, out_ref)


def output_rest_body(distances, lhs_ref, after_ref, *refs):
    output_tiles(distances, lhs_ref, refs[:-1], refs[-1])


def output_parts(distances, weights, width, operands, model_width=None):
    first = model_width is not None
    rows, depth = operands[0].shape
    count = len(distances)
    whole = pl.BlockSpec(memory_space=pltpu.VMEM)
    specs = [whole] * (len(operands) + len(weights))
    body = functools.partial(output_rest_body, distances)
    out_shape = [jax.ShapeDtypeStruct((count, rows, width), BF16)]
    if first:
        body = functools.partial(output_first_body, distances, len(operands) - 3, model_width)
        out_shape += [
            jax.ShapeDtypeStruct((rows, depth), BF16),
            jax.ShapeDtypeStruct((rows, 1), F32),
        ]
    else:
        specs[1] = pl.BlockSpec(memory_space=pl.ANY)
    return pl.pallas_call(
        body,
        out_shape=tuple(out_shape),
        in_specs=specs,
        out_specs=(whole,) * len(out_shape),
        compiler_params=params(),
        cost_estimate=cost(2 * rows * depth * width * count, 2 * depth * width * count),
        name="output_first" if first else "output_rest",
    )(*operands, *[in_vmem(w) for w in weights])


def split(values):
    high = values.astype(BF16)
    return high, (values - high.astype(F32)).astype(BF16)


def on_device(
    hidden,
    input_norm_scale,
    projection_signal,
    projection_gate,
    projection_step,
    projection_input_output,
    step_bias,
    head_decay_rate,
    head_skip_weight,
    gated_norm_scale,
    adapter_down_weight,
    adapter_up_weight,
    output_weight,
    scan_state,
    stream_tenant_index,
    live_block_rows,
):
    streams, positions, feature_width = hidden.shape
    rows = streams * positions
    heads_n = lax.axis_size("head")
    rows_n = lax.axis_size("row")
    model_width = feature_width * heads_n
    depth, inner = projection_signal.shape
    inner_width = inner * heads_n

    wide = jnp.swapaxes(hidden, 0, 1).astype(F32)
    scaled = (wide * input_norm_scale).astype(BF16)
    scaled_flat = scaled.reshape(rows, feature_width)

    squares = jnp.sum(wide * wide, -1).reshape(rows, 1)
    sums, up_rows = adapt(stream_tenant_index, scaled_flat, squares, adapter_down_weight, adapter_up_weight)

    weights = load(sums, [], projection_signal, projection_input_output, projection_gate)
    signal_weights = (*weights[:2], projection_step.T)
    middle = output_weight.shape[0] // 2
    if heads_n == rows_n and len(bits_of(rows_n)) == 2:
        turn = [(h * rows_n + r, r * rows_n + h) for h in range(heads_n) for r in range(rows_n)]
        turned = lax.ppermute(scaled_flat, ("head", "row"), turn)
        turned, _ = lax.optimization_barrier((turned, weights[0]))
        crossed = swap(turned, "head", 2)

        def order(distance):
            return [
                (lambda d=d: lax.axis_index("head") ^ d, 0) for d in (distance, distance ^ 1)
            ]

        near = [turned, swap(turned, "head", 1)]
        far = [crossed, swap(crossed, "head", 1)]
        (out_early,) = load(turned, [], (output_weight, 0, middle))
        after, _ = lax.optimization_barrier((crossed, out_early))
        near_send, near_keep, near_lhs = project_signal(near, order(0), 2, *signal_weights, after)
        near_other = swap(near_send, "row", 1)
        far_send, far_keep, far_lhs = project_signal(far, order(2), 2, *signal_weights, near_send)
        far_other = swap(far_send, "row", 1)
        gate_send, gate_keep = project_gate(rows, [near_lhs, far_lhs], weights[2], far_send)
        far_keep, out_late = load(gate_send, [far_keep], (output_weight, middle, middle))
        own = group_of_own(2) == 0
        pick = [(near_keep, far_keep), (near_other, far_other)]
        last_send = sum(jnp.where(own, f, n).astype(F32) for n, f in pick).astype(BF16)
        signal_terms = [jnp.where(own, n, f)[0] for n, f in pick]
        signal_terms = [swap(last_send, "row", 2)[0]] + signal_terms
        sums, _ = lax.optimization_barrier((sums, last_send))
        sums = sum_over(sums, "head")
    else:
        features = lax.all_gather(scaled_flat, "head", axis=1, tiled=True)
        blocks = lax.all_to_all(features, "row", split_axis=1, concat_axis=0, tiled=True)
        blocks = blocks.reshape(rows_n, rows, depth)
        blocks = [blocks[i] for i in range(rows_n)]
        order = [(lambda i=i: i, 0) for i in range(rows_n)]
        send, keep, lhs = project_signal(blocks, order, rows_n, *signal_weights, sums)
        received = swap(send, "row", 1)
        gate_send, gate_keep = project_gate(rows, [lhs], weights[2], send)
        sums = sum_over(sums, "head")
        keep, out_early, out_late = load(
            gate_send, [keep], (output_weight, 0, middle), (output_weight, middle, middle)
        )
        signal_terms, _ = scatter_rows(received, keep, "row")
    out_weights = [out_early, out_late]
    gate_terms, gate_last = scatter_rows(swap(gate_send, "row", 1), gate_keep, "row")

    result, feeds, bgate, both, state = recur(
        model_width,
        gate_last,
        live_block_rows,
        signal_terms,
        sums,
        up_rows,
        step_bias,
        head_decay_rate,
        head_skip_weight,
        scan_state,
    )

    distances = list(range(heads_n))
    first, out_lhs, gate_squares = output_parts(
        distances[3::4],
        out_weights,
        feature_width,
        [*gate_terms, sums, result, gated_norm_scale[None]],
        model_width,
    )
    (rest,) = output_parts(
        distances[2::4] + distances[1::4] + distances[0::4],
        out_weights,
        feature_width,
        [out_lhs, first],
    )
    quarter = rest.shape[0] // 3
    second, third, fourth = (rest[i * quarter : (i + 1) * quarter] for i in range(3))
    send = (swap(first, "head", 1).astype(F32) + second.astype(F32)).astype(BF16)
    kept = [swap(third, "head", 1), fourth]
    mixer, _ = scatter_rows(swap(send, "head", 2), kept, "head", done=2)
    mixer = sum(t.astype(F32) for t in mixer)
    gate_squares = sum_over(gate_squares, "head")
    mixer = mixer * lax.rsqrt(gate_squares / inner_width + EPSILON)
    mixer = mixer.reshape(positions, streams, feature_width)
    live = jnp.arange(streams) < live_block_rows[0]
    mixed = (wide + jnp.where(live[:, None], mixer, 0.0)).astype(BF16)

    spread = jnp.broadcast_to(both[..., None], both.shape + (bgate.shape[-1],))
    new_state = state_write(feeds, bgate, spread, state)
    return (jnp.swapaxes(mixed, 0, 1), new_state)


def solution(mesh):
    in_specs = (
        P(("rep", "row"), None, "head"),
        P("head"),
        P("row", "head"),
        P("row", "head"),
        P("row", "head"),
        P("row", None),
        P("head"),
        P("head"),
        P("head"),
        P("head"),
        P("row", "head", None),
        P("row", None, "head"),
        P("head", None),
        P(("rep", "row"), "head", None, None),
        P(("rep", "row")),
        P(("rep", "row")),
    )
    out_specs = (P(("rep", "row"), None, "head"), P(("rep", "row"), "head", None, None))
    return jax.shard_map(
        on_device, mesh=mesh, in_specs=in_specs, out_specs=out_specs, check_vma=False
    )
```

```python
import functools

import jax
import jax.numpy as jnp
from jax import lax
from jax.experimental import pallas as pl
from jax.experimental.pallas import tpu as pltpu
from jax.sharding import PartitionSpec as P

BF16 = jnp.bfloat16
EPSILON = 1e-05
F32 = jnp.float32
VMEM_GRANT = 12 * 1024 * 1024


def swap(values, axis, distance):
    size = lax.axis_size(axis)
    return lax.ppermute(values, axis, [(i, i ^ distance) for i in range(size)])


def bits_of(size):
    return [1 << i for i in range(size.bit_length() - 1)]


def sum_over(values, axis):
    for distance in bits_of(lax.axis_size(axis)):
        values = values + swap(values, axis, distance)
    return values


def reverse_bits(value, size):
    bits = size.bit_length() - 1
    return sum(((value >> i) & 1) << (bits - 1 - i) for i in range(bits))


def params(**more):
    return pltpu.CompilerParams(vmem_limit_bytes=VMEM_GRANT, **more)


def cost(flops, size):
    return pl.CostEstimate(flops=int(flops), bytes_accessed=int(size), transcendentals=0)


def in_hbm(values):
    return pltpu.with_memory_space_constraint(values, pltpu.HBM)


def in_vmem(values):
    return pltpu.with_memory_space_constraint(values, pltpu.VMEM)


def load_body(spans, after_ref, *refs):
    count = len(spans)
    sources, targets, semaphores = refs[:count], refs[count : 2 * count], refs[2 * count]
    copies = []
    for source, target, (start, rows, parts) in zip(sources, targets, spans):
        step = rows // parts
        for i in range(parts):
            copies.append(
                pltpu.make_async_copy(
                    source.at[pl.ds(start + i * step, step)],
                    target.at[pl.ds(i * step, step)],
                    semaphores.at[len(copies)],
                )
            )
    for copy in copies:
        copy.start()
    for copy in copies:
        copy.wait()


def load(after, passed, *weights):
    weights = [w if isinstance(w, tuple) else (w, 0, w.shape[0]) for w in weights]
    shapes = [p.shape for p in passed] + [(rows, *w.shape[1:]) for w, _, rows in weights]
    spans = [(0, p.shape[0], 1) for p in passed]
    spans += [(start, rows, 8 if rows % 128 == 0 else 1) for _, start, rows in weights]
    size = sum(rows * w.shape[1] * w.dtype.itemsize for w, _, rows in weights)
    return pl.pallas_call(
        functools.partial(load_body, spans),
        out_shape=tuple(pltpu.VMEM(shape, BF16) for shape in shapes),
        in_specs=[pl.BlockSpec(memory_space=pl.ANY)] * (1 + len(shapes)),
        out_specs=tuple(pl.BlockSpec(memory_space=pltpu.VMEM) for _ in shapes),
        scratch_shapes=[pltpu.SemaphoreType.DMA((sum(parts for _, _, parts in spans),))],
        compiler_params=params(),
        cost_estimate=cost(0, 2 * size),
        name="load",
    )(after, *passed, *[in_hbm(w) for w, _, _ in weights])


def own_columns(rows, streams, rank):
    row = lax.broadcasted_iota(jnp.int32, (rows, streams * rank), 0) % streams
    return row == lax.broadcasted_iota(jnp.int32, (rows, streams * rank), 1) // rank


def adapt_body(tenant_ref, scaled_ref, squares_ref, down_ref, up_ref, sums_ref, up_rows_ref, *scratch):
    down_rows_ref, semaphores = scratch
    rank = down_ref.shape[1]
    streams = tenant_ref.shape[0]
    rows = scaled_ref.shape[0]
    first = lax.axis_index("row") * down_ref.shape[0]
    downs, ups = [], []
    for s in range(streams):
        at = pl.ds(s * rank, rank)
        tenant = tenant_ref[s] - first
        downs.append(
            pltpu.make_async_copy(down_ref.at[tenant], down_rows_ref.at[at, :], semaphores.at[s])
        )
        ups.append(
            pltpu.make_async_copy(
                up_ref.at[tenant], up_rows_ref.at[at, :], semaphores.at[streams + s]
            )
        )
    for copy in downs + ups:
        copy.start()
    for copy in downs:
        copy.wait()
    every = lax.dot_general(
        scaled_ref[...],
        down_rows_ref[...],
        (((1,), (1,)), ((), ())),
        preferred_element_type=F32,
    )
    own = jnp.where(own_columns(rows, streams, rank), every, 0.0)
    fold = lax.broadcasted_iota(jnp.int32, (streams * rank, rank), 0) % rank
    fold = (fold == lax.broadcasted_iota(jnp.int32, (streams * rank, rank), 1)).astype(BF16)
    high, rest = split(own)
    middle, low = rest, (own - high.astype(F32) - rest.astype(F32)).astype(BF16)
    folded = sum(jnp.dot(x, fold, preferred_element_type=F32) for x in (high, middle, low))
    sums_ref[:, :rank] = folded
    sums_ref[:, rank:] = squares_ref[...]
    for copy in ups:
        copy.wait()


def adapt(tenants, scaled, squares, down, up):
    streams = tenants.shape[0]
    rows, depth = scaled.shape
    rank, inner = up.shape[1:]
    whole = pl.BlockSpec(memory_space=pltpu.VMEM)
    anywhere = pl.BlockSpec(memory_space=pl.ANY)
    return pl.pallas_call(
        adapt_body,
        out_shape=(
            jax.ShapeDtypeStruct((rows, rank + 1), F32),
            pltpu.VMEM((streams * rank, inner), BF16),
        ),
        in_specs=[pl.BlockSpec(memory_space=pltpu.SMEM), whole, whole, anywhere, anywhere],
        out_specs=(whole, whole),
        scratch_shapes=[
            pltpu.VMEM((streams * rank, depth), BF16),
            pltpu.SemaphoreType.DMA((2 * streams,)),
        ],
        compiler_params=params(),
        cost_estimate=cost(2 * rows * depth * streams * rank, 2 * streams * rank * (depth + inner)),
        name="adapt",
    )(tenants, scaled, squares, in_hbm(jnp.swapaxes(down, 1, 2)), in_hbm(up))


def project_signal_body(owners, order, *refs):
    blocks, refs = refs[: len(order)], refs[len(order) :]
    weight_ref, mix_ref, step_ref, send_ref, keep_ref, lhs_ref, semaphores = refs
    rows = blocks[0].shape[0]
    parts = len(blocks) // owners
    copies = []
    for i, block in enumerate(blocks):
        owner, part = order[i]
        away = (owner() ^ lax.axis_index("row")) % owners
        at = pl.multiple_of((away * parts + part) * rows, rows)
        copies.append(
            pltpu.make_async_copy(block, lhs_ref.at[pl.ds(at, rows), :], semaphores.at[i])
        )
    for copy in copies:
        copy.start()
    for copy in copies:
        copy.wait()
    lhs = lhs_ref[...]

    def put(acc, start):
        step = send_ref.shape[1]
        for k in range(owners):
            target = send_ref if k % 2 else keep_ref
            target[k // 2, :, start : start + acc.shape[1]] = acc[k * step : (k + 1) * step].astype(
                target.dtype
            )

    columns = weight_ref.shape[1]
    tile = min(columns, 512)
    for t in range(0, columns, tile):
        put(jnp.dot(lhs, weight_ref[:, t : t + tile], preferred_element_type=F32), t)
    put(jnp.dot(lhs, mix_ref[...], preferred_element_type=F32), columns)
    acc = lax.dot_general(lhs, step_ref[...], (((1,), (1,)), ((), ())), preferred_element_type=F32)
    put(acc, columns + mix_ref.shape[1])


def project_signal(blocks, order, owners, weight, mix, step, after):
    pieces = len(blocks)
    depth = blocks[0].shape[1]
    rows = pieces * blocks[0].shape[0]
    columns = weight.shape[1] + mix.shape[1] + step.shape[0]
    half = jax.ShapeDtypeStruct((owners // 2, rows // owners, columns), BF16)
    whole = pl.BlockSpec(memory_space=pltpu.VMEM)
    anywhere = pl.BlockSpec(memory_space=pl.ANY)

    def body(*refs):
        project_signal_body(owners, order, *refs[:pieces], *refs[pieces + 1 :])

    return pl.pallas_call(
        body,
        out_shape=(half, half, jax.ShapeDtypeStruct((rows, depth), BF16)),
        in_specs=[anywhere] * (pieces + 1) + [whole] * 3,
        out_specs=(whole,) * 3,
        scratch_shapes=[pltpu.SemaphoreType.DMA((pieces,))],
        compiler_params=params(),
        cost_estimate=cost(2 * rows * depth * columns, 2 * depth * columns),
        name="project_signal",
    )(*blocks, after, in_vmem(weight), in_vmem(mix), step)


def project_gate_body(groups, *refs):
    lhs_refs, refs = refs[:groups], refs[groups:]
    weight_ref, after_ref, send_ref, keep_ref = refs
    rows = send_ref.shape[1]
    columns = weight_ref.shape[1]
    tile = min(columns, 512)
    first = group_of_own(groups)
    for t in range(0, columns, tile):
        for g, lhs_ref in enumerate(lhs_refs):
            acc = jnp.dot(lhs_ref[...], weight_ref[:, t : t + tile], preferred_element_type=F32)
            pairs = lhs_ref.shape[0] // (2 * rows)
            for k in range(2 * pairs):
                target = send_ref if k % 2 else keep_ref
                at = (first ^ g) * pairs + k // 2
                target[at, :, t : t + tile] = acc[k * rows : (k + 1) * rows].astype(target.dtype)


def group_of_own(groups):
    if groups == 1:
        return 0
    return (lax.axis_index("head") ^ lax.axis_index("row")) >> 1


def project_gate(rows, lhs, weight, after):
    count = sum(part.shape[0] for part in lhs) // rows
    columns = weight.shape[1]
    half = jax.ShapeDtypeStruct((count // 2, rows, columns), BF16)
    whole = pl.BlockSpec(memory_space=pltpu.VMEM)
    return pl.pallas_call(
        functools.partial(project_gate_body, len(lhs)),
        out_shape=(half, half),
        in_specs=[whole] * (len(lhs) + 1) + [pl.BlockSpec(memory_space=pl.ANY)],
        out_specs=(whole,) * 2,
        compiler_params=params(),
        cost_estimate=cost(2 * count * rows * lhs[0].shape[1] * columns, 2 * weight.size),
        name="project_gate",
    )(*lhs, in_vmem(weight), after)


def scatter_rows(received, keep, axis, done=1):
    send = received
    terms = [received] + (keep if isinstance(keep, list) else [keep])
    for distance in bits_of(lax.axis_size(axis))[done:]:
        send = sum(t[1::2].astype(F32) for t in terms).astype(BF16)
        terms = [swap(send, axis, distance)] + [t[0::2] for t in terms]
    return [t[0] for t in terms], send


def softplus(values):
    return jnp.maximum(values, 0.0) + jnp.log1p(jnp.exp(-jnp.abs(values)))


def silu(values):
    return values / (1.0 + jnp.exp(-values))


def inverse_of(sums_ref, width):
    return lax.rsqrt(sums_ref[:, sums_ref.shape[1] - 1 :] / width + EPSILON)


def recur_body(
    terms,
    group,
    model_width,
    live_ref,
    *refs,
):
    term_refs = refs[:terms]
    sums_ref, up_ref, bias_ref, rate_ref, skip_ref, source_ref, _ = refs[terms : terms + 7]
    result_ref, feeds_ref, b_ref, both_ref, state_ref, *scratch = refs[terms + 7 :]
    c_ref, read_ref, spread_ref, signal_ref, semaphores = scratch
    heads, head, width = state_ref.shape[1:]
    streams, inner = feeds_ref.shape[1:]
    step = pl.program_id(0)

    def fetch(i):
        at = pl.ds(i * group, group)
        return pltpu.make_async_copy(source_ref.at[at], state_ref.at[at], semaphores.at[i])

    @pl.when(step == 0)
    def _():
        for i in range(streams // group):
            fetch(i).start()
        rows = sums_ref.shape[0]
        rank = sums_ref.shape[1] - 1
        inverse = inverse_of(sums_ref, model_width)
        lowrank = (sums_ref[:, :rank] * inverse).astype(BF16)
        repeat = lax.broadcasted_iota(jnp.int32, (rank, streams * rank), 1) % rank
        repeat = (repeat == lax.broadcasted_iota(jnp.int32, (rank, streams * rank), 0)).astype(BF16)
        every = jnp.dot(lowrank, repeat, preferred_element_type=F32)
        own = jnp.where(own_columns(rows, streams, rank), every, 0.0).astype(BF16)
        adapted = jnp.dot(own, up_ref[...], preferred_element_type=F32)
        total = sum(t[...].astype(F32) for t in term_refs) * inverse
        signal_ref[...] = silu(total[:, :inner] + adapted)
        gates = silu(total[:, inner : inner + 2 * width])
        steps_dt = softplus(total[:, inner + 2 * width :] + bias_ref[...])
        b = [gates[p * streams : (p + 1) * streams, :width] for p in range(2)]
        c = [gates[p * streams : (p + 1) * streams, width:] for p in range(2)]
        for p in range(2):
            b_ref[p] = b[p]
            c_ref[p] = c[p]
        live = lax.broadcasted_iota(jnp.int32, (streams, heads), 0) < live_ref[0]
        dt = [steps_dt[p * streams : (p + 1) * streams] for p in range(2)]
        decay = [jnp.where(live, jnp.exp(-d * rate_ref[...]), 1.0) for d in dt]
        fed = [jnp.where(live, d, 0.0) for d in dt]

        def match(i, j):
            return jnp.sum(b[i] * c[j], -1, keepdims=True)

        both = decay[0] * decay[1]
        both_ref[...] = both
        late = decay[1] * fed[0]
        skip = skip_ref[...]
        factors = jnp.concatenate(
            [
                decay[0],
                both,
                fed[0] * match(0, 0) + skip,
                fed[1] * match(1, 1) + skip,
                late * match(0, 1),
                late,
                fed[1],
            ],
            0,
        )
        high, low = split(factors)
        place = lax.broadcasted_iota(jnp.int32, (heads, inner), 1) // head
        ones = (place == lax.broadcasted_iota(jnp.int32, (heads, inner), 0)).astype(BF16)
        spread_ref[...] = jnp.dot(high, ones, preferred_element_type=F32) + jnp.dot(
            low, ones, preferred_element_type=F32
        )

    fetch(step).wait()
    at = pl.multiple_of(step * group, group)
    c = jnp.concatenate([c_ref[p, pl.ds(at, group), :] for p in range(2)], 0)
    lhs = jnp.concatenate(split(c), 0)
    for g in range(group):
        state = state_ref[at + g].reshape(inner, width)
        found = lax.dot_general(lhs, state, (((1,), (1,)), ((), ())), preferred_element_type=F32)
        for p in range(2):
            row = p * group + g
            low = 2 * group + row
            read_ref[p, pl.ds(at + g, 1), :] = found[row : row + 1] + found[low : low + 1]

    @pl.when(step == pl.num_programs(0) - 1)
    def _():
        factor = [spread_ref[i * streams : (i + 1) * streams, :] for i in range(7)]
        first = signal_ref[:streams, :]
        second = signal_ref[streams:, :]
        result_ref[:streams, :] = factor[0] * read_ref[0] + factor[2] * first
        result_ref[streams:, :] = factor[1] * read_ref[1] + factor[4] * first + factor[3] * second
        feeds_ref[0] = factor[5] * first
        feeds_ref[1] = factor[6] * second


def recur(model_width, after, live_rows, terms, sums, up_rows, bias, rate, skip, state):
    streams, heads, head, width = state.shape
    group = 8
    inner = heads * head
    rows = 2 * streams
    whole = pl.BlockSpec(memory_space=pltpu.VMEM)
    return pl.pallas_call(
        functools.partial(recur_body, len(terms), group, model_width),
        out_shape=(
            jax.ShapeDtypeStruct((rows, inner), F32),
            jax.ShapeDtypeStruct((2, streams, inner), F32),
            jax.ShapeDtypeStruct((2, streams, width), F32),
            jax.ShapeDtypeStruct((streams, heads), F32),
            pltpu.VMEM(state.shape, state.dtype),
        ),
        grid=(streams // group,),
        in_specs=[pl.BlockSpec(memory_space=pltpu.SMEM)]
        + [whole] * (len(terms) + 5)
        + [pl.BlockSpec(memory_space=pl.ANY)] * 2,
        out_specs=(whole,) * 5,
        scratch_shapes=[
            pltpu.VMEM((2, streams, width), F32),
            pltpu.VMEM((2, streams, inner), F32),
            pltpu.VMEM((7 * streams, inner), F32),
            pltpu.VMEM((rows, inner), F32),
            pltpu.SemaphoreType.DMA((streams // group,)),
        ],
        compiler_params=params(),
        cost_estimate=cost(64 * state.size, 2 * state.size + 32 * rows * inner),
        name="recur",
    )(
        live_rows,
        *terms,
        sums,
        up_rows,
        bias[None],
        rate[None],
        skip[None],
        in_hbm(state),
        after,
    )


def state_write_body(feeds_ref, b_ref, decay_ref, state_ref, out_ref):
    group, heads, head, width = out_ref.shape
    at = pl.multiple_of(pl.program_id(0) * group, group)
    feeds = [split(feeds_ref[p, pl.ds(at, group), :]) for p in range(2)]
    rights = [split(b_ref[p, pl.ds(at, group), :]) for p in range(2)]
    left = [f.astype(F32) for pair in feeds for f in (pair[0], pair[1], pair[0])]
    right = [f.astype(F32) for pair in rights for f in (pair[0], pair[0], pair[1])]
    left = jnp.concatenate(left, 0).astype(BF16)
    right = jnp.concatenate(right, 0)
    stream = lax.broadcasted_iota(jnp.int32, right.shape, 0) % group
    for g in range(0, group, 2):
        pair = jnp.concatenate([jnp.where(stream == g + i, right, 0.0) for i in range(2)], 1)
        outer = lax.dot_general(
            left, pair.astype(BF16), (((0,), (0,)), ((), ())), preferred_element_type=F32
        )
        for i in range(2):
            scaled = state_ref[at + g + i].astype(F32) * decay_ref[g + i][:, None, :]
            own = outer[:, i * width : (i + 1) * width].reshape(heads, head, width)
            out_ref[g + i] = (scaled + own).astype(out_ref.dtype)


def state_write(feeds, b, decay, state):
    streams, heads, head, width = state.shape
    group = 8
    whole = pl.BlockSpec(memory_space=pltpu.VMEM)
    return pl.pallas_call(
        state_write_body,
        out_shape=jax.ShapeDtypeStruct(state.shape, state.dtype),
        grid=(streams // group,),
        in_specs=[
            whole,
            whole,
            pl.BlockSpec((group, heads, width), lambda i: (i, 0, 0)),
            whole,
        ],
        out_specs=pl.BlockSpec((group, heads, head, width), lambda i: (i, 0, 0, 0)),
        compiler_params=params(),
        cost_estimate=cost(32 * state.size, 4 * state.size),
        name="state_write",
    )(feeds, b, decay, state)


def output_tiles(distances, lhs_ref, weight_refs, out_ref):
    width = out_ref.shape[2]
    tile = min(width, 512)
    for j, distance in enumerate(distances):
        for t in range(0, width, tile):
            at = pl.multiple_of((lax.axis_index("head") ^ distance) * width + t, tile)
            acc, start = 0.0, 0
            for weight_ref in weight_refs:
                stop = start + weight_ref.shape[0]
                acc += jnp.dot(
                    lhs_ref[:, start:stop],
                    weight_ref[:, pl.ds(at, tile)],
                    preferred_element_type=F32,
                )
                start = stop
            out_ref[j, :, t : t + tile] = acc.astype(out_ref.dtype)


def output_first_body(distances, terms, model_width, *refs):
    term_refs = refs[:terms]
    sums_ref, result_ref, scale_ref, *weight_refs, out_ref, lhs_ref, squares_ref = refs[terms:]
    total = sum(t[...].astype(F32) for t in term_refs) * inverse_of(sums_ref, model_width)
    gated = result_ref[...] * silu(total)
    squares_ref[...] = jnp.sum(gated * gated, -1, keepdims=True)
    lhs_ref[...] = (gated * scale_ref[...]).astype(lhs_ref.dtype)
    output_tiles(distances, lhs_ref, weight_refs, out_ref)


def output_rest_body(distances, lhs_ref, after_ref, *refs):
    output_tiles(distances, lhs_ref, refs[:-1], refs[-1])


def output_parts(distances, weights, width, operands, model_width=None):
    first = model_width is not None
    rows, depth = operands[0].shape
    count = len(distances)
    whole = pl.BlockSpec(memory_space=pltpu.VMEM)
    specs = [whole] * (len(operands) + len(weights))
    body = functools.partial(output_rest_body, distances)
    out_shape = [jax.ShapeDtypeStruct((count, rows, width), BF16)]
    if first:
        body = functools.partial(output_first_body, distances, len(operands) - 3, model_width)
        out_shape += [
            jax.ShapeDtypeStruct((rows, depth), BF16),
            jax.ShapeDtypeStruct((rows, 1), F32),
        ]
    else:
        specs[1] = pl.BlockSpec(memory_space=pl.ANY)
    return pl.pallas_call(
        body,
        out_shape=tuple(out_shape),
        in_specs=specs,
        out_specs=(whole,) * len(out_shape),
        compiler_params=params(),
        cost_estimate=cost(2 * rows * depth * width * count, 2 * depth * width * count),
        name="output_first" if first else "output_rest",
    )(*operands, *[in_vmem(w) for w in weights])


def split(values):
    high = values.astype(BF16)
    return high, (values - high.astype(F32)).astype(BF16)


def on_device(
    hidden,
    input_norm_scale,
    projection_signal,
    projection_gate,
    projection_step,
    projection_input_output,
    step_bias,
    head_decay_rate,
    head_skip_weight,
    gated_norm_scale,
    adapter_down_weight,
    adapter_up_weight,
    output_weight,
    scan_state,
    stream_tenant_index,
    live_block_rows,
):
    streams, positions, feature_width = hidden.shape
    rows = streams * positions
    heads_n = lax.axis_size("head")
    rows_n = lax.axis_size("row")
    model_width = feature_width * heads_n
    depth, inner = projection_signal.shape
    inner_width = inner * heads_n

    wide = jnp.swapaxes(hidden, 0, 1).astype(F32)
    scaled = (wide * input_norm_scale).astype(BF16)
    scaled_flat = scaled.reshape(rows, feature_width)

    squares = jnp.sum(wide * wide, -1).reshape(rows, 1)
    sums, up_rows = adapt(stream_tenant_index, scaled_flat, squares, adapter_down_weight, adapter_up_weight)

    own = group_of_own(2) == 0
    sums, own = lax.optimization_barrier((sums, own))
    weights = load(sums, [], projection_signal, projection_input_output, projection_gate)
    signal_weights = (*weights[:2], projection_step.T)
    middle = output_weight.shape[0] // 2
    if heads_n == rows_n and len(bits_of(rows_n)) == 2:
        turn = [(h * rows_n + r, r * rows_n + h) for h in range(heads_n) for r in range(rows_n)]
        turned = lax.ppermute(scaled_flat, ("head", "row"), turn)
        turned, _ = lax.optimization_barrier((turned, weights[0]))
        crossed = swap(turned, "head", 2)

        def order(distance):
            return [
                (lambda d=d: lax.axis_index("head") ^ d, 0) for d in (distance, distance ^ 1)
            ]

        near = [turned, swap(turned, "head", 1)]
        (out_early,) = load(turned, [], (output_weight, 0, middle))
        crossed, _ = lax.optimization_barrier((crossed, out_early))
        far = [crossed, swap(crossed, "head", 1)]
        near_send, near_keep, near_lhs = project_signal(near, order(0), 2, *signal_weights, crossed)
        near_other = swap(near_send, "row", 1)
        far_send, far_keep, far_lhs = project_signal(far, order(2), 2, *signal_weights, near_send)
        far_other = swap(far_send, "row", 1)
        gate_send, gate_keep = project_gate(rows, [near_lhs, far_lhs], weights[2], far_send)
        far_keep, out_late = load(gate_send, [far_keep], (output_weight, middle, middle))
        pick = [(near_keep, far_keep), (near_other, far_other)]
        last_send = sum(jnp.where(own, f, n).astype(F32) for n, f in pick).astype(BF16)
        signal_terms = [jnp.where(own, n, f)[0] for n, f in pick]
        last_other = swap(last_send, "row", 2)
        signal_terms = [last_other[0]] + signal_terms
        gate_terms = [swap(gate_send, "row", 1), gate_keep]
        gate_last = sum(t[1:].astype(F32) for t in gate_terms).astype(BF16)
        gate_last, _ = lax.optimization_barrier((gate_last, last_other))
        gate_terms = [t[0] for t in [swap(gate_last, "row", 2)] + gate_terms]
        sums, _ = lax.optimization_barrier((sums, last_send))
        sums = sum_over(sums, "head")
    else:
        features = lax.all_gather(scaled_flat, "head", axis=1, tiled=True)
        blocks = lax.all_to_all(features, "row", split_axis=1, concat_axis=0, tiled=True)
        blocks = blocks.reshape(rows_n, rows, depth)
        blocks = [blocks[i] for i in range(rows_n)]
        order = [(lambda i=i: i, 0) for i in range(rows_n)]
        send, keep, lhs = project_signal(blocks, order, rows_n, *signal_weights, sums)
        received = swap(send, "row", 1)
        gate_send, gate_keep = project_gate(rows, [lhs], weights[2], send)
        sums = sum_over(sums, "head")
        keep, out_early, out_late = load(
            gate_send, [keep], (output_weight, 0, middle), (output_weight, middle, middle)
        )
        signal_terms, _ = scatter_rows(received, keep, "row")
        gate_terms, gate_last = scatter_rows(swap(gate_send, "row", 1), gate_keep, "row")
    out_weights = [out_early, out_late]

    result, feeds, bgate, both, state = recur(
        model_width,
        gate_last,
        live_block_rows,
        signal_terms,
        sums,
        up_rows,
        step_bias,
        head_decay_rate,
        head_skip_weight,
        scan_state,
    )

    distances = list(range(heads_n))
    first, out_lhs, gate_squares = output_parts(
        distances[3::4],
        out_weights,
        feature_width,
        [*gate_terms, sums, result, gated_norm_scale[None]],
        model_width,
    )
    (second,) = output_parts(
        distances[2::4] + distances[1::4], out_weights, feature_width, [out_lhs, first]
    )
    half = second.shape[0] // 2
    send = (swap(first, "head", 1).astype(F32) + second[:half].astype(F32)).astype(BF16)
    received = swap(send, "head", 2)
    (rest,) = output_parts(distances[0::4], out_weights, feature_width, [out_lhs, send])
    feeds, _ = lax.optimization_barrier((feeds, rest))
    kept = [swap(second[half:], "head", 1), rest]
    mixer, _ = scatter_rows(received, kept, "head", done=2)
    mixer = sum(t.astype(F32) for t in mixer)
    gate_squares = sum_over(gate_squares, "head")
    mixer = mixer * lax.rsqrt(gate_squares / inner_width + EPSILON)
    mixer = mixer.reshape(positions, streams, feature_width)
    live = jnp.arange(streams) < live_block_rows[0]
    mixed = (wide + jnp.where(live[:, None], mixer, 0.0)).astype(BF16)

    spread = jnp.broadcast_to(both[..., None], both.shape + (bgate.shape[-1],))
    new_state = state_write(feeds, bgate, spread, state)
    return (jnp.swapaxes(mixed, 0, 1), new_state)


def solution(mesh):
    in_specs = (
        P(("rep", "row"), None, "head"),
        P("head"),
        P("row", "head"),
        P("row", "head"),
        P("row", "head"),
        P("row", None),
        P("head"),
        P("head"),
        P("head"),
        P("head"),
        P("row", "head", None),
        P("row", None, "head"),
        P("head", None),
        P(("rep", "row"), "head", None, None),
        P(("rep", "row")),
        P(("rep", "row")),
    )
    out_specs = (P(("rep", "row"), None, "head"), P(("rep", "row"), "head", None, None))
    return jax.shard_map(
        on_device, mesh=mesh, in_specs=in_specs, out_specs=out_specs, check_vma=False
    )
```

```python
import functools

import jax
import jax.numpy as jnp
from jax import lax
from jax.experimental import pallas as pl
from jax.experimental.pallas import tpu as pltpu
from jax.sharding import PartitionSpec as P

BF16 = jnp.bfloat16
EPSILON = 1e-05
F32 = jnp.float32
VMEM_GRANT = 12 * 1024 * 1024


def swap(values, axis, distance):
    size = lax.axis_size(axis)
    return lax.ppermute(values, axis, [(i, i ^ distance) for i in range(size)])


def bits_of(size):
    return [1 << i for i in range(size.bit_length() - 1)]


def sum_over(values, axis):
    for distance in bits_of(lax.axis_size(axis)):
        values = values + swap(values, axis, distance)
    return values


def reverse_bits(value, size):
    bits = size.bit_length() - 1
    return sum(((value >> i) & 1) << (bits - 1 - i) for i in range(bits))


def params(**more):
    return pltpu.CompilerParams(vmem_limit_bytes=VMEM_GRANT, **more)


def cost(flops, size):
    return pl.CostEstimate(flops=int(flops), bytes_accessed=int(size), transcendentals=0)


def in_hbm(values):
    return pltpu.with_memory_space_constraint(values, pltpu.HBM)


def in_vmem(values):
    return pltpu.with_memory_space_constraint(values, pltpu.VMEM)


def load_body(spans, after_ref, *refs):
    count = len(spans)
    sources, targets, semaphores = refs[:count], refs[count : 2 * count], refs[2 * count]
    copies = []
    for source, target, (start, rows, parts) in zip(sources, targets, spans):
        step = rows // parts
        for i in range(parts):
            copies.append(
                pltpu.make_async_copy(
                    source.at[pl.ds(start + i * step, step)],
                    target.at[pl.ds(i * step, step)],
                    semaphores.at[len(copies)],
                )
            )
    for copy in copies:
        copy.start()
    for copy in copies:
        copy.wait()


def load(after, passed, *weights):
    weights = [w if isinstance(w, tuple) else (w, 0, w.shape[0]) for w in weights]
    shapes = [p.shape for p in passed] + [(rows, *w.shape[1:]) for w, _, rows in weights]
    spans = [(0, p.shape[0], 1) for p in passed]
    spans += [(start, rows, 8 if rows % 128 == 0 else 1) for _, start, rows in weights]
    size = sum(rows * w.shape[1] * w.dtype.itemsize for w, _, rows in weights)
    return pl.pallas_call(
        functools.partial(load_body, spans),
        out_shape=tuple(pltpu.VMEM(shape, BF16) for shape in shapes),
        in_specs=[pl.BlockSpec(memory_space=pl.ANY)] * (1 + len(shapes)),
        out_specs=tuple(pl.BlockSpec(memory_space=pltpu.VMEM) for _ in shapes),
        scratch_shapes=[pltpu.SemaphoreType.DMA((sum(parts for _, _, parts in spans),))],
        compiler_params=params(),
        cost_estimate=cost(0, 2 * size),
        name="load",
    )(after, *passed, *[in_hbm(w) for w, _, _ in weights])


def own_columns(rows, streams, rank):
    row = lax.broadcasted_iota(jnp.int32, (rows, streams * rank), 0) % streams
    return row == lax.broadcasted_iota(jnp.int32, (rows, streams * rank), 1) // rank


def adapt_body(tenant_ref, scaled_ref, squares_ref, down_ref, up_ref, sums_ref, up_rows_ref, *scratch):
    down_rows_ref, semaphores = scratch
    rank = down_ref.shape[1]
    streams = tenant_ref.shape[0]
    rows = scaled_ref.shape[0]
    first = lax.axis_index("row") * down_ref.shape[0]
    downs, ups = [], []
    for s in range(streams):
        at = pl.ds(s * rank, rank)
        tenant = tenant_ref[s] - first
        downs.append(
            pltpu.make_async_copy(down_ref.at[tenant], down_rows_ref.at[at, :], semaphores.at[s])
        )
        ups.append(
            pltpu.make_async_copy(
                up_ref.at[tenant], up_rows_ref.at[at, :], semaphores.at[streams + s]
            )
        )
    for copy in downs + ups:
        copy.start()
    for copy in downs:
        copy.wait()
    every = lax.dot_general(
        scaled_ref[...],
        down_rows_ref[...],
        (((1,), (1,)), ((), ())),
        preferred_element_type=F32,
    )
    own = jnp.where(own_columns(rows, streams, rank), every, 0.0)
    fold = lax.broadcasted_iota(jnp.int32, (streams * rank, rank), 0) % rank
    fold = (fold == lax.broadcasted_iota(jnp.int32, (streams * rank, rank), 1)).astype(BF16)
    high, rest = split(own)
    middle, low = rest, (own - high.astype(F32) - rest.astype(F32)).astype(BF16)
    folded = sum(jnp.dot(x, fold, preferred_element_type=F32) for x in (high, middle, low))
    sums_ref[:, :rank] = folded
    sums_ref[:, rank:] = squares_ref[...]
    for copy in ups:
        copy.wait()


def adapt(tenants, scaled, squares, down, up):
    streams = tenants.shape[0]
    rows, depth = scaled.shape
    rank, inner = up.shape[1:]
    whole = pl.BlockSpec(memory_space=pltpu.VMEM)
    anywhere = pl.BlockSpec(memory_space=pl.ANY)
    return pl.pallas_call(
        adapt_body,
        out_shape=(
            jax.ShapeDtypeStruct((rows, rank + 1), F32),
            pltpu.VMEM((streams * rank, inner), BF16),
        ),
        in_specs=[pl.BlockSpec(memory_space=pltpu.SMEM), whole, whole, anywhere, anywhere],
        out_specs=(whole, whole),
        scratch_shapes=[
            pltpu.VMEM((streams * rank, depth), BF16),
            pltpu.SemaphoreType.DMA((2 * streams,)),
        ],
        compiler_params=params(),
        cost_estimate=cost(2 * rows * depth * streams * rank, 2 * streams * rank * (depth + inner)),
        name="adapt",
    )(tenants, scaled, squares, in_hbm(jnp.swapaxes(down, 1, 2)), in_hbm(up))


def project_signal_body(owners, order, *refs):
    blocks, refs = refs[: len(order)], refs[len(order) :]
    weight_ref, mix_ref, step_ref, send_ref, keep_ref, lhs_ref, semaphores = refs
    rows = blocks[0].shape[0]
    parts = len(blocks) // owners
    copies = []
    for i, block in enumerate(blocks):
        owner, part = order[i]
        away = (owner() ^ lax.axis_index("row")) % owners
        at = pl.multiple_of((away * parts + part) * rows, rows)
        copies.append(
            pltpu.make_async_copy(block, lhs_ref.at[pl.ds(at, rows), :], semaphores.at[i])
        )
    for copy in copies:
        copy.start()
    for copy in copies:
        copy.wait()
    lhs = lhs_ref[...]

    def put(acc, start):
        step = send_ref.shape[1]
        for k in range(owners):
            target = send_ref if k % 2 else keep_ref
            target[k // 2, :, start : start + acc.shape[1]] = acc[k * step : (k + 1) * step].astype(
                target.dtype
            )

    columns = weight_ref.shape[1]
    tile = min(columns, 512)
    for t in range(0, columns, tile):
        put(jnp.dot(lhs, weight_ref[:, t : t + tile], preferred_element_type=F32), t)
    put(jnp.dot(lhs, mix_ref[...], preferred_element_type=F32), columns)
    acc = lax.dot_general(lhs, step_ref[...], (((1,), (1,)), ((), ())), preferred_element_type=F32)
    put(acc, columns + mix_ref.shape[1])


def project_signal(blocks, order, owners, weight, mix, step, after):
    pieces = len(blocks)
    depth = blocks[0].shape[1]
    rows = pieces * blocks[0].shape[0]
    columns = weight.shape[1] + mix.shape[1] + step.shape[0]
    half = jax.ShapeDtypeStruct((owners // 2, rows // owners, columns), BF16)
    whole = pl.BlockSpec(memory_space=pltpu.VMEM)
    anywhere = pl.BlockSpec(memory_space=pl.ANY)

    def body(*refs):
        project_signal_body(owners, order, *refs[:pieces], *refs[pieces + 1 :])

    return pl.pallas_call(
        body,
        out_shape=(half, half, jax.ShapeDtypeStruct((rows, depth), BF16)),
        in_specs=[anywhere] * (pieces + 1) + [whole] * 3,
        out_specs=(whole,) * 3,
        scratch_shapes=[pltpu.SemaphoreType.DMA((pieces,))],
        compiler_params=params(),
        cost_estimate=cost(2 * rows * depth * columns, 2 * depth * columns),
        name="project_signal",
    )(*blocks, after, in_vmem(weight), in_vmem(mix), step)


def project_gate_body(groups, *refs):
    lhs_refs, refs = refs[:groups], refs[groups:]
    weight_ref, after_ref, send_ref, keep_ref = refs
    rows = send_ref.shape[1]
    columns = weight_ref.shape[1]
    tile = min(columns, 512)
    first = group_of_own(groups)
    for t in range(0, columns, tile):
        for g, lhs_ref in enumerate(lhs_refs):
            acc = jnp.dot(lhs_ref[...], weight_ref[:, t : t + tile], preferred_element_type=F32)
            pairs = lhs_ref.shape[0] // (2 * rows)
            for k in range(2 * pairs):
                target = send_ref if k % 2 else keep_ref
                at = (first ^ g) * pairs + k // 2
                target[at, :, t : t + tile] = acc[k * rows : (k + 1) * rows].astype(target.dtype)


def group_of_own(groups):
    if groups == 1:
        return 0
    return (lax.axis_index("head") ^ lax.axis_index("row")) >> 1


def project_gate(rows, lhs, weight, after):
    count = sum(part.shape[0] for part in lhs) // rows
    columns = weight.shape[1]
    half = jax.ShapeDtypeStruct((count // 2, rows, columns), BF16)
    whole = pl.BlockSpec(memory_space=pltpu.VMEM)
    return pl.pallas_call(
        functools.partial(project_gate_body, len(lhs)),
        out_shape=(half, half),
        in_specs=[whole] * (len(lhs) + 1) + [pl.BlockSpec(memory_space=pl.ANY)],
        out_specs=(whole,) * 2,
        compiler_params=params(),
        cost_estimate=cost(2 * count * rows * lhs[0].shape[1] * columns, 2 * weight.size),
        name="project_gate",
    )(*lhs, in_vmem(weight), after)


def scatter_rows(received, keep, axis, done=1):
    send = received
    terms = [received] + (keep if isinstance(keep, list) else [keep])
    for distance in bits_of(lax.axis_size(axis))[done:]:
        send = sum(t[1::2].astype(F32) for t in terms).astype(BF16)
        terms = [swap(send, axis, distance)] + [t[0::2] for t in terms]
    return [t[0] for t in terms], send


def softplus(values):
    return jnp.maximum(values, 0.0) + jnp.log1p(jnp.exp(-jnp.abs(values)))


def silu(values):
    return values / (1.0 + jnp.exp(-values))


def inverse_of(sums_ref, width):
    return lax.rsqrt(sums_ref[:, sums_ref.shape[1] - 1 :] / width + EPSILON)


def recur_body(
    terms,
    group,
    model_width,
    live_ref,
    *refs,
):
    term_refs = refs[:terms]
    sums_ref, up_ref, bias_ref, rate_ref, skip_ref, source_ref, _ = refs[terms : terms + 7]
    result_ref, feeds_ref, b_ref, both_ref, state_ref, *scratch = refs[terms + 7 :]
    c_ref, read_ref, spread_ref, signal_ref, semaphores = scratch
    heads, head, width = state_ref.shape[1:]
    streams, inner = feeds_ref.shape[1:]
    step = pl.program_id(0)

    def fetch(i):
        at = pl.ds(i * group, group)
        return pltpu.make_async_copy(source_ref.at[at], state_ref.at[at], semaphores.at[i])

    @pl.when(step == 0)
    def _():
        for i in range(streams // group):
            fetch(i).start()
        rows = sums_ref.shape[0]
        rank = sums_ref.shape[1] - 1
        inverse = inverse_of(sums_ref, model_width)
        lowrank = (sums_ref[:, :rank] * inverse).astype(BF16)
        repeat = lax.broadcasted_iota(jnp.int32, (rank, streams * rank), 1) % rank
        repeat = (repeat == lax.broadcasted_iota(jnp.int32, (rank, streams * rank), 0)).astype(BF16)
        every = jnp.dot(lowrank, repeat, preferred_element_type=F32)
        own = jnp.where(own_columns(rows, streams, rank), every, 0.0).astype(BF16)
        adapted = jnp.dot(own, up_ref[...], preferred_element_type=F32)
        total = sum(t[...].astype(F32) for t in term_refs) * inverse
        signal_ref[...] = silu(total[:, :inner] + adapted)
        gates = silu(total[:, inner : inner + 2 * width])
        steps_dt = softplus(total[:, inner + 2 * width :] + bias_ref[...])
        b = [gates[p * streams : (p + 1) * streams, :width] for p in range(2)]
        c = [gates[p * streams : (p + 1) * streams, width:] for p in range(2)]
        for p in range(2):
            b_ref[p] = b[p]
            c_ref[p] = c[p]
        live = lax.broadcasted_iota(jnp.int32, (streams, heads), 0) < live_ref[0]
        dt = [steps_dt[p * streams : (p + 1) * streams] for p in range(2)]
        decay = [jnp.where(live, jnp.exp(-d * rate_ref[...]), 1.0) for d in dt]
        fed = [jnp.where(live, d, 0.0) for d in dt]

        def match(i, j):
            return jnp.sum(b[i] * c[j], -1, keepdims=True)

        both = decay[0] * decay[1]
        both_ref[...] = both
        late = decay[1] * fed[0]
        skip = skip_ref[...]
        factors = jnp.concatenate(
            [
                decay[0],
                both,
                fed[0] * match(0, 0) + skip,
                fed[1] * match(1, 1) + skip,
                late * match(0, 1),
                late,
                fed[1],
            ],
            0,
        )
        high, low = split(factors)
        place = lax.broadcasted_iota(jnp.int32, (heads, inner), 1) // head
        ones = (place == lax.broadcasted_iota(jnp.int32, (heads, inner), 0)).astype(BF16)
        spread_ref[...] = jnp.dot(high, ones, preferred_element_type=F32) + jnp.dot(
            low, ones, preferred_element_type=F32
        )

    fetch(step).wait()
    at = pl.multiple_of(step * group, group)
    c = jnp.concatenate([c_ref[p, pl.ds(at, group), :] for p in range(2)], 0)
    lhs = jnp.concatenate(split(c), 0)
    for g in range(group):
        state = state_ref[at + g].reshape(inner, width)
        found = lax.dot_general(lhs, state, (((1,), (1,)), ((), ())), preferred_element_type=F32)
        for p in range(2):
            row = p * group + g
            low = 2 * group + row
            read_ref[p, pl.ds(at + g, 1), :] = found[row : row + 1] + found[low : low + 1]

    @pl.when(step == pl.num_programs(0) - 1)
    def _():
        factor = [spread_ref[i * streams : (i + 1) * streams, :] for i in range(7)]
        first = signal_ref[:streams, :]
        second = signal_ref[streams:, :]
        result_ref[:streams, :] = factor[0] * read_ref[0] + factor[2] * first
        result_ref[streams:, :] = factor[1] * read_ref[1] + factor[4] * first + factor[3] * second
        feeds_ref[0] = factor[5] * first
        feeds_ref[1] = factor[6] * second


def recur(model_width, after, live_rows, terms, sums, up_rows, bias, rate, skip, state):
    streams, heads, head, width = state.shape
    group = 8
    inner = heads * head
    rows = 2 * streams
    whole = pl.BlockSpec(memory_space=pltpu.VMEM)
    return pl.pallas_call(
        functools.partial(recur_body, len(terms), group, model_width),
        out_shape=(
            jax.ShapeDtypeStruct((rows, inner), F32),
            jax.ShapeDtypeStruct((2, streams, inner), F32),
            jax.ShapeDtypeStruct((2, streams, width), F32),
            jax.ShapeDtypeStruct((streams, heads), F32),
            pltpu.VMEM(state.shape, state.dtype),
        ),
        grid=(streams // group,),
        in_specs=[pl.BlockSpec(memory_space=pltpu.SMEM)]
        + [whole] * (len(terms) + 5)
        + [pl.BlockSpec(memory_space=pl.ANY)] * 2,
        out_specs=(whole,) * 5,
        scratch_shapes=[
            pltpu.VMEM((2, streams, width), F32),
            pltpu.VMEM((2, streams, inner), F32),
            pltpu.VMEM((7 * streams, inner), F32),
            pltpu.VMEM((rows, inner), F32),
            pltpu.SemaphoreType.DMA((streams // group,)),
        ],
        compiler_params=params(),
        cost_estimate=cost(64 * state.size, 2 * state.size + 32 * rows * inner),
        name="recur",
    )(
        live_rows,
        *terms,
        sums,
        up_rows,
        bias[None],
        rate[None],
        skip[None],
        in_hbm(state),
        after,
    )


def state_write_body(feeds_ref, b_ref, decay_ref, state_ref, out_ref):
    group, heads, head, width = out_ref.shape
    at = pl.multiple_of(pl.program_id(0) * group, group)
    feeds = [split(feeds_ref[p, pl.ds(at, group), :]) for p in range(2)]
    rights = [split(b_ref[p, pl.ds(at, group), :]) for p in range(2)]
    left = [f.astype(F32) for pair in feeds for f in (pair[0], pair[1], pair[0])]
    right = [f.astype(F32) for pair in rights for f in (pair[0], pair[0], pair[1])]
    left = jnp.concatenate(left, 0).astype(BF16)
    right = jnp.concatenate(right, 0)
    stream = lax.broadcasted_iota(jnp.int32, right.shape, 0) % group
    for g in range(0, group, 2):
        pair = jnp.concatenate([jnp.where(stream == g + i, right, 0.0) for i in range(2)], 1)
        outer = lax.dot_general(
            left, pair.astype(BF16), (((0,), (0,)), ((), ())), preferred_element_type=F32
        )
        for i in range(2):
            scaled = state_ref[at + g + i].astype(F32) * decay_ref[g + i][:, None, :]
            own = outer[:, i * width : (i + 1) * width].reshape(heads, head, width)
            out_ref[g + i] = (scaled + own).astype(out_ref.dtype)


def state_write(feeds, b, decay, state):
    streams, heads, head, width = state.shape
    group = 8
    whole = pl.BlockSpec(memory_space=pltpu.VMEM)
    return pl.pallas_call(
        state_write_body,
        out_shape=jax.ShapeDtypeStruct(state.shape, state.dtype),
        grid=(streams // group,),
        in_specs=[
            whole,
            whole,
            pl.BlockSpec((group, heads, width), lambda i: (i, 0, 0)),
            whole,
        ],
        out_specs=pl.BlockSpec((group, heads, head, width), lambda i: (i, 0, 0, 0)),
        compiler_params=params(),
        cost_estimate=cost(32 * state.size, 4 * state.size),
        name="state_write",
    )(feeds, b, decay, state)


def output_tiles(distances, lhs_ref, weight_refs, out_ref):
    width = out_ref.shape[2]
    tile = min(width, 512)
    for j, distance in enumerate(distances):
        for t in range(0, width, tile):
            at = pl.multiple_of((lax.axis_index("head") ^ distance) * width + t, tile)
            acc, start = 0.0, 0
            for weight_ref in weight_refs:
                stop = start + weight_ref.shape[0]
                acc += jnp.dot(
                    lhs_ref[:, start:stop],
                    weight_ref[:, pl.ds(at, tile)],
                    preferred_element_type=F32,
                )
                start = stop
            out_ref[j, :, t : t + tile] = acc.astype(out_ref.dtype)


def output_first_body(distances, terms, model_width, *refs):
    term_refs = refs[:terms]
    sums_ref, result_ref, scale_ref, *weight_refs, out_ref, lhs_ref, squares_ref = refs[terms:]
    total = sum(t[...].astype(F32) for t in term_refs) * inverse_of(sums_ref, model_width)
    gated = result_ref[...] * silu(total)
    squares_ref[...] = jnp.sum(gated * gated, -1, keepdims=True)
    lhs_ref[...] = (gated * scale_ref[...]).astype(lhs_ref.dtype)
    output_tiles(distances, lhs_ref, weight_refs, out_ref)


def output_rest_body(distances, lhs_ref, after_ref, *refs):
    output_tiles(distances, lhs_ref, refs[:-1], refs[-1])


def output_parts(distances, weights, width, operands, model_width=None):
    first = model_width is not None
    rows, depth = operands[0].shape
    count = len(distances)
    whole = pl.BlockSpec(memory_space=pltpu.VMEM)
    specs = [whole] * (len(operands) + len(weights))
    body = functools.partial(output_rest_body, distances)
    out_shape = [jax.ShapeDtypeStruct((count, rows, width), BF16)]
    if first:
        body = functools.partial(output_first_body, distances, len(operands) - 3, model_width)
        out_shape += [
            jax.ShapeDtypeStruct((rows, depth), BF16),
            jax.ShapeDtypeStruct((rows, 1), F32),
        ]
    else:
        specs[1] = pl.BlockSpec(memory_space=pl.ANY)
    return pl.pallas_call(
        body,
        out_shape=tuple(out_shape),
        in_specs=specs,
        out_specs=(whole,) * len(out_shape),
        compiler_params=params(),
        cost_estimate=cost(2 * rows * depth * width * count, 2 * depth * width * count),
        name="output_first" if first else "output_rest",
    )(*operands, *[in_vmem(w) for w in weights])


def split(values):
    high = values.astype(BF16)
    return high, (values - high.astype(F32)).astype(BF16)


def on_device(
    hidden,
    input_norm_scale,
    projection_signal,
    projection_gate,
    projection_step,
    projection_input_output,
    step_bias,
    head_decay_rate,
    head_skip_weight,
    gated_norm_scale,
    adapter_down_weight,
    adapter_up_weight,
    output_weight,
    scan_state,
    stream_tenant_index,
    live_block_rows,
):
    streams, positions, feature_width = hidden.shape
    rows = streams * positions
    heads_n = lax.axis_size("head")
    rows_n = lax.axis_size("row")
    model_width = feature_width * heads_n
    depth, inner = projection_signal.shape
    inner_width = inner * heads_n

    wide = jnp.swapaxes(hidden, 0, 1).astype(F32)
    scaled = (wide * input_norm_scale).astype(BF16)
    scaled_flat = scaled.reshape(rows, feature_width)

    squares = jnp.sum(wide * wide, -1).reshape(rows, 1)
    sums, up_rows = adapt(stream_tenant_index, scaled_flat, squares, adapter_down_weight, adapter_up_weight)

    own = group_of_own(2) == 0
    sums, own = lax.optimization_barrier((sums, own))
    weights = load(sums, [], projection_signal, projection_input_output, projection_gate)
    signal_weights = (*weights[:2], projection_step.T)
    middle = output_weight.shape[0] // 2
    if heads_n == rows_n and len(bits_of(rows_n)) == 2:
        turn = [(h * rows_n + r, r * rows_n + h) for h in range(heads_n) for r in range(rows_n)]
        turned = lax.ppermute(scaled_flat, ("head", "row"), turn)
        turned, _ = lax.optimization_barrier((turned, weights[0]))
        crossed = swap(turned, "head", 2)

        def order(distance):
            return [
                (lambda d=d: lax.axis_index("head") ^ d, 0) for d in (distance, distance ^ 1)
            ]

        near = [turned, swap(turned, "head", 1)]
        (out_early,) = load(turned, [], (output_weight, 0, middle))
        crossed, _ = lax.optimization_barrier((crossed, out_early))
        far = [crossed, swap(crossed, "head", 1)]
        near_send, near_keep, near_lhs = project_signal(near, order(0), 2, *signal_weights, crossed)
        near_other = swap(near_send, "row", 1)
        far_send, far_keep, far_lhs = project_signal(far, order(2), 2, *signal_weights, near_send)
        far_other = swap(far_send, "row", 1)
        gate_send, gate_keep = project_gate(rows, [near_lhs, far_lhs], weights[2], far_send)
        far_keep, out_late = load(gate_send, [far_keep], (output_weight, middle, middle))
        pick = [(near_keep, far_keep), (near_other, far_other)]
        last_send = sum(jnp.where(own, f, n).astype(F32) for n, f in pick).astype(BF16)
        signal_terms = [jnp.where(own, n, f)[0] for n, f in pick]
        last_other = swap(last_send, "row", 2)
        signal_terms = [last_other[0]] + signal_terms
        gate_terms = [swap(gate_send, "row", 1), gate_keep]
        gate_last = sum(t[1:].astype(F32) for t in gate_terms).astype(BF16)
        gate_last, _ = lax.optimization_barrier((gate_last, last_other))
        gate_terms = [t[0] for t in [swap(gate_last, "row", 2)] + gate_terms]
        sums, _ = lax.optimization_barrier((sums, last_send))
        sums = sum_over(sums, "head")
    else:
        features = lax.all_gather(scaled_flat, "head", axis=1, tiled=True)
        blocks = lax.all_to_all(features, "row", split_axis=1, concat_axis=0, tiled=True)
        blocks = blocks.reshape(rows_n, rows, depth)
        blocks = [blocks[i] for i in range(rows_n)]
        order = [(lambda i=i: i, 0) for i in range(rows_n)]
        send, keep, lhs = project_signal(blocks, order, rows_n, *signal_weights, sums)
        received = swap(send, "row", 1)
        gate_send, gate_keep = project_gate(rows, [lhs], weights[2], send)
        sums = sum_over(sums, "head")
        keep, out_early, out_late = load(
            gate_send, [keep], (output_weight, 0, middle), (output_weight, middle, middle)
        )
        signal_terms, _ = scatter_rows(received, keep, "row")
        gate_terms, gate_last = scatter_rows(swap(gate_send, "row", 1), gate_keep, "row")
    out_weights = [out_early, out_late]

    result, feeds, bgate, both, state = recur(
        model_width,
        gate_last,
        live_block_rows,
        signal_terms,
        sums,
        up_rows,
        step_bias,
        head_decay_rate,
        head_skip_weight,
        scan_state,
    )

    distances = list(range(heads_n))
    first, out_lhs, gate_squares = output_parts(
        distances[3::4],
        out_weights,
        feature_width,
        [*gate_terms, sums, result, gated_norm_scale[None]],
        model_width,
    )
    (second,) = output_parts(
        distances[2::4] + distances[1::4], out_weights, feature_width, [out_lhs, first]
    )
    half = second.shape[0] // 2
    send = (swap(first, "head", 1).astype(F32) + second[:half].astype(F32)).astype(BF16)
    received = swap(send, "head", 2)
    (rest,) = output_parts(distances[0::4], out_weights, feature_width, [out_lhs, send])
    feeds, _ = lax.optimization_barrier((feeds, rest))
    kept = [swap(second[half:], "head", 1), rest]
    mixer, _ = scatter_rows(received, kept, "head", done=2)
    mixer = sum(t.astype(F32) for t in mixer)
    gate_squares = sum_over(gate_squares, "head")
    gate_squares, _ = lax.optimization_barrier((gate_squares, received))
    mixer = mixer * lax.rsqrt(gate_squares / inner_width + EPSILON)
    mixer = mixer.reshape(positions, streams, feature_width)
    live = jnp.arange(streams) < live_block_rows[0]
    mixed = (wide + jnp.where(live[:, None], mixer, 0.0)).astype(BF16)

    spread = jnp.broadcast_to(both[..., None], both.shape + (bgate.shape[-1],))
    new_state = state_write(feeds, bgate, spread, state)
    return (jnp.swapaxes(mixed, 0, 1), new_state)


def solution(mesh):
    in_specs = (
        P(("rep", "row"), None, "head"),
        P("head"),
        P("row", "head"),
        P("row", "head"),
        P("row", "head"),
        P("row", None),
        P("head"),
        P("head"),
        P("head"),
        P("head"),
        P("row", "head", None),
        P("row", None, "head"),
        P("head", None),
        P(("rep", "row"), "head", None, None),
        P(("rep", "row")),
        P(("rep", "row")),
    )
    out_specs = (P(("rep", "row"), None, "head"), P(("rep", "row"), "head", None, None))
    return jax.shard_map(
        on_device, mesh=mesh, in_specs=in_specs, out_specs=out_specs, check_vma=False
    )
```

```python
import functools

import jax
import jax.numpy as jnp
from jax import lax
from jax.experimental import pallas as pl
from jax.experimental.pallas import tpu as pltpu
from jax.sharding import PartitionSpec as P

BF16 = jnp.bfloat16
EPSILON = 1e-05
F32 = jnp.float32
VMEM_GRANT = 12 * 1024 * 1024


def swap(values, axis, distance):
    size = lax.axis_size(axis)
    return lax.ppermute(values, axis, [(i, i ^ distance) for i in range(size)])


def bits_of(size):
    return [1 << i for i in range(size.bit_length() - 1)]


def sum_over(values, axis):
    for distance in bits_of(lax.axis_size(axis)):
        values = values + swap(values, axis, distance)
    return values


def reverse_bits(value, size):
    bits = size.bit_length() - 1
    return sum(((value >> i) & 1) << (bits - 1 - i) for i in range(bits))


def params(**more):
    return pltpu.CompilerParams(vmem_limit_bytes=VMEM_GRANT, **more)


def cost(flops, size):
    return pl.CostEstimate(flops=int(flops), bytes_accessed=int(size), transcendentals=0)


def in_hbm(values):
    return pltpu.with_memory_space_constraint(values, pltpu.HBM)


def in_vmem(values):
    return pltpu.with_memory_space_constraint(values, pltpu.VMEM)


def load_body(spans, after_ref, *refs):
    count = len(spans)
    sources, targets, semaphores = refs[:count], refs[count : 2 * count], refs[2 * count]
    copies = []
    for source, target, (start, rows, parts) in zip(sources, targets, spans):
        step = rows // parts
        for i in range(parts):
            copies.append(
                pltpu.make_async_copy(
                    source.at[pl.ds(start + i * step, step)],
                    target.at[pl.ds(i * step, step)],
                    semaphores.at[len(copies)],
                )
            )
    for copy in copies:
        copy.start()
    for copy in copies:
        copy.wait()


def load(after, passed, *weights):
    weights = [w if isinstance(w, tuple) else (w, 0, w.shape[0]) for w in weights]
    shapes = [p.shape for p in passed] + [(rows, *w.shape[1:]) for w, _, rows in weights]
    spans = [(0, p.shape[0], 1) for p in passed]
    spans += [(start, rows, 8 if rows % 128 == 0 else 1) for _, start, rows in weights]
    size = sum(rows * w.shape[1] * w.dtype.itemsize for w, _, rows in weights)
    return pl.pallas_call(
        functools.partial(load_body, spans),
        out_shape=tuple(pltpu.VMEM(shape, BF16) for shape in shapes),
        in_specs=[pl.BlockSpec(memory_space=pl.ANY)] * (1 + len(shapes)),
        out_specs=tuple(pl.BlockSpec(memory_space=pltpu.VMEM) for _ in shapes),
        scratch_shapes=[pltpu.SemaphoreType.DMA((sum(parts for _, _, parts in spans),))],
        compiler_params=params(),
        cost_estimate=cost(0, 2 * size),
        name="load",
    )(after, *passed, *[in_hbm(w) for w, _, _ in weights])


def own_columns(rows, streams, rank):
    row = lax.broadcasted_iota(jnp.int32, (rows, streams * rank), 0) % streams
    return row == lax.broadcasted_iota(jnp.int32, (rows, streams * rank), 1) // rank


def adapt_body(tenant_ref, scaled_ref, squares_ref, down_ref, up_ref, sums_ref, up_rows_ref, *scratch):
    down_rows_ref, semaphores = scratch
    rank = down_ref.shape[1]
    streams = tenant_ref.shape[0]
    rows = scaled_ref.shape[0]
    first = lax.axis_index("row") * down_ref.shape[0]
    downs, ups = [], []
    for s in range(streams):
        at = pl.ds(s * rank, rank)
        tenant = tenant_ref[s] - first
        downs.append(
            pltpu.make_async_copy(down_ref.at[tenant], down_rows_ref.at[at, :], semaphores.at[s])
        )
        ups.append(
            pltpu.make_async_copy(
                up_ref.at[tenant], up_rows_ref.at[at, :], semaphores.at[streams + s]
            )
        )
    for copy in downs + ups:
        copy.start()
    for copy in downs:
        copy.wait()
    every = lax.dot_general(
        scaled_ref[...],
        down_rows_ref[...],
        (((1,), (1,)), ((), ())),
        preferred_element_type=F32,
    )
    own = jnp.where(own_columns(rows, streams, rank), every, 0.0)
    fold = lax.broadcasted_iota(jnp.int32, (streams * rank, rank), 0) % rank
    fold = (fold == lax.broadcasted_iota(jnp.int32, (streams * rank, rank), 1)).astype(BF16)
    high, rest = split(own)
    middle, low = rest, (own - high.astype(F32) - rest.astype(F32)).astype(BF16)
    folded = sum(jnp.dot(x, fold, preferred_element_type=F32) for x in (high, middle, low))
    sums_ref[:, :rank] = folded
    sums_ref[:, rank:] = squares_ref[...]
    for copy in ups:
        copy.wait()


def adapt(tenants, scaled, squares, down, up):
    streams = tenants.shape[0]
    rows, depth = scaled.shape
    rank, inner = up.shape[1:]
    whole = pl.BlockSpec(memory_space=pltpu.VMEM)
    anywhere = pl.BlockSpec(memory_space=pl.ANY)
    return pl.pallas_call(
        adapt_body,
        out_shape=(
            jax.ShapeDtypeStruct((rows, rank + 1), F32),
            pltpu.VMEM((streams * rank, inner), BF16),
        ),
        in_specs=[pl.BlockSpec(memory_space=pltpu.SMEM), whole, whole, anywhere, anywhere],
        out_specs=(whole, whole),
        scratch_shapes=[
            pltpu.VMEM((streams * rank, depth), BF16),
            pltpu.SemaphoreType.DMA((2 * streams,)),
        ],
        compiler_params=params(),
        cost_estimate=cost(2 * rows * depth * streams * rank, 2 * streams * rank * (depth + inner)),
        name="adapt",
    )(tenants, scaled, squares, in_hbm(jnp.swapaxes(down, 1, 2)), in_hbm(up))


def project_signal_body(owners, order, *refs):
    blocks, refs = refs[: len(order)], refs[len(order) :]
    weight_ref, mix_ref, step_ref, send_ref, keep_ref, lhs_ref, semaphores = refs
    rows = blocks[0].shape[0]
    parts = len(blocks) // owners
    copies = []
    for i, block in enumerate(blocks):
        owner, part = order[i]
        away = (owner() ^ lax.axis_index("row")) % owners
        at = pl.multiple_of((away * parts + part) * rows, rows)
        copies.append(
            pltpu.make_async_copy(block, lhs_ref.at[pl.ds(at, rows), :], semaphores.at[i])
        )
    for copy in copies:
        copy.start()
    for copy in copies:
        copy.wait()
    lhs = lhs_ref[...]

    def put(acc, start):
        step = send_ref.shape[1]
        for k in range(owners):
            target = send_ref if k % 2 else keep_ref
            target[k // 2, :, start : start + acc.shape[1]] = acc[k * step : (k + 1) * step].astype(
                target.dtype
            )

    columns = weight_ref.shape[1]
    tile = min(columns, 512)
    for t in range(0, columns, tile):
        put(jnp.dot(lhs, weight_ref[:, t : t + tile], preferred_element_type=F32), t)
    put(jnp.dot(lhs, mix_ref[...], preferred_element_type=F32), columns)
    acc = lax.dot_general(lhs, step_ref[...], (((1,), (1,)), ((), ())), preferred_element_type=F32)
    put(acc, columns + mix_ref.shape[1])


def project_signal(blocks, order, owners, weight, mix, step, after):
    pieces = len(blocks)
    depth = blocks[0].shape[1]
    rows = pieces * blocks[0].shape[0]
    columns = weight.shape[1] + mix.shape[1] + step.shape[0]
    half = jax.ShapeDtypeStruct((owners // 2, rows // owners, columns), BF16)
    whole = pl.BlockSpec(memory_space=pltpu.VMEM)
    anywhere = pl.BlockSpec(memory_space=pl.ANY)

    def body(*refs):
        project_signal_body(owners, order, *refs[:pieces], *refs[pieces + 1 :])

    return pl.pallas_call(
        body,
        out_shape=(half, half, jax.ShapeDtypeStruct((rows, depth), BF16)),
        in_specs=[anywhere] * (pieces + 1) + [whole] * 3,
        out_specs=(whole,) * 3,
        scratch_shapes=[pltpu.SemaphoreType.DMA((pieces,))],
        compiler_params=params(),
        cost_estimate=cost(2 * rows * depth * columns, 2 * depth * columns),
        name="project_signal",
    )(*blocks, after, in_vmem(weight), in_vmem(mix), step)


def project_gate_body(groups, *refs):
    lhs_refs, refs = refs[:groups], refs[groups:]
    weight_ref, after_ref, send_ref, keep_ref = refs
    rows = send_ref.shape[1]
    columns = weight_ref.shape[1]
    tile = min(columns, 512)
    first = group_of_own(groups)
    for t in range(0, columns, tile):
        for g, lhs_ref in enumerate(lhs_refs):
            acc = jnp.dot(lhs_ref[...], weight_ref[:, t : t + tile], preferred_element_type=F32)
            pairs = lhs_ref.shape[0] // (2 * rows)
            for k in range(2 * pairs):
                target = send_ref if k % 2 else keep_ref
                at = (first ^ g) * pairs + k // 2
                target[at, :, t : t + tile] = acc[k * rows : (k + 1) * rows].astype(target.dtype)


def group_of_own(groups):
    if groups == 1:
        return 0
    return (lax.axis_index("head") ^ lax.axis_index("row")) >> 1


def project_gate(rows, lhs, weight, after):
    count = sum(part.shape[0] for part in lhs) // rows
    columns = weight.shape[1]
    half = jax.ShapeDtypeStruct((count // 2, rows, columns), BF16)
    whole = pl.BlockSpec(memory_space=pltpu.VMEM)
    return pl.pallas_call(
        functools.partial(project_gate_body, len(lhs)),
        out_shape=(half, half),
        in_specs=[whole] * (len(lhs) + 1) + [pl.BlockSpec(memory_space=pl.ANY)],
        out_specs=(whole,) * 2,
        compiler_params=params(),
        cost_estimate=cost(2 * count * rows * lhs[0].shape[1] * columns, 2 * weight.size),
        name="project_gate",
    )(*lhs, in_vmem(weight), after)


def scatter_rows(received, keep, axis, done=1):
    send = received
    terms = [received] + (keep if isinstance(keep, list) else [keep])
    for distance in bits_of(lax.axis_size(axis))[done:]:
        send = sum(t[1::2].astype(F32) for t in terms).astype(BF16)
        terms = [swap(send, axis, distance)] + [t[0::2] for t in terms]
    return [t[0] for t in terms], send


def softplus(values):
    return jnp.maximum(values, 0.0) + jnp.log1p(jnp.exp(-jnp.abs(values)))


def silu(values):
    return values / (1.0 + jnp.exp(-values))


def inverse_of(sums_ref, width):
    return lax.rsqrt(sums_ref[:, sums_ref.shape[1] - 1 :] / width + EPSILON)


def recur_body(
    terms,
    group,
    model_width,
    live_ref,
    *refs,
):
    term_refs = refs[:terms]
    sums_ref, up_ref, bias_ref, rate_ref, skip_ref, source_ref, _ = refs[terms : terms + 7]
    result_ref, feeds_ref, b_ref, both_ref, state_ref, *scratch = refs[terms + 7 :]
    c_ref, read_ref, spread_ref, signal_ref, semaphores = scratch
    heads, head, width = state_ref.shape[1:]
    streams, inner = feeds_ref.shape[1:]
    step = pl.program_id(0)

    def fetch(i):
        at = pl.ds(i * group, group)
        return pltpu.make_async_copy(source_ref.at[at], state_ref.at[at], semaphores.at[i])

    @pl.when(step == 0)
    def _():
        for i in range(streams // group):
            fetch(i).start()
        rows = sums_ref.shape[0]
        rank = sums_ref.shape[1] - 1
        inverse = inverse_of(sums_ref, model_width)
        lowrank = (sums_ref[:, :rank] * inverse).astype(BF16)
        repeat = lax.broadcasted_iota(jnp.int32, (rank, streams * rank), 1) % rank
        repeat = (repeat == lax.broadcasted_iota(jnp.int32, (rank, streams * rank), 0)).astype(BF16)
        every = jnp.dot(lowrank, repeat, preferred_element_type=F32)
        own = jnp.where(own_columns(rows, streams, rank), every, 0.0).astype(BF16)
        adapted = jnp.dot(own, up_ref[...], preferred_element_type=F32)
        total = sum(t[...].astype(F32) for t in term_refs) * inverse
        signal_ref[...] = silu(total[:, :inner] + adapted)
        gates = silu(total[:, inner : inner + 2 * width])
        steps_dt = softplus(total[:, inner + 2 * width :] + bias_ref[...])
        b = [gates[p * streams : (p + 1) * streams, :width] for p in range(2)]
        c = [gates[p * streams : (p + 1) * streams, width:] for p in range(2)]
        for p in range(2):
            b_ref[p] = b[p]
            c_ref[p] = c[p]
        live = lax.broadcasted_iota(jnp.int32, (streams, heads), 0) < live_ref[0]
        dt = [steps_dt[p * streams : (p + 1) * streams] for p in range(2)]
        decay = [jnp.where(live, jnp.exp(-d * rate_ref[...]), 1.0) for d in dt]
        fed = [jnp.where(live, d, 0.0) for d in dt]

        def match(i, j):
            return jnp.sum(b[i] * c[j], -1, keepdims=True)

        both = decay[0] * decay[1]
        both_ref[...] = both
        late = decay[1] * fed[0]
        skip = skip_ref[...]
        factors = jnp.concatenate(
            [
                decay[0],
                both,
                fed[0] * match(0, 0) + skip,
                fed[1] * match(1, 1) + skip,
                late * match(0, 1),
                late,
                fed[1],
            ],
            0,
        )
        high, low = split(factors)
        place = lax.broadcasted_iota(jnp.int32, (heads, inner), 1) // head
        ones = (place == lax.broadcasted_iota(jnp.int32, (heads, inner), 0)).astype(BF16)
        spread_ref[...] = jnp.dot(high, ones, preferred_element_type=F32) + jnp.dot(
            low, ones, preferred_element_type=F32
        )

    fetch(step).wait()
    at = pl.multiple_of(step * group, group)
    c = jnp.concatenate([c_ref[p, pl.ds(at, group), :] for p in range(2)], 0)
    lhs = jnp.concatenate(split(c), 0)
    for g in range(group):
        state = state_ref[at + g].reshape(inner, width)
        found = lax.dot_general(lhs, state, (((1,), (1,)), ((), ())), preferred_element_type=F32)
        for p in range(2):
            row = p * group + g
            low = 2 * group + row
            read_ref[p, pl.ds(at + g, 1), :] = found[row : row + 1] + found[low : low + 1]

    @pl.when(step == pl.num_programs(0) - 1)
    def _():
        factor = [spread_ref[i * streams : (i + 1) * streams, :] for i in range(7)]
        first = signal_ref[:streams, :]
        second = signal_ref[streams:, :]
        result_ref[:streams, :] = factor[0] * read_ref[0] + factor[2] * first
        result_ref[streams:, :] = factor[1] * read_ref[1] + factor[4] * first + factor[3] * second
        feeds_ref[0] = factor[5] * first
        feeds_ref[1] = factor[6] * second


def recur(model_width, after, live_rows, terms, sums, up_rows, bias, rate, skip, state):
    streams, heads, head, width = state.shape
    group = 8
    inner = heads * head
    rows = 2 * streams
    whole = pl.BlockSpec(memory_space=pltpu.VMEM)
    return pl.pallas_call(
        functools.partial(recur_body, len(terms), group, model_width),
        out_shape=(
            jax.ShapeDtypeStruct((rows, inner), F32),
            jax.ShapeDtypeStruct((2, streams, inner), F32),
            jax.ShapeDtypeStruct((2, streams, width), F32),
            jax.ShapeDtypeStruct((streams, heads), F32),
            pltpu.VMEM(state.shape, state.dtype),
        ),
        grid=(streams // group,),
        in_specs=[pl.BlockSpec(memory_space=pltpu.SMEM)]
        + [whole] * (len(terms) + 5)
        + [pl.BlockSpec(memory_space=pl.ANY)] * 2,
        out_specs=(whole,) * 5,
        scratch_shapes=[
            pltpu.VMEM((2, streams, width), F32),
            pltpu.VMEM((2, streams, inner), F32),
            pltpu.VMEM((7 * streams, inner), F32),
            pltpu.VMEM((rows, inner), F32),
            pltpu.SemaphoreType.DMA((streams // group,)),
        ],
        compiler_params=params(),
        cost_estimate=cost(64 * state.size, 2 * state.size + 32 * rows * inner),
        name="recur",
    )(
        live_rows,
        *terms,
        sums,
        up_rows,
        bias[None],
        rate[None],
        skip[None],
        in_hbm(state),
        after,
    )


def state_write_body(feeds_ref, b_ref, decay_ref, state_ref, out_ref):
    group, heads, head, width = out_ref.shape
    at = pl.multiple_of(pl.program_id(0) * group, group)
    feeds = [split(feeds_ref[p, pl.ds(at, group), :]) for p in range(2)]
    rights = [split(b_ref[p, pl.ds(at, group), :]) for p in range(2)]
    left = [f.astype(F32) for pair in feeds for f in (pair[0], pair[1], pair[0])]
    right = [f.astype(F32) for pair in rights for f in (pair[0], pair[0], pair[1])]
    left = jnp.concatenate(left, 0).astype(BF16)
    right = jnp.concatenate(right, 0)
    stream = lax.broadcasted_iota(jnp.int32, right.shape, 0) % group
    for g in range(0, group, 2):
        pair = jnp.concatenate([jnp.where(stream == g + i, right, 0.0) for i in range(2)], 1)
        outer = lax.dot_general(
            left, pair.astype(BF16), (((0,), (0,)), ((), ())), preferred_element_type=F32
        )
        for i in range(2):
            scaled = state_ref[at + g + i].astype(F32) * decay_ref[g + i][:, None, :]
            own = outer[:, i * width : (i + 1) * width].reshape(heads, head, width)
            out_ref[g + i] = (scaled + own).astype(out_ref.dtype)


def state_write(feeds, b, decay, state):
    streams, heads, head, width = state.shape
    group = 8
    whole = pl.BlockSpec(memory_space=pltpu.VMEM)
    return pl.pallas_call(
        state_write_body,
        out_shape=jax.ShapeDtypeStruct(state.shape, state.dtype),
        grid=(streams // group,),
        in_specs=[
            whole,
            whole,
            pl.BlockSpec((group, heads, width), lambda i: (i, 0, 0)),
            whole,
        ],
        out_specs=pl.BlockSpec((group, heads, head, width), lambda i: (i, 0, 0, 0)),
        compiler_params=params(),
        cost_estimate=cost(32 * state.size, 4 * state.size),
        name="state_write",
    )(feeds, b, decay, state)


def output_tiles(distances, lhs_ref, weight_refs, out_ref):
    width = out_ref.shape[2] // 256 * 256
    tile = min(width, 512)
    for j, distance in enumerate(distances):
        for t in range(0, width, tile):
            at = pl.multiple_of((lax.axis_index("head") ^ distance) * width + t, tile)
            acc, start = 0.0, 0
            for weight_ref in weight_refs:
                stop = start + weight_ref.shape[0]
                acc += jnp.dot(
                    lhs_ref[:, start:stop],
                    weight_ref[:, pl.ds(at, tile)],
                    preferred_element_type=F32,
                )
                start = stop
            out_ref[j, :, t : t + tile] = acc.astype(out_ref.dtype)


LANES = 128


def put_lanes(values, out_ref, j):
    lane = lax.broadcasted_iota(jnp.int32, (values.shape[0], LANES), 1)
    tail = jnp.zeros(lane.shape, F32)
    for i in range(3):
        term = values.astype(BF16).astype(F32)
        tail = jnp.where(lane == i, term, tail)
        values = values - term
    out_ref[j, :, out_ref.shape[2] - LANES :] = tail.astype(out_ref.dtype)


def meet_body(met_ref, own_ref, squares_ref, out_ref, total_ref):
    count = met_ref.shape[0]
    width = own_ref.shape[2]
    total = squares_ref[...] + join_lanes(met_ref[0, :, width:])
    total_ref[...] = total
    for j in range(count):
        both = met_ref[j, :, :width].astype(F32) + own_ref[j].astype(F32)
        out_ref[j, :, :width] = both.astype(out_ref.dtype)
        put_lanes(total, out_ref, j)


def meet(met, own, squares):
    whole = pl.BlockSpec(memory_space=pltpu.VMEM)
    return pl.pallas_call(
        meet_body,
        out_shape=(
            jax.ShapeDtypeStruct(met.shape, met.dtype),
            jax.ShapeDtypeStruct(squares.shape, squares.dtype),
        ),
        in_specs=[whole] * 3,
        out_specs=(whole, whole),
        compiler_params=params(),
        cost_estimate=cost(met.size, 6 * met.size),
        name="meet",
    )(met, own, squares)


def join_lanes(values):
    return jnp.sum(values.astype(F32), -1, keepdims=True)


def output_first_body(distances, terms, model_width, *refs):
    term_refs = refs[:terms]
    sums_ref, result_ref, scale_ref, *weight_refs, out_ref, lhs_ref, squares_ref = refs[terms:]
    total = sum(t[...].astype(F32) for t in term_refs) * inverse_of(sums_ref, model_width)
    gated = result_ref[...] * silu(total)
    squares_ref[...] = jnp.sum(gated * gated, -1, keepdims=True)
    lhs_ref[...] = (gated * scale_ref[...]).astype(lhs_ref.dtype)
    output_tiles(distances, lhs_ref, weight_refs, out_ref)
    for j in range(len(distances)):
        put_lanes(squares_ref[...], out_ref, j)


def output_rest_body(distances, lhs_ref, after_ref, *refs):
    output_tiles(distances, lhs_ref, refs[:-1], refs[-1])


def output_parts(distances, weights, width, operands, model_width=None):
    first = model_width is not None
    rows, depth = operands[0].shape
    count = len(distances)
    whole = pl.BlockSpec(memory_space=pltpu.VMEM)
    specs = [whole] * (len(operands) + len(weights))
    body = functools.partial(output_rest_body, distances)
    extra = LANES if first else 0
    out_shape = [jax.ShapeDtypeStruct((count, rows, width + extra), BF16)]
    if first:
        body = functools.partial(output_first_body, distances, len(operands) - 3, model_width)
        out_shape += [
            jax.ShapeDtypeStruct((rows, depth), BF16),
            jax.ShapeDtypeStruct((rows, 1), F32),
        ]
    else:
        specs[1] = pl.BlockSpec(memory_space=pl.ANY)
    return pl.pallas_call(
        body,
        out_shape=tuple(out_shape),
        in_specs=specs,
        out_specs=(whole,) * len(out_shape),
        compiler_params=params(),
        cost_estimate=cost(2 * rows * depth * width * count, 2 * depth * width * count),
        name="output_first" if first else "output_rest",
    )(*operands, *[in_vmem(w) for w in weights])


def split(values):
    high = values.astype(BF16)
    return high, (values - high.astype(F32)).astype(BF16)


def on_device(
    hidden,
    input_norm_scale,
    projection_signal,
    projection_gate,
    projection_step,
    projection_input_output,
    step_bias,
    head_decay_rate,
    head_skip_weight,
    gated_norm_scale,
    adapter_down_weight,
    adapter_up_weight,
    output_weight,
    scan_state,
    stream_tenant_index,
    live_block_rows,
):
    streams, positions, feature_width = hidden.shape
    rows = streams * positions
    heads_n = lax.axis_size("head")
    rows_n = lax.axis_size("row")
    model_width = feature_width * heads_n
    depth, inner = projection_signal.shape
    inner_width = inner * heads_n

    wide = jnp.swapaxes(hidden, 0, 1).astype(F32)
    scaled = (wide * input_norm_scale).astype(BF16)
    scaled_flat = scaled.reshape(rows, feature_width)

    squares = jnp.sum(wide * wide, -1).reshape(rows, 1)
    sums, up_rows = adapt(stream_tenant_index, scaled_flat, squares, adapter_down_weight, adapter_up_weight)

    own = group_of_own(2) == 0
    sums, own = lax.optimization_barrier((sums, own))
    weights = load(sums, [], projection_signal, projection_input_output, projection_gate)
    signal_weights = (*weights[:2], projection_step.T)
    middle = output_weight.shape[0] // 2
    if heads_n == rows_n and len(bits_of(rows_n)) == 2:
        turn = [(h * rows_n + r, r * rows_n + h) for h in range(heads_n) for r in range(rows_n)]
        turned = lax.ppermute(scaled_flat, ("head", "row"), turn)
        turned, _ = lax.optimization_barrier((turned, weights[0]))
        crossed = swap(turned, "head", 2)

        def order(distance):
            return [
                (lambda d=d: lax.axis_index("head") ^ d, 0) for d in (distance, distance ^ 1)
            ]

        near = [turned, swap(turned, "head", 1)]
        (out_early,) = load(turned, [], (output_weight, 0, middle))
        crossed, _ = lax.optimization_barrier((crossed, out_early))
        far = [crossed, swap(crossed, "head", 1)]
        near_send, near_keep, near_lhs = project_signal(near, order(0), 2, *signal_weights, crossed)
        near_other = swap(near_send, "row", 1)
        far_send, far_keep, far_lhs = project_signal(far, order(2), 2, *signal_weights, near_send)
        far_other = swap(far_send, "row", 1)
        gate_send, gate_keep = project_gate(rows, [near_lhs, far_lhs], weights[2], far_send)
        far_keep, out_late = load(gate_send, [far_keep], (output_weight, middle, middle))
        pick = [(near_keep, far_keep), (near_other, far_other)]
        last_send = sum(jnp.where(own, f, n).astype(F32) for n, f in pick).astype(BF16)
        signal_terms = [jnp.where(own, n, f)[0] for n, f in pick]
        last_other = swap(last_send, "row", 2)
        signal_terms = [last_other[0]] + signal_terms
        gate_send, _ = lax.optimization_barrier((gate_send, last_send))
        gate_terms = [swap(gate_send, "row", 1), gate_keep]
        gate_last = sum(t[1:].astype(F32) for t in gate_terms).astype(BF16)
        gate_last, _ = lax.optimization_barrier((gate_last, last_other))
        gate_terms = [t[0] for t in [swap(gate_last, "row", 2)] + gate_terms]
        sums, _ = lax.optimization_barrier((sums, last_send))
        sums = sum_over(sums, "head")
    else:
        features = lax.all_gather(scaled_flat, "head", axis=1, tiled=True)
        blocks = lax.all_to_all(features, "row", split_axis=1, concat_axis=0, tiled=True)
        blocks = blocks.reshape(rows_n, rows, depth)
        blocks = [blocks[i] for i in range(rows_n)]
        order = [(lambda i=i: i, 0) for i in range(rows_n)]
        send, keep, lhs = project_signal(blocks, order, rows_n, *signal_weights, sums)
        received = swap(send, "row", 1)
        gate_send, gate_keep = project_gate(rows, [lhs], weights[2], send)
        sums = sum_over(sums, "head")
        keep, out_early, out_late = load(
            gate_send, [keep], (output_weight, 0, middle), (output_weight, middle, middle)
        )
        signal_terms, _ = scatter_rows(received, keep, "row")
        gate_terms, gate_last = scatter_rows(swap(gate_send, "row", 1), gate_keep, "row")
    out_weights = [out_early, out_late]

    result, feeds, bgate, both, state = recur(
        model_width,
        gate_last,
        live_block_rows,
        signal_terms,
        sums,
        up_rows,
        step_bias,
        head_decay_rate,
        head_skip_weight,
        scan_state,
    )

    distances = list(range(heads_n))
    first, out_lhs, gate_squares = output_parts(
        distances[3::4],
        out_weights,
        feature_width,
        [*gate_terms, sums, result, gated_norm_scale[None]],
        model_width,
    )
    (second,) = output_parts(
        distances[2::4] + distances[1::4], out_weights, feature_width, [out_lhs, first]
    )
    half = second.shape[0] // 2
    send, gate_squares = meet(swap(first, "head", 1), second, gate_squares)
    (rest,) = output_parts(distances[0::4], out_weights, feature_width, [out_lhs, send])
    feeds, _ = lax.optimization_barrier((feeds, rest))
    kept = [swap(second[half:], "head", 1), rest]
    if len(bits_of(heads_n)) == 2:
        received = swap(send, "head", 2)
        mixer = sum(t[0].astype(F32) for t in [received[..., :feature_width]] + kept)
        gate_squares = gate_squares + join_lanes(received[0, :, feature_width:])
    else:
        received = swap(send[..., :feature_width], "head", 2)
        mixer, _ = scatter_rows(received, kept, "head", done=2)
        mixer = sum(t.astype(F32) for t in mixer)
        for distance in bits_of(heads_n)[1:]:
            gate_squares = gate_squares + swap(gate_squares, "head", distance)
    mixer = mixer * lax.rsqrt(gate_squares / inner_width + EPSILON)
    mixer = mixer.reshape(positions, streams, feature_width)
    live = jnp.arange(streams) < live_block_rows[0]
    mixed = (wide + jnp.where(live[:, None], mixer, 0.0)).astype(BF16)

    spread = jnp.broadcast_to(both[..., None], both.shape + (bgate.shape[-1],))
    new_state = state_write(feeds, bgate, spread, state)
    return (jnp.swapaxes(mixed, 0, 1), new_state)


def solution(mesh):
    in_specs = (
        P(("rep", "row"), None, "head"),
        P("head"),
        P("row", "head"),
        P("row", "head"),
        P("row", "head"),
        P("row", None),
        P("head"),
        P("head"),
        P("head"),
        P("head"),
        P("row", "head", None),
        P("row", None, "head"),
        P("head", None),
        P(("rep", "row"), "head", None, None),
        P(("rep", "row")),
        P(("rep", "row")),
    )
    out_specs = (P(("rep", "row"), None, "head"), P(("rep", "row"), "head", None, None))
    return jax.shard_map(
        on_device, mesh=mesh, in_specs=in_specs, out_specs=out_specs, check_vma=False
    )
```

```python
import functools

import jax
import jax.numpy as jnp
from jax import lax
from jax.experimental import pallas as pl
from jax.experimental.pallas import tpu as pltpu
from jax.sharding import PartitionSpec as P

BF16 = jnp.bfloat16
EPSILON = 1e-05
F32 = jnp.float32
VMEM_GRANT = 12 * 1024 * 1024


def swap(values, axis, distance):
    size = lax.axis_size(axis)
    return lax.ppermute(values, axis, [(i, i ^ distance) for i in range(size)])


def swap_halves(values, axis, distance, dim):
    return jnp.concatenate([swap(v, axis, distance) for v in jnp.split(values, 2, dim)], dim)


def bits_of(size):
    return [1 << i for i in range(size.bit_length() - 1)]


def sum_over(values, axis):
    for distance in bits_of(lax.axis_size(axis)):
        values = values + swap(values, axis, distance)
    return values


def reverse_bits(value, size):
    bits = size.bit_length() - 1
    return sum(((value >> i) & 1) << (bits - 1 - i) for i in range(bits))


def params(**more):
    return pltpu.CompilerParams(vmem_limit_bytes=VMEM_GRANT, **more)


def cost(flops, size):
    return pl.CostEstimate(flops=int(flops), bytes_accessed=int(size), transcendentals=0)


def in_hbm(values):
    return pltpu.with_memory_space_constraint(values, pltpu.HBM)


def in_vmem(values):
    return pltpu.with_memory_space_constraint(values, pltpu.VMEM)


def load_body(spans, after_ref, *refs):
    count = len(spans)
    sources, targets, semaphores = refs[:count], refs[count : 2 * count], refs[2 * count]
    copies = []
    for source, target, (start, rows, parts) in zip(sources, targets, spans):
        step = rows // parts
        for i in range(parts):
            copies.append(
                pltpu.make_async_copy(
                    source.at[pl.ds(start + i * step, step)],
                    target.at[pl.ds(i * step, step)],
                    semaphores.at[len(copies)],
                )
            )
    for copy in copies:
        copy.start()
    for copy in copies:
        copy.wait()


def load(after, passed, *weights):
    weights = [w if isinstance(w, tuple) else (w, 0, w.shape[0]) for w in weights]
    shapes = [p.shape for p in passed] + [(rows, *w.shape[1:]) for w, _, rows in weights]
    spans = [(0, p.shape[0], 1) for p in passed]
    spans += [(start, rows, 8 if rows % 128 == 0 else 1) for _, start, rows in weights]
    size = sum(rows * w.shape[1] * w.dtype.itemsize for w, _, rows in weights)
    return pl.pallas_call(
        functools.partial(load_body, spans),
        out_shape=tuple(pltpu.VMEM(shape, BF16) for shape in shapes),
        in_specs=[pl.BlockSpec(memory_space=pl.ANY)] * (1 + len(shapes)),
        out_specs=tuple(pl.BlockSpec(memory_space=pltpu.VMEM) for _ in shapes),
        scratch_shapes=[pltpu.SemaphoreType.DMA((sum(parts for _, _, parts in spans),))],
        compiler_params=params(),
        cost_estimate=cost(0, 2 * size),
        name="load",
    )(after, *passed, *[in_hbm(w) for w, _, _ in weights])


def own_columns(rows, streams, rank):
    row = lax.broadcasted_iota(jnp.int32, (rows, streams * rank), 0) % streams
    return row == lax.broadcasted_iota(jnp.int32, (rows, streams * rank), 1) // rank


def adapt_body(tenant_ref, scaled_ref, squares_ref, down_ref, up_ref, sums_ref, up_rows_ref, *scratch):
    down_rows_ref, semaphores = scratch
    rank = down_ref.shape[1]
    streams = tenant_ref.shape[0]
    rows = scaled_ref.shape[0]
    first = lax.axis_index("row") * down_ref.shape[0]
    downs, ups = [], []
    for s in range(streams):
        at = pl.ds(s * rank, rank)
        tenant = tenant_ref[s] - first
        downs.append(
            pltpu.make_async_copy(down_ref.at[tenant], down_rows_ref.at[at, :], semaphores.at[s])
        )
        ups.append(
            pltpu.make_async_copy(
                up_ref.at[tenant], up_rows_ref.at[at, :], semaphores.at[streams + s]
            )
        )
    for copy in downs + ups:
        copy.start()
    for copy in downs:
        copy.wait()
    every = lax.dot_general(
        scaled_ref[...],
        down_rows_ref[...],
        (((1,), (1,)), ((), ())),
        preferred_element_type=F32,
    )
    own = jnp.where(own_columns(rows, streams, rank), every, 0.0)
    fold = lax.broadcasted_iota(jnp.int32, (streams * rank, rank), 0) % rank
    fold = (fold == lax.broadcasted_iota(jnp.int32, (streams * rank, rank), 1)).astype(BF16)
    high, rest = split(own)
    middle, low = rest, (own - high.astype(F32) - rest.astype(F32)).astype(BF16)
    folded = sum(jnp.dot(x, fold, preferred_element_type=F32) for x in (high, middle, low))
    sums_ref[:, :rank] = folded
    sums_ref[:, rank:] = squares_ref[...]
    for copy in ups:
        copy.wait()


def adapt(tenants, scaled, squares, down, up):
    streams = tenants.shape[0]
    rows, depth = scaled.shape
    rank, inner = up.shape[1:]
    whole = pl.BlockSpec(memory_space=pltpu.VMEM)
    anywhere = pl.BlockSpec(memory_space=pl.ANY)
    return pl.pallas_call(
        adapt_body,
        out_shape=(
            jax.ShapeDtypeStruct((rows, rank + 1), F32),
            pltpu.VMEM((streams * rank, inner), BF16),
        ),
        in_specs=[pl.BlockSpec(memory_space=pltpu.SMEM), whole, whole, anywhere, anywhere],
        out_specs=(whole, whole),
        scratch_shapes=[
            pltpu.VMEM((streams * rank, depth), BF16),
            pltpu.SemaphoreType.DMA((2 * streams,)),
        ],
        compiler_params=params(),
        cost_estimate=cost(2 * rows * depth * streams * rank, 2 * streams * rank * (depth + inner)),
        name="adapt",
    )(tenants, scaled, squares, in_hbm(jnp.swapaxes(down, 1, 2)), in_hbm(up))


def project_signal_body(owners, order, *refs):
    blocks, refs = refs[: len(order)], refs[len(order) :]
    weight_ref, mix_ref, step_ref, send_ref, keep_ref, lhs_ref, semaphores = refs
    rows = blocks[0].shape[0]
    parts = len(blocks) // owners
    copies = []
    for i, block in enumerate(blocks):
        owner, part = order[i]
        away = (owner() ^ lax.axis_index("row")) % owners
        at = pl.multiple_of((away * parts + part) * rows, rows)
        copies.append(
            pltpu.make_async_copy(block, lhs_ref.at[pl.ds(at, rows), :], semaphores.at[i])
        )
    for copy in copies:
        copy.start()
    for copy in copies:
        copy.wait()
    lhs = lhs_ref[...]

    def put(acc, start):
        step = send_ref.shape[1]
        for k in range(owners):
            target = send_ref if k % 2 else keep_ref
            target[k // 2, :, start : start + acc.shape[1]] = acc[k * step : (k + 1) * step].astype(
                target.dtype
            )

    columns = weight_ref.shape[1]
    tile = min(columns, 512)
    for t in range(0, columns, tile):
        put(jnp.dot(lhs, weight_ref[:, t : t + tile], preferred_element_type=F32), t)
    put(jnp.dot(lhs, mix_ref[...], preferred_element_type=F32), columns)
    acc = lax.dot_general(lhs, step_ref[...], (((1,), (1,)), ((), ())), preferred_element_type=F32)
    put(acc, columns + mix_ref.shape[1])


def project_signal(blocks, order, owners, weight, mix, step, after):
    pieces = len(blocks)
    depth = blocks[0].shape[1]
    rows = pieces * blocks[0].shape[0]
    columns = weight.shape[1] + mix.shape[1] + step.shape[0]
    half = jax.ShapeDtypeStruct((owners // 2, rows // owners, columns), BF16)
    whole = pl.BlockSpec(memory_space=pltpu.VMEM)
    anywhere = pl.BlockSpec(memory_space=pl.ANY)

    def body(*refs):
        project_signal_body(owners, order, *refs[:pieces], *refs[pieces + 1 :])

    return pl.pallas_call(
        body,
        out_shape=(half, half, jax.ShapeDtypeStruct((rows, depth), BF16)),
        in_specs=[anywhere] * (pieces + 1) + [whole] * 3,
        out_specs=(whole,) * 3,
        scratch_shapes=[pltpu.SemaphoreType.DMA((pieces,))],
        compiler_params=params(),
        cost_estimate=cost(2 * rows * depth * columns, 2 * depth * columns),
        name="project_signal",
    )(*blocks, after, in_vmem(weight), in_vmem(mix), step)


def project_gate_body(groups, *refs):
    lhs_refs, refs = refs[:groups], refs[groups:]
    weight_ref, after_ref, send_ref, keep_ref = refs
    rows = send_ref.shape[1]
    columns = weight_ref.shape[1]
    tile = min(columns, 512)
    first = group_of_own(groups)
    for t in range(0, columns, tile):
        for g, lhs_ref in enumerate(lhs_refs):
            acc = jnp.dot(lhs_ref[...], weight_ref[:, t : t + tile], preferred_element_type=F32)
            pairs = lhs_ref.shape[0] // (2 * rows)
            for k in range(2 * pairs):
                target = send_ref if k % 2 else keep_ref
                at = (first ^ g) * pairs + k // 2
                target[at, :, t : t + tile] = acc[k * rows : (k + 1) * rows].astype(target.dtype)


def group_of_own(groups):
    if groups == 1:
        return 0
    return (lax.axis_index("head") ^ 2 ^ lax.axis_index("row")) >> 1


def project_gate(rows, lhs, weight, after):
    count = sum(part.shape[0] for part in lhs) // rows
    columns = weight.shape[1]
    half = jax.ShapeDtypeStruct((count // 2, rows, columns), BF16)
    whole = pl.BlockSpec(memory_space=pltpu.VMEM)
    return pl.pallas_call(
        functools.partial(project_gate_body, len(lhs)),
        out_shape=(half, half),
        in_specs=[whole] * (len(lhs) + 1) + [pl.BlockSpec(memory_space=pl.ANY)],
        out_specs=(whole,) * 2,
        compiler_params=params(),
        cost_estimate=cost(2 * count * rows * lhs[0].shape[1] * columns, 2 * weight.size),
        name="project_gate",
    )(*lhs, in_vmem(weight), after)


def scatter_rows(received, keep, axis, done=1):
    send = received
    terms = [received] + (keep if isinstance(keep, list) else [keep])
    for distance in bits_of(lax.axis_size(axis))[done:]:
        send = sum(t[1::2].astype(F32) for t in terms).astype(BF16)
        terms = [swap(send, axis, distance)] + [t[0::2] for t in terms]
    return [t[0] for t in terms], send


def softplus(values):
    return jnp.maximum(values, 0.0) + jnp.log1p(jnp.exp(-jnp.abs(values)))


def silu(values):
    return values / (1.0 + jnp.exp(-values))


def inverse_of(sums_ref, width):
    return lax.rsqrt(sums_ref[:, sums_ref.shape[1] - 1 :] / width + EPSILON)


def recur_body(
    terms,
    group,
    model_width,
    live_ref,
    *refs,
):
    term_refs = refs[:terms]
    sums_ref, up_ref, bias_ref, rate_ref, skip_ref, source_ref, _ = refs[terms : terms + 7]
    result_ref, feeds_ref, b_ref, both_ref, state_ref, *scratch = refs[terms + 7 :]
    c_ref, read_ref, spread_ref, signal_ref, semaphores = scratch
    heads, head, width = state_ref.shape[1:]
    streams, inner = feeds_ref.shape[1:]
    step = pl.program_id(0)

    def fetch(i):
        at = pl.ds(i * group, group)
        return pltpu.make_async_copy(source_ref.at[at], state_ref.at[at], semaphores.at[i])

    @pl.when(step == 0)
    def _():
        for i in range(streams // group):
            fetch(i).start()
        rows = sums_ref.shape[0]
        rank = sums_ref.shape[1] - 1
        inverse = inverse_of(sums_ref, model_width)
        lowrank = (sums_ref[:, :rank] * inverse).astype(BF16)
        repeat = lax.broadcasted_iota(jnp.int32, (rank, streams * rank), 1) % rank
        repeat = (repeat == lax.broadcasted_iota(jnp.int32, (rank, streams * rank), 0)).astype(BF16)
        every = jnp.dot(lowrank, repeat, preferred_element_type=F32)
        own = jnp.where(own_columns(rows, streams, rank), every, 0.0).astype(BF16)
        adapted = jnp.dot(own, up_ref[...], preferred_element_type=F32)
        total = sum(t[...].astype(F32) for t in term_refs) * inverse
        signal_ref[...] = silu(total[:, :inner] + adapted)
        gates = silu(total[:, inner : inner + 2 * width])
        steps_dt = softplus(total[:, inner + 2 * width :] + bias_ref[...])
        b = [gates[p * streams : (p + 1) * streams, :width] for p in range(2)]
        c = [gates[p * streams : (p + 1) * streams, width:] for p in range(2)]
        for p in range(2):
            b_ref[p] = b[p]
            c_ref[p] = c[p]
        live = lax.broadcasted_iota(jnp.int32, (streams, heads), 0) < live_ref[0]
        dt = [steps_dt[p * streams : (p + 1) * streams] for p in range(2)]
        decay = [jnp.where(live, jnp.exp(-d * rate_ref[...]), 1.0) for d in dt]
        fed = [jnp.where(live, d, 0.0) for d in dt]

        def match(i, j):
            return jnp.sum(b[i] * c[j], -1, keepdims=True)

        both = decay[0] * decay[1]
        both_ref[...] = both
        late = decay[1] * fed[0]
        skip = skip_ref[...]
        factors = jnp.concatenate(
            [
                decay[0],
                both,
                fed[0] * match(0, 0) + skip,
                fed[1] * match(1, 1) + skip,
                late * match(0, 1),
                late,
                fed[1],
            ],
            0,
        )
        high, low = split(factors)
        place = lax.broadcasted_iota(jnp.int32, (heads, inner), 1) // head
        ones = (place == lax.broadcasted_iota(jnp.int32, (heads, inner), 0)).astype(BF16)
        spread_ref[...] = jnp.dot(high, ones, preferred_element_type=F32) + jnp.dot(
            low, ones, preferred_element_type=F32
        )

    fetch(step).wait()
    at = pl.multiple_of(step * group, group)
    c = jnp.concatenate([c_ref[p, pl.ds(at, group), :] for p in range(2)], 0)
    lhs = jnp.concatenate(split(c), 0)
    for g in range(group):
        state = state_ref[at + g].reshape(inner, width)
        found = lax.dot_general(lhs, state, (((1,), (1,)), ((), ())), preferred_element_type=F32)
        for p in range(2):
            row = p * group + g
            low = 2 * group + row
            read_ref[p, pl.ds(at + g, 1), :] = found[row : row + 1] + found[low : low + 1]

    @pl.when(step == pl.num_programs(0) - 1)
    def _():
        factor = [spread_ref[i * streams : (i + 1) * streams, :] for i in range(7)]
        first = signal_ref[:streams, :]
        second = signal_ref[streams:, :]
        result_ref[:streams, :] = factor[0] * read_ref[0] + factor[2] * first
        result_ref[streams:, :] = factor[1] * read_ref[1] + factor[4] * first + factor[3] * second
        feeds_ref[0] = factor[5] * first
        feeds_ref[1] = factor[6] * second


def recur(model_width, after, live_rows, terms, sums, up_rows, bias, rate, skip, state):
    streams, heads, head, width = state.shape
    group = 8
    inner = heads * head
    rows = 2 * streams
    whole = pl.BlockSpec(memory_space=pltpu.VMEM)
    return pl.pallas_call(
        functools.partial(recur_body, len(terms), group, model_width),
        out_shape=(
            jax.ShapeDtypeStruct((rows, inner), F32),
            jax.ShapeDtypeStruct((2, streams, inner), F32),
            jax.ShapeDtypeStruct((2, streams, width), F32),
            jax.ShapeDtypeStruct((streams, heads), F32),
            pltpu.VMEM(state.shape, state.dtype),
        ),
        grid=(streams // group,),
        in_specs=[pl.BlockSpec(memory_space=pltpu.SMEM)]
        + [whole] * (len(terms) + 5)
        + [pl.BlockSpec(memory_space=pl.ANY)] * 2,
        out_specs=(whole,) * 5,
        scratch_shapes=[
            pltpu.VMEM((2, streams, width), F32),
            pltpu.VMEM((2, streams, inner), F32),
            pltpu.VMEM((7 * streams, inner), F32),
            pltpu.VMEM((rows, inner), F32),
            pltpu.SemaphoreType.DMA((streams // group,)),
        ],
        compiler_params=params(),
        cost_estimate=cost(64 * state.size, 2 * state.size + 32 * rows * inner),
        name="recur",
    )(
        live_rows,
        *terms,
        sums,
        up_rows,
        bias[None],
        rate[None],
        skip[None],
        in_hbm(state),
        after,
    )


def state_write_body(feeds_ref, b_ref, decay_ref, state_ref, out_ref):
    group, heads, head, width = out_ref.shape
    at = pl.multiple_of(pl.program_id(0) * group, group)
    feeds = [split(feeds_ref[p, pl.ds(at, group), :]) for p in range(2)]
    rights = [split(b_ref[p, pl.ds(at, group), :]) for p in range(2)]
    left = [f.astype(F32) for pair in feeds for f in (pair[0], pair[1], pair[0])]
    right = [f.astype(F32) for pair in rights for f in (pair[0], pair[0], pair[1])]
    left = jnp.concatenate(left, 0).astype(BF16)
    right = jnp.concatenate(right, 0)
    stream = lax.broadcasted_iota(jnp.int32, right.shape, 0) % group
    for g in range(0, group, 2):
        pair = jnp.concatenate([jnp.where(stream == g + i, right, 0.0) for i in range(2)], 1)
        outer = lax.dot_general(
            left, pair.astype(BF16), (((0,), (0,)), ((), ())), preferred_element_type=F32
        )
        for i in range(2):
            scaled = state_ref[at + g + i].astype(F32) * decay_ref[g + i][:, None, :]
            own = outer[:, i * width : (i + 1) * width].reshape(heads, head, width)
            out_ref[g + i] = (scaled + own).astype(out_ref.dtype)


def state_write(feeds, b, decay, state):
    streams, heads, head, width = state.shape
    group = 8
    whole = pl.BlockSpec(memory_space=pltpu.VMEM)
    return pl.pallas_call(
        state_write_body,
        out_shape=jax.ShapeDtypeStruct(state.shape, state.dtype),
        grid=(streams // group,),
        in_specs=[
            whole,
            whole,
            pl.BlockSpec((group, heads, width), lambda i: (i, 0, 0)),
            whole,
        ],
        out_specs=pl.BlockSpec((group, heads, head, width), lambda i: (i, 0, 0, 0)),
        compiler_params=params(),
        cost_estimate=cost(32 * state.size, 4 * state.size),
        name="state_write",
    )(feeds, b, decay, state)


def output_tiles(distances, lhs_ref, weight_refs, out_ref):
    width = out_ref.shape[2] // 256 * 256
    tile = min(width, 512)
    for j, distance in enumerate(distances):
        for t in range(0, width, tile):
            at = pl.multiple_of((lax.axis_index("head") ^ distance) * width + t, tile)
            acc, start = 0.0, 0
            for weight_ref in weight_refs:
                stop = start + weight_ref.shape[0]
                acc += jnp.dot(
                    lhs_ref[:, start:stop],
                    weight_ref[:, pl.ds(at, tile)],
                    preferred_element_type=F32,
                )
                start = stop
            out_ref[j, :, t : t + tile] = acc.astype(out_ref.dtype)


LANES = 128


def put_lanes(values, out_ref, j):
    lane = lax.broadcasted_iota(jnp.int32, (values.shape[0], LANES), 1)
    tail = jnp.zeros(lane.shape, F32)
    for i in range(3):
        term = values.astype(BF16).astype(F32)
        tail = jnp.where(lane == i, term, tail)
        values = values - term
    out_ref[j, :, out_ref.shape[2] - LANES :] = tail.astype(out_ref.dtype)


def meet_body(met_ref, own_ref, squares_ref, out_ref, total_ref):
    count = met_ref.shape[0]
    width = own_ref.shape[2]
    total = squares_ref[...] + join_lanes(met_ref[0, :, width:])
    total_ref[...] = total
    for j in range(count):
        both = met_ref[j, :, :width].astype(F32) + own_ref[j].astype(F32)
        out_ref[j, :, :width] = both.astype(out_ref.dtype)
        put_lanes(total, out_ref, j)


def meet(met, own, squares):
    whole = pl.BlockSpec(memory_space=pltpu.VMEM)
    return pl.pallas_call(
        meet_body,
        out_shape=(
            jax.ShapeDtypeStruct(met.shape, met.dtype),
            jax.ShapeDtypeStruct(squares.shape, squares.dtype),
        ),
        in_specs=[whole] * 3,
        out_specs=(whole, whole),
        compiler_params=params(),
        cost_estimate=cost(met.size, 6 * met.size),
        name="meet",
    )(met, own, squares)


def join_lanes(values):
    return jnp.sum(values.astype(F32), -1, keepdims=True)


def output_first_body(distances, terms, model_width, *refs):
    term_refs = refs[:terms]
    sums_ref, result_ref, scale_ref, *weight_refs, out_ref, lhs_ref, squares_ref = refs[terms:]
    total = sum(t[...].astype(F32) for t in term_refs) * inverse_of(sums_ref, model_width)
    gated = result_ref[...] * silu(total)
    squares_ref[...] = jnp.sum(gated * gated, -1, keepdims=True)
    lhs_ref[...] = (gated * scale_ref[...]).astype(lhs_ref.dtype)
    output_tiles(distances, lhs_ref, weight_refs, out_ref)
    for j in range(len(distances)):
        put_lanes(squares_ref[...], out_ref, j)


def output_rest_body(distances, lhs_ref, after_ref, *refs):
    output_tiles(distances, lhs_ref, refs[:-1], refs[-1])


def output_parts(distances, weights, width, operands, model_width=None):
    first = model_width is not None
    rows, depth = operands[0].shape
    count = len(distances)
    whole = pl.BlockSpec(memory_space=pltpu.VMEM)
    specs = [whole] * (len(operands) + len(weights))
    body = functools.partial(output_rest_body, distances)
    extra = LANES if first else 0
    out_shape = [jax.ShapeDtypeStruct((count, rows, width + extra), BF16)]
    if first:
        body = functools.partial(output_first_body, distances, len(operands) - 3, model_width)
        out_shape += [
            jax.ShapeDtypeStruct((rows, depth), BF16),
            jax.ShapeDtypeStruct((rows, 1), F32),
        ]
    else:
        specs[1] = pl.BlockSpec(memory_space=pl.ANY)
    return pl.pallas_call(
        body,
        out_shape=tuple(out_shape),
        in_specs=specs,
        out_specs=(whole,) * len(out_shape),
        compiler_params=params(),
        cost_estimate=cost(2 * rows * depth * width * count, 2 * depth * width * count),
        name="output_first" if first else "output_rest",
    )(*operands, *[in_vmem(w) for w in weights])


def split(values):
    high = values.astype(BF16)
    return high, (values - high.astype(F32)).astype(BF16)


def on_device(
    hidden,
    input_norm_scale,
    projection_signal,
    projection_gate,
    projection_step,
    projection_input_output,
    step_bias,
    head_decay_rate,
    head_skip_weight,
    gated_norm_scale,
    adapter_down_weight,
    adapter_up_weight,
    output_weight,
    scan_state,
    stream_tenant_index,
    live_block_rows,
):
    streams, positions, feature_width = hidden.shape
    rows = streams * positions
    heads_n = lax.axis_size("head")
    rows_n = lax.axis_size("row")
    model_width = feature_width * heads_n
    depth, inner = projection_signal.shape
    inner_width = inner * heads_n

    wide = jnp.swapaxes(hidden, 0, 1).astype(F32)
    scaled = (wide * input_norm_scale).astype(BF16)
    scaled_flat = scaled.reshape(rows, feature_width)

    squares = jnp.sum(wide * wide, -1).reshape(rows, 1)
    sums, up_rows = adapt(stream_tenant_index, scaled_flat, squares, adapter_down_weight, adapter_up_weight)

    own = group_of_own(2) == 0
    sums, own = lax.optimization_barrier((sums, own))
    weights = load(sums, [], projection_signal, projection_input_output, projection_gate)
    signal_weights = (*weights[:2], projection_step.T)
    middle = output_weight.shape[0] // 2
    if heads_n == rows_n and len(bits_of(rows_n)) == 2:
        turn = [
            (h * rows_n + r, (r ^ 2) * rows_n + h) for h in range(heads_n) for r in range(rows_n)
        ]
        turned = lax.ppermute(scaled_flat, ("head", "row"), turn)
        turned, _ = lax.optimization_barrier((turned, weights[0]))
        crossed = swap(turned, "head", 2)

        def order(distance):
            return [
                (lambda d=d: lax.axis_index("head") ^ 2 ^ d, 0) for d in (distance, distance ^ 1)
            ]

        near = [turned, swap(turned, "head", 1)]
        (out_early,) = load(turned, [], (output_weight, 0, middle))
        crossed, _ = lax.optimization_barrier((crossed, out_early))
        far = [crossed, swap(crossed, "head", 1)]
        near_send, near_keep, near_lhs = project_signal(near, order(0), 2, *signal_weights, crossed)
        near_other = swap(near_send, "row", 1)
        far_send, far_keep, far_lhs = project_signal(far, order(2), 2, *signal_weights, near_send)
        far_other = swap(far_send, "row", 1)
        gate_send, gate_keep = project_gate(rows, [near_lhs, far_lhs], weights[2], far_send)
        far_keep, out_late = load(gate_send, [far_keep], (output_weight, middle, middle))
        pick = [(near_keep, far_keep), (near_other, far_other)]
        last_send = sum(jnp.where(own, f, n).astype(F32) for n, f in pick).astype(BF16)
        signal_terms = [jnp.where(own, n, f)[0] for n, f in pick]
        last_other = swap_halves(last_send, "row", 2, 1)
        signal_terms = [last_other[0]] + signal_terms
        gate_terms = [swap_halves(gate_send, "row", 1, 0), gate_keep]
        gate_last = sum(t[1:].astype(F32) for t in gate_terms).astype(BF16)
        gate_last, _ = lax.optimization_barrier((gate_last, last_other))
        gate_terms = [t[0] for t in [swap_halves(gate_last, "row", 2, 1)] + gate_terms]
        sums, _ = lax.optimization_barrier((sums, last_send))
        sums = sum_over(sums, "head")
    else:
        features = lax.all_gather(scaled_flat, "head", axis=1, tiled=True)
        blocks = lax.all_to_all(features, "row", split_axis=1, concat_axis=0, tiled=True)
        blocks = blocks.reshape(rows_n, rows, depth)
        blocks = [blocks[i] for i in range(rows_n)]
        order = [(lambda i=i: i, 0) for i in range(rows_n)]
        send, keep, lhs = project_signal(blocks, order, rows_n, *signal_weights, sums)
        received = swap(send, "row", 1)
        gate_send, gate_keep = project_gate(rows, [lhs], weights[2], send)
        sums = sum_over(sums, "head")
        keep, out_early, out_late = load(
            gate_send, [keep], (output_weight, 0, middle), (output_weight, middle, middle)
        )
        signal_terms, _ = scatter_rows(received, keep, "row")
        gate_terms, gate_last = scatter_rows(swap(gate_send, "row", 1), gate_keep, "row")
    out_weights = [out_early, out_late]

    result, feeds, bgate, both, state = recur(
        model_width,
        gate_last,
        live_block_rows,
        signal_terms,
        sums,
        up_rows,
        step_bias,
        head_decay_rate,
        head_skip_weight,
        scan_state,
    )

    distances = list(range(heads_n))
    first, out_lhs, gate_squares = output_parts(
        distances[3::4],
        out_weights,
        feature_width,
        [*gate_terms, sums, result, gated_norm_scale[None]],
        model_width,
    )
    (second,) = output_parts(
        distances[2::4] + distances[1::4], out_weights, feature_width, [out_lhs, first]
    )
    half = second.shape[0] // 2
    send, gate_squares = meet(swap(first, "head", 1), second, gate_squares)
    (rest,) = output_parts(distances[0::4], out_weights, feature_width, [out_lhs, send])
    feeds, _ = lax.optimization_barrier((feeds, rest))
    kept = [swap(second[half:], "head", 1), rest]
    if len(bits_of(heads_n)) == 2:
        received = swap_halves(send, "head", 2, 1)
        mixer = sum(t[0].astype(F32) for t in [received[..., :feature_width]] + kept)
        gate_squares = gate_squares + join_lanes(received[0, :, feature_width:])
    else:
        received = swap(send[..., :feature_width], "head", 2)
        mixer, _ = scatter_rows(received, kept, "head", done=2)
        mixer = sum(t.astype(F32) for t in mixer)
        for distance in bits_of(heads_n)[1:]:
            gate_squares = gate_squares + swap(gate_squares, "head", distance)
    mixer = mixer * lax.rsqrt(gate_squares / inner_width + EPSILON)
    mixer = mixer.reshape(positions, streams, feature_width)
    live = jnp.arange(streams) < live_block_rows[0]
    mixed = (wide + jnp.where(live[:, None], mixer, 0.0)).astype(BF16)

    spread = jnp.broadcast_to(both[..., None], both.shape + (bgate.shape[-1],))
    new_state = state_write(feeds, bgate, spread, state)
    return (jnp.swapaxes(mixed, 0, 1), new_state)


def solution(mesh):
    in_specs = (
        P(("rep", "row"), None, "head"),
        P("head"),
        P("row", "head"),
        P("row", "head"),
        P("row", "head"),
        P("row", None),
        P("head"),
        P("head"),
        P("head"),
        P("head"),
        P("row", "head", None),
        P("row", None, "head"),
        P("head", None),
        P(("rep", "row"), "head", None, None),
        P(("rep", "row")),
        P(("rep", "row")),
    )
    out_specs = (P(("rep", "row"), None, "head"), P(("rep", "row"), "head", None, None))
    return jax.shard_map(
        on_device, mesh=mesh, in_specs=in_specs, out_specs=out_specs, check_vma=False
    )
```

```python
import functools

import jax
import jax.numpy as jnp
from jax import lax
from jax.experimental import pallas as pl
from jax.experimental.pallas import tpu as pltpu
from jax.sharding import PartitionSpec as P

BF16 = jnp.bfloat16
EPSILON = 1e-05
F32 = jnp.float32
VMEM_GRANT = 12 * 1024 * 1024


def swap(values, axis, distance):
    size = lax.axis_size(axis)
    return lax.ppermute(values, axis, [(i, i ^ distance) for i in range(size)])


def swap_halves(values, axis, distance, dim):
    return jnp.concatenate([swap(v, axis, distance) for v in jnp.split(values, 2, dim)], dim)


def bits_of(size):
    return [1 << i for i in range(size.bit_length() - 1)]


def sum_over(values, axis):
    for distance in bits_of(lax.axis_size(axis)):
        values = values + swap(values, axis, distance)
    return values


def reverse_bits(value, size):
    bits = size.bit_length() - 1
    return sum(((value >> i) & 1) << (bits - 1 - i) for i in range(bits))


def params(**more):
    return pltpu.CompilerParams(vmem_limit_bytes=VMEM_GRANT, **more)


def cost(flops, size):
    return pl.CostEstimate(flops=int(flops), bytes_accessed=int(size), transcendentals=0)


def in_hbm(values):
    return pltpu.with_memory_space_constraint(values, pltpu.HBM)


def in_vmem(values):
    return pltpu.with_memory_space_constraint(values, pltpu.VMEM)


def load_body(spans, after_ref, *refs):
    count = len(spans)
    sources, targets, semaphores = refs[:count], refs[count : 2 * count], refs[2 * count]
    copies = []
    for source, target, (start, rows, parts) in zip(sources, targets, spans):
        step = rows // parts
        for i in range(parts):
            copies.append(
                pltpu.make_async_copy(
                    source.at[pl.ds(start + i * step, step)],
                    target.at[pl.ds(i * step, step)],
                    semaphores.at[len(copies)],
                )
            )
    for copy in copies:
        copy.start()
    for copy in copies:
        copy.wait()


def load(after, passed, *weights):
    weights = [w if isinstance(w, tuple) else (w, 0, w.shape[0]) for w in weights]
    shapes = [p.shape for p in passed] + [(rows, *w.shape[1:]) for w, _, rows in weights]
    spans = [(0, p.shape[0], 1) for p in passed]
    spans += [(start, rows, 8 if rows % 128 == 0 else 1) for _, start, rows in weights]
    size = sum(rows * w.shape[1] * w.dtype.itemsize for w, _, rows in weights)
    return pl.pallas_call(
        functools.partial(load_body, spans),
        out_shape=tuple(pltpu.VMEM(shape, BF16) for shape in shapes),
        in_specs=[pl.BlockSpec(memory_space=pl.ANY)] * (1 + len(shapes)),
        out_specs=tuple(pl.BlockSpec(memory_space=pltpu.VMEM) for _ in shapes),
        scratch_shapes=[pltpu.SemaphoreType.DMA((sum(parts for _, _, parts in spans),))],
        compiler_params=params(),
        cost_estimate=cost(0, 2 * size),
        name="load",
    )(after, *passed, *[in_hbm(w) for w, _, _ in weights])


def own_columns(rows, streams, rank):
    row = lax.broadcasted_iota(jnp.int32, (rows, streams * rank), 0) % streams
    return row == lax.broadcasted_iota(jnp.int32, (rows, streams * rank), 1) // rank


def adapt_body(tenant_ref, scaled_ref, squares_ref, down_ref, up_ref, sums_ref, up_rows_ref, *scratch):
    down_rows_ref, semaphores = scratch
    rank = down_ref.shape[1]
    streams = tenant_ref.shape[0]
    rows = scaled_ref.shape[0]
    first = lax.axis_index("row") * down_ref.shape[0]
    downs, ups = [], []
    for s in range(streams):
        at = pl.ds(s * rank, rank)
        tenant = tenant_ref[s] - first
        downs.append(
            pltpu.make_async_copy(down_ref.at[tenant], down_rows_ref.at[at, :], semaphores.at[s])
        )
        ups.append(
            pltpu.make_async_copy(
                up_ref.at[tenant], up_rows_ref.at[at, :], semaphores.at[streams + s]
            )
        )
    for copy in downs + ups:
        copy.start()
    for copy in downs:
        copy.wait()
    every = lax.dot_general(
        scaled_ref[...],
        down_rows_ref[...],
        (((1,), (1,)), ((), ())),
        preferred_element_type=F32,
    )
    own = jnp.where(own_columns(rows, streams, rank), every, 0.0)
    fold = lax.broadcasted_iota(jnp.int32, (streams * rank, rank), 0) % rank
    fold = (fold == lax.broadcasted_iota(jnp.int32, (streams * rank, rank), 1)).astype(BF16)
    high, rest = split(own)
    middle, low = rest, (own - high.astype(F32) - rest.astype(F32)).astype(BF16)
    folded = sum(jnp.dot(x, fold, preferred_element_type=F32) for x in (high, middle, low))
    sums_ref[:, :rank] = folded
    sums_ref[:, rank:] = squares_ref[...]
    for copy in ups:
        copy.wait()


def adapt(tenants, scaled, squares, down, up):
    streams = tenants.shape[0]
    rows, depth = scaled.shape
    rank, inner = up.shape[1:]
    whole = pl.BlockSpec(memory_space=pltpu.VMEM)
    anywhere = pl.BlockSpec(memory_space=pl.ANY)
    return pl.pallas_call(
        adapt_body,
        out_shape=(
            jax.ShapeDtypeStruct((rows, rank + 1), F32),
            pltpu.VMEM((streams * rank, inner), BF16),
        ),
        in_specs=[pl.BlockSpec(memory_space=pltpu.SMEM), whole, whole, anywhere, anywhere],
        out_specs=(whole, whole),
        scratch_shapes=[
            pltpu.VMEM((streams * rank, depth), BF16),
            pltpu.SemaphoreType.DMA((2 * streams,)),
        ],
        compiler_params=params(),
        cost_estimate=cost(2 * rows * depth * streams * rank, 2 * streams * rank * (depth + inner)),
        name="adapt",
    )(tenants, scaled, squares, in_hbm(jnp.swapaxes(down, 1, 2)), in_hbm(up))


def project_signal_body(owners, order, *refs):
    blocks, refs = refs[: len(order)], refs[len(order) :]
    weight_ref, mix_ref, step_ref, send_ref, keep_ref, lhs_ref, semaphores = refs
    rows = blocks[0].shape[0]
    parts = len(blocks) // owners
    copies = []
    for i, block in enumerate(blocks):
        owner, part = order[i]
        away = (owner() ^ lax.axis_index("row")) % owners
        at = pl.multiple_of((away * parts + part) * rows, rows)
        copies.append(
            pltpu.make_async_copy(block, lhs_ref.at[pl.ds(at, rows), :], semaphores.at[i])
        )
    for copy in copies:
        copy.start()
    for copy in copies:
        copy.wait()
    lhs = lhs_ref[...]

    def put(acc, start):
        step = send_ref.shape[1]
        for k in range(owners):
            target = send_ref if k % 2 else keep_ref
            target[k // 2, :, start : start + acc.shape[1]] = acc[k * step : (k + 1) * step].astype(
                target.dtype
            )

    columns = weight_ref.shape[1]
    tile = min(columns, 512)
    for t in range(0, columns, tile):
        put(jnp.dot(lhs, weight_ref[:, t : t + tile], preferred_element_type=F32), t)
    put(jnp.dot(lhs, mix_ref[...], preferred_element_type=F32), columns)
    acc = lax.dot_general(lhs, step_ref[...], (((1,), (1,)), ((), ())), preferred_element_type=F32)
    put(acc, columns + mix_ref.shape[1])


def project_signal(blocks, order, owners, weight, mix, step, after):
    pieces = len(blocks)
    depth = blocks[0].shape[1]
    rows = pieces * blocks[0].shape[0]
    columns = weight.shape[1] + mix.shape[1] + step.shape[0]
    half = jax.ShapeDtypeStruct((owners // 2, rows // owners, columns), BF16)
    whole = pl.BlockSpec(memory_space=pltpu.VMEM)
    anywhere = pl.BlockSpec(memory_space=pl.ANY)

    def body(*refs):
        project_signal_body(owners, order, *refs[:pieces], *refs[pieces + 1 :])

    return pl.pallas_call(
        body,
        out_shape=(half, half, jax.ShapeDtypeStruct((rows, depth), BF16)),
        in_specs=[anywhere] * (pieces + 1) + [whole] * 3,
        out_specs=(whole,) * 3,
        scratch_shapes=[pltpu.SemaphoreType.DMA((pieces,))],
        compiler_params=params(),
        cost_estimate=cost(2 * rows * depth * columns, 2 * depth * columns),
        name="project_signal",
    )(*blocks, after, in_vmem(weight), in_vmem(mix), step)


def project_gate_body(groups, *refs):
    lhs_refs, refs = refs[:groups], refs[groups:]
    weight_ref, after_ref, send_ref, keep_ref = refs
    rows = send_ref.shape[1]
    columns = weight_ref.shape[1]
    tile = min(columns, 512)
    first = group_of_own(groups)
    for t in range(0, columns, tile):
        for g, lhs_ref in enumerate(lhs_refs):
            acc = jnp.dot(lhs_ref[...], weight_ref[:, t : t + tile], preferred_element_type=F32)
            pairs = lhs_ref.shape[0] // (2 * rows)
            for k in range(2 * pairs):
                target = send_ref if k % 2 else keep_ref
                at = (first ^ g) * pairs + k // 2
                target[at, :, t : t + tile] = acc[k * rows : (k + 1) * rows].astype(target.dtype)


def group_of_own(groups):
    if groups == 1:
        return 0
    return (lax.axis_index("head") ^ 2 ^ lax.axis_index("row")) >> 1


def project_gate(rows, lhs, weight, after):
    count = sum(part.shape[0] for part in lhs) // rows
    columns = weight.shape[1]
    half = jax.ShapeDtypeStruct((count // 2, rows, columns), BF16)
    whole = pl.BlockSpec(memory_space=pltpu.VMEM)
    return pl.pallas_call(
        functools.partial(project_gate_body, len(lhs)),
        out_shape=(half, half),
        in_specs=[whole] * (len(lhs) + 1) + [pl.BlockSpec(memory_space=pl.ANY)],
        out_specs=(whole,) * 2,
        compiler_params=params(),
        cost_estimate=cost(2 * count * rows * lhs[0].shape[1] * columns, 2 * weight.size),
        name="project_gate",
    )(*lhs, in_vmem(weight), after)


def scatter_rows(received, keep, axis, done=1):
    send = received
    terms = [received] + (keep if isinstance(keep, list) else [keep])
    for distance in bits_of(lax.axis_size(axis))[done:]:
        send = sum(t[1::2].astype(F32) for t in terms).astype(BF16)
        terms = [swap(send, axis, distance)] + [t[0::2] for t in terms]
    return [t[0] for t in terms], send


def softplus(values):
    return jnp.maximum(values, 0.0) + jnp.log1p(jnp.exp(-jnp.abs(values)))


def silu(values):
    return values / (1.0 + jnp.exp(-values))


def inverse_of(sums_ref, width):
    return lax.rsqrt(sums_ref[:, sums_ref.shape[1] - 1 :] / width + EPSILON)


def recur_body(
    terms,
    group,
    model_width,
    live_ref,
    *refs,
):
    term_refs = refs[:terms]
    sums_ref, up_ref, bias_ref, rate_ref, skip_ref, source_ref, _ = refs[terms : terms + 7]
    result_ref, feeds_ref, b_ref, both_ref, state_ref, *scratch = refs[terms + 7 :]
    c_ref, read_ref, spread_ref, signal_ref, semaphores = scratch
    heads, head, width = state_ref.shape[1:]
    streams, inner = feeds_ref.shape[1:]
    step = pl.program_id(0)

    def fetch(i):
        at = pl.ds(i * group, group)
        return pltpu.make_async_copy(source_ref.at[at], state_ref.at[at], semaphores.at[i])

    @pl.when(step == 0)
    def _():
        for i in range(streams // group):
            fetch(i).start()
        rows = sums_ref.shape[0]
        rank = sums_ref.shape[1] - 1
        inverse = inverse_of(sums_ref, model_width)
        lowrank = (sums_ref[:, :rank] * inverse).astype(BF16)
        repeat = lax.broadcasted_iota(jnp.int32, (rank, streams * rank), 1) % rank
        repeat = (repeat == lax.broadcasted_iota(jnp.int32, (rank, streams * rank), 0)).astype(BF16)
        every = jnp.dot(lowrank, repeat, preferred_element_type=F32)
        own = jnp.where(own_columns(rows, streams, rank), every, 0.0).astype(BF16)
        adapted = jnp.dot(own, up_ref[...], preferred_element_type=F32)
        total = sum(t[...].astype(F32) for t in term_refs) * inverse
        signal_ref[...] = silu(total[:, :inner] + adapted)
        gates = silu(total[:, inner : inner + 2 * width])
        steps_dt = softplus(total[:, inner + 2 * width :] + bias_ref[...])
        b = [gates[p * streams : (p + 1) * streams, :width] for p in range(2)]
        c = [gates[p * streams : (p + 1) * streams, width:] for p in range(2)]
        for p in range(2):
            b_ref[p] = b[p]
            c_ref[p] = c[p]
        live = lax.broadcasted_iota(jnp.int32, (streams, heads), 0) < live_ref[0]
        dt = [steps_dt[p * streams : (p + 1) * streams] for p in range(2)]
        decay = [jnp.where(live, jnp.exp(-d * rate_ref[...]), 1.0) for d in dt]
        fed = [jnp.where(live, d, 0.0) for d in dt]

        def match(i, j):
            return jnp.sum(b[i] * c[j], -1, keepdims=True)

        both = decay[0] * decay[1]
        both_ref[...] = both
        late = decay[1] * fed[0]
        skip = skip_ref[...]
        factors = jnp.concatenate(
            [
                decay[0],
                both,
                fed[0] * match(0, 0) + skip,
                fed[1] * match(1, 1) + skip,
                late * match(0, 1),
                late,
                fed[1],
            ],
            0,
        )
        high, low = split(factors)
        place = lax.broadcasted_iota(jnp.int32, (heads, inner), 1) // head
        ones = (place == lax.broadcasted_iota(jnp.int32, (heads, inner), 0)).astype(BF16)
        spread_ref[...] = jnp.dot(high, ones, preferred_element_type=F32) + jnp.dot(
            low, ones, preferred_element_type=F32
        )

    fetch(step).wait()
    at = pl.multiple_of(step * group, group)
    c = jnp.concatenate([c_ref[p, pl.ds(at, group), :] for p in range(2)], 0)
    lhs = jnp.concatenate(split(c), 0)
    for g in range(group):
        state = state_ref[at + g].reshape(inner, width)
        found = lax.dot_general(lhs, state, (((1,), (1,)), ((), ())), preferred_element_type=F32)
        for p in range(2):
            row = p * group + g
            low = 2 * group + row
            read_ref[p, pl.ds(at + g, 1), :] = found[row : row + 1] + found[low : low + 1]

    @pl.when(step == pl.num_programs(0) - 1)
    def _():
        factor = [spread_ref[i * streams : (i + 1) * streams, :] for i in range(7)]
        first = signal_ref[:streams, :]
        second = signal_ref[streams:, :]
        result_ref[:streams, :] = factor[0] * read_ref[0] + factor[2] * first
        result_ref[streams:, :] = factor[1] * read_ref[1] + factor[4] * first + factor[3] * second
        feeds_ref[0] = factor[5] * first
        feeds_ref[1] = factor[6] * second


def recur(model_width, after, live_rows, terms, sums, up_rows, bias, rate, skip, state):
    streams, heads, head, width = state.shape
    group = 8
    inner = heads * head
    rows = 2 * streams
    whole = pl.BlockSpec(memory_space=pltpu.VMEM)
    return pl.pallas_call(
        functools.partial(recur_body, len(terms), group, model_width),
        out_shape=(
            jax.ShapeDtypeStruct((rows, inner), F32),
            jax.ShapeDtypeStruct((2, streams, inner), F32),
            jax.ShapeDtypeStruct((2, streams, width), F32),
            jax.ShapeDtypeStruct((streams, heads), F32),
            pltpu.VMEM(state.shape, state.dtype),
        ),
        grid=(streams // group,),
        in_specs=[pl.BlockSpec(memory_space=pltpu.SMEM)]
        + [whole] * (len(terms) + 5)
        + [pl.BlockSpec(memory_space=pl.ANY)] * 2,
        out_specs=(whole,) * 5,
        scratch_shapes=[
            pltpu.VMEM((2, streams, width), F32),
            pltpu.VMEM((2, streams, inner), F32),
            pltpu.VMEM((7 * streams, inner), F32),
            pltpu.VMEM((rows, inner), F32),
            pltpu.SemaphoreType.DMA((streams // group,)),
        ],
        compiler_params=params(),
        cost_estimate=cost(64 * state.size, 2 * state.size + 32 * rows * inner),
        name="recur",
    )(
        live_rows,
        *terms,
        sums,
        up_rows,
        bias[None],
        rate[None],
        skip[None],
        in_hbm(state),
        after,
    )


def state_write_body(feeds_ref, b_ref, decay_ref, state_ref, out_ref):
    group, heads, head, width = out_ref.shape
    at = pl.multiple_of(pl.program_id(0) * group, group)
    feeds = [split(feeds_ref[p, pl.ds(at, group), :]) for p in range(2)]
    rights = [split(b_ref[p, pl.ds(at, group), :]) for p in range(2)]
    left = [f.astype(F32) for pair in feeds for f in (pair[0], pair[1], pair[0])]
    right = [f.astype(F32) for pair in rights for f in (pair[0], pair[0], pair[1])]
    left = jnp.concatenate(left, 0).astype(BF16)
    right = jnp.concatenate(right, 0)
    stream = lax.broadcasted_iota(jnp.int32, right.shape, 0) % group
    for g in range(0, group, 2):
        pair = jnp.concatenate([jnp.where(stream == g + i, right, 0.0) for i in range(2)], 1)
        outer = lax.dot_general(
            left, pair.astype(BF16), (((0,), (0,)), ((), ())), preferred_element_type=F32
        )
        for i in range(2):
            scaled = state_ref[at + g + i].astype(F32) * decay_ref[g + i][:, None, :]
            own = outer[:, i * width : (i + 1) * width].reshape(heads, head, width)
            out_ref[g + i] = (scaled + own).astype(out_ref.dtype)


def state_write(feeds, b, decay, state):
    streams, heads, head, width = state.shape
    group = 8
    whole = pl.BlockSpec(memory_space=pltpu.VMEM)
    return pl.pallas_call(
        state_write_body,
        out_shape=jax.ShapeDtypeStruct(state.shape, state.dtype),
        grid=(streams // group,),
        in_specs=[
            whole,
            whole,
            pl.BlockSpec((group, heads, width), lambda i: (i, 0, 0)),
            whole,
        ],
        out_specs=pl.BlockSpec((group, heads, head, width), lambda i: (i, 0, 0, 0)),
        compiler_params=params(),
        cost_estimate=cost(32 * state.size, 4 * state.size),
        name="state_write",
    )(feeds, b, decay, state)


def output_tiles(distances, lhs_ref, weight_refs, out_ref):
    width = out_ref.shape[2] // 256 * 256
    tile = min(width, 512)
    for j, distance in enumerate(distances):
        for t in range(0, width, tile):
            at = pl.multiple_of((lax.axis_index("head") ^ distance) * width + t, tile)
            acc, start = 0.0, 0
            for weight_ref in weight_refs:
                stop = start + weight_ref.shape[0]
                acc += jnp.dot(
                    lhs_ref[:, start:stop],
                    weight_ref[:, pl.ds(at, tile)],
                    preferred_element_type=F32,
                )
                start = stop
            out_ref[j, :, t : t + tile] = acc.astype(out_ref.dtype)


LANES = 128


def put_lanes(values, out_ref, j):
    lane = lax.broadcasted_iota(jnp.int32, (values.shape[0], LANES), 1)
    tail = jnp.zeros(lane.shape, F32)
    for i in range(3):
        term = values.astype(BF16).astype(F32)
        tail = jnp.where(lane == i, term, tail)
        values = values - term
    out_ref[j, :, out_ref.shape[2] - LANES :] = tail.astype(out_ref.dtype)


def meet_body(met_ref, own_ref, squares_ref, out_ref, total_ref):
    count = met_ref.shape[0]
    width = own_ref.shape[2]
    total = squares_ref[...] + join_lanes(met_ref[0, :, width:])
    total_ref[...] = total
    for j in range(count):
        both = met_ref[j, :, :width].astype(F32) + own_ref[j].astype(F32)
        out_ref[j, :, :width] = both.astype(out_ref.dtype)
        put_lanes(total, out_ref, j)


def meet(met, own, squares):
    whole = pl.BlockSpec(memory_space=pltpu.VMEM)
    return pl.pallas_call(
        meet_body,
        out_shape=(
            jax.ShapeDtypeStruct(met.shape, met.dtype),
            jax.ShapeDtypeStruct(squares.shape, squares.dtype),
        ),
        in_specs=[whole] * 3,
        out_specs=(whole, whole),
        compiler_params=params(),
        cost_estimate=cost(met.size, 6 * met.size),
        name="meet",
    )(met, own, squares)


def join_lanes(values):
    return jnp.sum(values.astype(F32), -1, keepdims=True)


def output_first_body(distances, terms, model_width, *refs):
    term_refs = refs[:terms]
    sums_ref, result_ref, scale_ref, *weight_refs, out_ref, lhs_ref, squares_ref = refs[terms:]
    total = sum(t[...].astype(F32) for t in term_refs) * inverse_of(sums_ref, model_width)
    gated = result_ref[...] * silu(total)
    squares_ref[...] = jnp.sum(gated * gated, -1, keepdims=True)
    lhs_ref[...] = (gated * scale_ref[...]).astype(lhs_ref.dtype)
    output_tiles(distances, lhs_ref, weight_refs, out_ref)
    for j in range(len(distances)):
        put_lanes(squares_ref[...], out_ref, j)


def output_rest_body(distances, lhs_ref, after_ref, *refs):
    output_tiles(distances, lhs_ref, refs[:-1], refs[-1])


def output_parts(distances, weights, width, operands, model_width=None):
    first = model_width is not None
    rows, depth = operands[0].shape
    count = len(distances)
    whole = pl.BlockSpec(memory_space=pltpu.VMEM)
    specs = [whole] * (len(operands) + len(weights))
    body = functools.partial(output_rest_body, distances)
    extra = LANES if first else 0
    out_shape = [jax.ShapeDtypeStruct((count, rows, width + extra), BF16)]
    if first:
        body = functools.partial(output_first_body, distances, len(operands) - 3, model_width)
        out_shape += [
            jax.ShapeDtypeStruct((rows, depth), BF16),
            jax.ShapeDtypeStruct((rows, 1), F32),
        ]
    else:
        specs[1] = pl.BlockSpec(memory_space=pl.ANY)
    return pl.pallas_call(
        body,
        out_shape=tuple(out_shape),
        in_specs=specs,
        out_specs=(whole,) * len(out_shape),
        compiler_params=params(),
        cost_estimate=cost(2 * rows * depth * width * count, 2 * depth * width * count),
        name="output_first" if first else "output_rest",
    )(*operands, *[in_vmem(w) for w in weights])


def split(values):
    high = values.astype(BF16)
    return high, (values - high.astype(F32)).astype(BF16)


def on_device(
    hidden,
    input_norm_scale,
    projection_signal,
    projection_gate,
    projection_step,
    projection_input_output,
    step_bias,
    head_decay_rate,
    head_skip_weight,
    gated_norm_scale,
    adapter_down_weight,
    adapter_up_weight,
    output_weight,
    scan_state,
    stream_tenant_index,
    live_block_rows,
):
    streams, positions, feature_width = hidden.shape
    rows = streams * positions
    heads_n = lax.axis_size("head")
    rows_n = lax.axis_size("row")
    model_width = feature_width * heads_n
    depth, inner = projection_signal.shape
    inner_width = inner * heads_n

    wide = jnp.swapaxes(hidden, 0, 1).astype(F32)
    scaled = (wide * input_norm_scale).astype(BF16)
    scaled_flat = scaled.reshape(rows, feature_width)

    squares = jnp.sum(wide * wide, -1).reshape(rows, 1)
    sums, up_rows = adapt(stream_tenant_index, scaled_flat, squares, adapter_down_weight, adapter_up_weight)

    own = group_of_own(2) == 0
    sums, own = lax.optimization_barrier((sums, own))
    weights = load(sums, [], projection_signal, projection_input_output, projection_gate)
    signal_weights = (*weights[:2], projection_step.T)
    middle = output_weight.shape[0] // 2
    if heads_n == rows_n and len(bits_of(rows_n)) == 2:
        turn = [
            (h * rows_n + r, (r ^ 2) * rows_n + h) for h in range(heads_n) for r in range(rows_n)
        ]
        turned = lax.ppermute(scaled_flat, ("head", "row"), turn)
        turned, _ = lax.optimization_barrier((turned, weights[0]))
        crossed = swap(turned, "head", 2)

        def order(distance):
            return [
                (lambda d=d: lax.axis_index("head") ^ 2 ^ d, 0) for d in (distance, distance ^ 1)
            ]

        near = [turned, swap(turned, "head", 1)]
        (out_early,) = load(turned, [], (output_weight, 0, middle))
        crossed, _ = lax.optimization_barrier((crossed, out_early))
        far = [crossed, swap(crossed, "head", 1)]
        near_send, near_keep, near_lhs = project_signal(near, order(0), 2, *signal_weights, crossed)
        near_other = swap(near_send, "row", 1)
        far_send, far_keep, far_lhs = project_signal(far, order(2), 2, *signal_weights, near_send)
        far_other = swap(far_send, "row", 1)
        sums, _ = lax.optimization_barrier((sums, far_send))
        sums = sum_over(sums, "head")
        gate_send, gate_keep = project_gate(rows, [near_lhs, far_lhs], weights[2], far_send)
        gate_own, gate_far = [swap(part, "row", 1) for part in jnp.split(gate_send, 2, 0)]
        pick = [(near_keep, far_keep), (near_other, far_other)]
        last_send = sum(jnp.where(own, f, n).astype(F32) for n, f in pick).astype(BF16)
        last_send, sums = lax.optimization_barrier((last_send, sums))
        last_other = [swap(part, "row", 2) for part in jnp.split(last_send, 2, 1)]
        (out_late,) = load(last_send, [], (output_weight, middle, middle))
        signal_terms = [jnp.where(own, n, f)[0] for n, f in pick]
        signal_terms = [jnp.concatenate(last_other, 1)[0]] + signal_terms
        gate_far, _ = lax.optimization_barrier((gate_far, last_other[0]))
        gate_last = (gate_far.astype(F32) + gate_keep[1:].astype(F32)).astype(BF16)
        gate_terms = [swap_halves(gate_last, "row", 2, 1)[0], gate_own[0], gate_keep[0]]
        gate_last, out_late = lax.optimization_barrier((gate_last, out_late))
    else:
        features = lax.all_gather(scaled_flat, "head", axis=1, tiled=True)
        blocks = lax.all_to_all(features, "row", split_axis=1, concat_axis=0, tiled=True)
        blocks = blocks.reshape(rows_n, rows, depth)
        blocks = [blocks[i] for i in range(rows_n)]
        order = [(lambda i=i: i, 0) for i in range(rows_n)]
        send, keep, lhs = project_signal(blocks, order, rows_n, *signal_weights, sums)
        received = swap(send, "row", 1)
        gate_send, gate_keep = project_gate(rows, [lhs], weights[2], send)
        sums = sum_over(sums, "head")
        keep, out_early, out_late = load(
            gate_send, [keep], (output_weight, 0, middle), (output_weight, middle, middle)
        )
        signal_terms, _ = scatter_rows(received, keep, "row")
        gate_terms, gate_last = scatter_rows(swap(gate_send, "row", 1), gate_keep, "row")
    out_weights = [out_early, out_late]

    result, feeds, bgate, both, state = recur(
        model_width,
        gate_last,
        live_block_rows,
        signal_terms,
        sums,
        up_rows,
        step_bias,
        head_decay_rate,
        head_skip_weight,
        scan_state,
    )

    distances = list(range(heads_n))
    first, out_lhs, gate_squares = output_parts(
        distances[3::4],
        out_weights,
        feature_width,
        [*gate_terms, sums, result, gated_norm_scale[None]],
        model_width,
    )
    (second,) = output_parts(
        distances[2::4] + distances[1::4], out_weights, feature_width, [out_lhs, first]
    )
    half = second.shape[0] // 2
    send, gate_squares = meet(swap(first, "head", 1), second, gate_squares)
    (rest,) = output_parts(distances[0::4], out_weights, feature_width, [out_lhs, send])
    feeds, _ = lax.optimization_barrier((feeds, rest))
    kept = [swap(second[half:], "head", 1), rest]
    if len(bits_of(heads_n)) == 2:
        received = swap_halves(send, "head", 2, 1)
        mixer = sum(t[0].astype(F32) for t in [received[..., :feature_width]] + kept)
        gate_squares = gate_squares + join_lanes(received[0, :, feature_width:])
    else:
        received = swap(send[..., :feature_width], "head", 2)
        mixer, _ = scatter_rows(received, kept, "head", done=2)
        mixer = sum(t.astype(F32) for t in mixer)
        for distance in bits_of(heads_n)[1:]:
            gate_squares = gate_squares + swap(gate_squares, "head", distance)
    mixer = mixer * lax.rsqrt(gate_squares / inner_width + EPSILON)
    mixer = mixer.reshape(positions, streams, feature_width)
    live = jnp.arange(streams) < live_block_rows[0]
    mixed = (wide + jnp.where(live[:, None], mixer, 0.0)).astype(BF16)

    spread = jnp.broadcast_to(both[..., None], both.shape + (bgate.shape[-1],))
    new_state = state_write(feeds, bgate, spread, state)
    return (jnp.swapaxes(mixed, 0, 1), new_state)


def solution(mesh):
    in_specs = (
        P(("rep", "row"), None, "head"),
        P("head"),
        P("row", "head"),
        P("row", "head"),
        P("row", "head"),
        P("row", None),
        P("head"),
        P("head"),
        P("head"),
        P("head"),
        P("row", "head", None),
        P("row", None, "head"),
        P("head", None),
        P(("rep", "row"), "head", None, None),
        P(("rep", "row")),
        P(("rep", "row")),
    )
    out_specs = (P(("rep", "row"), None, "head"), P(("rep", "row"), "head", None, None))
    return jax.shard_map(
        on_device, mesh=mesh, in_specs=in_specs, out_specs=out_specs, check_vma=False
    )
```

```python
import functools

import jax
import jax.numpy as jnp
from jax import lax
from jax.experimental import pallas as pl
from jax.experimental.pallas import tpu as pltpu
from jax.sharding import PartitionSpec as P

BF16 = jnp.bfloat16
EPSILON = 1e-05
LANES = 128
F32 = jnp.float32
VMEM_GRANT = 12 * 1024 * 1024


def swap(values, axis, distance):
    size = lax.axis_size(axis)
    return lax.ppermute(values, axis, [(i, i ^ distance) for i in range(size)])


def swap_halves(values, axis, distance, dim):
    return jnp.concatenate([swap(v, axis, distance) for v in jnp.split(values, 2, dim)], dim)


def bits_of(size):
    return [1 << i for i in range(size.bit_length() - 1)]


def sum_over(values, axis):
    for distance in bits_of(lax.axis_size(axis)):
        values = values + swap(values, axis, distance)
    return values


def reverse_bits(value, size):
    bits = size.bit_length() - 1
    return sum(((value >> i) & 1) << (bits - 1 - i) for i in range(bits))


def params(**more):
    return pltpu.CompilerParams(vmem_limit_bytes=VMEM_GRANT, **more)


def cost(flops, size):
    return pl.CostEstimate(flops=int(flops), bytes_accessed=int(size), transcendentals=0)


def in_hbm(values):
    return pltpu.with_memory_space_constraint(values, pltpu.HBM)


def in_vmem(values):
    return pltpu.with_memory_space_constraint(values, pltpu.VMEM)


def load_body(spans, after_ref, *refs):
    count = len(spans)
    sources, targets, semaphores = refs[:count], refs[count : 2 * count], refs[2 * count]
    copies = []
    for source, target, (start, rows, parts) in zip(sources, targets, spans):
        step = rows // parts
        for i in range(parts):
            copies.append(
                pltpu.make_async_copy(
                    source.at[pl.ds(start + i * step, step)],
                    target.at[pl.ds(i * step, step)],
                    semaphores.at[len(copies)],
                )
            )
    for copy in copies:
        copy.start()
    for copy in copies:
        copy.wait()


def load(after, passed, *weights):
    weights = [w if isinstance(w, tuple) else (w, 0, w.shape[0]) for w in weights]
    shapes = [p.shape for p in passed] + [(rows, *w.shape[1:]) for w, _, rows in weights]
    spans = [(0, p.shape[0], 1) for p in passed]
    spans += [(start, rows, 8 if rows % 128 == 0 else 1) for _, start, rows in weights]
    size = sum(rows * w.shape[1] * w.dtype.itemsize for w, _, rows in weights)
    return pl.pallas_call(
        functools.partial(load_body, spans),
        out_shape=tuple(pltpu.VMEM(shape, BF16) for shape in shapes),
        in_specs=[pl.BlockSpec(memory_space=pl.ANY)] * (1 + len(shapes)),
        out_specs=tuple(pl.BlockSpec(memory_space=pltpu.VMEM) for _ in shapes),
        scratch_shapes=[pltpu.SemaphoreType.DMA((sum(parts for _, _, parts in spans),))],
        compiler_params=params(),
        cost_estimate=cost(0, 2 * size),
        name="load",
    )(after, *passed, *[in_hbm(w) for w, _, _ in weights])


def own_columns(rows, streams, rank):
    row = lax.broadcasted_iota(jnp.int32, (rows, streams * rank), 0) % streams
    return row == lax.broadcasted_iota(jnp.int32, (rows, streams * rank), 1) // rank


def adapt_body(tenant_ref, scaled_ref, squares_ref, down_ref, up_ref, sums_ref, up_rows_ref, *scratch):
    down_rows_ref, semaphores = scratch
    rank = down_ref.shape[1]
    streams = tenant_ref.shape[0]
    rows = scaled_ref.shape[0]
    first = lax.axis_index("row") * down_ref.shape[0]
    downs, ups = [], []
    for s in range(streams):
        at = pl.ds(s * rank, rank)
        tenant = tenant_ref[s] - first
        downs.append(
            pltpu.make_async_copy(down_ref.at[tenant], down_rows_ref.at[at, :], semaphores.at[s])
        )
        ups.append(
            pltpu.make_async_copy(
                up_ref.at[tenant], up_rows_ref.at[at, :], semaphores.at[streams + s]
            )
        )
    for copy in downs + ups:
        copy.start()
    for copy in downs:
        copy.wait()
    every = lax.dot_general(
        scaled_ref[...],
        down_rows_ref[...],
        (((1,), (1,)), ((), ())),
        preferred_element_type=F32,
    )
    own = jnp.where(own_columns(rows, streams, rank), every, 0.0)
    fold = lax.broadcasted_iota(jnp.int32, (streams * rank, rank), 0) % rank
    fold = (fold == lax.broadcasted_iota(jnp.int32, (streams * rank, rank), 1)).astype(BF16)
    high, rest = split(own)
    middle, low = rest, (own - high.astype(F32) - rest.astype(F32)).astype(BF16)
    folded = sum(jnp.dot(x, fold, preferred_element_type=F32) for x in (high, middle, low))
    sums_ref[:, :rank] = folded
    sums_ref[:, rank:] = squares_ref[...]
    for copy in ups:
        copy.wait()


def adapt(tenants, scaled, squares, down, up):
    streams = tenants.shape[0]
    rows, depth = scaled.shape
    rank, inner = up.shape[1:]
    whole = pl.BlockSpec(memory_space=pltpu.VMEM)
    anywhere = pl.BlockSpec(memory_space=pl.ANY)
    return pl.pallas_call(
        adapt_body,
        out_shape=(
            jax.ShapeDtypeStruct((rows, rank + 1), F32),
            pltpu.VMEM((streams * rank, inner), BF16),
        ),
        in_specs=[pl.BlockSpec(memory_space=pltpu.SMEM), whole, whole, anywhere, anywhere],
        out_specs=(whole, whole),
        scratch_shapes=[
            pltpu.VMEM((streams * rank, depth), BF16),
            pltpu.SemaphoreType.DMA((2 * streams,)),
        ],
        compiler_params=params(),
        cost_estimate=cost(2 * rows * depth * streams * rank, 2 * streams * rank * (depth + inner)),
        name="adapt",
    )(tenants, scaled, squares, in_hbm(jnp.swapaxes(down, 1, 2)), in_hbm(up))


def lead_of(mix, steps):
    return -(-(mix + steps) // LANES) * LANES


def project_signal_body(owners, order, *refs):
    blocks, refs = refs[: len(order)], refs[len(order) :]
    weight_ref, mix_ref, step_ref, send_ref, keep_ref, lhs_ref, semaphores = refs
    rows = blocks[0].shape[0]
    parts = len(blocks) // owners
    copies = []
    for i, block in enumerate(blocks):
        owner, part = order[i]
        away = (owner() ^ lax.axis_index("row")) % owners
        at = pl.multiple_of((away * parts + part) * rows, rows)
        copies.append(
            pltpu.make_async_copy(block, lhs_ref.at[pl.ds(at, rows), :], semaphores.at[i])
        )
    for copy in copies:
        copy.start()
    for copy in copies:
        copy.wait()
    lhs = lhs_ref[...]

    def put(acc, start):
        step = send_ref.shape[1]
        for k in range(owners):
            target = send_ref if k % 2 else keep_ref
            target[k // 2, :, start : start + acc.shape[1]] = acc[k * step : (k + 1) * step].astype(
                target.dtype
            )

    mix = mix_ref.shape[1]
    put(jnp.dot(lhs, mix_ref[...], preferred_element_type=F32), 0)
    acc = lax.dot_general(lhs, step_ref[...], (((1,), (1,)), ((), ())), preferred_element_type=F32)
    put(acc, mix)
    columns = weight_ref.shape[1]
    lead = send_ref.shape[2] - columns
    put(jnp.zeros((lhs.shape[0], lead - mix - acc.shape[1]), F32), mix + acc.shape[1])
    tile = min(columns, 512)
    for t in range(0, columns, tile):
        put(jnp.dot(lhs, weight_ref[:, t : t + tile], preferred_element_type=F32), lead + t)


def project_signal(blocks, order, owners, weight, mix, step, after):
    pieces = len(blocks)
    depth = blocks[0].shape[1]
    rows = pieces * blocks[0].shape[0]
    columns = weight.shape[1] + lead_of(mix.shape[1], step.shape[0])
    half = jax.ShapeDtypeStruct((owners // 2, rows // owners, columns), BF16)
    whole = pl.BlockSpec(memory_space=pltpu.VMEM)
    anywhere = pl.BlockSpec(memory_space=pl.ANY)

    def body(*refs):
        project_signal_body(owners, order, *refs[:pieces], *refs[pieces + 1 :])

    return pl.pallas_call(
        body,
        out_shape=(half, half, jax.ShapeDtypeStruct((rows, depth), BF16)),
        in_specs=[anywhere] * (pieces + 1) + [whole] * 3,
        out_specs=(whole,) * 3,
        scratch_shapes=[pltpu.SemaphoreType.DMA((pieces,))],
        compiler_params=params(),
        cost_estimate=cost(2 * rows * depth * columns, 2 * depth * columns),
        name="project_signal",
    )(*blocks, after, in_vmem(weight), in_vmem(mix), step)


def project_gate_body(groups, *refs):
    lhs_refs, refs = refs[:groups], refs[groups:]
    weight_ref, after_ref, send_ref, keep_ref = refs
    rows = send_ref.shape[1]
    columns = weight_ref.shape[1]
    tile = min(columns, 512)
    first = group_of_own(groups)
    for t in range(0, columns, tile):
        for g, lhs_ref in enumerate(lhs_refs):
            acc = jnp.dot(lhs_ref[...], weight_ref[:, t : t + tile], preferred_element_type=F32)
            pairs = lhs_ref.shape[0] // (2 * rows)
            for k in range(2 * pairs):
                target = send_ref if k % 2 else keep_ref
                at = (first ^ g) * pairs + k // 2
                target[at, :, t : t + tile] = acc[k * rows : (k + 1) * rows].astype(target.dtype)


def group_of_own(groups):
    if groups == 1:
        return 0
    return (lax.axis_index("head") ^ 2 ^ lax.axis_index("row")) >> 1


def project_gate(rows, lhs, weight, after):
    count = sum(part.shape[0] for part in lhs) // rows
    columns = weight.shape[1]
    half = jax.ShapeDtypeStruct((count // 2, rows, columns), BF16)
    whole = pl.BlockSpec(memory_space=pltpu.VMEM)
    return pl.pallas_call(
        functools.partial(project_gate_body, len(lhs)),
        out_shape=(half, half),
        in_specs=[whole] * (len(lhs) + 1) + [pl.BlockSpec(memory_space=pl.ANY)],
        out_specs=(whole,) * 2,
        compiler_params=params(),
        cost_estimate=cost(2 * count * rows * lhs[0].shape[1] * columns, 2 * weight.size),
        name="project_gate",
    )(*lhs, in_vmem(weight), after)


def scatter_rows(received, keep, axis, done=1):
    send = received
    terms = [received] + (keep if isinstance(keep, list) else [keep])
    for distance in bits_of(lax.axis_size(axis))[done:]:
        send = sum(t[1::2].astype(F32) for t in terms).astype(BF16)
        terms = [swap(send, axis, distance)] + [t[0::2] for t in terms]
    return [t[0] for t in terms], send


def softplus(values):
    return jnp.maximum(values, 0.0) + jnp.log1p(jnp.exp(-jnp.abs(values)))


def silu(values):
    return values / (1.0 + jnp.exp(-values))


def inverse_of(sums_ref, width):
    return lax.rsqrt(sums_ref[:, sums_ref.shape[1] - 1 :] / width + EPSILON)


def read_body(terms, group, model_width, live_ref, *refs):
    term_refs = refs[:terms]
    sums_ref, up_ref, bias_ref, rate_ref, skip_ref, source_ref, _ = refs[terms : terms + 7]
    adapted_ref, read_ref, spread_ref, b_ref, both_ref, state_ref, *scratch = refs[terms + 7 :]
    c_ref, semaphores = scratch
    heads, head, width = state_ref.shape[1:]
    streams, inner = read_ref.shape[1:]
    step = pl.program_id(0)

    def fetch(i):
        at = pl.ds(i * group, group)
        return pltpu.make_async_copy(source_ref.at[at], state_ref.at[at], semaphores.at[i])

    @pl.when(step == 0)
    def _():
        for i in range(streams // group):
            fetch(i).start()
        rows = sums_ref.shape[0]
        rank = sums_ref.shape[1] - 1
        inverse = inverse_of(sums_ref, model_width)
        total = sum(t[:, : 2 * width + heads].astype(F32) for t in term_refs) * inverse
        gates = silu(total[:, : 2 * width])
        steps_dt = softplus(total[:, 2 * width :] + bias_ref[...])
        b = [gates[p * streams : (p + 1) * streams, :width] for p in range(2)]
        c = [gates[p * streams : (p + 1) * streams, width:] for p in range(2)]
        for p in range(2):
            b_ref[p] = b[p]
            c_ref[p] = c[p]
        live = lax.broadcasted_iota(jnp.int32, (streams, heads), 0) < live_ref[0]
        dt = [steps_dt[p * streams : (p + 1) * streams] for p in range(2)]
        decay = [jnp.where(live, jnp.exp(-d * rate_ref[...]), 1.0) for d in dt]
        fed = [jnp.where(live, d, 0.0) for d in dt]

        def match(i, j):
            return jnp.sum(b[i] * c[j], -1, keepdims=True)

        both = decay[0] * decay[1]
        both_ref[...] = both
        late = decay[1] * fed[0]
        skip = skip_ref[...]
        factors = jnp.concatenate(
            [
                decay[0],
                both,
                fed[0] * match(0, 0) + skip,
                fed[1] * match(1, 1) + skip,
                late * match(0, 1),
                late,
                fed[1],
            ],
            0,
        )
        high, low = split(factors)
        place = lax.broadcasted_iota(jnp.int32, (heads, inner), 1) // head
        ones = (place == lax.broadcasted_iota(jnp.int32, (heads, inner), 0)).astype(BF16)
        spread_ref[...] = jnp.dot(high, ones, preferred_element_type=F32) + jnp.dot(
            low, ones, preferred_element_type=F32
        )
        lowrank = (sums_ref[:, :rank] * inverse).astype(BF16)
        repeat = lax.broadcasted_iota(jnp.int32, (rank, streams * rank), 1) % rank
        repeat = (repeat == lax.broadcasted_iota(jnp.int32, (rank, streams * rank), 0)).astype(BF16)
        every = jnp.dot(lowrank, repeat, preferred_element_type=F32)
        own = jnp.where(own_columns(rows, streams, rank), every, 0.0).astype(BF16)
        adapted_ref[...] = jnp.dot(own, up_ref[...], preferred_element_type=F32)

    fetch(step).wait()
    at = pl.multiple_of(step * group, group)
    c = jnp.concatenate([c_ref[p, pl.ds(at, group), :] for p in range(2)], 0)
    lhs = jnp.concatenate(split(c), 0)
    for g in range(group):
        state = state_ref[at + g].reshape(inner, width)
        found = lax.dot_general(lhs, state, (((1,), (1,)), ((), ())), preferred_element_type=F32)
        for p in range(2):
            row = p * group + g
            low = 2 * group + row
            read_ref[p, pl.ds(at + g, 1), :] = found[row : row + 1] + found[low : low + 1]


def read_state(model_width, after, live_rows, terms, sums, up_rows, bias, rate, skip, state):
    streams, heads, head, width = state.shape
    group = 8
    inner = heads * head
    rows = 2 * streams
    whole = pl.BlockSpec(memory_space=pltpu.VMEM)
    return pl.pallas_call(
        functools.partial(read_body, len(terms), group, model_width),
        out_shape=(
            jax.ShapeDtypeStruct((rows, inner), F32),
            jax.ShapeDtypeStruct((2, streams, inner), F32),
            jax.ShapeDtypeStruct((7 * streams, inner), F32),
            jax.ShapeDtypeStruct((2, streams, width), F32),
            jax.ShapeDtypeStruct((streams, heads), F32),
            pltpu.VMEM(state.shape, state.dtype),
        ),
        grid=(streams // group,),
        in_specs=[pl.BlockSpec(memory_space=pltpu.SMEM)]
        + [whole] * (len(terms) + 5)
        + [pl.BlockSpec(memory_space=pl.ANY)] * 2,
        out_specs=(whole,) * 6,
        scratch_shapes=[
            pltpu.VMEM((2, streams, width), F32),
            pltpu.SemaphoreType.DMA((streams // group,)),
        ],
        compiler_params=params(),
        cost_estimate=cost(64 * state.size, 2 * state.size + 32 * rows * inner),
        name="read_state",
    )(
        live_rows,
        *terms,
        sums,
        up_rows,
        bias[None],
        rate[None],
        skip[None],
        in_hbm(state),
        after,
    )


def state_write_body(feeds_ref, b_ref, decay_ref, state_ref, out_ref):
    group, heads, head, width = out_ref.shape
    at = pl.multiple_of(pl.program_id(0) * group, group)
    feeds = [split(feeds_ref[p, pl.ds(at, group), :]) for p in range(2)]
    rights = [split(b_ref[p, pl.ds(at, group), :]) for p in range(2)]
    left = [f.astype(F32) for pair in feeds for f in (pair[0], pair[1], pair[0])]
    right = [f.astype(F32) for pair in rights for f in (pair[0], pair[0], pair[1])]
    left = jnp.concatenate(left, 0).astype(BF16)
    right = jnp.concatenate(right, 0)
    stream = lax.broadcasted_iota(jnp.int32, right.shape, 0) % group
    for g in range(0, group, 2):
        pair = jnp.concatenate([jnp.where(stream == g + i, right, 0.0) for i in range(2)], 1)
        outer = lax.dot_general(
            left, pair.astype(BF16), (((0,), (0,)), ((), ())), preferred_element_type=F32
        )
        for i in range(2):
            scaled = state_ref[at + g + i].astype(F32) * decay_ref[g + i][:, None, :]
            own = outer[:, i * width : (i + 1) * width].reshape(heads, head, width)
            out_ref[g + i] = (scaled + own).astype(out_ref.dtype)


def state_write(feeds, b, decay, state):
    streams, heads, head, width = state.shape
    group = 8
    whole = pl.BlockSpec(memory_space=pltpu.VMEM)
    return pl.pallas_call(
        state_write_body,
        out_shape=jax.ShapeDtypeStruct(state.shape, state.dtype),
        grid=(streams // group,),
        in_specs=[
            whole,
            whole,
            pl.BlockSpec((group, heads, width), lambda i: (i, 0, 0)),
            whole,
        ],
        out_specs=pl.BlockSpec((group, heads, head, width), lambda i: (i, 0, 0, 0)),
        compiler_params=params(),
        cost_estimate=cost(32 * state.size, 4 * state.size),
        name="state_write",
    )(feeds, b, decay, state)


def output_tiles(distances, lhs_ref, weight_refs, out_ref):
    width = out_ref.shape[2] // 256 * 256
    tile = min(width, 512)
    for j, distance in enumerate(distances):
        for t in range(0, width, tile):
            at = pl.multiple_of((lax.axis_index("head") ^ distance) * width + t, tile)
            acc, start = 0.0, 0
            for weight_ref in weight_refs:
                stop = start + weight_ref.shape[0]
                acc += jnp.dot(
                    lhs_ref[:, start:stop],
                    weight_ref[:, pl.ds(at, tile)],
                    preferred_element_type=F32,
                )
                start = stop
            out_ref[j, :, t : t + tile] = acc.astype(out_ref.dtype)


def put_lanes(values, out_ref, j):
    lane = lax.broadcasted_iota(jnp.int32, (values.shape[0], LANES), 1)
    tail = jnp.zeros(lane.shape, F32)
    for i in range(3):
        term = values.astype(BF16).astype(F32)
        tail = jnp.where(lane == i, term, tail)
        values = values - term
    out_ref[j, :, out_ref.shape[2] - LANES :] = tail.astype(out_ref.dtype)


def meet_body(met_ref, own_ref, squares_ref, out_ref, total_ref):
    count = met_ref.shape[0]
    width = own_ref.shape[2]
    total = squares_ref[...] + join_lanes(met_ref[0, :, width:])
    total_ref[...] = total
    for j in range(count):
        both = met_ref[j, :, :width].astype(F32) + own_ref[j].astype(F32)
        out_ref[j, :, :width] = both.astype(out_ref.dtype)
        put_lanes(total, out_ref, j)


def meet(met, own, squares):
    whole = pl.BlockSpec(memory_space=pltpu.VMEM)
    return pl.pallas_call(
        meet_body,
        out_shape=(
            jax.ShapeDtypeStruct(met.shape, met.dtype),
            jax.ShapeDtypeStruct(squares.shape, squares.dtype),
        ),
        in_specs=[whole] * 3,
        out_specs=(whole, whole),
        compiler_params=params(),
        cost_estimate=cost(met.size, 6 * met.size),
        name="meet",
    )(met, own, squares)


def join_lanes(values):
    return jnp.sum(values.astype(F32), -1, keepdims=True)


def output_first_body(distances, shapes, model_width, *refs):
    refs = list(refs)
    gate_refs = [refs.pop(0) for _ in range(shapes[0])]
    signal_refs = [[refs.pop(0) for _ in range(count)] for count in shapes[1:]]
    sums_ref, adapted_ref, read_ref, spread_ref, scale_ref, *weight_refs = refs[:-4]
    out_ref, lhs_ref, squares_ref, feeds_ref = refs[-4:]
    streams, inner = read_ref.shape[1:]
    inverse = inverse_of(sums_ref, model_width)
    total = 0.0
    for pieces in signal_refs:
        pieces = [piece[...] for piece in pieces]
        width = sum(piece.shape[1] for piece in pieces)
        pieces[0] = pieces[0][:, width - inner :]
        total += jnp.concatenate([piece.astype(F32) for piece in pieces], 1)
    signal = silu(total * inverse + adapted_ref[...])
    first, second = signal[:streams], signal[streams:]
    factor = [spread_ref[i * streams : (i + 1) * streams, :] for i in range(7)]
    feeds_ref[0] = factor[5] * first
    feeds_ref[1] = factor[6] * second
    result = [
        factor[0] * read_ref[0] + factor[2] * first,
        factor[1] * read_ref[1] + factor[4] * first + factor[3] * second,
    ]
    total = sum(t[...].astype(F32) for t in gate_refs) * inverse
    gated = jnp.concatenate(result, 0) * silu(total)
    squares_ref[...] = jnp.sum(gated * gated, -1, keepdims=True)
    lhs_ref[...] = (gated * scale_ref[...]).astype(lhs_ref.dtype)
    output_tiles(distances, lhs_ref, weight_refs, out_ref)
    for j in range(len(distances)):
        put_lanes(squares_ref[...], out_ref, j)


def put_lanes(values, out_ref, j):
    lane = lax.broadcasted_iota(jnp.int32, (values.shape[0], LANES), 1)
    tail = jnp.zeros(lane.shape, F32)
    for i in range(3):
        term = values.astype(BF16).astype(F32)
        tail = jnp.where(lane == i, term, tail)
        values = values - term
    out_ref[j, :, out_ref.shape[2] - LANES :] = tail.astype(out_ref.dtype)


def meet_body(met_ref, own_ref, squares_ref, out_ref, total_ref):
    count = met_ref.shape[0]
    width = own_ref.shape[2]
    total = squares_ref[...] + join_lanes(met_ref[0, :, width:])
    total_ref[...] = total
    for j in range(count):
        both = met_ref[j, :, :width].astype(F32) + own_ref[j].astype(F32)
        out_ref[j, :, :width] = both.astype(out_ref.dtype)
        put_lanes(total, out_ref, j)


def meet(met, own, squares):
    whole = pl.BlockSpec(memory_space=pltpu.VMEM)
    return pl.pallas_call(
        meet_body,
        out_shape=(
            jax.ShapeDtypeStruct(met.shape, met.dtype),
            jax.ShapeDtypeStruct(squares.shape, squares.dtype),
        ),
        in_specs=[whole] * 3,
        out_specs=(whole, whole),
        compiler_params=params(),
        cost_estimate=cost(met.size, 6 * met.size),
        name="meet",
    )(met, own, squares)


def join_lanes(values):
    return jnp.sum(values.astype(F32), -1, keepdims=True)


def output_rest_body(distances, lhs_ref, after_ref, *refs):
    output_tiles(distances, lhs_ref, refs[:-1], refs[-1])


def output_parts(distances, weights, width, operands, model_width=None, shapes=None):
    first = model_width is not None
    rows, depth = operands[0].shape
    count = len(distances)
    whole = pl.BlockSpec(memory_space=pltpu.VMEM)
    specs = [whole] * (len(operands) + len(weights))
    body = functools.partial(output_rest_body, distances)
    extra = LANES if first else 0
    out_shape = [jax.ShapeDtypeStruct((count, rows, width + extra), BF16)]
    if first:
        body = functools.partial(output_first_body, distances, shapes, model_width)
        out_shape += [
            jax.ShapeDtypeStruct((rows, depth), BF16),
            jax.ShapeDtypeStruct((rows, 1), F32),
            jax.ShapeDtypeStruct((2, rows // 2, depth), F32),
        ]
    else:
        specs[1] = pl.BlockSpec(memory_space=pl.ANY)
    return pl.pallas_call(
        body,
        out_shape=tuple(out_shape),
        in_specs=specs,
        out_specs=(whole,) * len(out_shape),
        compiler_params=params(),
        cost_estimate=cost(2 * rows * depth * width * count, 2 * depth * width * count),
        name="output_first" if first else "output_rest",
    )(*operands, *[in_vmem(w) for w in weights])


def split(values):
    high = values.astype(BF16)
    return high, (values - high.astype(F32)).astype(BF16)


def on_device(
    hidden,
    input_norm_scale,
    projection_signal,
    projection_gate,
    projection_step,
    projection_input_output,
    step_bias,
    head_decay_rate,
    head_skip_weight,
    gated_norm_scale,
    adapter_down_weight,
    adapter_up_weight,
    output_weight,
    scan_state,
    stream_tenant_index,
    live_block_rows,
):
    streams, positions, feature_width = hidden.shape
    rows = streams * positions
    heads_n = lax.axis_size("head")
    rows_n = lax.axis_size("row")
    model_width = feature_width * heads_n
    depth, inner = projection_signal.shape
    inner_width = inner * heads_n

    wide = jnp.swapaxes(hidden, 0, 1).astype(F32)
    scaled = (wide * input_norm_scale).astype(BF16)
    scaled_flat = scaled.reshape(rows, feature_width)

    squares = jnp.sum(wide * wide, -1).reshape(rows, 1)
    sums, up_rows = adapt(stream_tenant_index, scaled_flat, squares, adapter_down_weight, adapter_up_weight)

    own = group_of_own(2) == 0
    sums, own = lax.optimization_barrier((sums, own))
    weights = load(sums, [], projection_signal, projection_input_output, projection_gate)
    signal_weights = (*weights[:2], projection_step.T)
    middle = output_weight.shape[0] // 2
    if heads_n == rows_n and len(bits_of(rows_n)) == 2:
        turn = [
            (h * rows_n + r, (r ^ 2) * rows_n + h) for h in range(heads_n) for r in range(rows_n)
        ]
        turned = lax.ppermute(scaled_flat, ("head", "row"), turn)
        turned, _ = lax.optimization_barrier((turned, weights[0]))
        crossed = swap(turned, "head", 2)

        def order(distance):
            return [
                (lambda d=d: lax.axis_index("head") ^ 2 ^ d, 0) for d in (distance, distance ^ 1)
            ]

        near = [turned, swap(turned, "head", 1)]
        (out_early,) = load(turned, [], (output_weight, 0, middle))
        crossed, _ = lax.optimization_barrier((crossed, out_early))
        far = [crossed, swap(crossed, "head", 1)]
        near_send, near_keep, near_lhs = project_signal(near, order(0), 2, *signal_weights, crossed)
        near_other = swap(near_send, "row", 1)
        far_send, far_keep, far_lhs = project_signal(far, order(2), 2, *signal_weights, near_send)
        far_other = swap(far_send, "row", 1)
        sums, _ = lax.optimization_barrier((sums, far_send))
        sums = sum_over(sums, "head")
        gate_send, gate_keep = project_gate(rows, [near_lhs, far_lhs], weights[2], far_send)
        gate_own, gate_far = [swap(part, "row", 1) for part in jnp.split(gate_send, 2, 0)]
        pick = [(near_keep, far_keep), (near_other, far_other)]
        last_send = sum(jnp.where(own, f, n).astype(F32) for n, f in pick).astype(BF16)
        last_send, sums = lax.optimization_barrier((last_send, sums))
        lead = last_send.shape[-1] - inner
        cut = lead + inner * 3 // 8 // LANES * LANES
        last_other = [swap(part, "row", 2) for part in jnp.split(last_send, [cut], -1)]
        (out_late,) = load(last_send, [], (output_weight, middle, middle))
        signal_terms = [[part[0] for part in last_other]]
        signal_terms += [[jnp.where(own, n, f)[0]] for n, f in pick]
        gate_far, _ = lax.optimization_barrier((gate_far, last_other[0]))
        gate_last = (gate_far.astype(F32) + gate_keep[1:].astype(F32)).astype(BF16)
        gate_terms = [swap_halves(gate_last, "row", 2, 1)[0], gate_own[0], gate_keep[0]]
        gate_last, out_late = lax.optimization_barrier((gate_last, out_late))
    else:
        features = lax.all_gather(scaled_flat, "head", axis=1, tiled=True)
        blocks = lax.all_to_all(features, "row", split_axis=1, concat_axis=0, tiled=True)
        blocks = blocks.reshape(rows_n, rows, depth)
        blocks = [blocks[i] for i in range(rows_n)]
        order = [(lambda i=i: i, 0) for i in range(rows_n)]
        send, keep, lhs = project_signal(blocks, order, rows_n, *signal_weights, sums)
        received = swap(send, "row", 1)
        gate_send, gate_keep = project_gate(rows, [lhs], weights[2], send)
        sums = sum_over(sums, "head")
        keep, out_early, out_late = load(
            gate_send, [keep], (output_weight, 0, middle), (output_weight, middle, middle)
        )
        signal_terms, _ = scatter_rows(received, keep, "row")
        signal_terms = [[t] for t in signal_terms]
        gate_terms, gate_last = scatter_rows(swap(gate_send, "row", 1), gate_keep, "row")
    out_weights = [out_early, out_late]

    adapted, read, spread, bgate, both, state = read_state(
        model_width,
        gate_last,
        live_block_rows,
        [pieces[0] for pieces in signal_terms],
        sums,
        up_rows,
        step_bias,
        head_decay_rate,
        head_skip_weight,
        scan_state,
    )

    distances = list(range(heads_n))
    first, out_lhs, gate_squares, feeds = output_parts(
        distances[3::4],
        out_weights,
        feature_width,
        [
            *gate_terms,
            *[piece for pieces in signal_terms for piece in pieces],
            sums,
            adapted,
            read,
            spread,
            gated_norm_scale[None],
        ],
        model_width,
        [len(gate_terms)] + [len(pieces) for pieces in signal_terms],
    )
    (second,) = output_parts(
        distances[2::4] + distances[1::4], out_weights, feature_width, [out_lhs, first]
    )
    half = second.shape[0] // 2
    send, gate_squares = meet(swap(first, "head", 1), second, gate_squares)
    (rest,) = output_parts(distances[0::4], out_weights, feature_width, [out_lhs, send])
    feeds, _ = lax.optimization_barrier((feeds, rest))
    kept = [swap(second[half:], "head", 1), rest]
    if len(bits_of(heads_n)) == 2:
        received = swap_halves(send, "head", 2, 1)
        mixer = sum(t[0].astype(F32) for t in [received[..., :feature_width]] + kept)
        gate_squares = gate_squares + join_lanes(received[0, :, feature_width:])
    else:
        received = swap(send[..., :feature_width], "head", 2)
        mixer, _ = scatter_rows(received, kept, "head", done=2)
        mixer = sum(t.astype(F32) for t in mixer)
        for distance in bits_of(heads_n)[1:]:
            gate_squares = gate_squares + swap(gate_squares, "head", distance)
    mixer = mixer * lax.rsqrt(gate_squares / inner_width + EPSILON)
    mixer = mixer.reshape(positions, streams, feature_width)
    live = jnp.arange(streams) < live_block_rows[0]
    mixed = (wide + jnp.where(live[:, None], mixer, 0.0)).astype(BF16)

    decays = jnp.broadcast_to(both[..., None], both.shape + (bgate.shape[-1],))
    new_state = state_write(feeds, bgate, decays, state)
    return (jnp.swapaxes(mixed, 0, 1), new_state)


def solution(mesh):
    in_specs = (
        P(("rep", "row"), None, "head"),
        P("head"),
        P("row", "head"),
        P("row", "head"),
        P("row", "head"),
        P("row", None),
        P("head"),
        P("head"),
        P("head"),
        P("head"),
        P("row", "head", None),
        P("row", None, "head"),
        P("head", None),
        P(("rep", "row"), "head", None, None),
        P(("rep", "row")),
        P(("rep", "row")),
    )
    out_specs = (P(("rep", "row"), None, "head"), P(("rep", "row"), "head", None, None))
    return jax.shard_map(
        on_device, mesh=mesh, in_specs=in_specs, out_specs=out_specs, check_vma=False
    )
```

```python
import functools

import jax
import jax.numpy as jnp
from jax import lax
from jax.experimental import pallas as pl
from jax.experimental.pallas import tpu as pltpu
from jax.sharding import PartitionSpec as P

BF16 = jnp.bfloat16
EPSILON = 1e-05
LANES = 128
F32 = jnp.float32
VMEM_GRANT = 12 * 1024 * 1024


def swap(values, axis, distance):
    size = lax.axis_size(axis)
    return lax.ppermute(values, axis, [(i, i ^ distance) for i in range(size)])


def swap_halves(values, axis, distance, dim):
    return jnp.concatenate([swap(v, axis, distance) for v in jnp.split(values, 2, dim)], dim)


def bits_of(size):
    return [1 << i for i in range(size.bit_length() - 1)]


def sum_over(values, axis):
    for distance in bits_of(lax.axis_size(axis)):
        values = values + swap(values, axis, distance)
    return values


def reverse_bits(value, size):
    bits = size.bit_length() - 1
    return sum(((value >> i) & 1) << (bits - 1 - i) for i in range(bits))


def params(**more):
    return pltpu.CompilerParams(vmem_limit_bytes=VMEM_GRANT, **more)


def cost(flops, size):
    return pl.CostEstimate(flops=int(flops), bytes_accessed=int(size), transcendentals=0)


def in_hbm(values):
    return pltpu.with_memory_space_constraint(values, pltpu.HBM)


def in_vmem(values):
    return pltpu.with_memory_space_constraint(values, pltpu.VMEM)


def load_body(spans, after_ref, *refs):
    count = len(spans)
    sources, targets, semaphores = refs[:count], refs[count : 2 * count], refs[2 * count]
    copies = []
    for source, target, (start, rows, parts) in zip(sources, targets, spans):
        step = rows // parts
        for i in range(parts):
            copies.append(
                pltpu.make_async_copy(
                    source.at[pl.ds(start + i * step, step)],
                    target.at[pl.ds(i * step, step)],
                    semaphores.at[len(copies)],
                )
            )
    for copy in copies:
        copy.start()
    for copy in copies:
        copy.wait()


def load(after, passed, *weights):
    weights = [w if isinstance(w, tuple) else (w, 0, w.shape[0]) for w in weights]
    shapes = [p.shape for p in passed] + [(rows, *w.shape[1:]) for w, _, rows in weights]
    spans = [(0, p.shape[0], 1) for p in passed]
    spans += [(start, rows, 8 if rows % 128 == 0 else 1) for _, start, rows in weights]
    size = sum(rows * w.shape[1] * w.dtype.itemsize for w, _, rows in weights)
    return pl.pallas_call(
        functools.partial(load_body, spans),
        out_shape=tuple(pltpu.VMEM(shape, BF16) for shape in shapes),
        in_specs=[pl.BlockSpec(memory_space=pl.ANY)] * (1 + len(shapes)),
        out_specs=tuple(pl.BlockSpec(memory_space=pltpu.VMEM) for _ in shapes),
        scratch_shapes=[pltpu.SemaphoreType.DMA((sum(parts for _, _, parts in spans),))],
        compiler_params=params(),
        cost_estimate=cost(0, 2 * size),
        name="load",
    )(after, *passed, *[in_hbm(w) for w, _, _ in weights])


def own_columns(rows, streams, rank):
    row = lax.broadcasted_iota(jnp.int32, (rows, streams * rank), 0) % streams
    return row == lax.broadcasted_iota(jnp.int32, (rows, streams * rank), 1) // rank


def adapt_body(tenant_ref, scaled_ref, squares_ref, down_ref, up_ref, sums_ref, up_rows_ref, *scratch):
    down_rows_ref, semaphores = scratch
    rank = down_ref.shape[1]
    streams = tenant_ref.shape[0]
    rows = scaled_ref.shape[0]
    first = lax.axis_index("row") * down_ref.shape[0]
    downs, ups = [], []
    for s in range(streams):
        at = pl.ds(s * rank, rank)
        tenant = tenant_ref[s] - first
        downs.append(
            pltpu.make_async_copy(down_ref.at[tenant], down_rows_ref.at[at, :], semaphores.at[s])
        )
        ups.append(
            pltpu.make_async_copy(
                up_ref.at[tenant], up_rows_ref.at[at, :], semaphores.at[streams + s]
            )
        )
    for copy in downs + ups:
        copy.start()
    for copy in downs:
        copy.wait()
    every = lax.dot_general(
        scaled_ref[...],
        down_rows_ref[...],
        (((1,), (1,)), ((), ())),
        preferred_element_type=F32,
    )
    own = jnp.where(own_columns(rows, streams, rank), every, 0.0)
    fold = lax.broadcasted_iota(jnp.int32, (streams * rank, rank), 0) % rank
    fold = (fold == lax.broadcasted_iota(jnp.int32, (streams * rank, rank), 1)).astype(BF16)
    high, rest = split(own)
    middle, low = rest, (own - high.astype(F32) - rest.astype(F32)).astype(BF16)
    folded = sum(jnp.dot(x, fold, preferred_element_type=F32) for x in (high, middle, low))
    sums_ref[:, :rank] = folded
    sums_ref[:, rank:] = squares_ref[...]
    for copy in ups:
        copy.wait()


def adapt(tenants, scaled, squares, down, up):
    streams = tenants.shape[0]
    rows, depth = scaled.shape
    rank, inner = up.shape[1:]
    whole = pl.BlockSpec(memory_space=pltpu.VMEM)
    anywhere = pl.BlockSpec(memory_space=pl.ANY)
    return pl.pallas_call(
        adapt_body,
        out_shape=(
            jax.ShapeDtypeStruct((rows, rank + 1), F32),
            pltpu.VMEM((streams * rank, inner), BF16),
        ),
        in_specs=[pl.BlockSpec(memory_space=pltpu.SMEM), whole, whole, anywhere, anywhere],
        out_specs=(whole, whole),
        scratch_shapes=[
            pltpu.VMEM((streams * rank, depth), BF16),
            pltpu.SemaphoreType.DMA((2 * streams,)),
        ],
        compiler_params=params(),
        cost_estimate=cost(2 * rows * depth * streams * rank, 2 * streams * rank * (depth + inner)),
        name="adapt",
    )(tenants, scaled, squares, in_hbm(jnp.swapaxes(down, 1, 2)), in_hbm(up))


def lead_of(mix, steps):
    return -(-(mix + steps) // LANES) * LANES


def project_signal_body(owners, order, *refs):
    blocks, refs = refs[: len(order)], refs[len(order) :]
    weight_ref, mix_ref, step_ref, send_ref, keep_ref, lhs_ref, semaphores = refs
    rows = blocks[0].shape[0]
    parts = len(blocks) // owners
    copies = []
    for i, block in enumerate(blocks):
        owner, part = order[i]
        away = (owner() ^ lax.axis_index("row")) % owners
        at = pl.multiple_of((away * parts + part) * rows, rows)
        copies.append(
            pltpu.make_async_copy(block, lhs_ref.at[pl.ds(at, rows), :], semaphores.at[i])
        )
    for copy in copies:
        copy.start()
    for copy in copies:
        copy.wait()
    lhs = lhs_ref[...]

    def put(acc, start):
        step = send_ref.shape[1]
        for k in range(owners):
            target = send_ref if k % 2 else keep_ref
            target[k // 2, :, start : start + acc.shape[1]] = acc[k * step : (k + 1) * step].astype(
                target.dtype
            )

    mix = mix_ref.shape[1]
    put(jnp.dot(lhs, mix_ref[...], preferred_element_type=F32), 0)
    acc = lax.dot_general(lhs, step_ref[...], (((1,), (1,)), ((), ())), preferred_element_type=F32)
    put(acc, mix)
    columns = weight_ref.shape[1]
    lead = send_ref.shape[2] - columns
    put(jnp.zeros((lhs.shape[0], lead - mix - acc.shape[1]), F32), mix + acc.shape[1])
    tile = min(columns, 512)
    for t in range(0, columns, tile):
        put(jnp.dot(lhs, weight_ref[:, t : t + tile], preferred_element_type=F32), lead + t)


def project_signal(blocks, order, owners, weight, mix, step, after):
    pieces = len(blocks)
    depth = blocks[0].shape[1]
    rows = pieces * blocks[0].shape[0]
    columns = weight.shape[1] + lead_of(mix.shape[1], step.shape[0])
    half = jax.ShapeDtypeStruct((owners // 2, rows // owners, columns), BF16)
    whole = pl.BlockSpec(memory_space=pltpu.VMEM)
    anywhere = pl.BlockSpec(memory_space=pl.ANY)

    def body(*refs):
        project_signal_body(owners, order, *refs[:pieces], *refs[pieces + 1 :])

    return pl.pallas_call(
        body,
        out_shape=(half, half, jax.ShapeDtypeStruct((rows, depth), BF16)),
        in_specs=[anywhere] * (pieces + 1) + [whole] * 3,
        out_specs=(whole,) * 3,
        scratch_shapes=[pltpu.SemaphoreType.DMA((pieces,))],
        compiler_params=params(),
        cost_estimate=cost(2 * rows * depth * columns, 2 * depth * columns),
        name="project_signal",
    )(*blocks, after, in_vmem(weight), in_vmem(mix), step)


def project_gate_body(groups, *refs):
    lhs_refs, refs = refs[:groups], refs[groups:]
    weight_ref, after_ref, send_ref, keep_ref = refs
    rows = send_ref.shape[1]
    columns = weight_ref.shape[1]
    tile = min(columns, 512)
    first = group_of_own(groups)
    for t in range(0, columns, tile):
        for g, lhs_ref in enumerate(lhs_refs):
            acc = jnp.dot(lhs_ref[...], weight_ref[:, t : t + tile], preferred_element_type=F32)
            pairs = lhs_ref.shape[0] // (2 * rows)
            for k in range(2 * pairs):
                target = send_ref if k % 2 else keep_ref
                at = (first ^ g) * pairs + k // 2
                target[at, :, t : t + tile] = acc[k * rows : (k + 1) * rows].astype(target.dtype)


def group_of_own(groups):
    if groups == 1:
        return 0
    return (lax.axis_index("head") ^ 2 ^ lax.axis_index("row")) >> 1


def project_gate(rows, lhs, weight, after):
    count = sum(part.shape[0] for part in lhs) // rows
    columns = weight.shape[1]
    half = jax.ShapeDtypeStruct((count // 2, rows, columns), BF16)
    whole = pl.BlockSpec(memory_space=pltpu.VMEM)
    return pl.pallas_call(
        functools.partial(project_gate_body, len(lhs)),
        out_shape=(half, half),
        in_specs=[whole] * (len(lhs) + 1) + [pl.BlockSpec(memory_space=pl.ANY)],
        out_specs=(whole,) * 2,
        compiler_params=params(),
        cost_estimate=cost(2 * count * rows * lhs[0].shape[1] * columns, 2 * weight.size),
        name="project_gate",
    )(*lhs, in_vmem(weight), after)


def scatter_rows(received, keep, axis, done=1):
    send = received
    terms = [received] + (keep if isinstance(keep, list) else [keep])
    for distance in bits_of(lax.axis_size(axis))[done:]:
        send = sum(t[1::2].astype(F32) for t in terms).astype(BF16)
        terms = [swap(send, axis, distance)] + [t[0::2] for t in terms]
    return [t[0] for t in terms], send


def softplus(values):
    return jnp.maximum(values, 0.0) + jnp.log1p(jnp.exp(-jnp.abs(values)))


def silu(values):
    return values / (1.0 + jnp.exp(-values))


def inverse_of(sums_ref, width):
    return lax.rsqrt(sums_ref[:, sums_ref.shape[1] - 1 :] / width + EPSILON)


def read_body(terms, group, model_width, live_ref, *refs):
    term_refs = refs[:terms]
    sums_ref, up_ref, bias_ref, rate_ref, skip_ref, source_ref, _ = refs[terms : terms + 7]
    adapted_ref, read_ref, spread_ref, b_ref, both_ref, state_ref, *scratch = refs[terms + 7 :]
    c_ref, semaphores = scratch
    heads, head, width = state_ref.shape[1:]
    streams, inner = read_ref.shape[1:]
    step = pl.program_id(0)

    def fetch(i):
        at = pl.ds(i * group, group)
        return pltpu.make_async_copy(source_ref.at[at], state_ref.at[at], semaphores.at[i])

    @pl.when(step == 0)
    def _():
        for i in range(streams // group):
            fetch(i).start()
        rows = sums_ref.shape[0]
        rank = sums_ref.shape[1] - 1
        inverse = inverse_of(sums_ref, model_width)
        total = sum(t[:, : 2 * width + heads].astype(F32) for t in term_refs) * inverse
        gates = silu(total[:, : 2 * width])
        steps_dt = softplus(total[:, 2 * width :] + bias_ref[...])
        b = [gates[p * streams : (p + 1) * streams, :width] for p in range(2)]
        c = [gates[p * streams : (p + 1) * streams, width:] for p in range(2)]
        for p in range(2):
            b_ref[p] = b[p]
            c_ref[p] = c[p]
        live = lax.broadcasted_iota(jnp.int32, (streams, heads), 0) < live_ref[0]
        dt = [steps_dt[p * streams : (p + 1) * streams] for p in range(2)]
        decay = [jnp.where(live, jnp.exp(-d * rate_ref[...]), 1.0) for d in dt]
        fed = [jnp.where(live, d, 0.0) for d in dt]

        def match(i, j):
            return jnp.sum(b[i] * c[j], -1, keepdims=True)

        both = decay[0] * decay[1]
        both_ref[...] = both
        late = decay[1] * fed[0]
        skip = skip_ref[...]
        factors = jnp.concatenate(
            [
                decay[0],
                both,
                fed[0] * match(0, 0) + skip,
                fed[1] * match(1, 1) + skip,
                late * match(0, 1),
                late,
                fed[1],
            ],
            0,
        )
        high, low = split(factors)
        place = lax.broadcasted_iota(jnp.int32, (heads, inner), 1) // head
        ones = (place == lax.broadcasted_iota(jnp.int32, (heads, inner), 0)).astype(BF16)
        spread_ref[...] = jnp.dot(high, ones, preferred_element_type=F32) + jnp.dot(
            low, ones, preferred_element_type=F32
        )
        lowrank = (sums_ref[:, :rank] * inverse).astype(BF16)
        repeat = lax.broadcasted_iota(jnp.int32, (rank, streams * rank), 1) % rank
        repeat = (repeat == lax.broadcasted_iota(jnp.int32, (rank, streams * rank), 0)).astype(BF16)
        every = jnp.dot(lowrank, repeat, preferred_element_type=F32)
        own = jnp.where(own_columns(rows, streams, rank), every, 0.0).astype(BF16)
        adapted_ref[...] = jnp.dot(own, up_ref[...], preferred_element_type=F32)

    fetch(step).wait()
    at = pl.multiple_of(step * group, group)
    c = jnp.concatenate([c_ref[p, pl.ds(at, group), :] for p in range(2)], 0)
    lhs = jnp.concatenate(split(c), 0)
    for g in range(group):
        state = state_ref[at + g].reshape(inner, width)
        found = lax.dot_general(lhs, state, (((1,), (1,)), ((), ())), preferred_element_type=F32)
        for p in range(2):
            row = p * group + g
            low = 2 * group + row
            read_ref[p, pl.ds(at + g, 1), :] = found[row : row + 1] + found[low : low + 1]


def read_state(model_width, after, live_rows, terms, sums, up_rows, bias, rate, skip, state):
    streams, heads, head, width = state.shape
    group = 8
    inner = heads * head
    rows = 2 * streams
    whole = pl.BlockSpec(memory_space=pltpu.VMEM)
    return pl.pallas_call(
        functools.partial(read_body, len(terms), group, model_width),
        out_shape=(
            jax.ShapeDtypeStruct((rows, inner), F32),
            jax.ShapeDtypeStruct((2, streams, inner), F32),
            jax.ShapeDtypeStruct((7 * streams, inner), F32),
            jax.ShapeDtypeStruct((2, streams, width), F32),
            jax.ShapeDtypeStruct((streams, heads), F32),
            pltpu.VMEM(state.shape, state.dtype),
        ),
        grid=(streams // group,),
        in_specs=[pl.BlockSpec(memory_space=pltpu.SMEM)]
        + [whole] * (len(terms) + 5)
        + [pl.BlockSpec(memory_space=pl.ANY)] * 2,
        out_specs=(whole,) * 6,
        scratch_shapes=[
            pltpu.VMEM((2, streams, width), F32),
            pltpu.SemaphoreType.DMA((streams // group,)),
        ],
        compiler_params=params(),
        cost_estimate=cost(64 * state.size, 2 * state.size + 32 * rows * inner),
        name="read_state",
    )(
        live_rows,
        *terms,
        sums,
        up_rows,
        bias[None],
        rate[None],
        skip[None],
        in_hbm(state),
        after,
    )


def state_write_body(feeds_ref, b_ref, decay_ref, state_ref, out_ref):
    group, heads, head, width = out_ref.shape
    at = pl.multiple_of(pl.program_id(0) * group, group)
    feeds = [split(feeds_ref[p, pl.ds(at, group), :]) for p in range(2)]
    rights = [split(b_ref[p, pl.ds(at, group), :]) for p in range(2)]
    left = [f.astype(F32) for pair in feeds for f in (pair[0], pair[1], pair[0])]
    right = [f.astype(F32) for pair in rights for f in (pair[0], pair[0], pair[1])]
    left = jnp.concatenate(left, 0).astype(BF16)
    right = jnp.concatenate(right, 0)
    stream = lax.broadcasted_iota(jnp.int32, right.shape, 0) % group
    for g in range(0, group, 2):
        pair = jnp.concatenate([jnp.where(stream == g + i, right, 0.0) for i in range(2)], 1)
        outer = lax.dot_general(
            left, pair.astype(BF16), (((0,), (0,)), ((), ())), preferred_element_type=F32
        )
        for i in range(2):
            scaled = state_ref[at + g + i].astype(F32) * decay_ref[g + i][:, None, :]
            own = outer[:, i * width : (i + 1) * width].reshape(heads, head, width)
            out_ref[g + i] = (scaled + own).astype(out_ref.dtype)


def state_write(feeds, b, decay, state):
    streams, heads, head, width = state.shape
    group = 8
    whole = pl.BlockSpec(memory_space=pltpu.VMEM)
    return pl.pallas_call(
        state_write_body,
        out_shape=jax.ShapeDtypeStruct(state.shape, state.dtype),
        grid=(streams // group,),
        in_specs=[
            whole,
            whole,
            pl.BlockSpec((group, heads, width), lambda i: (i, 0, 0)),
            whole,
        ],
        out_specs=pl.BlockSpec((group, heads, head, width), lambda i: (i, 0, 0, 0)),
        compiler_params=params(),
        cost_estimate=cost(32 * state.size, 4 * state.size),
        name="state_write",
    )(feeds, b, decay, state)


def output_tiles(distances, lhs_ref, weight_refs, out_ref):
    width = out_ref.shape[2] // 256 * 256
    tile = min(width, 512)
    for j, distance in enumerate(distances):
        for t in range(0, width, tile):
            at = pl.multiple_of((lax.axis_index("head") ^ distance) * width + t, tile)
            acc, start = 0.0, 0
            for weight_ref in weight_refs:
                stop = start + weight_ref.shape[0]
                acc += jnp.dot(
                    lhs_ref[:, start:stop],
                    weight_ref[:, pl.ds(at, tile)],
                    preferred_element_type=F32,
                )
                start = stop
            out_ref[j, :, t : t + tile] = acc.astype(out_ref.dtype)


def put_lanes(values, out_ref, j):
    lane = lax.broadcasted_iota(jnp.int32, (values.shape[0], LANES), 1)
    tail = jnp.zeros(lane.shape, F32)
    for i in range(3):
        term = values.astype(BF16).astype(F32)
        tail = jnp.where(lane == i, term, tail)
        values = values - term
    out_ref[j, :, out_ref.shape[2] - LANES :] = tail.astype(out_ref.dtype)


def meet_body(met_ref, own_ref, squares_ref, out_ref, total_ref):
    count = met_ref.shape[0]
    width = own_ref.shape[2]
    total = squares_ref[...] + join_lanes(met_ref[0, :, width:])
    total_ref[...] = total
    for j in range(count):
        both = met_ref[j, :, :width].astype(F32) + own_ref[j].astype(F32)
        out_ref[j, :, :width] = both.astype(out_ref.dtype)
        put_lanes(total, out_ref, j)


def meet(met, own, squares):
    whole = pl.BlockSpec(memory_space=pltpu.VMEM)
    return pl.pallas_call(
        meet_body,
        out_shape=(
            jax.ShapeDtypeStruct(met.shape, met.dtype),
            jax.ShapeDtypeStruct(squares.shape, squares.dtype),
        ),
        in_specs=[whole] * 3,
        out_specs=(whole, whole),
        compiler_params=params(),
        cost_estimate=cost(met.size, 6 * met.size),
        name="meet",
    )(met, own, squares)


def join_lanes(values):
    return jnp.sum(values.astype(F32), -1, keepdims=True)


def output_first_body(distances, terms, model_width, *refs):
    gate_refs, signal_refs, refs = refs[:terms], refs[terms : 2 * terms], refs[2 * terms :]
    sums_ref, adapted_ref, read_ref, spread_ref, scale_ref, *weight_refs = refs[:-4]
    out_ref, lhs_ref, squares_ref, feeds_ref = refs[-4:]
    streams, inner = read_ref.shape[1:]
    inverse = inverse_of(sums_ref, model_width)
    total = sum(t[:, t.shape[1] - inner :].astype(F32) for t in signal_refs)
    signal = silu(total * inverse + adapted_ref[...])
    first, second = signal[:streams], signal[streams:]
    factor = [spread_ref[i * streams : (i + 1) * streams, :] for i in range(7)]
    feeds_ref[0] = factor[5] * first
    feeds_ref[1] = factor[6] * second
    result = [
        factor[0] * read_ref[0] + factor[2] * first,
        factor[1] * read_ref[1] + factor[4] * first + factor[3] * second,
    ]
    total = sum(t[...].astype(F32) for t in gate_refs) * inverse
    gated = jnp.concatenate(result, 0) * silu(total)
    squares_ref[...] = jnp.sum(gated * gated, -1, keepdims=True)
    lhs_ref[...] = (gated * scale_ref[...]).astype(lhs_ref.dtype)
    output_tiles(distances, lhs_ref, weight_refs, out_ref)
    for j in range(len(distances)):
        put_lanes(squares_ref[...], out_ref, j)


def put_lanes(values, out_ref, j):
    lane = lax.broadcasted_iota(jnp.int32, (values.shape[0], LANES), 1)
    tail = jnp.zeros(lane.shape, F32)
    for i in range(3):
        term = values.astype(BF16).astype(F32)
        tail = jnp.where(lane == i, term, tail)
        values = values - term
    out_ref[j, :, out_ref.shape[2] - LANES :] = tail.astype(out_ref.dtype)


def meet_body(met_ref, own_ref, squares_ref, out_ref, total_ref):
    count = met_ref.shape[0]
    width = own_ref.shape[2]
    total = squares_ref[...] + join_lanes(met_ref[0, :, width:])
    total_ref[...] = total
    for j in range(count):
        both = met_ref[j, :, :width].astype(F32) + own_ref[j].astype(F32)
        out_ref[j, :, :width] = both.astype(out_ref.dtype)
        put_lanes(total, out_ref, j)


def meet(met, own, squares):
    whole = pl.BlockSpec(memory_space=pltpu.VMEM)
    return pl.pallas_call(
        meet_body,
        out_shape=(
            jax.ShapeDtypeStruct(met.shape, met.dtype),
            jax.ShapeDtypeStruct(squares.shape, squares.dtype),
        ),
        in_specs=[whole] * 3,
        out_specs=(whole, whole),
        compiler_params=params(),
        cost_estimate=cost(met.size, 6 * met.size),
        name="meet",
    )(met, own, squares)


def join_lanes(values):
    return jnp.sum(values.astype(F32), -1, keepdims=True)


def output_rest_body(distances, lhs_ref, after_ref, *refs):
    output_tiles(distances, lhs_ref, refs[:-1], refs[-1])


def output_parts(distances, weights, width, operands, model_width=None, terms=None):
    first = model_width is not None
    rows, depth = operands[0].shape
    count = len(distances)
    whole = pl.BlockSpec(memory_space=pltpu.VMEM)
    specs = [whole] * (len(operands) + len(weights))
    body = functools.partial(output_rest_body, distances)
    extra = LANES if first else 0
    out_shape = [jax.ShapeDtypeStruct((count, rows, width + extra), BF16)]
    if first:
        body = functools.partial(output_first_body, distances, terms, model_width)
        out_shape += [
            jax.ShapeDtypeStruct((rows, depth), BF16),
            jax.ShapeDtypeStruct((rows, 1), F32),
            jax.ShapeDtypeStruct((2, rows // 2, depth), F32),
        ]
    else:
        specs[1] = pl.BlockSpec(memory_space=pl.ANY)
    return pl.pallas_call(
        body,
        out_shape=tuple(out_shape),
        in_specs=specs,
        out_specs=(whole,) * len(out_shape),
        compiler_params=params(),
        cost_estimate=cost(2 * rows * depth * width * count, 2 * depth * width * count),
        name="output_first" if first else "output_rest",
    )(*operands, *[in_vmem(w) for w in weights])


def split(values):
    high = values.astype(BF16)
    return high, (values - high.astype(F32)).astype(BF16)


def on_device(
    hidden,
    input_norm_scale,
    projection_signal,
    projection_gate,
    projection_step,
    projection_input_output,
    step_bias,
    head_decay_rate,
    head_skip_weight,
    gated_norm_scale,
    adapter_down_weight,
    adapter_up_weight,
    output_weight,
    scan_state,
    stream_tenant_index,
    live_block_rows,
):
    streams, positions, feature_width = hidden.shape
    rows = streams * positions
    heads_n = lax.axis_size("head")
    rows_n = lax.axis_size("row")
    model_width = feature_width * heads_n
    depth, inner = projection_signal.shape
    inner_width = inner * heads_n

    wide = jnp.swapaxes(hidden, 0, 1).astype(F32)
    scaled = (wide * input_norm_scale).astype(BF16)
    scaled_flat = scaled.reshape(rows, feature_width)

    squares = jnp.sum(wide * wide, -1).reshape(rows, 1)
    sums, up_rows = adapt(stream_tenant_index, scaled_flat, squares, adapter_down_weight, adapter_up_weight)

    own = group_of_own(2) == 0
    sums, own = lax.optimization_barrier((sums, own))
    middle = output_weight.shape[0] // 2
    *weights, out_early = load(
        sums,
        [],
        projection_signal,
        projection_input_output,
        projection_gate,
        (output_weight, 0, middle),
    )
    signal_weights = (*weights[:2], projection_step.T)
    if heads_n == rows_n and len(bits_of(rows_n)) == 2:
        turn = [
            (h * rows_n + r, (r ^ 2) * rows_n + h) for h in range(heads_n) for r in range(rows_n)
        ]
        turned = lax.ppermute(scaled_flat, ("head", "row"), turn)
        turned, _ = lax.optimization_barrier((turned, weights[0]))
        crossed = swap(turned, "head", 2)

        def order(distance):
            return [
                (lambda d=d: lax.axis_index("head") ^ 2 ^ d, 0) for d in (distance, distance ^ 1)
            ]

        near = [turned, swap(turned, "head", 1)]
        (out_late,) = load(turned, [], (output_weight, middle, middle))
        crossed, _ = lax.optimization_barrier((crossed, out_late))
        far = [crossed, swap(crossed, "head", 1)]
        near_send, near_keep, near_lhs = project_signal(near, order(0), 2, *signal_weights, crossed)
        near_other = swap(near_send, "row", 1)
        far_send, far_keep, far_lhs = project_signal(far, order(2), 2, *signal_weights, near_send)
        far_other = swap(far_send, "row", 1)
        sums, _ = lax.optimization_barrier((sums, far_send))
        sums = sum_over(sums, "head")
        gate_send, gate_keep = project_gate(rows, [near_lhs, far_lhs], weights[2], far_send)
        gate_own, gate_far = [swap(part, "row", 1) for part in jnp.split(gate_send, 2, 0)]
        pick = [(near_keep, far_keep), (near_other, far_other)]
        last_send = sum(jnp.where(own, f, n).astype(F32) for n, f in pick).astype(BF16)
        last_send, sums = lax.optimization_barrier((last_send, sums))
        lead = last_send.shape[-1] - inner
        last_other = [swap(part, "row", 2) for part in jnp.split(last_send, [lead], -1)]
        kept = [jnp.where(own, n, f)[0] for n, f in pick]
        lead_terms = [last_other[0][0]] + kept
        signal_terms = [last_other[1][0]] + kept
        gate_far, _ = lax.optimization_barrier((gate_far, last_other[0]))
        gate_last = (gate_far.astype(F32) + gate_keep[1:].astype(F32)).astype(BF16)
        gate_terms = [swap_halves(gate_last, "row", 2, 1)[0], gate_own[0], gate_keep[0]]
    else:
        features = lax.all_gather(scaled_flat, "head", axis=1, tiled=True)
        blocks = lax.all_to_all(features, "row", split_axis=1, concat_axis=0, tiled=True)
        blocks = blocks.reshape(rows_n, rows, depth)
        blocks = [blocks[i] for i in range(rows_n)]
        order = [(lambda i=i: i, 0) for i in range(rows_n)]
        send, keep, lhs = project_signal(blocks, order, rows_n, *signal_weights, sums)
        received = swap(send, "row", 1)
        gate_send, gate_keep = project_gate(rows, [lhs], weights[2], send)
        sums = sum_over(sums, "head")
        keep, out_late = load(gate_send, [keep], (output_weight, middle, middle))
        signal_terms, _ = scatter_rows(received, keep, "row")
        lead_terms = signal_terms
        gate_terms, gate_last = scatter_rows(swap(gate_send, "row", 1), gate_keep, "row")
    out_weights = [out_early, out_late]

    adapted, read, spread, bgate, both, state = read_state(
        model_width,
        gate_last,
        live_block_rows,
        lead_terms,
        sums,
        up_rows,
        step_bias,
        head_decay_rate,
        head_skip_weight,
        scan_state,
    )

    distances = list(range(heads_n))
    first, out_lhs, gate_squares, feeds = output_parts(
        distances[3::4],
        out_weights,
        feature_width,
        [
            *gate_terms,
            *signal_terms,
            sums,
            adapted,
            read,
            spread,
            gated_norm_scale[None],
        ],
        model_width,
        len(gate_terms),
    )
    (second,) = output_parts(
        distances[2::4] + distances[1::4], out_weights, feature_width, [out_lhs, first]
    )
    half = second.shape[0] // 2
    send, gate_squares = meet(swap(first, "head", 1), second, gate_squares)
    (rest,) = output_parts(distances[0::4], out_weights, feature_width, [out_lhs, send])
    feeds, _ = lax.optimization_barrier((feeds, rest))
    kept = [swap(second[half:], "head", 1), rest]
    if len(bits_of(heads_n)) == 2:
        received = swap_halves(send, "head", 2, 1)
        mixer = sum(t[0].astype(F32) for t in [received[..., :feature_width]] + kept)
        gate_squares = gate_squares + join_lanes(received[0, :, feature_width:])
    else:
        received = swap(send[..., :feature_width], "head", 2)
        mixer, _ = scatter_rows(received, kept, "head", done=2)
        mixer = sum(t.astype(F32) for t in mixer)
        for distance in bits_of(heads_n)[1:]:
            gate_squares = gate_squares + swap(gate_squares, "head", distance)
    mixer = mixer * lax.rsqrt(gate_squares / inner_width + EPSILON)
    mixer = mixer.reshape(positions, streams, feature_width)
    live = jnp.arange(streams) < live_block_rows[0]
    mixed = (wide + jnp.where(live[:, None], mixer, 0.0)).astype(BF16)

    decays = jnp.broadcast_to(both[..., None], both.shape + (bgate.shape[-1],))
    new_state = state_write(feeds, bgate, decays, state)
    return (jnp.swapaxes(mixed, 0, 1), new_state)


def solution(mesh):
    in_specs = (
        P(("rep", "row"), None, "head"),
        P("head"),
        P("row", "head"),
        P("row", "head"),
        P("row", "head"),
        P("row", None),
        P("head"),
        P("head"),
        P("head"),
        P("head"),
        P("row", "head", None),
        P("row", None, "head"),
        P("head", None),
        P(("rep", "row"), "head", None, None),
        P(("rep", "row")),
        P(("rep", "row")),
    )
    out_specs = (P(("rep", "row"), None, "head"), P(("rep", "row"), "head", None, None))
    return jax.shard_map(
        on_device, mesh=mesh, in_specs=in_specs, out_specs=out_specs, check_vma=False
    )
```

```python
import functools

import jax
import jax.numpy as jnp
from jax import lax
from jax.experimental import pallas as pl
from jax.experimental.pallas import tpu as pltpu
from jax.sharding import PartitionSpec as P

BF16 = jnp.bfloat16
EPSILON = 1e-05
LANES = 128
F32 = jnp.float32
VMEM_GRANT = 12 * 1024 * 1024


def swap(values, axis, distance):
    size = lax.axis_size(axis)
    return lax.ppermute(values, axis, [(i, i ^ distance) for i in range(size)])


def swap_halves(values, axis, distance, dim):
    return jnp.concatenate([swap(v, axis, distance) for v in jnp.split(values, 2, dim)], dim)


def bits_of(size):
    return [1 << i for i in range(size.bit_length() - 1)]


def sum_over(values, axis):
    for distance in bits_of(lax.axis_size(axis)):
        values = values + swap(values, axis, distance)
    return values


def reverse_bits(value, size):
    bits = size.bit_length() - 1
    return sum(((value >> i) & 1) << (bits - 1 - i) for i in range(bits))


def params(**more):
    return pltpu.CompilerParams(vmem_limit_bytes=VMEM_GRANT, **more)


def cost(flops, size):
    return pl.CostEstimate(flops=int(flops), bytes_accessed=int(size), transcendentals=0)


def in_hbm(values):
    return pltpu.with_memory_space_constraint(values, pltpu.HBM)


def in_vmem(values):
    return pltpu.with_memory_space_constraint(values, pltpu.VMEM)


def load_body(spans, after_ref, *refs):
    count = len(spans)
    sources, targets, semaphores = refs[:count], refs[count : 2 * count], refs[2 * count]
    copies = []
    for source, target, (start, rows, parts) in zip(sources, targets, spans):
        step = rows // parts
        for i in range(parts):
            copies.append(
                pltpu.make_async_copy(
                    source.at[pl.ds(start + i * step, step)],
                    target.at[pl.ds(i * step, step)],
                    semaphores.at[len(copies)],
                )
            )
    for copy in copies:
        copy.start()
    for copy in copies:
        copy.wait()


def load(after, passed, *weights):
    weights = [w if isinstance(w, tuple) else (w, 0, w.shape[0]) for w in weights]
    shapes = [p.shape for p in passed] + [(rows, *w.shape[1:]) for w, _, rows in weights]
    spans = [(0, p.shape[0], 1) for p in passed]
    spans += [(start, rows, 8 if rows % 128 == 0 else 1) for _, start, rows in weights]
    size = sum(rows * w.shape[1] * w.dtype.itemsize for w, _, rows in weights)
    return pl.pallas_call(
        functools.partial(load_body, spans),
        out_shape=tuple(pltpu.VMEM(shape, BF16) for shape in shapes),
        in_specs=[pl.BlockSpec(memory_space=pl.ANY)] * (1 + len(shapes)),
        out_specs=tuple(pl.BlockSpec(memory_space=pltpu.VMEM) for _ in shapes),
        scratch_shapes=[pltpu.SemaphoreType.DMA((sum(parts for _, _, parts in spans),))],
        compiler_params=params(),
        cost_estimate=cost(0, 2 * size),
        name="load",
    )(after, *passed, *[in_hbm(w) for w, _, _ in weights])


def own_columns(rows, streams, rank):
    row = lax.broadcasted_iota(jnp.int32, (rows, streams * rank), 0) % streams
    return row == lax.broadcasted_iota(jnp.int32, (rows, streams * rank), 1) // rank


def adapt_body(tenant_ref, scaled_ref, squares_ref, down_ref, up_ref, sums_ref, up_rows_ref, *scratch):
    down_rows_ref, semaphores = scratch
    rank = down_ref.shape[1]
    streams = tenant_ref.shape[0]
    rows = scaled_ref.shape[0]
    first = lax.axis_index("row") * down_ref.shape[0]
    downs, ups = [], []
    for s in range(streams):
        at = pl.ds(s * rank, rank)
        tenant = tenant_ref[s] - first
        downs.append(
            pltpu.make_async_copy(down_ref.at[tenant], down_rows_ref.at[at, :], semaphores.at[s])
        )
        ups.append(
            pltpu.make_async_copy(
                up_ref.at[tenant], up_rows_ref.at[at, :], semaphores.at[streams + s]
            )
        )
    for copy in downs + ups:
        copy.start()
    for copy in downs:
        copy.wait()
    every = lax.dot_general(
        scaled_ref[...],
        down_rows_ref[...],
        (((1,), (1,)), ((), ())),
        preferred_element_type=F32,
    )
    own = jnp.where(own_columns(rows, streams, rank), every, 0.0)
    fold = lax.broadcasted_iota(jnp.int32, (streams * rank, rank), 0) % rank
    fold = (fold == lax.broadcasted_iota(jnp.int32, (streams * rank, rank), 1)).astype(BF16)
    high, rest = split(own)
    middle, low = rest, (own - high.astype(F32) - rest.astype(F32)).astype(BF16)
    folded = sum(jnp.dot(x, fold, preferred_element_type=F32) for x in (high, middle, low))
    sums_ref[:, :rank] = folded
    sums_ref[:, rank:] = squares_ref[...]
    for copy in ups:
        copy.wait()


def adapt(tenants, scaled, squares, down, up):
    streams = tenants.shape[0]
    rows, depth = scaled.shape
    rank, inner = up.shape[1:]
    whole = pl.BlockSpec(memory_space=pltpu.VMEM)
    anywhere = pl.BlockSpec(memory_space=pl.ANY)
    return pl.pallas_call(
        adapt_body,
        out_shape=(
            jax.ShapeDtypeStruct((rows, rank + 1), F32),
            pltpu.VMEM((streams * rank, inner), BF16),
        ),
        in_specs=[pl.BlockSpec(memory_space=pltpu.SMEM), whole, whole, anywhere, anywhere],
        out_specs=(whole, whole),
        scratch_shapes=[
            pltpu.VMEM((streams * rank, depth), BF16),
            pltpu.SemaphoreType.DMA((2 * streams,)),
        ],
        compiler_params=params(),
        cost_estimate=cost(2 * rows * depth * streams * rank, 2 * streams * rank * (depth + inner)),
        name="adapt",
    )(tenants, scaled, squares, in_hbm(jnp.swapaxes(down, 1, 2)), in_hbm(up))


def lead_of(mix, steps):
    return -(-(mix + steps) // LANES) * LANES


def project_signal_body(owners, order, *refs):
    blocks, refs = refs[: len(order)], refs[len(order) :]
    weight_ref, mix_ref, step_ref, send_ref, keep_ref, lhs_ref, semaphores = refs
    rows = blocks[0].shape[0]
    parts = len(blocks) // owners
    copies = []
    for i, block in enumerate(blocks):
        owner, part = order[i]
        away = (owner() ^ lax.axis_index("row")) % owners
        at = pl.multiple_of((away * parts + part) * rows, rows)
        copies.append(
            pltpu.make_async_copy(block, lhs_ref.at[pl.ds(at, rows), :], semaphores.at[i])
        )
    for copy in copies:
        copy.start()
    for copy in copies:
        copy.wait()
    lhs = lhs_ref[...]

    def put(acc, start):
        step = send_ref.shape[1]
        for k in range(owners):
            target = send_ref if k % 2 else keep_ref
            target[k // 2, :, start : start + acc.shape[1]] = acc[k * step : (k + 1) * step].astype(
                target.dtype
            )

    mix = mix_ref.shape[1]
    put(jnp.dot(lhs, mix_ref[...], preferred_element_type=F32), 0)
    acc = lax.dot_general(lhs, step_ref[...], (((1,), (1,)), ((), ())), preferred_element_type=F32)
    put(acc, mix)
    columns = weight_ref.shape[1]
    lead = send_ref.shape[2] - columns
    put(jnp.zeros((lhs.shape[0], lead - mix - acc.shape[1]), F32), mix + acc.shape[1])
    tile = min(columns, 512)
    for t in range(0, columns, tile):
        put(jnp.dot(lhs, weight_ref[:, t : t + tile], preferred_element_type=F32), lead + t)


def project_signal(blocks, order, owners, weight, mix, step, after):
    pieces = len(blocks)
    depth = blocks[0].shape[1]
    rows = pieces * blocks[0].shape[0]
    columns = weight.shape[1] + lead_of(mix.shape[1], step.shape[0])
    half = jax.ShapeDtypeStruct((owners // 2, rows // owners, columns), BF16)
    whole = pl.BlockSpec(memory_space=pltpu.VMEM)
    anywhere = pl.BlockSpec(memory_space=pl.ANY)

    def body(*refs):
        project_signal_body(owners, order, *refs[:pieces], *refs[pieces + 1 :])

    return pl.pallas_call(
        body,
        out_shape=(half, half, jax.ShapeDtypeStruct((rows, depth), BF16)),
        in_specs=[anywhere] * (pieces + 1) + [whole] * 3,
        out_specs=(whole,) * 3,
        scratch_shapes=[pltpu.SemaphoreType.DMA((pieces,))],
        compiler_params=params(),
        cost_estimate=cost(2 * rows * depth * columns, 2 * depth * columns),
        name="project_signal",
    )(*blocks, after, in_vmem(weight), in_vmem(mix), step)


def project_gate_body(groups, *refs):
    lhs_refs, refs = refs[:groups], refs[groups:]
    weight_ref, after_ref, send_ref, keep_ref = refs
    rows = send_ref.shape[1]
    columns = weight_ref.shape[1]
    tile = min(columns, 512)
    first = group_of_own(groups)
    for t in range(0, columns, tile):
        for g, lhs_ref in enumerate(lhs_refs):
            acc = jnp.dot(lhs_ref[...], weight_ref[:, t : t + tile], preferred_element_type=F32)
            pairs = lhs_ref.shape[0] // (2 * rows)
            for k in range(2 * pairs):
                target = send_ref if k % 2 else keep_ref
                at = (first ^ g) * pairs + k // 2
                target[at, :, t : t + tile] = acc[k * rows : (k + 1) * rows].astype(target.dtype)


def group_of_own(groups):
    if groups == 1:
        return 0
    return (lax.axis_index("head") ^ 2 ^ lax.axis_index("row")) >> 1


def project_gate(rows, lhs, weight, after):
    count = sum(part.shape[0] for part in lhs) // rows
    columns = weight.shape[1]
    half = jax.ShapeDtypeStruct((count // 2, rows, columns), BF16)
    whole = pl.BlockSpec(memory_space=pltpu.VMEM)
    return pl.pallas_call(
        functools.partial(project_gate_body, len(lhs)),
        out_shape=(half, half),
        in_specs=[whole] * (len(lhs) + 1) + [pl.BlockSpec(memory_space=pl.ANY)],
        out_specs=(whole,) * 2,
        compiler_params=params(),
        cost_estimate=cost(2 * count * rows * lhs[0].shape[1] * columns, 2 * weight.size),
        name="project_gate",
    )(*lhs, in_vmem(weight), after)


def scatter_rows(received, keep, axis, done=1):
    send = received
    terms = [received] + (keep if isinstance(keep, list) else [keep])
    for distance in bits_of(lax.axis_size(axis))[done:]:
        send = sum(t[1::2].astype(F32) for t in terms).astype(BF16)
        terms = [swap(send, axis, distance)] + [t[0::2] for t in terms]
    return [t[0] for t in terms], send


def softplus(values):
    return jnp.maximum(values, 0.0) + jnp.log1p(jnp.exp(-jnp.abs(values)))


def silu(values):
    return values / (1.0 + jnp.exp(-values))


def inverse_of(sums_ref, width):
    return lax.rsqrt(sums_ref[:, sums_ref.shape[1] - 1 :] / width + EPSILON)


def read_body(terms, group, model_width, live_ref, *refs):
    term_refs = refs[:terms]
    sums_ref, up_ref, bias_ref, rate_ref, skip_ref, source_ref, _ = refs[terms : terms + 7]
    adapted_ref, read_ref, spread_ref, b_ref, both_ref, state_ref, *scratch = refs[terms + 7 :]
    c_ref, semaphores = scratch
    heads, head, width = state_ref.shape[1:]
    streams, inner = read_ref.shape[1:]
    step = pl.program_id(0)

    def fetch(i):
        at = pl.ds(i * group, group)
        return pltpu.make_async_copy(source_ref.at[at], state_ref.at[at], semaphores.at[i])

    @pl.when(step == 0)
    def _():
        for i in range(streams // group):
            fetch(i).start()
        rows = sums_ref.shape[0]
        rank = sums_ref.shape[1] - 1
        inverse = inverse_of(sums_ref, model_width)
        total = sum(t[:, : 2 * width + heads].astype(F32) for t in term_refs) * inverse
        gates = silu(total[:, : 2 * width])
        steps_dt = softplus(total[:, 2 * width :] + bias_ref[...])
        b = [gates[p * streams : (p + 1) * streams, :width] for p in range(2)]
        c = [gates[p * streams : (p + 1) * streams, width:] for p in range(2)]
        for p in range(2):
            b_ref[p] = b[p]
            c_ref[p] = c[p]
        live = lax.broadcasted_iota(jnp.int32, (streams, heads), 0) < live_ref[0]
        dt = [steps_dt[p * streams : (p + 1) * streams] for p in range(2)]
        decay = [jnp.where(live, jnp.exp(-d * rate_ref[...]), 1.0) for d in dt]
        fed = [jnp.where(live, d, 0.0) for d in dt]

        def match(i, j):
            return jnp.sum(b[i] * c[j], -1, keepdims=True)

        both = decay[0] * decay[1]
        both_ref[...] = both
        late = decay[1] * fed[0]
        skip = skip_ref[...]
        factors = jnp.concatenate(
            [
                decay[0],
                both,
                fed[0] * match(0, 0) + skip,
                fed[1] * match(1, 1) + skip,
                late * match(0, 1),
                late,
                fed[1],
            ],
            0,
        )
        high, low = split(factors)
        place = lax.broadcasted_iota(jnp.int32, (heads, inner), 1) // head
        ones = (place == lax.broadcasted_iota(jnp.int32, (heads, inner), 0)).astype(BF16)
        spread_ref[...] = jnp.dot(high, ones, preferred_element_type=F32) + jnp.dot(
            low, ones, preferred_element_type=F32
        )
        lowrank = (sums_ref[:, :rank] * inverse).astype(BF16)
        repeat = lax.broadcasted_iota(jnp.int32, (rank, streams * rank), 1) % rank
        repeat = (repeat == lax.broadcasted_iota(jnp.int32, (rank, streams * rank), 0)).astype(BF16)
        every = jnp.dot(lowrank, repeat, preferred_element_type=F32)
        own = jnp.where(own_columns(rows, streams, rank), every, 0.0).astype(BF16)
        adapted_ref[...] = jnp.dot(own, up_ref[...], preferred_element_type=F32)

    fetch(step).wait()
    at = pl.multiple_of(step * group, group)
    c = jnp.concatenate([c_ref[p, pl.ds(at, group), :] for p in range(2)], 0)
    lhs = jnp.concatenate(split(c), 0)
    for g in range(group):
        state = state_ref[at + g].reshape(inner, width)
        found = lax.dot_general(lhs, state, (((1,), (1,)), ((), ())), preferred_element_type=F32)
        for p in range(2):
            row = p * group + g
            low = 2 * group + row
            read_ref[p, pl.ds(at + g, 1), :] = found[row : row + 1] + found[low : low + 1]


def read_state(model_width, after, live_rows, terms, sums, up_rows, bias, rate, skip, state):
    streams, heads, head, width = state.shape
    group = 8
    inner = heads * head
    rows = 2 * streams
    whole = pl.BlockSpec(memory_space=pltpu.VMEM)
    return pl.pallas_call(
        functools.partial(read_body, len(terms), group, model_width),
        out_shape=(
            jax.ShapeDtypeStruct((rows, inner), F32),
            jax.ShapeDtypeStruct((2, streams, inner), F32),
            jax.ShapeDtypeStruct((7 * streams, inner), F32),
            jax.ShapeDtypeStruct((2, streams, width), F32),
            jax.ShapeDtypeStruct((streams, heads), F32),
            pltpu.VMEM(state.shape, state.dtype),
        ),
        grid=(streams // group,),
        in_specs=[pl.BlockSpec(memory_space=pltpu.SMEM)]
        + [whole] * (len(terms) + 5)
        + [pl.BlockSpec(memory_space=pl.ANY)] * 2,
        out_specs=(whole,) * 6,
        scratch_shapes=[
            pltpu.VMEM((2, streams, width), F32),
            pltpu.SemaphoreType.DMA((streams // group,)),
        ],
        compiler_params=params(),
        cost_estimate=cost(64 * state.size, 2 * state.size + 32 * rows * inner),
        name="read_state",
    )(
        live_rows,
        *terms,
        sums,
        up_rows,
        bias[None],
        rate[None],
        skip[None],
        in_hbm(state),
        after,
    )


def state_write_body(feeds_ref, b_ref, decay_ref, state_ref, out_ref):
    group, heads, head, width = out_ref.shape
    at = pl.multiple_of(pl.program_id(0) * group, group)
    feeds = [split(feeds_ref[p, pl.ds(at, group), :]) for p in range(2)]
    rights = [split(b_ref[p, pl.ds(at, group), :]) for p in range(2)]
    left = [f.astype(F32) for pair in feeds for f in (pair[0], pair[1], pair[0])]
    right = [f.astype(F32) for pair in rights for f in (pair[0], pair[0], pair[1])]
    left = jnp.concatenate(left, 0).astype(BF16)
    right = jnp.concatenate(right, 0)
    stream = lax.broadcasted_iota(jnp.int32, right.shape, 0) % group
    for g in range(0, group, 2):
        pair = jnp.concatenate([jnp.where(stream == g + i, right, 0.0) for i in range(2)], 1)
        outer = lax.dot_general(
            left, pair.astype(BF16), (((0,), (0,)), ((), ())), preferred_element_type=F32
        )
        for i in range(2):
            scaled = state_ref[at + g + i].astype(F32) * decay_ref[g + i][:, None, :]
            own = outer[:, i * width : (i + 1) * width].reshape(heads, head, width)
            out_ref[g + i] = (scaled + own).astype(out_ref.dtype)


def state_write(feeds, b, decay, state):
    streams, heads, head, width = state.shape
    group = 8
    whole = pl.BlockSpec(memory_space=pltpu.VMEM)
    return pl.pallas_call(
        state_write_body,
        out_shape=jax.ShapeDtypeStruct(state.shape, state.dtype),
        grid=(streams // group,),
        in_specs=[
            whole,
            whole,
            pl.BlockSpec((group, heads, width), lambda i: (i, 0, 0)),
            whole,
        ],
        out_specs=pl.BlockSpec((group, heads, head, width), lambda i: (i, 0, 0, 0)),
        compiler_params=params(),
        cost_estimate=cost(32 * state.size, 4 * state.size),
        name="state_write",
    )(feeds, b, decay, state)


def output_tiles(distances, lhs_ref, weight_refs, out_ref):
    width = out_ref.shape[2] // 256 * 256
    tile = min(width, 512)
    for j, distance in enumerate(distances):
        for t in range(0, width, tile):
            at = pl.multiple_of((lax.axis_index("head") ^ distance) * width + t, tile)
            acc, start = 0.0, 0
            for weight_ref in weight_refs:
                stop = start + weight_ref.shape[0]
                acc += jnp.dot(
                    lhs_ref[:, start:stop],
                    weight_ref[:, pl.ds(at, tile)],
                    preferred_element_type=F32,
                )
                start = stop
            out_ref[j, :, t : t + tile] = acc.astype(out_ref.dtype)


def put_lanes(values, out_ref, j):
    lane = lax.broadcasted_iota(jnp.int32, (values.shape[0], LANES), 1)
    tail = jnp.zeros(lane.shape, F32)
    for i in range(3):
        term = values.astype(BF16).astype(F32)
        tail = jnp.where(lane == i, term, tail)
        values = values - term
    out_ref[j, :, out_ref.shape[2] - LANES :] = tail.astype(out_ref.dtype)


def meet_body(met_ref, own_ref, squares_ref, out_ref, total_ref):
    count = met_ref.shape[0]
    width = own_ref.shape[2]
    total = squares_ref[...] + join_lanes(met_ref[0, :, width:])
    total_ref[...] = total
    for j in range(count):
        both = met_ref[j, :, :width].astype(F32) + own_ref[j].astype(F32)
        out_ref[j, :, :width] = both.astype(out_ref.dtype)
        put_lanes(total, out_ref, j)


def meet(met, own, squares):
    whole = pl.BlockSpec(memory_space=pltpu.VMEM)
    return pl.pallas_call(
        meet_body,
        out_shape=(
            jax.ShapeDtypeStruct(met.shape, met.dtype),
            jax.ShapeDtypeStruct(squares.shape, squares.dtype),
        ),
        in_specs=[whole] * 3,
        out_specs=(whole, whole),
        compiler_params=params(),
        cost_estimate=cost(met.size, 6 * met.size),
        name="meet",
    )(met, own, squares)


def join_lanes(values):
    return jnp.sum(values.astype(F32), -1, keepdims=True)


def output_first_body(distances, terms, model_width, *refs):
    gate_refs, signal_refs, refs = refs[:terms], refs[terms : 2 * terms], refs[2 * terms :]
    sums_ref, adapted_ref, read_ref, spread_ref, scale_ref, *weight_refs = refs[:-4]
    out_ref, lhs_ref, squares_ref, feeds_ref = refs[-4:]
    streams, inner = read_ref.shape[1:]
    inverse = inverse_of(sums_ref, model_width)
    total = sum(t[:, t.shape[1] - inner :].astype(F32) for t in signal_refs)
    signal = silu(total * inverse + adapted_ref[...])
    first, second = signal[:streams], signal[streams:]
    factor = [spread_ref[i * streams : (i + 1) * streams, :] for i in range(7)]
    feeds_ref[0] = factor[5] * first
    feeds_ref[1] = factor[6] * second
    result = [
        factor[0] * read_ref[0] + factor[2] * first,
        factor[1] * read_ref[1] + factor[4] * first + factor[3] * second,
    ]
    total = sum(t[...].astype(F32) for t in gate_refs) * inverse
    gated = jnp.concatenate(result, 0) * silu(total)
    squares_ref[...] = jnp.sum(gated * gated, -1, keepdims=True)
    lhs_ref[...] = (gated * scale_ref[...]).astype(lhs_ref.dtype)
    output_tiles(distances, lhs_ref, weight_refs, out_ref)
    for j in range(len(distances)):
        put_lanes(squares_ref[...], out_ref, j)


def put_lanes(values, out_ref, j):
    lane = lax.broadcasted_iota(jnp.int32, (values.shape[0], LANES), 1)
    tail = jnp.zeros(lane.shape, F32)
    for i in range(3):
        term = values.astype(BF16).astype(F32)
        tail = jnp.where(lane == i, term, tail)
        values = values - term
    out_ref[j, :, out_ref.shape[2] - LANES :] = tail.astype(out_ref.dtype)


def meet_body(met_ref, own_ref, squares_ref, out_ref, total_ref):
    count = met_ref.shape[0]
    width = own_ref.shape[2]
    total = squares_ref[...] + join_lanes(met_ref[0, :, width:])
    total_ref[...] = total
    for j in range(count):
        both = met_ref[j, :, :width].astype(F32) + own_ref[j].astype(F32)
        out_ref[j, :, :width] = both.astype(out_ref.dtype)
        put_lanes(total, out_ref, j)


def meet(met, own, squares):
    whole = pl.BlockSpec(memory_space=pltpu.VMEM)
    return pl.pallas_call(
        meet_body,
        out_shape=(
            jax.ShapeDtypeStruct(met.shape, met.dtype),
            jax.ShapeDtypeStruct(squares.shape, squares.dtype),
        ),
        in_specs=[whole] * 3,
        out_specs=(whole, whole),
        compiler_params=params(),
        cost_estimate=cost(met.size, 6 * met.size),
        name="meet",
    )(met, own, squares)


def join_lanes(values):
    return jnp.sum(values.astype(F32), -1, keepdims=True)


def output_rest_body(distances, lhs_ref, after_ref, *refs):
    output_tiles(distances, lhs_ref, refs[:-1], refs[-1])


def output_parts(distances, weights, width, operands, model_width=None, terms=None):
    first = model_width is not None
    rows, depth = operands[0].shape
    count = len(distances)
    whole = pl.BlockSpec(memory_space=pltpu.VMEM)
    specs = [whole] * (len(operands) + len(weights))
    body = functools.partial(output_rest_body, distances)
    extra = LANES if first else 0
    out_shape = [jax.ShapeDtypeStruct((count, rows, width + extra), BF16)]
    if first:
        body = functools.partial(output_first_body, distances, terms, model_width)
        out_shape += [
            jax.ShapeDtypeStruct((rows, depth), BF16),
            jax.ShapeDtypeStruct((rows, 1), F32),
            jax.ShapeDtypeStruct((2, rows // 2, depth), F32),
        ]
    else:
        specs[1] = pl.BlockSpec(memory_space=pl.ANY)
    return pl.pallas_call(
        body,
        out_shape=tuple(out_shape),
        in_specs=specs,
        out_specs=(whole,) * len(out_shape),
        compiler_params=params(),
        cost_estimate=cost(2 * rows * depth * width * count, 2 * depth * width * count),
        name="output_first" if first else "output_rest",
    )(*operands, *[in_vmem(w) for w in weights])


def split(values):
    high = values.astype(BF16)
    return high, (values - high.astype(F32)).astype(BF16)


def on_device(
    hidden,
    input_norm_scale,
    projection_signal,
    projection_gate,
    projection_step,
    projection_input_output,
    step_bias,
    head_decay_rate,
    head_skip_weight,
    gated_norm_scale,
    adapter_down_weight,
    adapter_up_weight,
    output_weight,
    scan_state,
    stream_tenant_index,
    live_block_rows,
):
    streams, positions, feature_width = hidden.shape
    rows = streams * positions
    heads_n = lax.axis_size("head")
    rows_n = lax.axis_size("row")
    model_width = feature_width * heads_n
    depth, inner = projection_signal.shape
    inner_width = inner * heads_n

    wide = jnp.swapaxes(hidden, 0, 1).astype(F32)
    scaled = (wide * input_norm_scale).astype(BF16)
    scaled_flat = scaled.reshape(rows, feature_width)

    squares = jnp.sum(wide * wide, -1).reshape(rows, 1)
    sums, up_rows = adapt(stream_tenant_index, scaled_flat, squares, adapter_down_weight, adapter_up_weight)

    own = group_of_own(2) == 0
    sums, own = lax.optimization_barrier((sums, own))
    middle = output_weight.shape[0] // 2
    *weights, out_early = load(
        sums,
        [],
        projection_signal,
        projection_input_output,
        projection_gate,
        (output_weight, 0, middle),
    )
    signal_weights = (*weights[:2], projection_step.T)
    if heads_n == rows_n and len(bits_of(rows_n)) == 2:
        turn = [
            (h * rows_n + r, (r ^ 2) * rows_n + h) for h in range(heads_n) for r in range(rows_n)
        ]
        turned = lax.ppermute(scaled_flat, ("head", "row"), turn)
        turned, _ = lax.optimization_barrier((turned, weights[0]))
        crossed = swap(turned, "head", 2)

        def order(distance):
            return [
                (lambda d=d: lax.axis_index("head") ^ 2 ^ d, 0) for d in (distance, distance ^ 1)
            ]

        near = [turned, swap(turned, "head", 1)]
        (out_late,) = load(turned, [], (output_weight, middle, middle))
        crossed, _ = lax.optimization_barrier((crossed, out_late))
        far = [crossed, swap(crossed, "head", 1)]
        near_send, near_keep, near_lhs = project_signal(near, order(0), 2, *signal_weights, crossed)
        near_other = swap(near_send, "row", 1)
        far_send, far_keep, far_lhs = project_signal(far, order(2), 2, *signal_weights, near_send)
        far_other = swap(far_send, "row", 1)
        sums, _ = lax.optimization_barrier((sums, far_send))
        sums = sum_over(sums, "head")
        gate_send, gate_keep = project_gate(rows, [near_lhs, far_lhs], weights[2], far_send)
        gate_far = swap(gate_send[1:], "row", 1)
        pick = [(near_keep, far_keep), (near_other, far_other)]
        last_send = sum(jnp.where(own, f, n).astype(F32) for n, f in pick).astype(BF16)
        last_send, sums = lax.optimization_barrier((last_send, sums))
        lead = last_send.shape[-1] - inner
        last_other = [swap(part, "row", 2) for part in jnp.split(last_send, [lead], -1)]
        kept = [jnp.where(own, n, f)[0] for n, f in pick]
        lead_terms = [last_other[0][0]] + kept
        signal_terms = [last_other[1][0]] + kept
        gate_far, _ = lax.optimization_barrier((gate_far, last_other[0]))
        gate_last = (gate_far.astype(F32) + gate_keep[1:].astype(F32)).astype(BF16)
        own_send, _ = lax.optimization_barrier((gate_send[:1], last_other[0]))
        gate_terms = [
            swap_halves(gate_last, "row", 2, 1)[0],
            swap(own_send, "row", 1)[0],
            gate_keep[0],
        ]
    else:
        features = lax.all_gather(scaled_flat, "head", axis=1, tiled=True)
        blocks = lax.all_to_all(features, "row", split_axis=1, concat_axis=0, tiled=True)
        blocks = blocks.reshape(rows_n, rows, depth)
        blocks = [blocks[i] for i in range(rows_n)]
        order = [(lambda i=i: i, 0) for i in range(rows_n)]
        send, keep, lhs = project_signal(blocks, order, rows_n, *signal_weights, sums)
        received = swap(send, "row", 1)
        gate_send, gate_keep = project_gate(rows, [lhs], weights[2], send)
        sums = sum_over(sums, "head")
        keep, out_late = load(gate_send, [keep], (output_weight, middle, middle))
        signal_terms, _ = scatter_rows(received, keep, "row")
        lead_terms = signal_terms
        gate_terms, gate_last = scatter_rows(swap(gate_send, "row", 1), gate_keep, "row")
    out_weights = [out_early, out_late]

    adapted, read, spread, bgate, both, state = read_state(
        model_width,
        gate_last,
        live_block_rows,
        lead_terms,
        sums,
        up_rows,
        step_bias,
        head_decay_rate,
        head_skip_weight,
        scan_state,
    )

    distances = list(range(heads_n))
    first, out_lhs, gate_squares, feeds = output_parts(
        distances[3::4],
        out_weights,
        feature_width,
        [
            *gate_terms,
            *signal_terms,
            sums,
            adapted,
            read,
            spread,
            gated_norm_scale[None],
        ],
        model_width,
        len(gate_terms),
    )
    (second,) = output_parts(
        distances[2::4] + distances[1::4], out_weights, feature_width, [out_lhs, first]
    )
    half = second.shape[0] // 2
    send, gate_squares = meet(swap(first, "head", 1), second, gate_squares)
    (rest,) = output_parts(distances[0::4], out_weights, feature_width, [out_lhs, send])
    feeds, _ = lax.optimization_barrier((feeds, rest))
    kept = [swap(second[half:], "head", 1), rest]
    if len(bits_of(heads_n)) == 2:
        received = swap_halves(send, "head", 2, 1)
        mixer = sum(t[0].astype(F32) for t in [received[..., :feature_width]] + kept)
        gate_squares = gate_squares + join_lanes(received[0, :, feature_width:])
    else:
        received = swap(send[..., :feature_width], "head", 2)
        mixer, _ = scatter_rows(received, kept, "head", done=2)
        mixer = sum(t.astype(F32) for t in mixer)
        for distance in bits_of(heads_n)[1:]:
            gate_squares = gate_squares + swap(gate_squares, "head", distance)
    mixer = mixer * lax.rsqrt(gate_squares / inner_width + EPSILON)
    mixer = mixer.reshape(positions, streams, feature_width)
    live = jnp.arange(streams) < live_block_rows[0]
    mixed = (wide + jnp.where(live[:, None], mixer, 0.0)).astype(BF16)

    decays = jnp.broadcast_to(both[..., None], both.shape + (bgate.shape[-1],))
    new_state = state_write(feeds, bgate, decays, state)
    return (jnp.swapaxes(mixed, 0, 1), new_state)


def solution(mesh):
    in_specs = (
        P(("rep", "row"), None, "head"),
        P("head"),
        P("row", "head"),
        P("row", "head"),
        P("row", "head"),
        P("row", None),
        P("head"),
        P("head"),
        P("head"),
        P("head"),
        P("row", "head", None),
        P("row", None, "head"),
        P("head", None),
        P(("rep", "row"), "head", None, None),
        P(("rep", "row")),
        P(("rep", "row")),
    )
    out_specs = (P(("rep", "row"), None, "head"), P(("rep", "row"), "head", None, None))
    return jax.shard_map(
        on_device, mesh=mesh, in_specs=in_specs, out_specs=out_specs, check_vma=False
    )
```

```python
import functools

import jax
import jax.numpy as jnp
from jax import lax
from jax.experimental import pallas as pl
from jax.experimental.pallas import tpu as pltpu
from jax.sharding import PartitionSpec as P

BF16 = jnp.bfloat16
EPSILON = 1e-05
F32 = jnp.float32
VMEM_GRANT = 12 * 1024 * 1024


def swap(values, axis, distance):
    size = lax.axis_size(axis)
    return lax.ppermute(values, axis, [(i, i ^ distance) for i in range(size)])


def swap_halves(values, axis, distance, dim):
    return jnp.concatenate([swap(v, axis, distance) for v in jnp.split(values, 2, dim)], dim)


def bits_of(size):
    return [1 << i for i in range(size.bit_length() - 1)]


def sum_over(values, axis):
    for distance in bits_of(lax.axis_size(axis)):
        values = values + swap(values, axis, distance)
    return values


def reverse_bits(value, size):
    bits = size.bit_length() - 1
    return sum(((value >> i) & 1) << (bits - 1 - i) for i in range(bits))


def params(**more):
    return pltpu.CompilerParams(vmem_limit_bytes=VMEM_GRANT, **more)


def cost(flops, size):
    return pl.CostEstimate(flops=int(flops), bytes_accessed=int(size), transcendentals=0)


def in_hbm(values):
    return pltpu.with_memory_space_constraint(values, pltpu.HBM)


def in_vmem(values):
    return pltpu.with_memory_space_constraint(values, pltpu.VMEM)


def load_body(spans, after_ref, *refs):
    count = len(spans)
    sources, targets, semaphores = refs[:count], refs[count : 2 * count], refs[2 * count]
    copies = []
    for source, target, (start, rows, parts) in zip(sources, targets, spans):
        step = rows // parts
        for i in range(parts):
            copies.append(
                pltpu.make_async_copy(
                    source.at[pl.ds(start + i * step, step)],
                    target.at[pl.ds(i * step, step)],
                    semaphores.at[len(copies)],
                )
            )
    for copy in copies:
        copy.start()
    for copy in copies:
        copy.wait()


def load(after, passed, *weights):
    weights = [w if isinstance(w, tuple) else (w, 0, w.shape[0]) for w in weights]
    shapes = [p.shape for p in passed] + [(rows, *w.shape[1:]) for w, _, rows in weights]
    spans = [(0, p.shape[0], 1) for p in passed]
    spans += [(start, rows, 8 if rows % 128 == 0 else 1) for _, start, rows in weights]
    size = sum(rows * w.shape[1] * w.dtype.itemsize for w, _, rows in weights)
    return pl.pallas_call(
        functools.partial(load_body, spans),
        out_shape=tuple(pltpu.VMEM(shape, BF16) for shape in shapes),
        in_specs=[pl.BlockSpec(memory_space=pl.ANY)] * (1 + len(shapes)),
        out_specs=tuple(pl.BlockSpec(memory_space=pltpu.VMEM) for _ in shapes),
        scratch_shapes=[pltpu.SemaphoreType.DMA((sum(parts for _, _, parts in spans),))],
        compiler_params=params(),
        cost_estimate=cost(0, 2 * size),
        name="load",
    )(after, *passed, *[in_hbm(w) for w, _, _ in weights])


def own_columns(rows, streams, rank):
    row = lax.broadcasted_iota(jnp.int32, (rows, streams * rank), 0) % streams
    return row == lax.broadcasted_iota(jnp.int32, (rows, streams * rank), 1) // rank


def adapt_body(tenant_ref, scaled_ref, squares_ref, down_ref, up_ref, sums_ref, up_rows_ref, *scratch):
    down_rows_ref, semaphores = scratch
    rank = down_ref.shape[1]
    streams = tenant_ref.shape[0]
    rows = scaled_ref.shape[0]
    first = lax.axis_index("row") * down_ref.shape[0]
    downs, ups = [], []
    for s in range(streams):
        at = pl.ds(s * rank, rank)
        tenant = tenant_ref[s] - first
        downs.append(
            pltpu.make_async_copy(down_ref.at[tenant], down_rows_ref.at[at, :], semaphores.at[s])
        )
        ups.append(
            pltpu.make_async_copy(
                up_ref.at[tenant], up_rows_ref.at[at, :], semaphores.at[streams + s]
            )
        )
    for copy in downs + ups:
        copy.start()
    for copy in downs:
        copy.wait()
    every = lax.dot_general(
        scaled_ref[...],
        down_rows_ref[...],
        (((1,), (1,)), ((), ())),
        preferred_element_type=F32,
    )
    own = jnp.where(own_columns(rows, streams, rank), every, 0.0)
    fold = lax.broadcasted_iota(jnp.int32, (streams * rank, rank), 0) % rank
    fold = (fold == lax.broadcasted_iota(jnp.int32, (streams * rank, rank), 1)).astype(BF16)
    high, rest = split(own)
    middle, low = rest, (own - high.astype(F32) - rest.astype(F32)).astype(BF16)
    folded = sum(jnp.dot(x, fold, preferred_element_type=F32) for x in (high, middle, low))
    sums_ref[:, :rank] = folded
    sums_ref[:, rank:] = squares_ref[...]
    for copy in ups:
        copy.wait()


def adapt(tenants, scaled, squares, down, up):
    streams = tenants.shape[0]
    rows, depth = scaled.shape
    rank, inner = up.shape[1:]
    whole = pl.BlockSpec(memory_space=pltpu.VMEM)
    anywhere = pl.BlockSpec(memory_space=pl.ANY)
    return pl.pallas_call(
        adapt_body,
        out_shape=(
            jax.ShapeDtypeStruct((rows, rank + 1), F32),
            pltpu.VMEM((streams * rank, inner), BF16),
        ),
        in_specs=[pl.BlockSpec(memory_space=pltpu.SMEM), whole, whole, anywhere, anywhere],
        out_specs=(whole, whole),
        scratch_shapes=[
            pltpu.VMEM((streams * rank, depth), BF16),
            pltpu.SemaphoreType.DMA((2 * streams,)),
        ],
        compiler_params=params(),
        cost_estimate=cost(2 * rows * depth * streams * rank, 2 * streams * rank * (depth + inner)),
        name="adapt",
    )(tenants, scaled, squares, in_hbm(jnp.swapaxes(down, 1, 2)), in_hbm(up))


def project_signal_body(owners, order, *refs):
    blocks, refs = refs[: len(order)], refs[len(order) :]
    weight_ref, mix_ref, step_ref, send_ref, keep_ref, lhs_ref, semaphores = refs
    rows = blocks[0].shape[0]
    parts = len(blocks) // owners
    copies = []
    for i, block in enumerate(blocks):
        owner, part = order[i]
        away = (owner() ^ lax.axis_index("row")) % owners
        at = pl.multiple_of((away * parts + part) * rows, rows)
        copies.append(
            pltpu.make_async_copy(block, lhs_ref.at[pl.ds(at, rows), :], semaphores.at[i])
        )
    for copy in copies:
        copy.start()
    for copy in copies:
        copy.wait()
    lhs = lhs_ref[...]

    def put(acc, start):
        step = send_ref.shape[1]
        for k in range(owners):
            target = send_ref if k % 2 else keep_ref
            target[k // 2, :, start : start + acc.shape[1]] = acc[k * step : (k + 1) * step].astype(
                target.dtype
            )

    columns = weight_ref.shape[1]
    tile = min(columns, 512)
    for t in range(0, columns, tile):
        put(jnp.dot(lhs, weight_ref[:, t : t + tile], preferred_element_type=F32), t)
    put(jnp.dot(lhs, mix_ref[...], preferred_element_type=F32), columns)
    acc = lax.dot_general(lhs, step_ref[...], (((1,), (1,)), ((), ())), preferred_element_type=F32)
    put(acc, columns + mix_ref.shape[1])


def project_signal(blocks, order, owners, weight, mix, step, after):
    pieces = len(blocks)
    depth = blocks[0].shape[1]
    rows = pieces * blocks[0].shape[0]
    columns = weight.shape[1] + mix.shape[1] + step.shape[0]
    half = jax.ShapeDtypeStruct((owners // 2, rows // owners, columns), BF16)
    whole = pl.BlockSpec(memory_space=pltpu.VMEM)
    anywhere = pl.BlockSpec(memory_space=pl.ANY)

    def body(*refs):
        project_signal_body(owners, order, *refs[:pieces], *refs[pieces + 1 :])

    return pl.pallas_call(
        body,
        out_shape=(half, half, jax.ShapeDtypeStruct((rows, depth), BF16)),
        in_specs=[anywhere] * (pieces + 1) + [whole] * 3,
        out_specs=(whole,) * 3,
        scratch_shapes=[pltpu.SemaphoreType.DMA((pieces,))],
        compiler_params=params(),
        cost_estimate=cost(2 * rows * depth * columns, 2 * depth * columns),
        name="project_signal",
    )(*blocks, after, in_vmem(weight), in_vmem(mix), step)


def project_gate_body(groups, *refs):
    lhs_refs, refs = refs[:groups], refs[groups:]
    weight_ref, after_ref, send_ref, keep_ref = refs
    rows = send_ref.shape[1]
    columns = weight_ref.shape[1]
    tile = min(columns, 512)
    first = group_of_own(groups)
    for t in range(0, columns, tile):
        for g, lhs_ref in enumerate(lhs_refs):
            acc = jnp.dot(lhs_ref[...], weight_ref[:, t : t + tile], preferred_element_type=F32)
            pairs = lhs_ref.shape[0] // (2 * rows)
            for k in range(2 * pairs):
                target = send_ref if k % 2 else keep_ref
                at = (first ^ g) * pairs + k // 2
                target[at, :, t : t + tile] = acc[k * rows : (k + 1) * rows].astype(target.dtype)


def group_of_own(groups):
    if groups == 1:
        return 0
    return (lax.axis_index("head") ^ 2 ^ lax.axis_index("row")) >> 1


def project_gate(rows, lhs, weight, after):
    count = sum(part.shape[0] for part in lhs) // rows
    columns = weight.shape[1]
    half = jax.ShapeDtypeStruct((count // 2, rows, columns), BF16)
    whole = pl.BlockSpec(memory_space=pltpu.VMEM)
    return pl.pallas_call(
        functools.partial(project_gate_body, len(lhs)),
        out_shape=(half, half),
        in_specs=[whole] * (len(lhs) + 1) + [pl.BlockSpec(memory_space=pl.ANY)],
        out_specs=(whole,) * 2,
        compiler_params=params(),
        cost_estimate=cost(2 * count * rows * lhs[0].shape[1] * columns, 2 * weight.size),
        name="project_gate",
    )(*lhs, in_vmem(weight), after)


def scatter_rows(received, keep, axis, done=1):
    send = received
    terms = [received] + (keep if isinstance(keep, list) else [keep])
    for distance in bits_of(lax.axis_size(axis))[done:]:
        send = sum(t[1::2].astype(F32) for t in terms).astype(BF16)
        terms = [swap(send, axis, distance)] + [t[0::2] for t in terms]
    return [t[0] for t in terms], send


def softplus(values):
    return jnp.maximum(values, 0.0) + jnp.log1p(jnp.exp(-jnp.abs(values)))


def silu(values):
    return values / (1.0 + jnp.exp(-values))


def inverse_of(sums_ref, width):
    return lax.rsqrt(sums_ref[:, sums_ref.shape[1] - 1 :] / width + EPSILON)


def recur_body(
    terms,
    group,
    model_width,
    live_ref,
    *refs,
):
    term_refs = refs[:terms]
    sums_ref, up_ref, bias_ref, rate_ref, skip_ref, source_ref, _ = refs[terms : terms + 7]
    result_ref, feeds_ref, b_ref, both_ref, state_ref, *scratch = refs[terms + 7 :]
    c_ref, read_ref, spread_ref, signal_ref, semaphores = scratch
    heads, head, width = state_ref.shape[1:]
    streams, inner = feeds_ref.shape[1:]
    step = pl.program_id(0)

    def fetch(i):
        at = pl.ds(i * group, group)
        return pltpu.make_async_copy(source_ref.at[at], state_ref.at[at], semaphores.at[i])

    @pl.when(step == 0)
    def _():
        for i in range(streams // group):
            fetch(i).start()
        rows = sums_ref.shape[0]
        rank = sums_ref.shape[1] - 1
        inverse = inverse_of(sums_ref, model_width)
        lowrank = (sums_ref[:, :rank] * inverse).astype(BF16)
        repeat = lax.broadcasted_iota(jnp.int32, (rank, streams * rank), 1) % rank
        repeat = (repeat == lax.broadcasted_iota(jnp.int32, (rank, streams * rank), 0)).astype(BF16)
        every = jnp.dot(lowrank, repeat, preferred_element_type=F32)
        own = jnp.where(own_columns(rows, streams, rank), every, 0.0).astype(BF16)
        adapted = jnp.dot(own, up_ref[...], preferred_element_type=F32)
        total = sum(t[...].astype(F32) for t in term_refs) * inverse
        signal_ref[...] = silu(total[:, :inner] + adapted)
        gates = silu(total[:, inner : inner + 2 * width])
        steps_dt = softplus(total[:, inner + 2 * width :] + bias_ref[...])
        b = [gates[p * streams : (p + 1) * streams, :width] for p in range(2)]
        c = [gates[p * streams : (p + 1) * streams, width:] for p in range(2)]
        for p in range(2):
            b_ref[p] = b[p]
            c_ref[p] = c[p]
        live = lax.broadcasted_iota(jnp.int32, (streams, heads), 0) < live_ref[0]
        dt = [steps_dt[p * streams : (p + 1) * streams] for p in range(2)]
        decay = [jnp.where(live, jnp.exp(-d * rate_ref[...]), 1.0) for d in dt]
        fed = [jnp.where(live, d, 0.0) for d in dt]

        def match(i, j):
            return jnp.sum(b[i] * c[j], -1, keepdims=True)

        both = decay[0] * decay[1]
        both_ref[...] = both
        late = decay[1] * fed[0]
        skip = skip_ref[...]
        factors = jnp.concatenate(
            [
                decay[0],
                both,
                fed[0] * match(0, 0) + skip,
                fed[1] * match(1, 1) + skip,
                late * match(0, 1),
                late,
                fed[1],
            ],
            0,
        )
        high, low = split(factors)
        place = lax.broadcasted_iota(jnp.int32, (heads, inner), 1) // head
        ones = (place == lax.broadcasted_iota(jnp.int32, (heads, inner), 0)).astype(BF16)
        spread_ref[...] = jnp.dot(high, ones, preferred_element_type=F32) + jnp.dot(
            low, ones, preferred_element_type=F32
        )

    fetch(step).wait()
    at = pl.multiple_of(step * group, group)
    c = jnp.concatenate([c_ref[p, pl.ds(at, group), :] for p in range(2)], 0)
    lhs = jnp.concatenate(split(c), 0)
    for g in range(group):
        state = state_ref[at + g].reshape(inner, width)
        found = lax.dot_general(lhs, state, (((1,), (1,)), ((), ())), preferred_element_type=F32)
        for p in range(2):
            row = p * group + g
            low = 2 * group + row
            read_ref[p, pl.ds(at + g, 1), :] = found[row : row + 1] + found[low : low + 1]

    @pl.when(step == pl.num_programs(0) - 1)
    def _():
        factor = [spread_ref[i * streams : (i + 1) * streams, :] for i in range(7)]
        first = signal_ref[:streams, :]
        second = signal_ref[streams:, :]
        result_ref[:streams, :] = factor[0] * read_ref[0] + factor[2] * first
        result_ref[streams:, :] = factor[1] * read_ref[1] + factor[4] * first + factor[3] * second
        feeds_ref[0] = factor[5] * first
        feeds_ref[1] = factor[6] * second


def recur(model_width, after, live_rows, terms, sums, up_rows, bias, rate, skip, state):
    streams, heads, head, width = state.shape
    group = 8
    inner = heads * head
    rows = 2 * streams
    whole = pl.BlockSpec(memory_space=pltpu.VMEM)
    return pl.pallas_call(
        functools.partial(recur_body, len(terms), group, model_width),
        out_shape=(
            jax.ShapeDtypeStruct((rows, inner), F32),
            jax.ShapeDtypeStruct((2, streams, inner), F32),
            jax.ShapeDtypeStruct((2, streams, width), F32),
            jax.ShapeDtypeStruct((streams, heads), F32),
            pltpu.VMEM(state.shape, state.dtype),
        ),
        grid=(streams // group,),
        in_specs=[pl.BlockSpec(memory_space=pltpu.SMEM)]
        + [whole] * (len(terms) + 5)
        + [pl.BlockSpec(memory_space=pl.ANY)] * 2,
        out_specs=(whole,) * 5,
        scratch_shapes=[
            pltpu.VMEM((2, streams, width), F32),
            pltpu.VMEM((2, streams, inner), F32),
            pltpu.VMEM((7 * streams, inner), F32),
            pltpu.VMEM((rows, inner), F32),
            pltpu.SemaphoreType.DMA((streams // group,)),
        ],
        compiler_params=params(),
        cost_estimate=cost(64 * state.size, 2 * state.size + 32 * rows * inner),
        name="recur",
    )(
        live_rows,
        *terms,
        sums,
        up_rows,
        bias[None],
        rate[None],
        skip[None],
        in_hbm(state),
        after,
    )


def state_write_body(feeds_ref, b_ref, decay_ref, state_ref, out_ref):
    group, heads, head, width = out_ref.shape
    at = pl.multiple_of(pl.program_id(0) * group, group)
    feeds = [split(feeds_ref[p, pl.ds(at, group), :]) for p in range(2)]
    rights = [split(b_ref[p, pl.ds(at, group), :]) for p in range(2)]
    left = [f.astype(F32) for pair in feeds for f in (pair[0], pair[1], pair[0])]
    right = [f.astype(F32) for pair in rights for f in (pair[0], pair[0], pair[1])]
    left = jnp.concatenate(left, 0).astype(BF16)
    right = jnp.concatenate(right, 0)
    stream = lax.broadcasted_iota(jnp.int32, right.shape, 0) % group
    for g in range(0, group, 2):
        pair = jnp.concatenate([jnp.where(stream == g + i, right, 0.0) for i in range(2)], 1)
        outer = lax.dot_general(
            left, pair.astype(BF16), (((0,), (0,)), ((), ())), preferred_element_type=F32
        )
        for i in range(2):
            scaled = state_ref[at + g + i].astype(F32) * decay_ref[g + i][:, None, :]
            own = outer[:, i * width : (i + 1) * width].reshape(heads, head, width)
            out_ref[g + i] = (scaled + own).astype(out_ref.dtype)


def state_write(feeds, b, decay, state):
    streams, heads, head, width = state.shape
    group = 8
    whole = pl.BlockSpec(memory_space=pltpu.VMEM)
    return pl.pallas_call(
        state_write_body,
        out_shape=jax.ShapeDtypeStruct(state.shape, state.dtype),
        grid=(streams // group,),
        in_specs=[
            whole,
            whole,
            pl.BlockSpec((group, heads, width), lambda i: (i, 0, 0)),
            whole,
        ],
        out_specs=pl.BlockSpec((group, heads, head, width), lambda i: (i, 0, 0, 0)),
        compiler_params=params(),
        cost_estimate=cost(32 * state.size, 4 * state.size),
        name="state_write",
    )(feeds, b, decay, state)


def output_tiles(distances, lhs_ref, weight_refs, out_ref):
    width = out_ref.shape[2] // 256 * 256
    tile = min(width, 512)
    for j, distance in enumerate(distances):
        for t in range(0, width, tile):
            at = pl.multiple_of((lax.axis_index("head") ^ distance) * width + t, tile)
            acc, start = 0.0, 0
            for weight_ref in weight_refs:
                stop = start + weight_ref.shape[0]
                acc += jnp.dot(
                    lhs_ref[:, start:stop],
                    weight_ref[:, pl.ds(at, tile)],
                    preferred_element_type=F32,
                )
                start = stop
            out_ref[j, :, t : t + tile] = acc.astype(out_ref.dtype)


LANES = 128


def put_lanes(values, out_ref, j):
    lane = lax.broadcasted_iota(jnp.int32, (values.shape[0], LANES), 1)
    tail = jnp.zeros(lane.shape, F32)
    for i in range(3):
        term = values.astype(BF16).astype(F32)
        tail = jnp.where(lane == i, term, tail)
        values = values - term
    out_ref[j, :, out_ref.shape[2] - LANES :] = tail.astype(out_ref.dtype)


def meet_body(met_ref, own_ref, squares_ref, out_ref, total_ref):
    count = met_ref.shape[0]
    width = own_ref.shape[2]
    total = squares_ref[...] + join_lanes(met_ref[0, :, width:])
    total_ref[...] = total
    for j in range(count):
        both = met_ref[j, :, :width].astype(F32) + own_ref[j].astype(F32)
        out_ref[j, :, :width] = both.astype(out_ref.dtype)
        put_lanes(total, out_ref, j)


def meet(met, own, squares):
    whole = pl.BlockSpec(memory_space=pltpu.VMEM)
    return pl.pallas_call(
        meet_body,
        out_shape=(
            jax.ShapeDtypeStruct(met.shape, met.dtype),
            jax.ShapeDtypeStruct(squares.shape, squares.dtype),
        ),
        in_specs=[whole] * 3,
        out_specs=(whole, whole),
        compiler_params=params(),
        cost_estimate=cost(met.size, 6 * met.size),
        name="meet",
    )(met, own, squares)


def join_lanes(values):
    return jnp.sum(values.astype(F32), -1, keepdims=True)


def output_first_body(distances, terms, model_width, *refs):
    term_refs = refs[:terms]
    sums_ref, result_ref, scale_ref, *weight_refs, out_ref, lhs_ref, squares_ref = refs[terms:]
    total = sum(t[...].astype(F32) for t in term_refs) * inverse_of(sums_ref, model_width)
    gated = result_ref[...] * silu(total)
    squares_ref[...] = jnp.sum(gated * gated, -1, keepdims=True)
    lhs_ref[...] = (gated * scale_ref[...]).astype(lhs_ref.dtype)
    output_tiles(distances, lhs_ref, weight_refs, out_ref)
    for j in range(len(distances)):
        put_lanes(squares_ref[...], out_ref, j)


def output_rest_body(distances, lhs_ref, after_ref, *refs):
    output_tiles(distances, lhs_ref, refs[:-1], refs[-1])


def output_parts(distances, weights, width, operands, model_width=None):
    first = model_width is not None
    rows, depth = operands[0].shape
    count = len(distances)
    whole = pl.BlockSpec(memory_space=pltpu.VMEM)
    specs = [whole] * (len(operands) + len(weights))
    body = functools.partial(output_rest_body, distances)
    extra = LANES if first else 0
    out_shape = [jax.ShapeDtypeStruct((count, rows, width + extra), BF16)]
    if first:
        body = functools.partial(output_first_body, distances, len(operands) - 3, model_width)
        out_shape += [
            jax.ShapeDtypeStruct((rows, depth), BF16),
            jax.ShapeDtypeStruct((rows, 1), F32),
        ]
    else:
        specs[1] = pl.BlockSpec(memory_space=pl.ANY)
    return pl.pallas_call(
        body,
        out_shape=tuple(out_shape),
        in_specs=specs,
        out_specs=(whole,) * len(out_shape),
        compiler_params=params(),
        cost_estimate=cost(2 * rows * depth * width * count, 2 * depth * width * count),
        name="output_first" if first else "output_rest",
    )(*operands, *[in_vmem(w) for w in weights])


def split(values):
    high = values.astype(BF16)
    return high, (values - high.astype(F32)).astype(BF16)


def on_device(
    hidden,
    input_norm_scale,
    projection_signal,
    projection_gate,
    projection_step,
    projection_input_output,
    step_bias,
    head_decay_rate,
    head_skip_weight,
    gated_norm_scale,
    adapter_down_weight,
    adapter_up_weight,
    output_weight,
    scan_state,
    stream_tenant_index,
    live_block_rows,
):
    streams, positions, feature_width = hidden.shape
    rows = streams * positions
    heads_n = lax.axis_size("head")
    rows_n = lax.axis_size("row")
    model_width = feature_width * heads_n
    depth, inner = projection_signal.shape
    inner_width = inner * heads_n

    wide = jnp.swapaxes(hidden, 0, 1).astype(F32)
    scaled = (wide * input_norm_scale).astype(BF16)
    scaled_flat = scaled.reshape(rows, feature_width)

    squares = jnp.sum(wide * wide, -1).reshape(rows, 1)
    sums, up_rows = adapt(stream_tenant_index, scaled_flat, squares, adapter_down_weight, adapter_up_weight)

    own = group_of_own(2) == 0
    sums, own = lax.optimization_barrier((sums, own))
    weights = load(sums, [], projection_signal, projection_input_output, projection_gate)
    signal_weights = (*weights[:2], projection_step.T)
    middle = output_weight.shape[0] // 2
    if heads_n == rows_n and len(bits_of(rows_n)) == 2:
        turn = [
            (h * rows_n + r, (r ^ 2) * rows_n + h) for h in range(heads_n) for r in range(rows_n)
        ]
        turned = [lax.ppermute(scaled[p], ("head", "row"), turn) for p in range(positions)]
        turned, _ = lax.optimization_barrier((turned, weights[0]))
        crossed = [swap(part, "head", 2) for part in turned]

        def order(distance):
            return [
                (lambda d=d: lax.axis_index("head") ^ 2 ^ d, p)
                for d in (distance, distance ^ 1)
                for p in range(positions)
            ]

        near = turned + [swap(part, "head", 1) for part in turned]
        (out_early,) = load(turned[0], [], (output_weight, 0, middle))
        crossed, _ = lax.optimization_barrier((crossed, out_early))
        far = crossed + [swap(part, "head", 1) for part in crossed]
        near_send, near_keep, near_lhs = project_signal(near, order(0), 2, *signal_weights, crossed[0])
        near_other = swap(near_send, "row", 1)
        far_send, far_keep, far_lhs = project_signal(far, order(2), 2, *signal_weights, near_send)
        far_other = swap(far_send, "row", 1)
        sums, _ = lax.optimization_barrier((sums, far_send))
        sums = sum_over(sums, "head")
        gate_send, gate_keep = project_gate(rows, [near_lhs, far_lhs], weights[2], far_send)
        gate_own, gate_far = [swap(part, "row", 1) for part in jnp.split(gate_send, 2, 0)]
        pick = [(near_keep, far_keep), (near_other, far_other)]
        last_send = sum(jnp.where(own, f, n).astype(F32) for n, f in pick).astype(BF16)
        last_send, sums = lax.optimization_barrier((last_send, sums))
        last_other = [swap(part, "row", 2) for part in jnp.split(last_send, 2, 1)]
        (out_late,) = load(last_send, [], (output_weight, middle, middle))
        signal_terms = [jnp.where(own, n, f)[0] for n, f in pick]
        signal_terms = [jnp.concatenate(last_other, 1)[0]] + signal_terms
        gate_far, _ = lax.optimization_barrier((gate_far, last_other[0]))
        gate_last = (gate_far.astype(F32) + gate_keep[1:].astype(F32)).astype(BF16)
        gate_terms = [swap_halves(gate_last, "row", 2, 1)[0], gate_own[0], gate_keep[0]]
        gate_last, out_late = lax.optimization_barrier((gate_last, out_late))
    else:
        features = lax.all_gather(scaled_flat, "head", axis=1, tiled=True)
        blocks = lax.all_to_all(features, "row", split_axis=1, concat_axis=0, tiled=True)
        blocks = blocks.reshape(rows_n, rows, depth)
        blocks = [blocks[i] for i in range(rows_n)]
        order = [(lambda i=i: i, 0) for i in range(rows_n)]
        send, keep, lhs = project_signal(blocks, order, rows_n, *signal_weights, sums)
        received = swap(send, "row", 1)
        gate_send, gate_keep = project_gate(rows, [lhs], weights[2], send)
        sums = sum_over(sums, "head")
        keep, out_early, out_late = load(
            gate_send, [keep], (output_weight, 0, middle), (output_weight, middle, middle)
        )
        signal_terms, _ = scatter_rows(received, keep, "row")
        gate_terms, gate_last = scatter_rows(swap(gate_send, "row", 1), gate_keep, "row")
    out_weights = [out_early, out_late]

    result, feeds, bgate, both, state = recur(
        model_width,
        gate_last,
        live_block_rows,
        signal_terms,
        sums,
        up_rows,
        step_bias,
        head_decay_rate,
        head_skip_weight,
        scan_state,
    )

    distances = list(range(heads_n))
    first, out_lhs, gate_squares = output_parts(
        distances[3::4],
        out_weights,
        feature_width,
        [*gate_terms, sums, result, gated_norm_scale[None]],
        model_width,
    )
    (second,) = output_parts(
        distances[2::4] + distances[1::4], out_weights, feature_width, [out_lhs, first]
    )
    half = second.shape[0] // 2
    send, gate_squares = meet(swap(first, "head", 1), second, gate_squares)
    (rest,) = output_parts(distances[0::4], out_weights, feature_width, [out_lhs, send])
    feeds, _ = lax.optimization_barrier((feeds, rest))
    kept = [swap(second[half:], "head", 1), rest]
    if len(bits_of(heads_n)) == 2:
        received = swap_halves(send, "head", 2, 1)
        mixer = sum(t[0].astype(F32) for t in [received[..., :feature_width]] + kept)
        gate_squares = gate_squares + join_lanes(received[0, :, feature_width:])
    else:
        received = swap(send[..., :feature_width], "head", 2)
        mixer, _ = scatter_rows(received, kept, "head", done=2)
        mixer = sum(t.astype(F32) for t in mixer)
        for distance in bits_of(heads_n)[1:]:
            gate_squares = gate_squares + swap(gate_squares, "head", distance)
    mixer = mixer * lax.rsqrt(gate_squares / inner_width + EPSILON)
    mixer = mixer.reshape(positions, streams, feature_width)
    live = jnp.arange(streams) < live_block_rows[0]
    mixed = (wide + jnp.where(live[:, None], mixer, 0.0)).astype(BF16)

    spread = jnp.broadcast_to(both[..., None], both.shape + (bgate.shape[-1],))
    new_state = state_write(feeds, bgate, spread, state)
    return (jnp.swapaxes(mixed, 0, 1), new_state)


def solution(mesh):
    in_specs = (
        P(("rep", "row"), None, "head"),
        P("head"),
        P("row", "head"),
        P("row", "head"),
        P("row", "head"),
        P("row", None),
        P("head"),
        P("head"),
        P("head"),
        P("head"),
        P("row", "head", None),
        P("row", None, "head"),
        P("head", None),
        P(("rep", "row"), "head", None, None),
        P(("rep", "row")),
        P(("rep", "row")),
    )
    out_specs = (P(("rep", "row"), None, "head"), P(("rep", "row"), "head", None, None))
    return jax.shard_map(
        on_device, mesh=mesh, in_specs=in_specs, out_specs=out_specs, check_vma=False
    )
```

```python
import functools

import jax
import jax.numpy as jnp
from jax import lax
from jax.experimental import pallas as pl
from jax.experimental.pallas import tpu as pltpu
from jax.sharding import PartitionSpec as P

BF16 = jnp.bfloat16
EPSILON = 1e-05
F32 = jnp.float32
VMEM_GRANT = 12 * 1024 * 1024


def swap(values, axis, distance):
    size = lax.axis_size(axis)
    return lax.ppermute(values, axis, [(i, i ^ distance) for i in range(size)])


def swap_halves(values, axis, distance, dim):
    return jnp.concatenate([swap(v, axis, distance) for v in jnp.split(values, 2, dim)], dim)


def bits_of(size):
    return [1 << i for i in range(size.bit_length() - 1)]


def sum_over(values, axis):
    for distance in bits_of(lax.axis_size(axis)):
        values = values + swap(values, axis, distance)
    return values


def reverse_bits(value, size):
    bits = size.bit_length() - 1
    return sum(((value >> i) & 1) << (bits - 1 - i) for i in range(bits))


def params(**more):
    return pltpu.CompilerParams(vmem_limit_bytes=VMEM_GRANT, **more)


def cost(flops, size):
    return pl.CostEstimate(flops=int(flops), bytes_accessed=int(size), transcendentals=0)


def in_hbm(values):
    return pltpu.with_memory_space_constraint(values, pltpu.HBM)


def in_vmem(values):
    return pltpu.with_memory_space_constraint(values, pltpu.VMEM)


def load_body(spans, after_ref, *refs):
    count = len(spans)
    sources, targets, semaphores = refs[:count], refs[count : 2 * count], refs[2 * count]
    copies = []
    for source, target, (start, rows, parts) in zip(sources, targets, spans):
        step = rows // parts
        for i in range(parts):
            copies.append(
                pltpu.make_async_copy(
                    source.at[pl.ds(start + i * step, step)],
                    target.at[pl.ds(i * step, step)],
                    semaphores.at[len(copies)],
                )
            )
    for copy in copies:
        copy.start()
    for copy in copies:
        copy.wait()


def load(after, passed, *weights):
    weights = [w if isinstance(w, tuple) else (w, 0, w.shape[0]) for w in weights]
    shapes = [p.shape for p in passed] + [(rows, *w.shape[1:]) for w, _, rows in weights]
    spans = [(0, p.shape[0], 1) for p in passed]
    spans += [(start, rows, 8 if rows % 128 == 0 else 1) for _, start, rows in weights]
    size = sum(rows * w.shape[1] * w.dtype.itemsize for w, _, rows in weights)
    return pl.pallas_call(
        functools.partial(load_body, spans),
        out_shape=tuple(pltpu.VMEM(shape, BF16) for shape in shapes),
        in_specs=[pl.BlockSpec(memory_space=pl.ANY)] * (1 + len(shapes)),
        out_specs=tuple(pl.BlockSpec(memory_space=pltpu.VMEM) for _ in shapes),
        scratch_shapes=[pltpu.SemaphoreType.DMA((sum(parts for _, _, parts in spans),))],
        compiler_params=params(),
        cost_estimate=cost(0, 2 * size),
        name="load",
    )(after, *passed, *[in_hbm(w) for w, _, _ in weights])


def own_columns(rows, streams, rank):
    row = lax.broadcasted_iota(jnp.int32, (rows, streams * rank), 0) % streams
    return row == lax.broadcasted_iota(jnp.int32, (rows, streams * rank), 1) // rank


def adapt_body(tenant_ref, scaled_ref, squares_ref, down_ref, up_ref, sums_ref, up_rows_ref, *scratch):
    down_rows_ref, semaphores = scratch
    rank = down_ref.shape[1]
    streams = tenant_ref.shape[0]
    rows = scaled_ref.shape[0]
    first = lax.axis_index("row") * down_ref.shape[0]
    downs, ups = [], []
    for s in range(streams):
        at = pl.ds(s * rank, rank)
        tenant = tenant_ref[s] - first
        downs.append(
            pltpu.make_async_copy(down_ref.at[tenant], down_rows_ref.at[at, :], semaphores.at[s])
        )
        ups.append(
            pltpu.make_async_copy(
                up_ref.at[tenant], up_rows_ref.at[at, :], semaphores.at[streams + s]
            )
        )
    for copy in downs + ups:
        copy.start()
    for copy in downs:
        copy.wait()
    every = lax.dot_general(
        scaled_ref[...],
        down_rows_ref[...],
        (((1,), (1,)), ((), ())),
        preferred_element_type=F32,
    )
    own = jnp.where(own_columns(rows, streams, rank), every, 0.0)
    fold = lax.broadcasted_iota(jnp.int32, (streams * rank, rank), 0) % rank
    fold = (fold == lax.broadcasted_iota(jnp.int32, (streams * rank, rank), 1)).astype(BF16)
    high, rest = split(own)
    middle, low = rest, (own - high.astype(F32) - rest.astype(F32)).astype(BF16)
    folded = sum(jnp.dot(x, fold, preferred_element_type=F32) for x in (high, middle, low))
    sums_ref[:, :rank] = folded
    sums_ref[:, rank:] = squares_ref[...]
    for copy in ups:
        copy.wait()


def adapt(tenants, scaled, squares, down, up):
    streams = tenants.shape[0]
    rows, depth = scaled.shape
    rank, inner = up.shape[1:]
    whole = pl.BlockSpec(memory_space=pltpu.VMEM)
    anywhere = pl.BlockSpec(memory_space=pl.ANY)
    return pl.pallas_call(
        adapt_body,
        out_shape=(
            jax.ShapeDtypeStruct((rows, rank + 1), F32),
            pltpu.VMEM((streams * rank, inner), BF16),
        ),
        in_specs=[pl.BlockSpec(memory_space=pltpu.SMEM), whole, whole, anywhere, anywhere],
        out_specs=(whole, whole),
        scratch_shapes=[
            pltpu.VMEM((streams * rank, depth), BF16),
            pltpu.SemaphoreType.DMA((2 * streams,)),
        ],
        compiler_params=params(),
        cost_estimate=cost(2 * rows * depth * streams * rank, 2 * streams * rank * (depth + inner)),
        name="adapt",
    )(tenants, scaled, squares, in_hbm(jnp.swapaxes(down, 1, 2)), in_hbm(up))


def project_signal_body(owners, order, *refs):
    blocks, refs = refs[: len(order)], refs[len(order) :]
    weight_ref, mix_ref, step_ref, send_ref, keep_ref, lhs_ref, semaphores = refs
    rows = blocks[0].shape[0]
    parts = len(blocks) // owners
    copies = []
    for i, block in enumerate(blocks):
        owner, part = order[i]
        away = (owner() ^ lax.axis_index("row")) % owners
        at = pl.multiple_of((away * parts + part) * rows, rows)
        copies.append(
            pltpu.make_async_copy(block, lhs_ref.at[pl.ds(at, rows), :], semaphores.at[i])
        )
    for copy in copies:
        copy.start()
    for copy in copies:
        copy.wait()
    lhs = lhs_ref[...]

    def put(acc, start):
        step = send_ref.shape[1]
        for k in range(owners):
            target = send_ref if k % 2 else keep_ref
            target[k // 2, :, start : start + acc.shape[1]] = acc[k * step : (k + 1) * step].astype(
                target.dtype
            )

    columns = weight_ref.shape[1]
    tile = min(columns, 512)
    for t in range(0, columns, tile):
        put(jnp.dot(lhs, weight_ref[:, t : t + tile], preferred_element_type=F32), t)
    put(jnp.dot(lhs, mix_ref[...], preferred_element_type=F32), columns)
    acc = lax.dot_general(lhs, step_ref[...], (((1,), (1,)), ((), ())), preferred_element_type=F32)
    put(acc, columns + mix_ref.shape[1])


def project_signal(blocks, order, owners, weight, mix, step, after):
    pieces = len(blocks)
    depth = blocks[0].shape[1]
    rows = pieces * blocks[0].shape[0]
    columns = weight.shape[1] + mix.shape[1] + step.shape[0]
    half = jax.ShapeDtypeStruct((owners // 2, rows // owners, columns), BF16)
    whole = pl.BlockSpec(memory_space=pltpu.VMEM)
    anywhere = pl.BlockSpec(memory_space=pl.ANY)

    def body(*refs):
        project_signal_body(owners, order, *refs[:pieces], *refs[pieces + 1 :])

    return pl.pallas_call(
        body,
        out_shape=(half, half, jax.ShapeDtypeStruct((rows, depth), BF16)),
        in_specs=[anywhere] * (pieces + 1) + [whole] * 3,
        out_specs=(whole,) * 3,
        scratch_shapes=[pltpu.SemaphoreType.DMA((pieces,))],
        compiler_params=params(),
        cost_estimate=cost(2 * rows * depth * columns, 2 * depth * columns),
        name="project_signal",
    )(*blocks, after, in_vmem(weight), in_vmem(mix), step)


def project_gate_body(groups, *refs):
    lhs_refs, refs = refs[:groups], refs[groups:]
    weight_ref, after_ref, send_ref, keep_ref = refs
    rows = send_ref.shape[1]
    columns = weight_ref.shape[1]
    tile = min(columns, 512)
    first = group_of_own(groups)
    for t in range(0, columns, tile):
        for g, lhs_ref in enumerate(lhs_refs):
            acc = jnp.dot(lhs_ref[...], weight_ref[:, t : t + tile], preferred_element_type=F32)
            pairs = lhs_ref.shape[0] // (2 * rows)
            for k in range(2 * pairs):
                target = send_ref if k % 2 else keep_ref
                at = (first ^ g) * pairs + k // 2
                target[at, :, t : t + tile] = acc[k * rows : (k + 1) * rows].astype(target.dtype)


def group_of_own(groups):
    if groups == 1:
        return 0
    return (lax.axis_index("head") ^ 2 ^ lax.axis_index("row")) >> 1


def project_gate(rows, lhs, weight, after):
    count = sum(part.shape[0] for part in lhs) // rows
    columns = weight.shape[1]
    half = jax.ShapeDtypeStruct((count // 2, rows, columns), BF16)
    whole = pl.BlockSpec(memory_space=pltpu.VMEM)
    return pl.pallas_call(
        functools.partial(project_gate_body, len(lhs)),
        out_shape=(half, half),
        in_specs=[whole] * (len(lhs) + 1) + [pl.BlockSpec(memory_space=pl.ANY)],
        out_specs=(whole,) * 2,
        compiler_params=params(),
        cost_estimate=cost(2 * count * rows * lhs[0].shape[1] * columns, 2 * weight.size),
        name="project_gate",
    )(*lhs, in_vmem(weight), after)


def scatter_rows(received, keep, axis, done=1):
    send = received
    terms = [received] + (keep if isinstance(keep, list) else [keep])
    for distance in bits_of(lax.axis_size(axis))[done:]:
        send = sum(t[1::2].astype(F32) for t in terms).astype(BF16)
        terms = [swap(send, axis, distance)] + [t[0::2] for t in terms]
    return [t[0] for t in terms], send


def softplus(values):
    return jnp.maximum(values, 0.0) + jnp.log1p(jnp.exp(-jnp.abs(values)))


def silu(values):
    return values / (1.0 + jnp.exp(-values))


def inverse_of(sums_ref, width):
    return lax.rsqrt(sums_ref[:, sums_ref.shape[1] - 1 :] / width + EPSILON)


def recur_body(
    terms,
    group,
    model_width,
    live_ref,
    *refs,
):
    term_refs = refs[:terms]
    sums_ref, up_ref, bias_ref, rate_ref, skip_ref, source_ref, _ = refs[terms : terms + 7]
    result_ref, feeds_ref, b_ref, both_ref, state_ref, *scratch = refs[terms + 7 :]
    c_ref, read_ref, spread_ref, signal_ref, semaphores = scratch
    heads, head, width = state_ref.shape[1:]
    streams, inner = feeds_ref.shape[1:]
    step = pl.program_id(0)

    def fetch(i):
        at = pl.ds(i * group, group)
        return pltpu.make_async_copy(source_ref.at[at], state_ref.at[at], semaphores.at[i])

    @pl.when(step == 0)
    def _():
        for i in range(streams // group):
            fetch(i).start()
        rows = sums_ref.shape[0]
        rank = sums_ref.shape[1] - 1
        inverse = inverse_of(sums_ref, model_width)
        lowrank = (sums_ref[:, :rank] * inverse).astype(BF16)
        repeat = lax.broadcasted_iota(jnp.int32, (rank, streams * rank), 1) % rank
        repeat = (repeat == lax.broadcasted_iota(jnp.int32, (rank, streams * rank), 0)).astype(BF16)
        every = jnp.dot(lowrank, repeat, preferred_element_type=F32)
        own = jnp.where(own_columns(rows, streams, rank), every, 0.0).astype(BF16)
        adapted = jnp.dot(own, up_ref[...], preferred_element_type=F32)
        total = sum(t[...].astype(F32) for t in term_refs) * inverse
        signal_ref[...] = silu(total[:, :inner] + adapted)
        gates = silu(total[:, inner : inner + 2 * width])
        steps_dt = softplus(total[:, inner + 2 * width :] + bias_ref[...])
        b = [gates[p * streams : (p + 1) * streams, :width] for p in range(2)]
        c = [gates[p * streams : (p + 1) * streams, width:] for p in range(2)]
        for p in range(2):
            b_ref[p] = b[p]
            c_ref[p] = c[p]
        live = lax.broadcasted_iota(jnp.int32, (streams, heads), 0) < live_ref[0]
        dt = [steps_dt[p * streams : (p + 1) * streams] for p in range(2)]
        decay = [jnp.where(live, jnp.exp(-d * rate_ref[...]), 1.0) for d in dt]
        fed = [jnp.where(live, d, 0.0) for d in dt]

        def match(i, j):
            return jnp.sum(b[i] * c[j], -1, keepdims=True)

        both = decay[0] * decay[1]
        both_ref[...] = both
        late = decay[1] * fed[0]
        skip = skip_ref[...]
        factors = jnp.concatenate(
            [
                decay[0],
                both,
                fed[0] * match(0, 0) + skip,
                fed[1] * match(1, 1) + skip,
                late * match(0, 1),
                late,
                fed[1],
            ],
            0,
        )
        high, low = split(factors)
        place = lax.broadcasted_iota(jnp.int32, (heads, inner), 1) // head
        ones = (place == lax.broadcasted_iota(jnp.int32, (heads, inner), 0)).astype(BF16)
        spread_ref[...] = jnp.dot(high, ones, preferred_element_type=F32) + jnp.dot(
            low, ones, preferred_element_type=F32
        )

    fetch(step).wait()
    at = pl.multiple_of(step * group, group)
    c = jnp.concatenate([c_ref[p, pl.ds(at, group), :] for p in range(2)], 0)
    lhs = jnp.concatenate(split(c), 0)
    for g in range(group):
        state = state_ref[at + g].reshape(inner, width)
        found = lax.dot_general(lhs, state, (((1,), (1,)), ((), ())), preferred_element_type=F32)
        for p in range(2):
            row = p * group + g
            low = 2 * group + row
            read_ref[p, pl.ds(at + g, 1), :] = found[row : row + 1] + found[low : low + 1]

    @pl.when(step == pl.num_programs(0) - 1)
    def _():
        factor = [spread_ref[i * streams : (i + 1) * streams, :] for i in range(7)]
        first = signal_ref[:streams, :]
        second = signal_ref[streams:, :]
        result_ref[:streams, :] = factor[0] * read_ref[0] + factor[2] * first
        result_ref[streams:, :] = factor[1] * read_ref[1] + factor[4] * first + factor[3] * second
        feeds_ref[0] = factor[5] * first
        feeds_ref[1] = factor[6] * second


def recur(model_width, after, live_rows, terms, sums, up_rows, bias, rate, skip, state):
    streams, heads, head, width = state.shape
    group = 8
    inner = heads * head
    rows = 2 * streams
    whole = pl.BlockSpec(memory_space=pltpu.VMEM)
    return pl.pallas_call(
        functools.partial(recur_body, len(terms), group, model_width),
        out_shape=(
            jax.ShapeDtypeStruct((rows, inner), F32),
            jax.ShapeDtypeStruct((2, streams, inner), F32),
            jax.ShapeDtypeStruct((2, streams, width), F32),
            jax.ShapeDtypeStruct((streams, heads), F32),
            pltpu.VMEM(state.shape, state.dtype),
        ),
        grid=(streams // group,),
        in_specs=[pl.BlockSpec(memory_space=pltpu.SMEM)]
        + [whole] * (len(terms) + 5)
        + [pl.BlockSpec(memory_space=pl.ANY)] * 2,
        out_specs=(whole,) * 5,
        scratch_shapes=[
            pltpu.VMEM((2, streams, width), F32),
            pltpu.VMEM((2, streams, inner), F32),
            pltpu.VMEM((7 * streams, inner), F32),
            pltpu.VMEM((rows, inner), F32),
            pltpu.SemaphoreType.DMA((streams // group,)),
        ],
        compiler_params=params(),
        cost_estimate=cost(64 * state.size, 2 * state.size + 32 * rows * inner),
        name="recur",
    )(
        live_rows,
        *terms,
        sums,
        up_rows,
        bias[None],
        rate[None],
        skip[None],
        in_hbm(state),
        after,
    )


def state_write_body(feeds_ref, b_ref, decay_ref, state_ref, out_ref):
    group, heads, head, width = out_ref.shape
    at = pl.multiple_of(pl.program_id(0) * group, group)
    feeds = [split(feeds_ref[p, pl.ds(at, group), :]) for p in range(2)]
    rights = [split(b_ref[p, pl.ds(at, group), :]) for p in range(2)]
    left = [f.astype(F32) for pair in feeds for f in (pair[0], pair[1], pair[0])]
    right = [f.astype(F32) for pair in rights for f in (pair[0], pair[0], pair[1])]
    left = jnp.concatenate(left, 0).astype(BF16)
    right = jnp.concatenate(right, 0)
    stream = lax.broadcasted_iota(jnp.int32, right.shape, 0) % group
    for g in range(0, group, 2):
        pair = jnp.concatenate([jnp.where(stream == g + i, right, 0.0) for i in range(2)], 1)
        outer = lax.dot_general(
            left, pair.astype(BF16), (((0,), (0,)), ((), ())), preferred_element_type=F32
        )
        for i in range(2):
            scaled = state_ref[at + g + i].astype(F32) * decay_ref[g + i][:, None, :]
            own = outer[:, i * width : (i + 1) * width].reshape(heads, head, width)
            out_ref[g + i] = (scaled + own).astype(out_ref.dtype)


def state_write(feeds, b, decay, state):
    streams, heads, head, width = state.shape
    group = 8
    whole = pl.BlockSpec(memory_space=pltpu.VMEM)
    return pl.pallas_call(
        state_write_body,
        out_shape=jax.ShapeDtypeStruct(state.shape, state.dtype),
        grid=(streams // group,),
        in_specs=[
            whole,
            whole,
            pl.BlockSpec((group, heads, width), lambda i: (i, 0, 0)),
            whole,
        ],
        out_specs=pl.BlockSpec((group, heads, head, width), lambda i: (i, 0, 0, 0)),
        compiler_params=params(),
        cost_estimate=cost(32 * state.size, 4 * state.size),
        name="state_write",
    )(feeds, b, decay, state)


def output_tiles(distances, lhs_ref, weight_refs, out_ref):
    width = out_ref.shape[2] // 256 * 256
    tile = min(width, 512)
    for j, distance in enumerate(distances):
        for t in range(0, width, tile):
            at = pl.multiple_of((lax.axis_index("head") ^ distance) * width + t, tile)
            acc, start = 0.0, 0
            for weight_ref in weight_refs:
                stop = start + weight_ref.shape[0]
                acc += jnp.dot(
                    lhs_ref[:, start:stop],
                    weight_ref[:, pl.ds(at, tile)],
                    preferred_element_type=F32,
                )
                start = stop
            out_ref[j, :, t : t + tile] = acc.astype(out_ref.dtype)


LANES = 128


def put_lanes(values, out_ref, j):
    lane = lax.broadcasted_iota(jnp.int32, (values.shape[0], LANES), 1)
    tail = jnp.zeros(lane.shape, F32)
    for i in range(3):
        term = values.astype(BF16).astype(F32)
        tail = jnp.where(lane == i, term, tail)
        values = values - term
    out_ref[j, :, out_ref.shape[2] - LANES :] = tail.astype(out_ref.dtype)


def meet_body(met_ref, own_ref, squares_ref, out_ref, total_ref):
    count = met_ref.shape[0]
    width = own_ref.shape[2]
    total = squares_ref[...] + join_lanes(met_ref[0, :, width:])
    total_ref[...] = total
    for j in range(count):
        both = met_ref[j, :, :width].astype(F32) + own_ref[j].astype(F32)
        out_ref[j, :, :width] = both.astype(out_ref.dtype)
        put_lanes(total, out_ref, j)


def meet(met, own, squares):
    whole = pl.BlockSpec(memory_space=pltpu.VMEM)
    return pl.pallas_call(
        meet_body,
        out_shape=(
            jax.ShapeDtypeStruct(met.shape, met.dtype),
            jax.ShapeDtypeStruct(squares.shape, squares.dtype),
        ),
        in_specs=[whole] * 3,
        out_specs=(whole, whole),
        compiler_params=params(),
        cost_estimate=cost(met.size, 6 * met.size),
        name="meet",
    )(met, own, squares)


def join_lanes(values):
    return jnp.sum(values.astype(F32), -1, keepdims=True)


def output_first_body(distances, terms, model_width, *refs):
    term_refs = refs[:terms]
    sums_ref, result_ref, scale_ref, *weight_refs, out_ref, lhs_ref, squares_ref = refs[terms:]
    total = sum(t[...].astype(F32) for t in term_refs) * inverse_of(sums_ref, model_width)
    gated = result_ref[...] * silu(total)
    squares_ref[...] = jnp.sum(gated * gated, -1, keepdims=True)
    lhs_ref[...] = (gated * scale_ref[...]).astype(lhs_ref.dtype)
    output_tiles(distances, lhs_ref, weight_refs, out_ref)
    for j in range(len(distances)):
        put_lanes(squares_ref[...], out_ref, j)


def output_rest_body(distances, lhs_ref, after_ref, *refs):
    output_tiles(distances, lhs_ref, refs[:-1], refs[-1])


def output_parts(distances, weights, width, operands, model_width=None):
    first = model_width is not None
    rows, depth = operands[0].shape
    count = len(distances)
    whole = pl.BlockSpec(memory_space=pltpu.VMEM)
    specs = [whole] * (len(operands) + len(weights))
    body = functools.partial(output_rest_body, distances)
    extra = LANES if first else 0
    out_shape = [jax.ShapeDtypeStruct((count, rows, width + extra), BF16)]
    if first:
        body = functools.partial(output_first_body, distances, len(operands) - 3, model_width)
        out_shape += [
            jax.ShapeDtypeStruct((rows, depth), BF16),
            jax.ShapeDtypeStruct((rows, 1), F32),
        ]
    else:
        specs[1] = pl.BlockSpec(memory_space=pl.ANY)
    return pl.pallas_call(
        body,
        out_shape=tuple(out_shape),
        in_specs=specs,
        out_specs=(whole,) * len(out_shape),
        compiler_params=params(),
        cost_estimate=cost(2 * rows * depth * width * count, 2 * depth * width * count),
        name="output_first" if first else "output_rest",
    )(*operands, *[in_vmem(w) for w in weights])


def split(values):
    high = values.astype(BF16)
    return high, (values - high.astype(F32)).astype(BF16)


def on_device(
    hidden,
    input_norm_scale,
    projection_signal,
    projection_gate,
    projection_step,
    projection_input_output,
    step_bias,
    head_decay_rate,
    head_skip_weight,
    gated_norm_scale,
    adapter_down_weight,
    adapter_up_weight,
    output_weight,
    scan_state,
    stream_tenant_index,
    live_block_rows,
):
    streams, positions, feature_width = hidden.shape
    rows = streams * positions
    heads_n = lax.axis_size("head")
    rows_n = lax.axis_size("row")
    model_width = feature_width * heads_n
    depth, inner = projection_signal.shape
    inner_width = inner * heads_n

    wide = jnp.swapaxes(hidden, 0, 1).astype(F32)
    scaled = (wide * input_norm_scale).astype(BF16)
    scaled_flat = scaled.reshape(rows, feature_width)

    squares = jnp.sum(wide * wide, -1).reshape(rows, 1)
    sums, up_rows = adapt(stream_tenant_index, scaled_flat, squares, adapter_down_weight, adapter_up_weight)

    own = group_of_own(2) == 0
    sums, own = lax.optimization_barrier((sums, own))
    weights = load(sums, [], projection_signal, projection_input_output, projection_gate)
    signal_weights = (*weights[:2], projection_step.T)
    middle = output_weight.shape[0] // 2
    if heads_n == rows_n and len(bits_of(rows_n)) == 2:
        turn = [
            (h * rows_n + r, (r ^ 2) * rows_n + h) for h in range(heads_n) for r in range(rows_n)
        ]
        turned = lax.ppermute(scaled_flat, ("head", "row"), turn)
        turned, _ = lax.optimization_barrier((turned, weights[0]))
        crossed = swap(turned, "head", 2)

        def order(distance):
            return [
                (lambda d=d: lax.axis_index("head") ^ 2 ^ d, 0) for d in (distance, distance ^ 1)
            ]

        near = [turned, swap(turned, "head", 1)]
        (out_early,) = load(turned, [], (output_weight, 0, middle))
        crossed, _ = lax.optimization_barrier((crossed, out_early))
        far = [crossed, swap(crossed, "head", 1)]
        near_send, near_keep, near_lhs = project_signal(near, order(0), 2, *signal_weights, crossed)
        near_other = swap(near_send, "row", 1)
        far_send, far_keep, far_lhs = project_signal(far, order(2), 2, *signal_weights, near_send)
        far_other = swap(far_send, "row", 1)
        sums, _ = lax.optimization_barrier((sums, far_send))
        sums = sum_over(sums, "head")
        gate_send, gate_keep = project_gate(rows, [near_lhs, far_lhs], weights[2], far_send)
        gate_own, gate_far = [swap(part, "row", 1) for part in jnp.split(gate_send, 2, 0)]
        pick = [(near_keep, far_keep), (near_other, far_other)]
        last_send = sum(jnp.where(own, f, n).astype(F32) for n, f in pick).astype(BF16)
        last_send, sums = lax.optimization_barrier((last_send, sums))
        last_other = [swap(part, "row", 2) for part in jnp.split(last_send, 2, 1)]
        (out_late,) = load(last_send, [], (output_weight, middle, middle))
        signal_terms = [jnp.where(own, n, f)[0] for n, f in pick]
        signal_terms = [jnp.concatenate(last_other, 1)[0]] + signal_terms
        gate_far, _ = lax.optimization_barrier((gate_far, last_other[0]))
        gate_last = (gate_far.astype(F32) + gate_keep[1:].astype(F32)).astype(BF16)
        gate_terms = [swap_halves(gate_last, "row", 2, 1)[0], gate_own[0], gate_keep[0]]
        gate_last, out_late = lax.optimization_barrier((gate_last, out_late))
    else:
        features = lax.all_gather(scaled_flat, "head", axis=1, tiled=True)
        blocks = lax.all_to_all(features, "row", split_axis=1, concat_axis=0, tiled=True)
        blocks = blocks.reshape(rows_n, rows, depth)
        blocks = [blocks[i] for i in range(rows_n)]
        order = [(lambda i=i: i, 0) for i in range(rows_n)]
        send, keep, lhs = project_signal(blocks, order, rows_n, *signal_weights, sums)
        received = swap(send, "row", 1)
        gate_send, gate_keep = project_gate(rows, [lhs], weights[2], send)
        sums = sum_over(sums, "head")
        keep, out_early, out_late = load(
            gate_send, [keep], (output_weight, 0, middle), (output_weight, middle, middle)
        )
        signal_terms, _ = scatter_rows(received, keep, "row")
        gate_terms, gate_last = scatter_rows(swap(gate_send, "row", 1), gate_keep, "row")
    out_weights = [out_early, out_late]

    result, feeds, bgate, both, state = recur(
        model_width,
        gate_last,
        live_block_rows,
        signal_terms,
        sums,
        up_rows,
        step_bias,
        head_decay_rate,
        head_skip_weight,
        scan_state,
    )

    distances = list(range(heads_n))
    first, out_lhs, gate_squares = output_parts(
        distances[3::4],
        out_weights,
        feature_width,
        [*gate_terms, sums, result, gated_norm_scale[None]],
        model_width,
    )
    (second,) = output_parts(distances[2::4], out_weights, feature_width, [out_lhs, first])
    send, gate_squares = meet(swap(first, "head", 1), second, gate_squares)
    (rest,) = output_parts(
        distances[1::4] + distances[0::4], out_weights, feature_width, [out_lhs, send]
    )
    half = rest.shape[0] // 2
    feeds, _ = lax.optimization_barrier((feeds, rest))
    kept = [swap(rest[:half], "head", 1), rest[half:]]
    if len(bits_of(heads_n)) == 2:
        received = swap_halves(send, "head", 2, 1)
        mixer = sum(t[0].astype(F32) for t in [received[..., :feature_width]] + kept)
        gate_squares = gate_squares + join_lanes(received[0, :, feature_width:])
    else:
        received = swap(send[..., :feature_width], "head", 2)
        mixer, _ = scatter_rows(received, kept, "head", done=2)
        mixer = sum(t.astype(F32) for t in mixer)
        for distance in bits_of(heads_n)[1:]:
            gate_squares = gate_squares + swap(gate_squares, "head", distance)
    mixer = mixer * lax.rsqrt(gate_squares / inner_width + EPSILON)
    mixer = mixer.reshape(positions, streams, feature_width)
    live = jnp.arange(streams) < live_block_rows[0]
    mixed = (wide + jnp.where(live[:, None], mixer, 0.0)).astype(BF16)

    spread = jnp.broadcast_to(both[..., None], both.shape + (bgate.shape[-1],))
    new_state = state_write(feeds, bgate, spread, state)
    return (jnp.swapaxes(mixed, 0, 1), new_state)


def solution(mesh):
    in_specs = (
        P(("rep", "row"), None, "head"),
        P("head"),
        P("row", "head"),
        P("row", "head"),
        P("row", "head"),
        P("row", None),
        P("head"),
        P("head"),
        P("head"),
        P("head"),
        P("row", "head", None),
        P("row", None, "head"),
        P("head", None),
        P(("rep", "row"), "head", None, None),
        P(("rep", "row")),
        P(("rep", "row")),
    )
    out_specs = (P(("rep", "row"), None, "head"), P(("rep", "row"), "head", None, None))
    return jax.shard_map(
        on_device, mesh=mesh, in_specs=in_specs, out_specs=out_specs, check_vma=False
    )
```

```python
import functools

import jax
import jax.numpy as jnp
from jax import lax
from jax.experimental import pallas as pl
from jax.experimental.pallas import tpu as pltpu
from jax.sharding import PartitionSpec as P

BF16 = jnp.bfloat16
EPSILON = 1e-05
F32 = jnp.float32
VMEM_GRANT = 12 * 1024 * 1024


def swap(values, axis, distance):
    size = lax.axis_size(axis)
    return lax.ppermute(values, axis, [(i, i ^ distance) for i in range(size)])


def swap_halves(values, axis, distance, dim):
    return jnp.concatenate([swap(v, axis, distance) for v in jnp.split(values, 2, dim)], dim)


def bits_of(size):
    return [1 << i for i in range(size.bit_length() - 1)]


def sum_over(values, axis):
    for distance in bits_of(lax.axis_size(axis)):
        values = values + swap(values, axis, distance)
    return values


def reverse_bits(value, size):
    bits = size.bit_length() - 1
    return sum(((value >> i) & 1) << (bits - 1 - i) for i in range(bits))


def params(**more):
    return pltpu.CompilerParams(vmem_limit_bytes=VMEM_GRANT, **more)


def cost(flops, size):
    return pl.CostEstimate(flops=int(flops), bytes_accessed=int(size), transcendentals=0)


def in_hbm(values):
    return pltpu.with_memory_space_constraint(values, pltpu.HBM)


def in_vmem(values):
    return pltpu.with_memory_space_constraint(values, pltpu.VMEM)


def load_body(spans, after_ref, *refs):
    count = len(spans)
    sources, targets, semaphores = refs[:count], refs[count : 2 * count], refs[2 * count]
    copies = []
    for source, target, (start, rows, parts) in zip(sources, targets, spans):
        step = rows // parts
        for i in range(parts):
            copies.append(
                pltpu.make_async_copy(
                    source.at[pl.ds(start + i * step, step)],
                    target.at[pl.ds(i * step, step)],
                    semaphores.at[len(copies)],
                )
            )
    for copy in copies:
        copy.start()
    for copy in copies:
        copy.wait()


def load(after, passed, *weights):
    weights = [w if isinstance(w, tuple) else (w, 0, w.shape[0]) for w in weights]
    shapes = [p.shape for p in passed] + [(rows, *w.shape[1:]) for w, _, rows in weights]
    spans = [(0, p.shape[0], 1) for p in passed]
    spans += [(start, rows, 8 if rows % 128 == 0 else 1) for _, start, rows in weights]
    size = sum(rows * w.shape[1] * w.dtype.itemsize for w, _, rows in weights)
    return pl.pallas_call(
        functools.partial(load_body, spans),
        out_shape=tuple(pltpu.VMEM(shape, BF16) for shape in shapes),
        in_specs=[pl.BlockSpec(memory_space=pl.ANY)] * (1 + len(shapes)),
        out_specs=tuple(pl.BlockSpec(memory_space=pltpu.VMEM) for _ in shapes),
        scratch_shapes=[pltpu.SemaphoreType.DMA((sum(parts for _, _, parts in spans),))],
        compiler_params=params(),
        cost_estimate=cost(0, 2 * size),
        name="load",
    )(after, *passed, *[in_hbm(w) for w, _, _ in weights])


def own_columns(rows, streams, rank):
    row = lax.broadcasted_iota(jnp.int32, (rows, streams * rank), 0) % streams
    return row == lax.broadcasted_iota(jnp.int32, (rows, streams * rank), 1) // rank


def adapt_body(tenant_ref, scaled_ref, squares_ref, down_ref, up_ref, sums_ref, up_rows_ref, *scratch):
    down_rows_ref, semaphores = scratch
    rank = down_ref.shape[1]
    streams = tenant_ref.shape[0]
    rows = scaled_ref.shape[0]
    first = lax.axis_index("row") * down_ref.shape[0]
    downs, ups = [], []
    for s in range(streams):
        at = pl.ds(s * rank, rank)
        tenant = tenant_ref[s] - first
        downs.append(
            pltpu.make_async_copy(down_ref.at[tenant], down_rows_ref.at[at, :], semaphores.at[s])
        )
        ups.append(
            pltpu.make_async_copy(
                up_ref.at[tenant], up_rows_ref.at[at, :], semaphores.at[streams + s]
            )
        )
    for copy in downs + ups:
        copy.start()
    for copy in downs:
        copy.wait()
    every = lax.dot_general(
        scaled_ref[...],
        down_rows_ref[...],
        (((1,), (1,)), ((), ())),
        preferred_element_type=F32,
    )
    own = jnp.where(own_columns(rows, streams, rank), every, 0.0)
    fold = lax.broadcasted_iota(jnp.int32, (streams * rank, rank), 0) % rank
    fold = (fold == lax.broadcasted_iota(jnp.int32, (streams * rank, rank), 1)).astype(BF16)
    high, rest = split(own)
    middle, low = rest, (own - high.astype(F32) - rest.astype(F32)).astype(BF16)
    folded = sum(jnp.dot(x, fold, preferred_element_type=F32) for x in (high, middle, low))
    sums_ref[:, :rank] = folded
    sums_ref[:, rank:] = squares_ref[...]
    for copy in ups:
        copy.wait()


def adapt(tenants, scaled, squares, down, up):
    streams = tenants.shape[0]
    rows, depth = scaled.shape
    rank, inner = up.shape[1:]
    whole = pl.BlockSpec(memory_space=pltpu.VMEM)
    anywhere = pl.BlockSpec(memory_space=pl.ANY)
    return pl.pallas_call(
        adapt_body,
        out_shape=(
            jax.ShapeDtypeStruct((rows, rank + 1), F32),
            pltpu.VMEM((streams * rank, inner), BF16),
        ),
        in_specs=[pl.BlockSpec(memory_space=pltpu.SMEM), whole, whole, anywhere, anywhere],
        out_specs=(whole, whole),
        scratch_shapes=[
            pltpu.VMEM((streams * rank, depth), BF16),
            pltpu.SemaphoreType.DMA((2 * streams,)),
        ],
        compiler_params=params(),
        cost_estimate=cost(2 * rows * depth * streams * rank, 2 * streams * rank * (depth + inner)),
        name="adapt",
    )(tenants, scaled, squares, in_hbm(jnp.swapaxes(down, 1, 2)), in_hbm(up))


def project_signal_body(owners, order, *refs):
    blocks, refs = refs[: len(order)], refs[len(order) :]
    weight_ref, mix_ref, step_ref, send_ref, keep_ref, lhs_ref, semaphores = refs
    rows = blocks[0].shape[0]
    parts = len(blocks) // owners
    copies = []
    for i, block in enumerate(blocks):
        owner, part = order[i]
        away = (owner() ^ lax.axis_index("row")) % owners
        at = pl.multiple_of((away * parts + part) * rows, rows)
        copies.append(
            pltpu.make_async_copy(block, lhs_ref.at[pl.ds(at, rows), :], semaphores.at[i])
        )
    for copy in copies:
        copy.start()
    for copy in copies:
        copy.wait()
    lhs = lhs_ref[...]

    def put(acc, start):
        step = send_ref.shape[1]
        for k in range(owners):
            target = send_ref if k % 2 else keep_ref
            target[k // 2, :, start : start + acc.shape[1]] = acc[k * step : (k + 1) * step].astype(
                target.dtype
            )

    columns = weight_ref.shape[1]
    tile = min(columns, 512)
    for t in range(0, columns, tile):
        put(jnp.dot(lhs, weight_ref[:, t : t + tile], preferred_element_type=F32), t)
    put(jnp.dot(lhs, mix_ref[...], preferred_element_type=F32), columns)
    acc = lax.dot_general(lhs, step_ref[...], (((1,), (1,)), ((), ())), preferred_element_type=F32)
    put(acc, columns + mix_ref.shape[1])


def project_signal(blocks, order, owners, weight, mix, step, after):
    pieces = len(blocks)
    depth = blocks[0].shape[1]
    rows = pieces * blocks[0].shape[0]
    columns = weight.shape[1] + mix.shape[1] + step.shape[0]
    half = jax.ShapeDtypeStruct((owners // 2, rows // owners, columns), BF16)
    whole = pl.BlockSpec(memory_space=pltpu.VMEM)
    anywhere = pl.BlockSpec(memory_space=pl.ANY)

    def body(*refs):
        project_signal_body(owners, order, *refs[:pieces], *refs[pieces + 1 :])

    return pl.pallas_call(
        body,
        out_shape=(half, half, jax.ShapeDtypeStruct((rows, depth), BF16)),
        in_specs=[anywhere] * (pieces + 1) + [whole] * 3,
        out_specs=(whole,) * 3,
        scratch_shapes=[pltpu.SemaphoreType.DMA((pieces,))],
        compiler_params=params(),
        cost_estimate=cost(2 * rows * depth * columns, 2 * depth * columns),
        name="project_signal",
    )(*blocks, after, in_vmem(weight), in_vmem(mix), step)


def project_gate_body(groups, *refs):
    lhs_refs, refs = refs[:groups], refs[groups:]
    weight_ref, after_ref, send_ref, keep_ref = refs
    rows = send_ref.shape[1]
    columns = weight_ref.shape[1]
    tile = min(columns, 512)
    first = group_of_own(groups)
    for t in range(0, columns, tile):
        for g, lhs_ref in enumerate(lhs_refs):
            acc = jnp.dot(lhs_ref[...], weight_ref[:, t : t + tile], preferred_element_type=F32)
            pairs = lhs_ref.shape[0] // (2 * rows)
            for k in range(2 * pairs):
                target = send_ref if k % 2 else keep_ref
                at = (first ^ g) * pairs + k // 2
                target[at, :, t : t + tile] = acc[k * rows : (k + 1) * rows].astype(target.dtype)


def group_of_own(groups):
    if groups == 1:
        return 0
    return (lax.axis_index("head") ^ 2 ^ lax.axis_index("row")) >> 1


def project_gate(rows, lhs, weight, after):
    count = sum(part.shape[0] for part in lhs) // rows
    columns = weight.shape[1]
    half = jax.ShapeDtypeStruct((count // 2, rows, columns), BF16)
    whole = pl.BlockSpec(memory_space=pltpu.VMEM)
    return pl.pallas_call(
        functools.partial(project_gate_body, len(lhs)),
        out_shape=(half, half),
        in_specs=[whole] * (len(lhs) + 1) + [pl.BlockSpec(memory_space=pl.ANY)],
        out_specs=(whole,) * 2,
        compiler_params=params(),
        cost_estimate=cost(2 * count * rows * lhs[0].shape[1] * columns, 2 * weight.size),
        name="project_gate",
    )(*lhs, in_vmem(weight), after)


def scatter_rows(received, keep, axis, done=1):
    send = received
    terms = [received] + (keep if isinstance(keep, list) else [keep])
    for distance in bits_of(lax.axis_size(axis))[done:]:
        send = sum(t[1::2].astype(F32) for t in terms).astype(BF16)
        terms = [swap(send, axis, distance)] + [t[0::2] for t in terms]
    return [t[0] for t in terms], send


def softplus(values):
    return jnp.maximum(values, 0.0) + jnp.log1p(jnp.exp(-jnp.abs(values)))


def silu(values):
    return values / (1.0 + jnp.exp(-values))


def inverse_of(sums_ref, width):
    return lax.rsqrt(sums_ref[:, sums_ref.shape[1] - 1 :] / width + EPSILON)


def recur_body(
    terms,
    group,
    model_width,
    live_ref,
    *refs,
):
    term_refs = refs[:terms]
    sums_ref, up_ref, bias_ref, rate_ref, skip_ref, source_ref, _ = refs[terms : terms + 7]
    result_ref, feeds_ref, b_ref, both_ref, state_ref, *scratch = refs[terms + 7 :]
    c_ref, read_ref, spread_ref, signal_ref, semaphores = scratch
    heads, head, width = state_ref.shape[1:]
    streams, inner = feeds_ref.shape[1:]
    step = pl.program_id(0)

    def fetch(i):
        at = pl.ds(i * group, group)
        return pltpu.make_async_copy(source_ref.at[at], state_ref.at[at], semaphores.at[i])

    @pl.when(step == 0)
    def _():
        for i in range(streams // group):
            fetch(i).start()
        rows = sums_ref.shape[0]
        rank = sums_ref.shape[1] - 1
        inverse = inverse_of(sums_ref, model_width)
        lowrank = (sums_ref[:, :rank] * inverse).astype(BF16)
        repeat = lax.broadcasted_iota(jnp.int32, (rank, streams * rank), 1) % rank
        repeat = (repeat == lax.broadcasted_iota(jnp.int32, (rank, streams * rank), 0)).astype(BF16)
        every = jnp.dot(lowrank, repeat, preferred_element_type=F32)
        own = jnp.where(own_columns(rows, streams, rank), every, 0.0).astype(BF16)
        adapted = jnp.dot(own, up_ref[...], preferred_element_type=F32)
        total = sum(t[...].astype(F32) for t in term_refs) * inverse
        signal_ref[...] = silu(total[:, :inner] + adapted)
        gates = silu(total[:, inner : inner + 2 * width])
        steps_dt = softplus(total[:, inner + 2 * width :] + bias_ref[...])
        b = [gates[p * streams : (p + 1) * streams, :width] for p in range(2)]
        c = [gates[p * streams : (p + 1) * streams, width:] for p in range(2)]
        for p in range(2):
            b_ref[p] = b[p]
            c_ref[p] = c[p]
        live = lax.broadcasted_iota(jnp.int32, (streams, heads), 0) < live_ref[0]
        dt = [steps_dt[p * streams : (p + 1) * streams] for p in range(2)]
        decay = [jnp.where(live, jnp.exp(-d * rate_ref[...]), 1.0) for d in dt]
        fed = [jnp.where(live, d, 0.0) for d in dt]

        def match(i, j):
            return jnp.sum(b[i] * c[j], -1, keepdims=True)

        both = decay[0] * decay[1]
        both_ref[...] = both
        late = decay[1] * fed[0]
        skip = skip_ref[...]
        factors = jnp.concatenate(
            [
                decay[0],
                both,
                fed[0] * match(0, 0) + skip,
                fed[1] * match(1, 1) + skip,
                late * match(0, 1),
                late,
                fed[1],
            ],
            0,
        )
        high, low = split(factors)
        place = lax.broadcasted_iota(jnp.int32, (heads, inner), 1) // head
        ones = (place == lax.broadcasted_iota(jnp.int32, (heads, inner), 0)).astype(BF16)
        spread_ref[...] = jnp.dot(high, ones, preferred_element_type=F32) + jnp.dot(
            low, ones, preferred_element_type=F32
        )

    fetch(step).wait()
    at = pl.multiple_of(step * group, group)
    c = jnp.concatenate([c_ref[p, pl.ds(at, group), :] for p in range(2)], 0)
    lhs = jnp.concatenate(split(c), 0)
    for g in range(group):
        state = state_ref[at + g].reshape(inner, width)
        found = lax.dot_general(lhs, state, (((1,), (1,)), ((), ())), preferred_element_type=F32)
        for p in range(2):
            row = p * group + g
            low = 2 * group + row
            read_ref[p, pl.ds(at + g, 1), :] = found[row : row + 1] + found[low : low + 1]

    @pl.when(step == pl.num_programs(0) - 1)
    def _():
        factor = [spread_ref[i * streams : (i + 1) * streams, :] for i in range(7)]
        first = signal_ref[:streams, :]
        second = signal_ref[streams:, :]
        result_ref[:streams, :] = factor[0] * read_ref[0] + factor[2] * first
        result_ref[streams:, :] = factor[1] * read_ref[1] + factor[4] * first + factor[3] * second
        feeds_ref[0] = factor[5] * first
        feeds_ref[1] = factor[6] * second


def recur(model_width, after, live_rows, terms, sums, up_rows, bias, rate, skip, state):
    streams, heads, head, width = state.shape
    group = 8
    inner = heads * head
    rows = 2 * streams
    whole = pl.BlockSpec(memory_space=pltpu.VMEM)
    return pl.pallas_call(
        functools.partial(recur_body, len(terms), group, model_width),
        out_shape=(
            jax.ShapeDtypeStruct((rows, inner), F32),
            jax.ShapeDtypeStruct((2, streams, inner), F32),
            jax.ShapeDtypeStruct((2, streams, width), F32),
            jax.ShapeDtypeStruct((streams, heads), F32),
            pltpu.VMEM(state.shape, state.dtype),
        ),
        grid=(streams // group,),
        in_specs=[pl.BlockSpec(memory_space=pltpu.SMEM)]
        + [whole] * (len(terms) + 5)
        + [pl.BlockSpec(memory_space=pl.ANY)] * 2,
        out_specs=(whole,) * 5,
        scratch_shapes=[
            pltpu.VMEM((2, streams, width), F32),
            pltpu.VMEM((2, streams, inner), F32),
            pltpu.VMEM((7 * streams, inner), F32),
            pltpu.VMEM((rows, inner), F32),
            pltpu.SemaphoreType.DMA((streams // group,)),
        ],
        compiler_params=params(),
        cost_estimate=cost(64 * state.size, 2 * state.size + 32 * rows * inner),
        name="recur",
    )(
        live_rows,
        *terms,
        sums,
        up_rows,
        bias[None],
        rate[None],
        skip[None],
        in_hbm(state),
        after,
    )


def state_write_body(feeds_ref, b_ref, decay_ref, state_ref, out_ref):
    group, heads, head, width = out_ref.shape
    at = pl.multiple_of(pl.program_id(0) * group, group)
    feeds = [split(feeds_ref[p, pl.ds(at, group), :]) for p in range(2)]
    rights = [split(b_ref[p, pl.ds(at, group), :]) for p in range(2)]
    left = [f.astype(F32) for pair in feeds for f in (pair[0], pair[1], pair[0])]
    right = [f.astype(F32) for pair in rights for f in (pair[0], pair[0], pair[1])]
    left = jnp.concatenate(left, 0).astype(BF16)
    right = jnp.concatenate(right, 0)
    stream = lax.broadcasted_iota(jnp.int32, right.shape, 0) % group
    for g in range(0, group, 2):
        pair = jnp.concatenate([jnp.where(stream == g + i, right, 0.0) for i in range(2)], 1)
        outer = lax.dot_general(
            left, pair.astype(BF16), (((0,), (0,)), ((), ())), preferred_element_type=F32
        )
        for i in range(2):
            scaled = state_ref[at + g + i].astype(F32) * decay_ref[g + i][:, None, :]
            own = outer[:, i * width : (i + 1) * width].reshape(heads, head, width)
            out_ref[g + i] = (scaled + own).astype(out_ref.dtype)


def state_write(feeds, b, decay, state):
    streams, heads, head, width = state.shape
    group = 8
    whole = pl.BlockSpec(memory_space=pltpu.VMEM)
    return pl.pallas_call(
        state_write_body,
        out_shape=jax.ShapeDtypeStruct(state.shape, state.dtype),
        grid=(streams // group,),
        in_specs=[
            whole,
            whole,
            pl.BlockSpec((group, heads, width), lambda i: (i, 0, 0)),
            whole,
        ],
        out_specs=pl.BlockSpec((group, heads, head, width), lambda i: (i, 0, 0, 0)),
        compiler_params=params(),
        cost_estimate=cost(32 * state.size, 4 * state.size),
        name="state_write",
    )(feeds, b, decay, state)


def output_tiles(distances, lhs_ref, weight_refs, out_ref):
    width = out_ref.shape[2] // 256 * 256
    tile = min(width, 512)
    for j, distance in enumerate(distances):
        for t in range(0, width, tile):
            at = pl.multiple_of((lax.axis_index("head") ^ distance) * width + t, tile)
            acc, start = 0.0, 0
            for weight_ref in weight_refs:
                stop = start + weight_ref.shape[0]
                acc += jnp.dot(
                    lhs_ref[:, start:stop],
                    weight_ref[:, pl.ds(at, tile)],
                    preferred_element_type=F32,
                )
                start = stop
            out_ref[j, :, t : t + tile] = acc.astype(out_ref.dtype)


LANES = 128


def put_lanes(values, out_ref, j):
    lane = lax.broadcasted_iota(jnp.int32, (values.shape[0], LANES), 1)
    tail = jnp.zeros(lane.shape, F32)
    for i in range(3):
        term = values.astype(BF16).astype(F32)
        tail = jnp.where(lane == i, term, tail)
        values = values - term
    out_ref[j, :, out_ref.shape[2] - LANES :] = tail.astype(out_ref.dtype)


def meet_body(met_ref, own_ref, squares_ref, out_ref, total_ref):
    count = met_ref.shape[0]
    width = own_ref.shape[2]
    total = squares_ref[...] + join_lanes(met_ref[0, :, width:])
    total_ref[...] = total
    for j in range(count):
        both = met_ref[j, :, :width].astype(F32) + own_ref[j].astype(F32)
        out_ref[j, :, :width] = both.astype(out_ref.dtype)
        put_lanes(total, out_ref, j)


def meet(met, own, squares):
    whole = pl.BlockSpec(memory_space=pltpu.VMEM)
    return pl.pallas_call(
        meet_body,
        out_shape=(
            jax.ShapeDtypeStruct(met.shape, met.dtype),
            jax.ShapeDtypeStruct(squares.shape, squares.dtype),
        ),
        in_specs=[whole] * 3,
        out_specs=(whole, whole),
        compiler_params=params(),
        cost_estimate=cost(met.size, 6 * met.size),
        name="meet",
    )(met, own, squares)


def join_lanes(values):
    return jnp.sum(values.astype(F32), -1, keepdims=True)


def output_first_body(distances, terms, model_width, *refs):
    term_refs = refs[:terms]
    sums_ref, result_ref, scale_ref, *weight_refs, out_ref, lhs_ref, squares_ref = refs[terms:]
    total = sum(t[...].astype(F32) for t in term_refs) * inverse_of(sums_ref, model_width)
    gated = result_ref[...] * silu(total)
    squares_ref[...] = jnp.sum(gated * gated, -1, keepdims=True)
    lhs_ref[...] = (gated * scale_ref[...]).astype(lhs_ref.dtype)
    output_tiles(distances, lhs_ref, weight_refs, out_ref)
    for j in range(len(distances)):
        put_lanes(squares_ref[...], out_ref, j)


def output_rest_body(distances, lhs_ref, after_ref, *refs):
    output_tiles(distances, lhs_ref, refs[:-1], refs[-1])


def output_parts(distances, weights, width, operands, model_width=None):
    first = model_width is not None
    rows, depth = operands[0].shape
    count = len(distances)
    whole = pl.BlockSpec(memory_space=pltpu.VMEM)
    specs = [whole] * (len(operands) + len(weights))
    body = functools.partial(output_rest_body, distances)
    extra = LANES if first else 0
    out_shape = [jax.ShapeDtypeStruct((count, rows, width + extra), BF16)]
    if first:
        body = functools.partial(output_first_body, distances, len(operands) - 3, model_width)
        out_shape += [
            jax.ShapeDtypeStruct((rows, depth), BF16),
            jax.ShapeDtypeStruct((rows, 1), F32),
        ]
    else:
        specs[1] = pl.BlockSpec(memory_space=pl.ANY)
    return pl.pallas_call(
        body,
        out_shape=tuple(out_shape),
        in_specs=specs,
        out_specs=(whole,) * len(out_shape),
        compiler_params=params(),
        cost_estimate=cost(2 * rows * depth * width * count, 2 * depth * width * count),
        name="output_first" if first else "output_rest",
    )(*operands, *[in_vmem(w) for w in weights])


def split(values):
    high = values.astype(BF16)
    return high, (values - high.astype(F32)).astype(BF16)


def on_device(
    hidden,
    input_norm_scale,
    projection_signal,
    projection_gate,
    projection_step,
    projection_input_output,
    step_bias,
    head_decay_rate,
    head_skip_weight,
    gated_norm_scale,
    adapter_down_weight,
    adapter_up_weight,
    output_weight,
    scan_state,
    stream_tenant_index,
    live_block_rows,
):
    streams, positions, feature_width = hidden.shape
    rows = streams * positions
    heads_n = lax.axis_size("head")
    rows_n = lax.axis_size("row")
    model_width = feature_width * heads_n
    depth, inner = projection_signal.shape
    inner_width = inner * heads_n

    wide = jnp.swapaxes(hidden, 0, 1).astype(F32)
    scaled = (wide * input_norm_scale).astype(BF16)
    scaled_flat = scaled.reshape(rows, feature_width)

    later, _ = lax.optimization_barrier((hidden, scaled_flat))
    later = jnp.swapaxes(later, 0, 1).astype(F32)
    squares = jnp.sum(later * later, -1).reshape(rows, 1)
    sums, up_rows = adapt(stream_tenant_index, scaled_flat, squares, adapter_down_weight, adapter_up_weight)

    own = group_of_own(2) == 0
    sums, own = lax.optimization_barrier((sums, own))
    weights = load(sums, [], projection_signal, projection_input_output, projection_gate)
    signal_weights = (*weights[:2], projection_step.T)
    middle = output_weight.shape[0] // 2
    if heads_n == rows_n and len(bits_of(rows_n)) == 2:
        turn = [
            (h * rows_n + r, (r ^ 2) * rows_n + h) for h in range(heads_n) for r in range(rows_n)
        ]
        turned = lax.ppermute(scaled_flat, ("head", "row"), turn)
        turned, _ = lax.optimization_barrier((turned, weights[0]))
        crossed = swap(turned, "head", 2)

        def order(distance):
            return [
                (lambda d=d: lax.axis_index("head") ^ 2 ^ d, 0) for d in (distance, distance ^ 1)
            ]

        near = [turned, swap(turned, "head", 1)]
        (out_early,) = load(turned, [], (output_weight, 0, middle))
        crossed, _ = lax.optimization_barrier((crossed, out_early))
        far = [crossed, swap(crossed, "head", 1)]
        near_send, near_keep, near_lhs = project_signal(near, order(0), 2, *signal_weights, crossed)
        near_other = swap(near_send, "row", 1)
        far_send, far_keep, far_lhs = project_signal(far, order(2), 2, *signal_weights, near_send)
        far_other = swap(far_send, "row", 1)
        sums, _ = lax.optimization_barrier((sums, far_send))
        sums = sum_over(sums, "head")
        gate_send, gate_keep = project_gate(rows, [near_lhs, far_lhs], weights[2], far_send)
        gate_own, gate_far = [swap(part, "row", 1) for part in jnp.split(gate_send, 2, 0)]
        pick = [(near_keep, far_keep), (near_other, far_other)]
        last_send = sum(jnp.where(own, f, n).astype(F32) for n, f in pick).astype(BF16)
        last_send, sums = lax.optimization_barrier((last_send, sums))
        last_other = [swap(part, "row", 2) for part in jnp.split(last_send, 2, 1)]
        (out_late,) = load(last_send, [], (output_weight, middle, middle))
        signal_terms = [jnp.where(own, n, f)[0] for n, f in pick]
        signal_terms = [jnp.concatenate(last_other, 1)[0]] + signal_terms
        gate_far, _ = lax.optimization_barrier((gate_far, last_other[0]))
        gate_last = (gate_far.astype(F32) + gate_keep[1:].astype(F32)).astype(BF16)
        gate_terms = [swap_halves(gate_last, "row", 2, 1)[0], gate_own[0], gate_keep[0]]
        gate_last, out_late = lax.optimization_barrier((gate_last, out_late))
    else:
        features = lax.all_gather(scaled_flat, "head", axis=1, tiled=True)
        blocks = lax.all_to_all(features, "row", split_axis=1, concat_axis=0, tiled=True)
        blocks = blocks.reshape(rows_n, rows, depth)
        blocks = [blocks[i] for i in range(rows_n)]
        order = [(lambda i=i: i, 0) for i in range(rows_n)]
        send, keep, lhs = project_signal(blocks, order, rows_n, *signal_weights, sums)
        received = swap(send, "row", 1)
        gate_send, gate_keep = project_gate(rows, [lhs], weights[2], send)
        sums = sum_over(sums, "head")
        keep, out_early, out_late = load(
            gate_send, [keep], (output_weight, 0, middle), (output_weight, middle, middle)
        )
        signal_terms, _ = scatter_rows(received, keep, "row")
        gate_terms, gate_last = scatter_rows(swap(gate_send, "row", 1), gate_keep, "row")
    out_weights = [out_early, out_late]

    result, feeds, bgate, both, state = recur(
        model_width,
        gate_last,
        live_block_rows,
        signal_terms,
        sums,
        up_rows,
        step_bias,
        head_decay_rate,
        head_skip_weight,
        scan_state,
    )

    distances = list(range(heads_n))
    first, out_lhs, gate_squares = output_parts(
        distances[3::4],
        out_weights,
        feature_width,
        [*gate_terms, sums, result, gated_norm_scale[None]],
        model_width,
    )
    (second,) = output_parts(
        distances[2::4] + distances[1::4], out_weights, feature_width, [out_lhs, first]
    )
    half = second.shape[0] // 2
    send, gate_squares = meet(swap(first, "head", 1), second, gate_squares)
    (rest,) = output_parts(distances[0::4], out_weights, feature_width, [out_lhs, send])
    feeds, _ = lax.optimization_barrier((feeds, rest))
    kept = [swap(second[half:], "head", 1), rest]
    if len(bits_of(heads_n)) == 2:
        received = swap_halves(send, "head", 2, 1)
        mixer = sum(t[0].astype(F32) for t in [received[..., :feature_width]] + kept)
        gate_squares = gate_squares + join_lanes(received[0, :, feature_width:])
    else:
        received = swap(send[..., :feature_width], "head", 2)
        mixer, _ = scatter_rows(received, kept, "head", done=2)
        mixer = sum(t.astype(F32) for t in mixer)
        for distance in bits_of(heads_n)[1:]:
            gate_squares = gate_squares + swap(gate_squares, "head", distance)
    mixer = mixer * lax.rsqrt(gate_squares / inner_width + EPSILON)
    mixer = mixer.reshape(positions, streams, feature_width)
    live = jnp.arange(streams) < live_block_rows[0]
    mixed = (wide + jnp.where(live[:, None], mixer, 0.0)).astype(BF16)

    spread = jnp.broadcast_to(both[..., None], both.shape + (bgate.shape[-1],))
    new_state = state_write(feeds, bgate, spread, state)
    return (jnp.swapaxes(mixed, 0, 1), new_state)


def solution(mesh):
    in_specs = (
        P(("rep", "row"), None, "head"),
        P("head"),
        P("row", "head"),
        P("row", "head"),
        P("row", "head"),
        P("row", None),
        P("head"),
        P("head"),
        P("head"),
        P("head"),
        P("row", "head", None),
        P("row", None, "head"),
        P("head", None),
        P(("rep", "row"), "head", None, None),
        P(("rep", "row")),
        P(("rep", "row")),
    )
    out_specs = (P(("rep", "row"), None, "head"), P(("rep", "row"), "head", None, None))
    return jax.shard_map(
        on_device, mesh=mesh, in_specs=in_specs, out_specs=out_specs, check_vma=False
    )
```
